32 devices in a mesh: section: 2 (over core), tok: 16 (over z, y, x).
Axes of the slice: x: 2, y: 2, z: 4, core: 2. Of those that a mesh axis runs over, the one named last changes fastest.
Arguments:
- tokens: bfloat16 [3, 128, 16, 32, 192], P(None, 'tok'), may hold values from -6 to 6
- cotangent: bfloat16 [3, 128, 16, 32, 192], P(None, 'tok'), may hold values from -6 to 6
- ln1_gain: bfloat16 [2, 192], P('section'), may hold values from 0.25 to 1.75
- ln1_bias: bfloat16 [2, 192], P('section'), may hold values from -3 to 3
- q_weight: bfloat16 [2, 192, 192], P('section'), may hold values from -0.4375 to 0.4375
- q_bias: bfloat16 [2, 192], P('section'), may hold values from -3 to 3
- kv_weight: bfloat16 [192, 384], replicated, may hold values from -0.4375 to 0.4375
- v_bias: bfloat16 [192], replicated, may hold values from -3 to 3
- out_weight: bfloat16 [2, 192, 192], P('section'), may hold values from -1.25 to 1.25
- out_bias: bfloat16 [2, 192], P('section'), may hold values from -3 to 3
- rel_table: bfloat16 [2, 6, 343], P('section'), may hold values from -4 to 4
- ln2_gain: bfloat16 [2, 192], P('section'), may hold values from 0.25 to 1.75
- ln2_bias: bfloat16 [2, 192], P('section'), may hold values from -3 to 3
- up_weight: bfloat16 [2, 192, 768], P('section'), may hold values from -0.4375 to 0.4375
- up_bias: bfloat16 [2, 768], P('section'), may hold values from -3 to 3
- down_weight: bfloat16 [2, 768, 192], P('section'), may hold values from -0.21875 to 0.21875
- down_bias: bfloat16 [2, 192], P('section'), may hold values from -3 to 3
Outputs:
- ends: float32 [2, 3, 128, 16, 32, 192], P('section', None, 'tok')
- ln1_gain_grad: float32 [2, 192], P('section')
- ln1_bias_grad: float32 [2, 192], P('section')
- q_weight_grad: float32 [2, 192, 192], P('section')
- q_bias_grad: float32 [2, 192], P('section')
- kv_weight_grad: float32 [2, 192, 384], P('section')
- v_bias_grad: float32 [2, 192], P('section')
- out_weight_grad: float32 [2, 192, 192], P('section')
- out_bias_grad: float32 [2, 192], P('section')
- rel_table_grad: float32 [2, 6, 343], P('section')
- ln2_gain_grad: float32 [2, 192], P('section')
- ln2_bias_grad: float32 [2, 192], P('section')
- up_weight_grad: float32 [2, 192, 768], P('section')
- up_bias_grad: float32 [2, 768], P('section')
- down_weight_grad: float32 [2, 768, 192], P('section')
- down_bias_grad: float32 [2, 192], P('section')
The draws below stay inside these ranges and needn't reach their ends.
All inputs are finite; a program needn't handle non-finite values.
Results may differ from the reference program's by a relative error of at most 0.012.
The reference program's roundings to bfloat16 on the way count: a program that leaves them out, or rounds other values in their place, can miss the bound.
Values may be sent and summed in bfloat16 or wider, within the bound.
A program may use at most 512 MiB of HBM per device.

```python
import jax
import jax.numpy as jnp
from jax import lax

D = 192
HEADS = 6
HD = 32
FF = 768
WIN = 4
SHIFT = 2
MB = 3
CY = 16
CZ = 32
NX = 128


def block_scale(own_key, shape, split, low, high):
    level, own = 1.0, jax.random.fold_in(own_key, 6)
    for position, blocks in split:
        draws = jnp.exp(jax.random.uniform(jax.random.fold_in(own, position), (blocks,), jnp.float32, low / len(split), high / len(split)))
        level = level * jnp.repeat(draws, shape[position] // blocks).reshape([-1 if axis == position else 1 for axis in range(len(shape))])
    return level


def scatter_about(stream_key, extent, scale, limit, pieces=(), dtype=jnp.bfloat16):
    entries = scale * jax.random.normal(stream_key, extent, jnp.float32)
    if pieces:
        entries = entries * block_scale(stream_key, extent, pieces, -0.22, 0.18)
    return jnp.clip(entries, -limit, limit).astype(dtype)


def setup_inputs(seed: int = 0) -> dict:
    arg_keys = jax.random.split(jax.random.key(seed), 18)
    tokens = scatter_about(arg_keys[0], (MB, NX, CY, CZ, D), 1.0, 6.0, ((1, 16),))
    cotangent = scatter_about(arg_keys[1], (MB, NX, CY, CZ, D), 1.0, 6.0, ((1, 16),))
    ln1_gain = jnp.clip(1.0 + 0.15 * jax.random.normal(arg_keys[2], (2, D), jnp.float32), 0.25, 1.75).astype(jnp.bfloat16)
    ln1_bias = scatter_about(arg_keys[3], (2, D), 0.3, 3.0, ((0, 2),))
    q_weight = scatter_about(arg_keys[4], (2, D, D), D ** -0.5, 0.4375, ((0, 2),))
    q_bias = scatter_about(arg_keys[5], (2, D), 0.5, 3.0, ((0, 2),))
    kv_weight = scatter_about(arg_keys[6], (D, 2 * D), D ** -0.5, 0.4375)
    v_bias = scatter_about(arg_keys[7], (D,), 0.5, 3.0)
    out_weight = scatter_about(arg_keys[8], (2, D, D), (D // 8) ** -0.5, 1.25, ((0, 2),))
    out_bias = scatter_about(arg_keys[9], (2, D), 0.3, 3.0, ((0, 2),))
    rel_table = scatter_about(arg_keys[10], (2, HEADS, (2 * WIN - 1) ** 3), 1.0, 4.0, ((0, 2),))
    ln2_gain = jnp.clip(1.0 + 0.15 * jax.random.normal(arg_keys[11], (2, D), jnp.float32), 0.25, 1.75).astype(jnp.bfloat16)
    ln2_bias = scatter_about(arg_keys[12], (2, D), 0.3, 3.0, ((0, 2),))
    up_weight = scatter_about(arg_keys[13], (2, D, FF), D ** -0.5, 0.4375, ((0, 2),))
    up_bias = scatter_about(arg_keys[14], (2, FF), 0.5, 3.0, ((0, 2),))
    down_weight = scatter_about(arg_keys[15], (2, FF, D), FF ** -0.5, 0.21875, ((0, 2),))
    down_bias = scatter_about(arg_keys[16], (2, D), 0.3, 3.0, ((0, 2),))
    return dict(tokens=tokens, cotangent=cotangent, ln1_gain=ln1_gain, ln1_bias=ln1_bias, q_weight=q_weight, q_bias=q_bias, kv_weight=kv_weight, v_bias=v_bias, out_weight=out_weight, out_bias=out_bias, rel_table=rel_table, ln2_gain=ln2_gain, ln2_bias=ln2_bias, up_weight=up_weight, up_bias=up_bias, down_weight=down_weight, down_bias=down_bias)


eps_norm = 1e-05
mask_fill = -100.0

@jax.custom_vjp
def low(v):
    return lax.optimization_barrier(v.astype(jnp.bfloat16)).astype(jnp.float32)

@jax.custom_vjp
def low_back(v):
    return v

def low_keep(v):
    return (low(v), None)

def low_pass(kept, grad):
    return (grad,)

def back_keep(v):
    return (v, None)

def back_low(kept, grad):
    return (low(grad),)
low.defvjp(low_keep, low_pass)
low_back.defvjp(back_keep, back_low)

def matmul_high(left_side, right_side):
    return jnp.matmul(left_side, right_side, precision=lax.Precision.HIGHEST)

def layer_norm(field_rows, gain_vec, offset):
    mean_value = lax.optimization_barrier(jnp.mean(field_rows, -1, keepdims=True))
    centered = field_rows - mean_value
    return centered * lax.rsqrt(lax.optimization_barrier(jnp.mean(centered * centered, -1, keepdims=True)) + eps_norm) * gain_vec + offset

def to_windows(field_rows):
    planes, rows_y, rows_z, channels = field_rows.shape
    blocks = field_rows.reshape(planes // WIN, WIN, rows_y // WIN, WIN, rows_z // WIN, WIN, channels)
    return blocks.transpose(0, 2, 4, 1, 3, 5, 6).reshape(-1, WIN ** 3, channels)

def from_windows(windows, planes, rows_y, rows_z):
    channels = windows.shape[-1]
    blocks = windows.reshape(planes // WIN, rows_y // WIN, rows_z // WIN, WIN, WIN, WIN, channels)
    return blocks.transpose(0, 3, 1, 4, 2, 5, 6).reshape(planes, rows_y, rows_z, channels)

def relative_index():
    cell_ids = jnp.arange(WIN ** 3)
    cell_x = cell_ids // (WIN * WIN)
    cell_y = cell_ids // WIN % WIN
    cell_z = cell_ids % WIN
    span_size = 2 * WIN - 1
    return ((cell_x[:, None] - cell_x[None, :] + WIN - 1) * span_size + cell_y[:, None] - cell_y[None, :] + WIN - 1) * span_size + cell_z[:, None] - cell_z[None, :] + WIN - 1

def region_ids(coords, length):
    return (coords >= length - WIN).astype(jnp.int32) + (coords >= length - SHIFT).astype(jnp.int32)

def shift_mask():
    region_field = region_ids(jnp.arange(NX), NX)[:, None, None] * 9 + region_ids(jnp.arange(CY), CY)[None, :, None] * 3 + region_ids(jnp.arange(CZ), CZ)[None, None, :]
    win_ids = to_windows(region_field[..., None])[..., 0]
    return jnp.where(win_ids[:, :, None] == win_ids[:, None, :], 0.0, mask_fill).astype(jnp.float32)

def window_attention(queries, key_rows, value_rows, bias_table, mask_add):
    windows_count = queries.shape[0]
    heads_q = queries.reshape(windows_count, WIN ** 3, HEADS, HD)
    heads_k = key_rows.reshape(windows_count, WIN ** 3, HEADS, HD)
    heads_v = value_rows.reshape(windows_count, WIN ** 3, HEADS, HD)
    bias_full = bias_table[:, relative_index()]
    scores = jnp.einsum('wqhd,wkhd->whqk', heads_q, heads_k, precision=lax.Precision.HIGHEST) * HD ** (-0.5) + bias_full[None] + mask_add[:, None]
    scores = low_back(scores)
    soft_probs = low(jax.nn.softmax(scores, -1))
    mixed_rows = jnp.einsum('whqk,wkhd->wqhd', soft_probs, heads_v, precision=lax.Precision.HIGHEST)
    return mixed_rows.reshape(windows_count, WIN ** 3, HEADS * HD)

def block_layer(entry_field, section_index, params, skip_rows, mask_add):
    ln1_gain, ln1_bias, q_weight, q_bias, kv_weight, v_bias, out_weight, out_bias, rel_table, ln2_gain, ln2_bias, up_weight, up_bias, down_weight, down_bias = params
    planes, rows_y, rows_z, channels = entry_field.shape
    normed = low(layer_norm(entry_field, ln1_gain[section_index], ln1_bias[section_index]))
    queries = low(low_back(matmul_high(normed, q_weight[section_index]) + q_bias[section_index]))
    if skip_rows is None:
        both_rows = matmul_high(normed, kv_weight) + jnp.concatenate([jnp.zeros_like(v_bias), v_bias])
        key_rows = low(low_back(both_rows[..., :channels]))
        value_rows = low(low_back(both_rows[..., channels:]))
        shared = (key_rows, value_rows)
    else:
        key_rows, value_rows = skip_rows
        shared = None
    attended = window_attention(to_windows(queries), to_windows(key_rows), to_windows(value_rows), rel_table[section_index], mask_add)
    attended = low(low_back(from_windows(attended, planes, rows_y, rows_z)))
    middle = entry_field + low_back(matmul_high(attended, out_weight[section_index]) + out_bias[section_index])
    normed_two = low(layer_norm(middle, ln2_gain[section_index], ln2_bias[section_index]))
    pre_act = low_back(matmul_high(normed_two, up_weight[section_index]) + up_bias[section_index])
    hidden = low(jax.nn.gelu(pre_act, approximate=False))
    return (middle + low_back(matmul_high(hidden, down_weight[section_index]) + down_bias[section_index]), shared)

def network(tokens_all, params):
    mask_add = shift_mask()
    zero_mask = jnp.zeros_like(mask_add)
    outputs = []
    for batch_index in range(MB):
        encoded, shared = block_layer(tokens_all[batch_index], 0, params, None, zero_mask)
        handed = jnp.roll(low(low_back(encoded)), (-SHIFT, -SHIFT, -SHIFT), (0, 1, 2))
        skip_rows = (low_back(jnp.roll(shared[0], (-SHIFT, -SHIFT, -SHIFT), (0, 1, 2))), low_back(jnp.roll(shared[1], (-SHIFT, -SHIFT, -SHIFT), (0, 1, 2))))
        decoded, unused = block_layer(handed, 1, params, skip_rows, mask_add)
        outputs.append(jnp.roll(decoded, (SHIFT, SHIFT, SHIFT), (0, 1, 2)))
    return jnp.stack(outputs)

def reference(tokens, cotangent, ln1_gain, ln1_bias, q_weight, q_bias, kv_weight, v_bias, out_weight, out_bias, rel_table, ln2_gain, ln2_bias, up_weight, up_bias, down_weight, down_bias):
    params = tuple((item.astype(jnp.float32) for item in (ln1_gain, ln1_bias, q_weight, q_bias, kv_weight, v_bias, out_weight, out_bias, rel_table, ln2_gain, ln2_bias, up_weight, up_bias, down_weight, down_bias)))
    outputs, pullback = jax.vjp(network, tokens.astype(jnp.float32), params)
    d_tokens, d_params = pullback(cotangent.astype(jnp.float32))
    g_ln1_gain, g_ln1_bias, g_q_weight, g_q_bias, g_kv_weight, g_v_bias, g_out_weight, g_out_bias, g_rel_table, g_ln2_gain, g_ln2_bias, g_up_weight, g_up_bias, g_down_weight, g_down_bias = d_params
    return (jnp.stack([d_tokens, outputs]), g_ln1_gain, g_ln1_bias, g_q_weight, g_q_bias, jnp.stack([g_kv_weight, g_kv_weight]), jnp.stack([g_v_bias, g_v_bias]), g_out_weight, g_out_bias, g_rel_table, g_ln2_gain, g_ln2_bias, g_up_weight, g_up_bias, g_down_weight, g_down_bias)
```

```python
import functools

import jax
import jax.numpy as jnp
import numpy as np
from jax import lax
from jax.experimental import pallas as pl
from jax.experimental.pallas import tpu as pltpu
from jax.sharding import PartitionSpec as P

HEADS = 6
HD = 32
WIN = 4
SHIFT = 2
CELLS = WIN**3
SPAN = 2 * WIN - 1
HEADS_A = 4
LANES_A = HEADS_A * HD
COLS_A = HEADS_A * CELLS

eps_norm = 1e-05
mask_fill = -100.0
log2_e = 1.4426950408889634
root_half = 0.7071067811865476
inv_root_two_pi = 0.3989422804014327
scale = HD ** (-0.5)
VMEM_BYTES = 56 * 1024 * 1024

F32 = jnp.float32
BF16 = jnp.bfloat16


def nn(left, right):
    return lax.dot_general(left, right, (((1,), (0,)), ((), ())), preferred_element_type=F32)


def nt(left, right):
    return lax.dot_general(left, right, (((1,), (1,)), ((), ())), preferred_element_type=F32)


def tn(left, right):
    return lax.dot_general(left, right, (((0,), (0,)), ((), ())), preferred_element_type=F32)


def order_matrix(rows_z, rolled):
    count = 4 * rows_z
    matrix = np.zeros((count, count), np.float32)
    units = rows_z // 2
    for unit in range(units):
        for dx in range(2):
            for dy in range(2):
                for dz in range(2):
                    z = (2 * (unit + rolled) + dz) % rows_z
                    matrix[unit * 8 + dx * 4 + dy * 2 + dz, (dx * 2 + dy) * rows_z + z] = 1.0
    return matrix


def cell_coords():
    ids = np.arange(CELLS)
    x = 2 * (ids // 32) + ids // 4 % 2
    y = 2 * (ids // 16 % 2) + ids // 2 % 2
    z = 2 * (ids // 8 % 2) + ids % 2
    return x, y, z


def relative_index():
    x, y, z = cell_coords()

    def offset(c):
        return c[None, :] - c[:, None] + WIN - 1

    return (offset(x) * SPAN + offset(y)) * SPAN + offset(z)


def windows_of(pieces):
    count, rows, channels = pieces.shape
    return pieces.reshape(count, rows // 16, 16, channels).transpose(1, 0, 2, 3).reshape(-1, channels)


def pieces_of(windows):
    rows, channels = windows.shape
    return (
        windows.reshape(rows // CELLS, 4, 16, channels)
        .transpose(1, 0, 2, 3)
        .reshape(4, rows // 4, channels)
    )


def roll_rows(pieces, steps):
    return jnp.concatenate([pieces[:, steps:], pieces[:, :steps]], 1)


def normalize(rows):
    mean = jnp.mean(rows, -1, keepdims=True)
    centered = rows - mean
    inv_std = lax.rsqrt(jnp.mean(centered * centered, -1, keepdims=True) + eps_norm)
    return centered * inv_std, inv_std


def norm_back(grad_rows, unit_rows, inv_std, gain):
    scaled = grad_rows * gain
    return inv_std * (
        scaled
        - jnp.mean(scaled, -1, keepdims=True)
        - unit_rows * jnp.mean(scaled * unit_rows, -1, keepdims=True)
    )


def gelu_pair(rows):
    size = jnp.abs(rows)
    t = 1.0 / (1.0 + (0.3275911 * root_half) * size)
    bell = jnp.exp2(rows * rows * (-0.5 * log2_e))
    poly = (
        (((0.5 * 1.061405429 * t - 0.5 * 1.453152027) * t + 0.5 * 1.421413741) * t - 0.5 * 0.284496736)
        * t
        + 0.5 * 0.254829592
    ) * t
    tail = poly * bell
    upper = jnp.where(rows < 0.0, tail, 1.0 - tail)
    return rows * upper, upper + rows * bell * inv_root_two_pi


def head_masks(width):
    heads = lax.broadcasted_iota(jnp.int32, (1, width), 1) // HD
    return [jnp.where(heads == h, 1.0, 0.0).astype(BF16) for h in range(width // HD)]


def expand(rows):
    masks = head_masks(rows.shape[1])
    return jnp.concatenate([rows * mask for mask in masks], 0)


def collapse(stacked):
    width = stacked.shape[1]
    lanes = lax.broadcasted_iota(jnp.int32, (CELLS, width), 1)
    total = stacked[:CELLS]
    for h in range(1, width // HD):
        total = jnp.where(lanes >= h * HD, stacked[h * CELLS : (h + 1) * CELLS], total)
    return total


def split(rows):
    return rows[:, :LANES_A], rows[:, LANES_A:]


def attend(queries, keys, values, bias):
    q_a, q_b = split(queries)
    k_a, k_b = split(keys)
    v_a, v_b = split(values)
    scores = jnp.concatenate([nt(k_a, expand(q_a)), nt(k_b, expand(q_b))], 1)
    scores = scores * (scale * log2_e) + bias
    exponent = jnp.exp2(scores - jnp.max(scores, 0, keepdims=True))
    probs = exponent * (1.0 / jnp.sum(exponent, 0, keepdims=True))
    low = probs.astype(BF16)
    mixed = jnp.concatenate(
        [collapse(tn(low[:, :COLS_A], v_a)), collapse(tn(low[:, COLS_A:], v_b))], 1
    )
    return mixed.astype(BF16), probs


def attend_back(queries, keys, values, probs, grad_mixed):
    q_a, q_b = [expand(part) for part in split(queries)]
    k_a, k_b = split(keys)
    v_a, v_b = split(values)
    g_a, g_b = [expand(part) for part in split(grad_mixed)]
    d_probs = jnp.concatenate([nt(v_a, g_a), nt(v_b, g_b)], 1)
    d_scores = probs * (d_probs - jnp.sum(d_probs * probs, 0, keepdims=True))
    low = probs.astype(BF16)
    low_d = d_scores.astype(BF16)
    d_values = jnp.concatenate([nn(low[:, :COLS_A], g_a), nn(low[:, COLS_A:], g_b)], 1)
    d_keys = jnp.concatenate([nn(low_d[:, :COLS_A], q_a), nn(low_d[:, COLS_A:], q_b)], 1) * scale
    d_queries = (
        jnp.concatenate(
            [collapse(tn(low_d[:, :COLS_A], k_a)), collapse(tn(low_d[:, COLS_A:], k_b))], 1
        )
        * scale
    )
    return d_queries, d_keys, d_values, d_scores


def with_ones(rows):
    return jnp.concatenate([rows.T, jnp.ones((16, rows.shape[0]), BF16)], 0)


def col_sum(rows):
    return jnp.sum(rows, 0, keepdims=True)


def start_sums(first, old_refs, new_refs):
    @pl.when(pl.program_id(0) == 0)
    def _():
        for k, new in enumerate(new_refs):
            new[...] = jnp.zeros_like(new) if first else old_refs[k][...]


def restore(matrix, rows):
    high = rows.astype(BF16)
    low = (rows - high.astype(F32)).astype(BF16)
    return tn(matrix, high) + tn(matrix, low)


CHUNK = 256


def encoder_forward(
    core_ref, tok, order, vec, w_qkv, b_qkv, bias, w_out, w_up, b_up, w_down,
    send, keep, n1_out, n2_out, rs_out, qkv_out, p_out, o_out, a_out, s_out,
):
    rows_z = tok.shape[3]
    size = 4 * rows_z
    pieces = []
    for x in range(2):
        for y in range(2):
            part = tok[0, 2 * x : 2 * x + 2, 2 * y : 2 * y + 2].reshape(size, -1)
            pieces.append(nn(order[...], part))
    entry = windows_of(jnp.stack(pieces))
    unit, inv_std = normalize(entry)
    n1_out[0] = unit
    rs_out[0, :, :128] = jnp.broadcast_to(inv_std, (entry.shape[0], 128))
    left = (unit * vec[0:1] + vec[1:2]).astype(BF16)
    triple = nn(left, w_qkv[...]) + b_qkv[...]
    qkv_out[0] = triple.astype(BF16)
    for k in range(entry.shape[0] // CELLS):
        rows = slice(k * CELLS, (k + 1) * CELLS)
        mixed, probs = attend(
            qkv_out[0, rows, 0:192], qkv_out[0, rows, 256:448], qkv_out[0, rows, 512:704], bias[...]
        )
        p_out[0, k] = probs
        o_out[0, rows] = mixed
    middle = entry + nn(o_out[0], w_out[...]) + vec[4:5]
    unit, inv_std = normalize(middle)
    n2_out[0] = unit
    rs_out[0, :, 128:] = jnp.broadcast_to(inv_std, (entry.shape[0], 128))
    left = (unit * vec[2:3] + vec[3:4]).astype(BF16)
    results = []
    for k in range(entry.shape[0] // CHUNK):
        rows = slice(k * CHUNK, (k + 1) * CHUNK)
        hidden, slope = gelu_pair(nn(left[rows], w_up[...]) + b_up[...])
        hidden = hidden.astype(BF16)
        a_out[0, rows] = hidden
        s_out[0, rows] = slope
        results.append(nn(hidden, w_down[...]))
    result = middle + jnp.concatenate(results, 0) + vec[5:6]
    for field, rows in enumerate((result, triple[:, 256:448], triple[:, 512:704])):
        rolled = roll_rows(pieces_of(rows), 8).astype(BF16)
        send[0, :, field] = rolled[:2]
        keep[0, :, field] = rolled[2:]


def mlp_back(grad, grad_low, hidden, slope, left_two, unit, inv_std, w_up, w_down, vec, sums):
    g_up, g_down, g_vec = sums
    backs = []
    total_up = None
    turned = grad_low.T
    ones = with_ones(left_two)
    for k in range(grad.shape[0] // CHUNK):
        rows = slice(k * CHUNK, (k + 1) * CHUNK)
        d_pre = (nt(grad_low[rows], w_down[...]) * slope(rows)).astype(BF16)
        part = nn(ones[:, rows], d_pre)
        total_up = part if total_up is None else total_up + part
        backs.append(nt(d_pre, w_up[...]))
    g_up[...] += total_up
    g_down[...] += nn(turned, hidden)
    d_normed = jnp.concatenate(backs, 0)
    g_vec[2:3] += col_sum(d_normed * unit)
    g_vec[3:4] += col_sum(d_normed)
    g_vec[4:5] += col_sum(grad)
    return grad + norm_back(d_normed, unit, inv_std, vec[2:3])


def encoder_backward(
    first, order, vec, w_qkv, w_out, w_up, w_down,
    keep_a, keep_b, recv_a, recv_b,
    n1_in, n2_in, rs_in, qkv_in, p_in, o_in, a_in, s_in, *rest,
):
    old, (out, *sums, dqkv) = ([], rest) if first else (rest[:6], rest[6:])
    g_up, g_down, g_qkv, g_out, g_vec, g_bias = sums
    start_sums(first, old, sums)
    fields = []
    for field in range(3):
        pieces = jnp.stack(
            [recv_b[0, 0, field], recv_a[0, 0, field], keep_b[0, 0, field], keep_a[0, 0, field]]
        )
        fields.append(windows_of(pieces))
    grad_low, d_key_1, d_value_1 = fields
    grad = grad_low.astype(F32)
    unit_1, unit_2 = n1_in[0], n2_in[0]
    wide_1, wide_2 = [
        jnp.concatenate([r, r[:, :64]], 1) for r in (rs_in[0, :, :128], rs_in[0, :, 128:])
    ]
    left_1 = (unit_1 * vec[0:1] + vec[1:2]).astype(BF16)
    left_2 = (unit_2 * vec[2:3] + vec[3:4]).astype(BF16)
    d_middle = mlp_back(
        grad, grad_low, a_in[0], lambda rows: s_in[0, rows], left_2, unit_2, wide_2, w_up, w_down, vec,
        (g_up, g_down, g_vec),
    )
    branch = d_middle.astype(BF16)
    g_out[...] += nn(with_ones(o_in[0]), branch)
    d_mixed = nt(branch, w_out[...]).astype(BF16)
    d_table = None
    for k in range(grad.shape[0] // CELLS):
        rows = slice(k * CELLS, (k + 1) * CELLS)
        d_q, d_k, d_v, d_s = attend_back(
            qkv_in[0, rows, 0:192], qkv_in[0, rows, 256:448], qkv_in[0, rows, 512:704],
            p_in[0, k], d_mixed[rows],
        )
        dqkv[0, rows] = d_q.astype(BF16)
        dqkv[1, rows] = (d_k + d_key_1[rows].astype(F32)).astype(BF16)
        dqkv[2, rows] = (d_v + d_value_1[rows].astype(F32)).astype(BF16)
        d_table = d_s if d_table is None else d_table + d_s
    g_bias[...] += d_table
    ones = with_ones(left_1)
    d_normed = None
    for field in range(3):
        cols = slice(field * 256, field * 256 + 192)
        g_qkv[:, cols] += nn(ones, dqkv[field])
        part = nt(dqkv[field], w_qkv[:, cols])
        d_normed = part if d_normed is None else d_normed + part
    g_vec[0:1] += col_sum(d_normed * unit_1)
    g_vec[1:2] += col_sum(d_normed)
    result = pieces_of(d_middle + norm_back(d_normed, unit_1, wide_1, vec[0:1]))
    rows_z = out.shape[2]
    for x in range(2):
        for y in range(2):
            part = restore(order[...], result[2 * x + y])
            out[2 * x : 2 * x + 2, 2 * y : 2 * y + 2] = part.reshape(2, 2, rows_z, -1)


def decoder(
    first, core_ref, order, vec, w_q, b_q, bias, w_out, w_up, b_up, w_down,
    keep_1, keep_0, recv_1, recv_0, cot_1, cot_0, cot_r1, cot_r0, *rest,
):
    old, new = ([], rest) if first else (rest[:6], rest[6:])
    out, own, halo, *sums, p_scr, o_scr, a_scr, s_scr, dqkv = new
    g_up, g_down, g_q, g_out, g_vec, g_bias = sums
    start_sums(first, old, sums)
    fields = []
    for field in range(3):
        pieces = jnp.stack([ref[0, 0, field] for ref in (keep_1, keep_0, recv_1, recv_0)])
        fields.append(windows_of(pieces))
    entry_low, keys, values = fields
    entry = entry_low.astype(F32)
    unit_1, inv_1 = normalize(entry)
    left_1 = (unit_1 * vec[0:1] + vec[1:2]).astype(BF16)
    queries = (nn(left_1, w_q[...]) + b_q[...]).astype(BF16)
    windows = entry.shape[0] // CELLS
    for k in range(windows):
        rows = slice(k * CELLS, (k + 1) * CELLS)
        mixed, probs = attend(
            queries[rows], keys[rows], values[rows], bias[0, 1 if k == windows - 1 else 0]
        )
        p_scr[k] = probs
        o_scr[rows] = mixed
    middle = entry + nn(o_scr[...], w_out[...]) + vec[4:5]
    unit_2, inv_2 = normalize(middle)
    left_2 = (unit_2 * vec[2:3] + vec[3:4]).astype(BF16)
    results = []
    for k in range(entry.shape[0] // CHUNK):
        rows = slice(k * CHUNK, (k + 1) * CHUNK)
        hidden, slope = gelu_pair(nn(left_2[rows], w_up[...]) + b_up[...])
        hidden = hidden.astype(BF16)
        a_scr[rows] = hidden
        s_scr[rows] = slope
        results.append(nn(hidden, w_down[...]))
    result = pieces_of(middle + jnp.concatenate(results, 0) + vec[5:6])
    rows_z = out.shape[2]
    size = 4 * rows_z
    for x in range(2):
        for y in range(2):
            part = restore(order[...], result[2 * x + y])
            out[2 * x : 2 * x + 2, 2 * y : 2 * y + 2] = part.reshape(2, 2, rows_z, -1)

    cots = [
        nn(order[...], ref[0].reshape(size, -1)).astype(BF16) for ref in (cot_1, cot_0, cot_r1, cot_r0)
    ]
    grad_low = windows_of(jnp.stack(cots))
    grad = grad_low.astype(F32)
    d_middle = mlp_back(
        grad, grad_low, a_scr[...], lambda rows: s_scr[rows], left_2, unit_2, inv_2, w_up, w_down, vec,
        (g_up, g_down, g_vec),
    )
    branch = d_middle.astype(BF16)
    g_out[...] += nn(with_ones(o_scr[...]), branch)
    d_mixed = nt(branch, w_out[...]).astype(BF16)
    d_table = None
    for k in range(windows):
        rows = slice(k * CELLS, (k + 1) * CELLS)
        d_q, d_k, d_v, d_s = attend_back(
            queries[rows], keys[rows], values[rows], p_scr[k], d_mixed[rows]
        )
        dqkv[0, rows] = d_q
        dqkv[1, rows] = d_k
        dqkv[2, rows] = d_v
        d_table = d_s if d_table is None else d_table + d_s
    g_bias[...] += d_table
    d_queries = dqkv[0].astype(BF16)
    g_q[...] += nn(with_ones(left_1), d_queries)
    d_normed = nt(d_queries, w_q[...])
    g_vec[0:1] += col_sum(d_normed * unit_1)
    g_vec[1:2] += col_sum(d_normed)
    d_entry = d_middle + norm_back(d_normed, unit_1, inv_1, vec[0:1])
    for field, rows in enumerate((d_entry, dqkv[1], dqkv[2])):
        turned = roll_rows(pieces_of(rows), size - 8).astype(BF16)
        own[0, :, field] = turned[:2]
        halo[0, :, field] = turned[2:]


def whole(array):
    zeros = (0,) * array.ndim
    return pl.BlockSpec(array.shape, lambda *_: zeros)


def sums_shapes(channels, hidden, q_cols):
    return [
        jax.ShapeDtypeStruct(shape, F32)
        for shape in (
            (channels + 16, hidden),
            (channels, hidden),
            (channels + 16, q_cols),
            (channels + 16, channels),
            (8, channels),
            (CELLS, HEADS * CELLS),
        )
    ]


def cost(cells, per_cell, hbm):
    return pl.CostEstimate(
        flops=2 * cells * per_cell, bytes_accessed=hbm, transcendentals=cells * 1536
    )


params = pltpu.CompilerParams(
    dimension_semantics=("arbitrary",), vmem_limit_bytes=VMEM_BYTES
)


def run_encoder(core, tokens, batch, consts):
    _, _, rows_y, rows_z, channels = tokens.shape
    groups, size = rows_y // WIN, 4 * rows_z
    cells, windows = 4 * size, rows_z // WIN
    hidden = consts[6].shape[1]
    slab = jax.ShapeDtypeStruct((groups, 2, 3, size, channels), BF16)
    outs = [
        slab,
        slab,
        jax.ShapeDtypeStruct((groups, cells, channels), F32),
        jax.ShapeDtypeStruct((groups, cells, channels), F32),
        jax.ShapeDtypeStruct((groups, cells, 256), F32),
        jax.ShapeDtypeStruct((groups, cells, 768), BF16),
        jax.ShapeDtypeStruct((groups, windows, CELLS, HEADS * CELLS), F32),
        jax.ShapeDtypeStruct((groups, cells, channels), BF16),
        jax.ShapeDtypeStruct((groups, cells, hidden), BF16),
        jax.ShapeDtypeStruct((groups, cells, hidden), F32),
    ]

    def row(array):
        zeros = (0,) * (array.ndim - 1)
        return pl.BlockSpec((1, *array.shape[1:]), lambda i, c: (i, *zeros))

    return pl.pallas_call(
        encoder_forward,
        grid_spec=pltpu.PrefetchScalarGridSpec(
            num_scalar_prefetch=1,
            grid=(groups,),
            in_specs=[
                pl.BlockSpec(
                    (1, WIN, WIN, rows_z, channels), lambda i, c: (batch, c[0], i, 0, 0)
                ),
                *[whole(a) for a in consts],
            ],
            out_specs=[row(a) for a in outs],
        ),
        out_shape=outs,
        compiler_params=params,
        cost_estimate=cost(groups * cells, 466944, groups * cells * 7500),
        name="encoder_forward",
    )(core, tokens, *consts)


def run_encoder_back(own, halo, saved, old, consts, rows_z):
    groups, _, _, size, channels = own.shape
    hidden = consts[4].shape[1]
    first = old is None
    shapes = sums_shapes(channels, hidden, 768)
    outs = [jax.ShapeDtypeStruct((WIN, groups * WIN, rows_z, channels), F32), *shapes]

    def slab(unit):
        def place(i):
            return ((i if unit == 0 else (i + groups - 1) % groups), unit, 0, 0, 0)

        return pl.BlockSpec((1, 1, 3, size, channels), place)

    def row(array):
        zeros = (0,) * (array.ndim - 1)
        return pl.BlockSpec((1, *array.shape[1:]), lambda i: (i, *zeros))

    olds = [] if first else list(old)
    return pl.pallas_call(
        functools.partial(encoder_backward, first),
        grid=(groups,),
        in_specs=[
            *[whole(a) for a in consts],
            slab(0),
            slab(1),
            slab(0),
            slab(1),
            *[row(a) for a in saved],
            *[whole(a) for a in olds],
        ],
        out_specs=[
            pl.BlockSpec((WIN, WIN, rows_z, channels), lambda i: (0, i, 0, 0)),
            *[whole(a) for a in shapes],
        ],
        out_shape=outs,
        scratch_shapes=[pltpu.VMEM((3, 4 * size, channels), BF16)],
        compiler_params=params,
        cost_estimate=cost(groups * 4 * size, 933888, groups * 4 * size * 9000),
        name="encoder_backward",
    )(*consts, own, own, halo, halo, *saved, *olds)


def run_decoder(core, keep, recv, cotangent, cot_recv, batch, old, consts):
    groups, _, _, size, channels = keep.shape
    rows_z = size // 4
    hidden = consts[6].shape[1]
    windows = rows_z // WIN
    first = old is None
    shapes = sums_shapes(channels, hidden, channels)
    slab_shape = jax.ShapeDtypeStruct((groups, 2, 3, size, channels), BF16)
    outs = [
        jax.ShapeDtypeStruct((WIN, groups * WIN, rows_z, channels), F32),
        slab_shape,
        slab_shape,
        *shapes,
    ]

    def slab(unit):
        def place(i, c):
            return ((i if unit == 1 else (i + 1) % groups), unit, 0, 0, 0)

        return pl.BlockSpec((1, 1, 3, size, channels), place)

    def cot(unit, own):
        def place(i, c):
            y = 2 * i + 1 if unit == 1 else (2 * i + 2) % (2 * groups)
            return (batch, 2 * c[0] + 1 if own else 0, y, 0, 0)

        return pl.BlockSpec((1, 2, 2, rows_z, channels), place)

    def bias_place(i, c):
        return (i // (groups - 1), 0, 0, 0)

    specs = [whole(a) for a in consts]
    specs[4] = pl.BlockSpec((1, *consts[4].shape[1:]), bias_place)
    olds = [] if first else list(old)
    out_slab = pl.BlockSpec((1, 2, 3, size, channels), lambda i, c: (i, 0, 0, 0, 0))
    return pl.pallas_call(
        functools.partial(decoder, first),
        grid_spec=pltpu.PrefetchScalarGridSpec(
            num_scalar_prefetch=1,
            grid=(groups,),
            in_specs=[
                *specs,
                slab(1),
                slab(0),
                slab(1),
                slab(0),
                cot(1, True),
                cot(0, True),
                cot(1, False),
                cot(0, False),
                *[whole(a) for a in olds],
            ],
            out_specs=[
                pl.BlockSpec((WIN, WIN, rows_z, channels), lambda i, c: (0, i, 0, 0)),
                out_slab,
                out_slab,
                *[whole(a) for a in shapes],
            ],
            scratch_shapes=[
                pltpu.VMEM((windows, CELLS, HEADS * CELLS), F32),
                pltpu.VMEM((4 * size, channels), BF16),
                pltpu.VMEM((4 * size, hidden), BF16),
                pltpu.VMEM((4 * size, hidden), F32),
                pltpu.VMEM((3, 4 * size, channels), F32),
            ],
        ),
        out_shape=outs,
        compiler_params=params,
        cost_estimate=cost(groups * 4 * size, 1253376, groups * 4 * size * 4000),
        name="decoder",
    )(core, *consts, keep, keep, recv, recv, cotangent, cotangent, cot_recv, cot_recv, *olds)


def body(
    tokens,
    cotangent,
    ln1_gain,
    ln1_bias,
    q_weight,
    q_bias,
    kv_weight,
    v_bias,
    out_weight,
    out_bias,
    rel_table,
    ln2_gain,
    ln2_bias,
    up_weight,
    up_bias,
    down_weight,
    down_bias,
):
    batches, planes, rows_y, rows_z, channels = tokens.shape
    axes = ("section", "tok")
    core = lax.axis_index("section")
    block = lax.axis_index("tok")
    blocks = lax.axis_size("tok")
    is_encoder = core == 0
    core_arg = core.astype(jnp.int32).reshape(1)

    def device(position):
        position = position % (2 * blocks)
        return (position % 2) * blocks + position // 2

    to_previous = [(device(r), device(r - 1)) for r in range(2 * blocks)]
    to_next = [(device(r), device(r + 1)) for r in range(2 * blocks)]

    def both(array):
        return lax.all_gather(array, "section", axis=0, tiled=True)

    vec = jnp.concatenate(
        [
            v.astype(F32)[:, None]
            for v in map(both, (ln1_gain, ln1_bias, ln2_gain, ln2_bias, out_bias, down_bias))
        ],
        1,
    )
    vec = jnp.pad(vec, ((0, 0), (0, 2), (0, 0)))
    w_q, w_out, w_up, w_down = map(both, (q_weight, out_weight, up_weight, down_weight))
    b_q, b_up, table = map(both, (q_bias, up_bias, rel_table))
    b_up = b_up.astype(F32)[:, None]
    b_q = b_q.astype(F32)[:, None]
    pad = ((0, 0), (0, 256 - channels))
    w_qkv = jnp.concatenate(
        [
            jnp.pad(w, pad)
            for w in (w_q[0], kv_weight[:, :channels], kv_weight[:, channels:])
        ],
        1,
    )
    b_qkv = jnp.concatenate(
        [
            jnp.pad(b, pad)
            for b in (b_q[0], jnp.zeros((1, channels), F32), v_bias.astype(F32)[None])
        ],
        1,
    )
    index = relative_index()
    one_hot = (
        jnp.asarray(index.reshape(-1))[None, :] == jnp.arange(SPAN**3)[:, None]
    ).astype(F32)
    bias = jnp.dot(
        table.astype(F32).reshape(2 * HEADS, -1), one_hot, precision=lax.Precision.HIGHEST
    ).reshape(2, HEADS, CELLS, CELLS)
    bias = bias.transpose(0, 2, 1, 3) * log2_e
    bias_enc = bias[0].reshape(CELLS, HEADS * CELLS)
    units = np.stack([np.arange(CELLS) // 32, np.arange(CELLS) // 16 % 2, np.arange(CELLS) // 8 % 2])
    differ = units[:, :, None] != units[:, None, :]
    is_last = (core == 1) & (block == blocks - 1)
    apart = (
        (is_last & jnp.asarray(differ[0]))[None, None]
        | jnp.asarray(np.arange(2)[:, None, None, None] * differ[1] > 0)
        | jnp.asarray(np.arange(2)[None, :, None, None] * differ[2] > 0)
    )
    mask = jnp.where(apart, mask_fill * log2_e, 0.0).astype(F32)
    bias_dec = (bias[1][None, None] + mask[:, :, :, None, :]).reshape(
        2, 2, CELLS, HEADS * CELLS
    )
    order = jnp.asarray(order_matrix(rows_z, 0), BF16)
    order_rolled = jnp.asarray(order_matrix(rows_z, 1), BF16)

    half = lax.dynamic_slice_in_dim(cotangent, core * WIN, SHIFT, 1)
    cot_recv = lax.ppermute(half, axes, to_previous)

    enc_consts = (order, vec[0], w_qkv, b_qkv, bias_enc, w_out[0], w_up[0], b_up[0], w_down[0])
    enc_back_consts = (order, vec[0], w_qkv, w_out[0], w_up[0], w_down[0])
    dec_consts = (
        order_rolled, vec[1], w_q[1], b_q[1], bias_dec, w_out[1], w_up[1], b_up[1], w_down[1],
    )

    handed, saved = [], []
    for batch in range(batches):
        send, keep, *rest = run_encoder(core_arg, tokens, batch, enc_consts)
        handed.append((keep, lax.ppermute(send, axes, to_previous)))
        saved.append(rest)
    dec_sums = None
    returned, outputs, sib_outputs, halo_outputs = [], [], [], []
    to_decoder = [(t, blocks + t) for t in range(blocks)]
    to_encoder = [(blocks + t, t) for t in range(blocks)]
    to_after = [(blocks + t, blocks + (t + 1) % blocks) for t in range(blocks)]
    for batch in range(batches):
        out, own, halo, *dec_sums = run_decoder(
            core_arg, *handed[batch], cotangent, cot_recv, batch, dec_sums, dec_consts
        )
        returned.append((own, lax.ppermute(halo, axes, to_next)))
        outputs.append(out)
        halo_outputs.append(lax.ppermute(out[SHIFT:], axes, to_after))
        sib_outputs.append(lax.ppermute(out, axes, to_decoder))
    enc_sums = None
    grads, sib_grads = [], []
    for batch in range(batches):
        out, *enc_sums = run_encoder_back(
            *returned[batch], saved[batch], enc_sums, enc_back_consts, rows_z
        )
        grads.append(out)
        sib_grads.append(lax.ppermute(out, axes, to_encoder))

    ends = jnp.stack(
        [
            jnp.where(
                is_encoder,
                jnp.concatenate([grads[b], sib_grads[b]], 0),
                jnp.roll(
                    jnp.concatenate([halo_outputs[b], sib_outputs[b], outputs[b][:SHIFT]], 0),
                    SHIFT,
                    1,
                ),
            )
            for b in range(batches)
        ]
    )[None]

    def pack(sums):
        s_up, s_down, s_q, s_out, s_vec, s_bias = sums
        s_table = jnp.dot(
            s_bias.reshape(CELLS, HEADS, CELLS).transpose(1, 0, 2).reshape(HEADS, -1),
            one_hot.T,
            precision=lax.Precision.HIGHEST,
        )
        return [s_up, s_down, s_q[:, :channels], s_out, s_vec, s_table]

    enc_grads, dec_grads = pack(enc_sums), pack(dec_sums)
    kv_sums = jnp.concatenate([enc_sums[2][:, 256:448], enc_sums[2][:, 512:704]], 1)

    def flat(arrays):
        return jnp.concatenate([a.reshape(-1) for a in arrays])

    flat_enc, flat_dec = flat(enc_grads), flat(dec_grads)
    mine = jnp.where(is_encoder, flat_enc, flat_dec)
    theirs = jnp.where(is_encoder, flat_dec, flat_enc)
    swapped = lax.ppermute(theirs, "section", [(0, 1), (1, 0)])
    kv_flat = kv_sums.reshape(-1)
    kv_swapped = lax.ppermute(kv_flat, "section", [(0, 1), (1, 0)])
    total = lax.psum(jnp.concatenate([mine + swapped, kv_flat + kv_swapped]), "tok")
    parts, start = [], 0
    for array in [*enc_grads, kv_sums]:
        parts.append(total[start : start + array.size].reshape(array.shape))
        start += array.size
    t_up, t_down, t_q, t_out, t_vec, t_table, t_kv = parts
    return (
        ends,
        t_vec[0:1],
        t_vec[1:2],
        t_q[None, :channels],
        t_q[channels : channels + 1],
        t_kv[None, :channels],
        t_kv[channels : channels + 1, channels:],
        t_out[None, :channels],
        t_out[channels : channels + 1],
        t_table[None],
        t_vec[2:3],
        t_vec[3:4],
        t_up[None, :channels],
        t_up[channels : channels + 1],
        t_down.T[None],
        t_vec[4:5],
    )


def solution(mesh):
    in_specs = (
        P(None, "tok", None, None, None),
        P(None, "tok", None, None, None),
        P("section", None),
        P("section", None),
        P("section", None, None),
        P("section", None),
        P(),
        P(),
        P("section", None, None),
        P("section", None),
        P("section", None, None),
        P("section", None),
        P("section", None),
        P("section", None, None),
        P("section", None),
        P("section", None, None),
        P("section", None),
    )
    out_specs = (
        P("section", None, "tok", None, None, None),
        P("section", None),
        P("section", None),
        P("section", None, None),
        P("section", None),
        P("section", None, None),
        P("section", None),
        P("section", None, None),
        P("section", None),
        P("section", None, None),
        P("section", None),
        P("section", None),
        P("section", None, None),
        P("section", None),
        P("section", None, None),
        P("section", None),
    )
    return jax.shard_map(body, mesh=mesh, in_specs=in_specs, out_specs=out_specs, check_vma=False)
```

```python
import functools

import jax
import jax.numpy as jnp
import numpy as np
from jax import lax
from jax.experimental import pallas as pl
from jax.experimental.pallas import tpu as pltpu
from jax.sharding import PartitionSpec as P

HEADS = 6
HD = 32
WIN = 4
SHIFT = 2
CELLS = WIN**3
SPAN = 2 * WIN - 1
HEADS_A = 4
LANES_A = HEADS_A * HD
COLS_A = HEADS_A * CELLS

eps_norm = 1e-05
mask_fill = -100.0
log2_e = 1.4426950408889634
root_half = 0.7071067811865476
inv_root_two_pi = 0.3989422804014327
scale = HD ** (-0.5)
VMEM_BYTES = 56 * 1024 * 1024

F32 = jnp.float32
BF16 = jnp.bfloat16


def nn(left, right):
    return lax.dot_general(left, right, (((1,), (0,)), ((), ())), preferred_element_type=F32)


def nt(left, right):
    return lax.dot_general(left, right, (((1,), (1,)), ((), ())), preferred_element_type=F32)


def tn(left, right):
    return lax.dot_general(left, right, (((0,), (0,)), ((), ())), preferred_element_type=F32)


def order_matrix(rows_z, rolled):
    count = 4 * rows_z
    matrix = np.zeros((count, count), np.float32)
    units = rows_z // 2
    for unit in range(units):
        for dx in range(2):
            for dy in range(2):
                for dz in range(2):
                    z = (2 * (unit + rolled) + dz) % rows_z
                    matrix[unit * 8 + dx * 4 + dy * 2 + dz, (dx * 2 + dy) * rows_z + z] = 1.0
    return matrix


def cell_coords():
    ids = np.arange(CELLS)
    x = 2 * (ids // 32) + ids // 4 % 2
    y = 2 * (ids // 16 % 2) + ids // 2 % 2
    z = 2 * (ids // 8 % 2) + ids % 2
    return x, y, z


def relative_index():
    x, y, z = cell_coords()

    def offset(c):
        return c[None, :] - c[:, None] + WIN - 1

    return (offset(x) * SPAN + offset(y)) * SPAN + offset(z)


def windows_of(pieces):
    count, rows, channels = pieces.shape
    return pieces.reshape(count, rows // 16, 16, channels).transpose(1, 0, 2, 3).reshape(-1, channels)


def pieces_of(windows):
    rows, channels = windows.shape
    return (
        windows.reshape(rows // CELLS, 4, 16, channels)
        .transpose(1, 0, 2, 3)
        .reshape(4, rows // 4, channels)
    )


def roll_rows(pieces, steps):
    return jnp.concatenate([pieces[:, steps:], pieces[:, :steps]], 1)


def pack_slab(pieces):
    half = pieces.shape[1] // 2
    rest = pieces[:, :, LANES_A:]
    return jnp.concatenate(
        [pieces[:, :, :LANES_A], jnp.concatenate([rest[:, :half], rest[:, half:]], 2)], 1
    ).astype(BF16)


def unpack_slab(block):
    size = block.shape[0] * 2 // 3
    half = LANES_A // 2
    rest = jnp.concatenate([block[size:, :half], block[size:, half:]], 0)
    return jnp.concatenate([block[:size], rest], 1)


def normalize(rows):
    mean = jnp.mean(rows, -1, keepdims=True)
    centered = rows - mean
    inv_std = lax.rsqrt(jnp.mean(centered * centered, -1, keepdims=True) + eps_norm)
    return centered * inv_std, inv_std


def norm_back(grad_rows, unit_rows, inv_std, gain):
    scaled = grad_rows * gain
    return inv_std * (
        scaled
        - jnp.mean(scaled, -1, keepdims=True)
        - unit_rows * jnp.mean(scaled * unit_rows, -1, keepdims=True)
    )


def gelu_pair(rows):
    upper = 0.5 * lax.erf(rows * root_half) + 0.5
    bell = jnp.exp2(rows * rows * (-0.5 * log2_e))
    return rows * upper, upper + rows * bell * inv_root_two_pi


def head_masks(width):
    heads = lax.broadcasted_iota(jnp.int32, (1, width), 1) // HD
    return [jnp.where(heads == h, 1.0, 0.0).astype(BF16) for h in range(width // HD)]


def expand(rows):
    masks = head_masks(rows.shape[1])
    return jnp.concatenate([rows * mask for mask in masks], 0)


def collapse(stacked):
    width = stacked.shape[1]
    lanes = lax.broadcasted_iota(jnp.int32, (CELLS, width), 1)
    total = stacked[:CELLS]
    for h in range(1, width // HD):
        total = jnp.where(lanes >= h * HD, stacked[h * CELLS : (h + 1) * CELLS], total)
    return total


def split(rows):
    return rows[:, :LANES_A], rows[:, LANES_A:]


def attend(parts, bias):
    queries, keys, values = zip(*[[split(rows) for rows in part] for part in parts])
    wide = [[expand(half) for half in q] for q in queries]
    scores = [
        jnp.concatenate([nt(k[0], q[0]), nt(k[1], q[1])], 1) for k, q in zip(keys, wide)
    ]
    scores = [s * (scale * log2_e) + b for s, b in zip(scores, bias)]
    exponents = [jnp.exp2(s - jnp.max(s, 0, keepdims=True)) for s in scores]
    probs = [e * (1.0 / jnp.sum(e, 0, keepdims=True)) for e in exponents]
    low = [p.astype(BF16) for p in probs]
    mixed = [
        (tn(p[:, :COLS_A], v[0]), tn(p[:, COLS_A:], v[1])) for p, v in zip(low, values)
    ]
    mixed = [jnp.concatenate([collapse(m[0]), collapse(m[1])], 1).astype(BF16) for m in mixed]
    return mixed, probs


def attend_back(parts):
    queries, keys, values, grads = zip(
        *[[split(rows) for rows in part[:3] + part[4:]] for part in parts]
    )
    probs = [part[3] for part in parts]
    wide_g = [[expand(half) for half in g] for g in grads]
    d_probs = [
        jnp.concatenate([nt(v[0], g[0]), nt(v[1], g[1])], 1) for v, g in zip(values, wide_g)
    ]
    low = [p.astype(BF16) for p in probs]
    d_values = [
        jnp.concatenate([nn(p[:, :COLS_A], g[0]), nn(p[:, COLS_A:], g[1])], 1)
        for p, g in zip(low, wide_g)
    ]
    wide_q = [[expand(half) for half in q] for q in queries]
    d_scores = [
        p * (d - jnp.sum(d * p, 0, keepdims=True)) for p, d in zip(probs, d_probs)
    ]
    low_d = [d.astype(BF16) for d in d_scores]
    d_keys = [
        jnp.concatenate([nn(d[:, :COLS_A], q[0]), nn(d[:, COLS_A:], q[1])], 1) * scale
        for d, q in zip(low_d, wide_q)
    ]
    d_queries = [
        (tn(d[:, :COLS_A], k[0]), tn(d[:, COLS_A:], k[1])) for d, k in zip(low_d, keys)
    ]
    d_queries = [
        jnp.concatenate([collapse(d[0]), collapse(d[1])], 1) * scale for d in d_queries
    ]
    table = d_scores[0]
    for d in d_scores[1:]:
        table = table + d
    return d_queries, d_keys, d_values, table


def window_groups(count):
    return [range(k, min(k + TOGETHER, count)) for k in range(0, count, TOGETHER)]


def window_rows(k):
    return slice(k * CELLS, (k + 1) * CELLS)


def with_ones(rows):
    return jnp.concatenate([rows.T, jnp.ones((16, rows.shape[0]), BF16)], 0)


def col_sum(rows):
    return jnp.sum(rows, 0, keepdims=True)


def start_sums(first, old_refs, new_refs):
    @pl.when(pl.program_id(0) == 0)
    def _():
        for k, new in enumerate(new_refs):
            new[...] = jnp.zeros_like(new) if first else old_refs[k][...]


def restore(matrix, rows):
    high = rows.astype(BF16)
    low = (rows - high.astype(F32)).astype(BF16)
    return tn(matrix, high) + tn(matrix, low)


CHUNK = 256
TOGETHER = 4


def encoder_forward(
    cuts, core_ref, tok, order, vec, w_qkv, b_qkv, bias, w_out, w_up, b_up, w_down, *rest,
):
    cut_in, rest = rest[:cuts], rest[cuts:]
    send, keep, n1_out, n2_out, rs_out, qkv_out, p_out, o_out, a_out, s_out, *cut_out = rest
    for source, target in zip(cut_in, cut_out):
        target[...] = source[...]
    rows_z = tok.shape[3]
    size = 4 * rows_z
    pieces = []
    for x in range(2):
        for y in range(2):
            part = tok[0, 2 * x : 2 * x + 2, 2 * y : 2 * y + 2].reshape(size, -1)
            pieces.append(nn(order[...], part))
    entry = windows_of(jnp.stack(pieces))
    unit, inv_std = normalize(entry)
    n1_out[0] = unit
    rs_out[0, :, :128] = jnp.broadcast_to(inv_std, (entry.shape[0], 128))
    left = (unit * vec[0:1] + vec[1:2]).astype(BF16)
    triple = nn(left, w_qkv[...]) + b_qkv[...]
    qkv_out[0] = triple.astype(BF16)
    for together in window_groups(entry.shape[0] // CELLS):
        parts = [
            [qkv_out[0, window_rows(k), 256 * f : 256 * f + 192] for f in range(3)] for k in together
        ]
        mixed, probs = attend(parts, [bias[...]] * len(parts))
        for k, o, p in zip(together, mixed, probs):
            p_out[0, k] = p
            o_out[0, window_rows(k)] = o
    middle = entry + nn(o_out[0], w_out[...]) + vec[4:5]
    unit, inv_std = normalize(middle)
    n2_out[0] = unit
    rs_out[0, :, 128:] = jnp.broadcast_to(inv_std, (entry.shape[0], 128))
    left = (unit * vec[2:3] + vec[3:4]).astype(BF16)
    results = []
    for k in range(entry.shape[0] // CHUNK):
        rows = slice(k * CHUNK, (k + 1) * CHUNK)
        hidden, slope = gelu_pair(nn(left[rows], w_up[...]) + b_up[...])
        hidden = hidden.astype(BF16)
        a_out[0, rows] = hidden
        s_out[0, rows] = slope
        results.append(nn(hidden, w_down[...]))
    result = middle + jnp.concatenate(results, 0) + vec[5:6]
    for field, rows in enumerate((result, triple[:, 256:448], triple[:, 512:704])):
        rolled = pack_slab(roll_rows(pieces_of(rows), 8))
        send[0, :, field] = rolled[:2]
        keep[0, :, field] = rolled[2:]


def mlp_back(grad, grad_low, hidden, slope, left_two, unit, inv_std, w_up, w_down, vec, sums):
    g_up, g_down, g_vec = sums
    backs = []
    total_up = None
    turned = grad_low.T
    ones = with_ones(left_two)
    for k in range(grad.shape[0] // CHUNK):
        rows = slice(k * CHUNK, (k + 1) * CHUNK)
        d_pre = (nt(grad_low[rows], w_down[...]) * slope(rows)).astype(BF16)
        part = nn(ones[:, rows], d_pre)
        total_up = part if total_up is None else total_up + part
        backs.append(nt(d_pre, w_up[...]))
    g_up[...] += total_up
    g_down[...] += nn(turned, hidden)
    d_normed = jnp.concatenate(backs, 0)
    g_vec[2:3] += col_sum(d_normed * unit)
    g_vec[3:4] += col_sum(d_normed)
    g_vec[4:5] += col_sum(grad)
    return grad + norm_back(d_normed, unit, inv_std, vec[2:3])


def start_all(copies):
    for copy in copies:
        copy.start()


def wait_all(copies):
    for copy in copies:
        copy.wait()


def encoder_backward(
    first, batch, returns, core_ref, order, vec, w_qkv, w_out, w_up, w_down,
    y_own, y_halo, y_sib,
    keep_a, keep_b, recv_a, recv_b,
    n1_in, n2_in, rs_in, qkv_in, p_in, o_in, a_in, s_in, *rest,
):
    returned, rest = rest[:returns], rest[returns:]
    old, rest = ([], rest) if first else (rest[:8], rest[9:])
    ends, back, *sums, dqkv, buffer, out_sem, copy_sem = rest
    g_up, g_down, g_q, g_k, g_v, g_out, g_vec, g_bias = sums
    step, steps = pl.program_id(0), pl.num_programs(0)
    is_encoder = core_ref[0] == 0
    rows_y = ends.shape[2]
    slot = lax.rem(step, 2)

    def output_copies():
        copies = []
        for start, planes, ref in ((0, 2, y_halo), (2, 4, y_sib), (6, 2, y_own)):
            for half in range(2):
                rows = pl.ds(lax.rem(step * WIN + SHIFT + 2 * half, rows_y), 2)
                target = ends.at[batch, pl.ds(start, planes), rows]
                copies.append((ref.at[:, pl.ds(2 * half, 2)], target))
        return [
            pltpu.make_async_copy(source, target, copy_sem.at[k])
            for k, (source, target) in enumerate(copies)
        ]

    def gradient_copies():
        return [
            pltpu.make_async_copy(
                ref, ends.at[k, pl.ds(WIN, WIN), pl.ds(step * WIN, WIN)], copy_sem.at[8 + k]
            )
            for k, ref in enumerate(returned)
        ]

    def result_copy(index, to_ends):
        target = (
            ends.at[batch, pl.ds(0, WIN), pl.ds(index * WIN, WIN)]
            if to_ends
            else back.at[:, pl.ds(index * WIN, WIN)]
        )
        at = lax.rem(index, 2)
        return pltpu.make_async_copy(buffer.at[at], target, out_sem.at[at])

    def for_core(encoder_work, decoder_work):
        pl.when(is_encoder)(encoder_work)
        pl.when(jnp.logical_not(is_encoder))(decoder_work)

    for_core(lambda: start_all(gradient_copies()), lambda: start_all(output_copies()))
    start_sums(first, old, sums)
    fields = []
    for field in range(3):
        pieces = jnp.stack(
            [unpack_slab(ref[0, 0, field]) for ref in (recv_b, recv_a, keep_b, keep_a)]
        )
        fields.append(windows_of(pieces))
    grad_low, d_key_1, d_value_1 = fields
    grad = grad_low.astype(F32)
    unit_1, unit_2 = n1_in[0], n2_in[0]
    wide_1, wide_2 = [
        jnp.concatenate([r, r[:, :64]], 1) for r in (rs_in[0, :, :128], rs_in[0, :, 128:])
    ]
    left_1 = (unit_1 * vec[0:1] + vec[1:2]).astype(BF16)
    left_2 = (unit_2 * vec[2:3] + vec[3:4]).astype(BF16)
    d_middle = mlp_back(
        grad, grad_low, a_in[0], lambda rows: s_in[0, rows], left_2, unit_2, wide_2, w_up, w_down, vec,
        (g_up, g_down, g_vec),
    )
    branch = d_middle.astype(BF16)
    g_out[...] += nn(with_ones(o_in[0]), branch)
    d_mixed = nt(branch, w_out[...]).astype(BF16)
    d_table = None
    for together in window_groups(grad.shape[0] // CELLS):
        parts = [
            [qkv_in[0, window_rows(k), 256 * f : 256 * f + 192] for f in range(3)]
            + [p_in[0, k], d_mixed[window_rows(k)]]
            for k in together
        ]
        *d_qkv, d_s = attend_back(parts)
        for k, d_q, d_k, d_v in zip(together, *d_qkv):
            rows = window_rows(k)
            dqkv[0, rows] = d_q.astype(BF16)
            dqkv[1, rows] = (d_k + d_key_1[rows].astype(F32)).astype(BF16)
            dqkv[2, rows] = (d_v + d_value_1[rows].astype(F32)).astype(BF16)
        d_table = d_s if d_table is None else d_table + d_s
    g_bias[...] += d_table
    ones = with_ones(left_1)
    d_normed = None
    for field, g_field in enumerate((g_q, g_k, g_v)):
        cols = slice(field * 256, field * 256 + 192)
        g_field[...] += nn(ones, dqkv[field])
        part = nt(dqkv[field], w_qkv[:, cols])
        d_normed = part if d_normed is None else d_normed + part
    g_vec[0:1] += col_sum(d_normed * unit_1)
    g_vec[1:2] += col_sum(d_normed)
    result = pieces_of(d_middle + norm_back(d_normed, unit_1, wide_1, vec[0:1]))
    rows_z = ends.shape[3]

    @pl.when(step >= 2)
    def _():
        for_core(
            lambda: result_copy(step - 2, True).wait(), lambda: result_copy(step - 2, False).wait()
        )

    for x in range(2):
        for y in range(2):
            part = restore(order[...], result[2 * x + y])
            buffer[slot, 2 * x : 2 * x + 2, 2 * y : 2 * y + 2] = part.reshape(2, 2, rows_z, -1)
    for_core(lambda: result_copy(step, True).start(), lambda: result_copy(step, False).start())

    @pl.when(step == steps - 1)
    def _():
        def finish(to_ends):
            result_copy(step - 1, to_ends).wait()
            result_copy(step, to_ends).wait()

        for_core(lambda: finish(True), lambda: finish(False))

    for_core(lambda: wait_all(gradient_copies()), lambda: wait_all(output_copies()))


def decoder(
    first, core_ref, order, vec, w_q, b_q, bias, w_out, w_up, b_up, w_down,
    keep_1, keep_0, recv_1, recv_0, cot_1, cot_0, cot_r1, cot_r0, *rest,
):
    old, new = ([], rest) if first else (rest[:6], rest[6:])
    out_all, out_tail, own, halo, *sums, p_scr, o_scr, a_scr, s_scr, dqkv = new
    g_up, g_down, g_q, g_out, g_vec, g_bias = sums
    start_sums(first, old, sums)
    fields = []
    for field in range(3):
        pieces = jnp.stack([unpack_slab(ref[0, 0, field]) for ref in (keep_1, keep_0, recv_1, recv_0)])
        fields.append(windows_of(pieces))
    entry_low, keys, values = fields
    entry = entry_low.astype(F32)
    unit_1, inv_1 = normalize(entry)
    left_1 = (unit_1 * vec[0:1] + vec[1:2]).astype(BF16)
    queries = (nn(left_1, w_q[...]) + b_q[...]).astype(BF16)
    windows = entry.shape[0] // CELLS
    for together in window_groups(windows):
        parts = [[rows[window_rows(k)] for rows in (queries, keys, values)] for k in together]
        mixed, probs = attend(parts, [bias[0, 1 if k == windows - 1 else 0] for k in together])
        for k, o, p in zip(together, mixed, probs):
            p_scr[k] = p
            o_scr[window_rows(k)] = o
    middle = entry + nn(o_scr[...], w_out[...]) + vec[4:5]
    unit_2, inv_2 = normalize(middle)
    left_2 = (unit_2 * vec[2:3] + vec[3:4]).astype(BF16)
    results = []
    for k in range(entry.shape[0] // CHUNK):
        rows = slice(k * CHUNK, (k + 1) * CHUNK)
        hidden, slope = gelu_pair(nn(left_2[rows], w_up[...]) + b_up[...])
        hidden = hidden.astype(BF16)
        a_scr[rows] = hidden
        s_scr[rows] = slope
        results.append(nn(hidden, w_down[...]))
    result = pieces_of(middle + jnp.concatenate(results, 0) + vec[5:6])
    rows_z = out_all.shape[2]
    size = 4 * rows_z
    for x in range(2):
        for y in range(2):
            part = restore(order[...], result[2 * x + y]).reshape(2, 2, rows_z, -1)
            out_all[2 * x : 2 * x + 2, 2 * y : 2 * y + 2] = part
            if x == 1:
                out_tail[:, 2 * y : 2 * y + 2] = part

    cots = [
        nn(order[...], ref[0].reshape(size, -1)).astype(BF16) for ref in (cot_1, cot_0, cot_r1, cot_r0)
    ]
    grad_low = windows_of(jnp.stack(cots))
    grad = grad_low.astype(F32)
    d_middle = mlp_back(
        grad, grad_low, a_scr[...], lambda rows: s_scr[rows], left_2, unit_2, inv_2, w_up, w_down, vec,
        (g_up, g_down, g_vec),
    )
    branch = d_middle.astype(BF16)
    g_out[...] += nn(with_ones(o_scr[...]), branch)
    d_mixed = nt(branch, w_out[...]).astype(BF16)
    d_table = None
    for together in window_groups(windows):
        parts = [
            [rows[window_rows(k)] for rows in (queries, keys, values)]
            + [p_scr[k], d_mixed[window_rows(k)]]
            for k in together
        ]
        *d_qkv, d_s = attend_back(parts)
        for k, *grads in zip(together, *d_qkv):
            for f in range(3):
                dqkv[f, window_rows(k)] = grads[f]
        d_table = d_s if d_table is None else d_table + d_s
    g_bias[...] += d_table
    d_queries = dqkv[0].astype(BF16)
    g_q[...] += nn(with_ones(left_1), d_queries)
    d_normed = nt(d_queries, w_q[...])
    g_vec[0:1] += col_sum(d_normed * unit_1)
    g_vec[1:2] += col_sum(d_normed)
    d_entry = d_middle + norm_back(d_normed, unit_1, inv_1, vec[0:1])
    for field, rows in enumerate((d_entry, dqkv[1], dqkv[2])):
        turned = pack_slab(roll_rows(pieces_of(rows), size - 8))
        own[0, :, field] = turned[:2]
        halo[0, :, field] = turned[2:]


def whole(array):
    zeros = (0,) * array.ndim
    return pl.BlockSpec(array.shape, lambda *_: zeros)


def sums_shapes(channels, hidden, products):
    return [
        jax.ShapeDtypeStruct(shape, F32)
        for shape in (
            (channels + 16, hidden),
            (channels, hidden),
            *[(channels + 16, channels)] * products,
            (channels + 16, channels),
            (8, channels),
            (CELLS, HEADS * CELLS),
        )
    ]


def cost(cells, per_cell, hbm):
    return pl.CostEstimate(
        flops=2 * cells * per_cell, bytes_accessed=hbm, transcendentals=cells * 1536
    )


params = pltpu.CompilerParams(
    dimension_semantics=("arbitrary",), vmem_limit_bytes=VMEM_BYTES
)


class Layout:
    def __init__(self, channels, hidden, blocks):
        tall = channels + 16
        self.tall, self.channels = tall, channels
        self.tiles = hidden // LANES_A
        self.up = 0
        self.down = self.tiles * tall
        self.q = self.down + self.tiles * channels
        self.out = self.q + tall
        self.rest = self.out + tall
        self.kv = self.rest + tall
        self.bias = self.kv + 2 * tall
        self.end = self.bias + HEADS * CELLS // LANES_A * CELLS
        self.chunk = -(-self.end // (16 * blocks)) * 16
        self.rows = self.chunk * blocks


def fill(buffer, layout, up, down, q, out, kv, bias):
    kind, half = buffer.dtype, LANES_A // 2
    tall, channels = layout.tall, layout.channels
    for k in range(layout.tiles):
        cols = slice(k * LANES_A, (k + 1) * LANES_A)
        buffer[layout.up + k * tall : layout.up + (k + 1) * tall] = up[:, cols].astype(kind)
        buffer[layout.down + k * channels : layout.down + (k + 1) * channels] = down[
            :, cols
        ].astype(kind)
    buffer[layout.q : layout.q + tall] = q[:, :LANES_A].astype(kind)
    buffer[layout.out : layout.out + tall] = out[:, :LANES_A].astype(kind)
    rests = jnp.concatenate([q[:, LANES_A:], out[:, LANES_A:]], 1)
    buffer[layout.rest : layout.rest + tall] = rests.astype(kind)
    buffer[layout.kv : layout.kv + tall] = kv[:, :LANES_A].astype(kind)
    rests = jnp.concatenate([kv[:, LANES_A:], jnp.zeros((tall, half), F32)], 1)
    buffer[layout.kv + tall : layout.kv + 2 * tall] = rests.astype(kind)
    for k in range(HEADS * CELLS // LANES_A):
        start = layout.bias + k * CELLS
        buffer[start : start + CELLS] = bias[:, k * LANES_A : (k + 1) * LANES_A].astype(kind)
    if layout.rows > layout.end:
        buffer[layout.end :] = jnp.zeros((layout.rows - layout.end, LANES_A), kind)


MESH = pl.DeviceIdType.MESH


def sum_gradients(layout, blocks, *refs):
    enc, dec, rest = refs[:8], refs[8:14], refs[14:]
    (
        total_out, kv_out, vec_out,
        own, theirs, from_sib, low, landed, total, sib_kv, vec_send, vec_sib, vec_own, vec_landed,
        sib_send, sib_recv, send_sem, recv_sem, vec_ssem, vec_rsem, out_ssem, out_rsem,
    ) = rest
    core, me = lax.axis_index("section"), lax.axis_index("tok")
    sibling = {"section": 1 - core}

    def peer(offset):
        return lax.rem(me + offset, blocks)

    barrier = pltpu.get_barrier_semaphore()
    pl.semaphore_signal(barrier, inc=1, device_id=sibling, device_id_type=MESH)

    def greet(offset, carry):
        pl.semaphore_signal(
            barrier, inc=1, device_id={"tok": peer(offset)}, device_id_type=MESH
        )
        return carry

    lax.fori_loop(1, blocks, greet, 0)

    e_up, e_down, e_q, e_k, e_v, e_out, e_vec, e_bias = enc
    d_up, d_down, d_q, d_out, d_vec, d_bias = dec

    @pl.when(core == 0)
    def _():
        fill(theirs, layout, d_up, d_down, d_q, d_out, e_v, d_bias)
        fill(own, layout, e_up, e_down, e_q, e_out, e_k, e_bias)
        vec_send[...] = d_vec[...]
        vec_own[...] = e_vec[...]

    @pl.when(core == 1)
    def _():
        fill(theirs, layout, e_up, e_down, e_q, e_out, e_k, e_bias)
        fill(own, layout, d_up, d_down, d_q, d_out, e_v, d_bias)
        vec_send[...] = e_vec[...]
        vec_own[...] = d_vec[...]

    pl.semaphore_wait(barrier, blocks)

    def to_sibling(source, target, k):
        return pltpu.make_async_remote_copy(
            src_ref=source, dst_ref=target, send_sem=sib_send.at[k], recv_sem=sib_recv.at[k],
            device_id=sibling, device_id_type=MESH,
        )

    first = to_sibling(theirs, from_sib, 0)
    second = to_sibling(vec_send, vec_sib, 1)
    first.start()
    second.start()
    first.wait()
    second.wait()
    own[...] += from_sib[...].astype(F32)
    low[...] = own[...].astype(BF16)
    vec_own[...] += vec_sib[...]

    def rows_of(position):
        return pl.ds(pl.multiple_of(position * layout.chunk, 16), layout.chunk)

    def scatter(offset):
        return pltpu.make_async_remote_copy(
            src_ref=low.at[rows_of(peer(offset))], dst_ref=landed.at[offset],
            send_sem=send_sem.at[offset], recv_sem=recv_sem.at[offset],
            device_id={"tok": peer(offset)}, device_id_type=MESH,
        )

    def scatter_vec(offset):
        return pltpu.make_async_remote_copy(
            src_ref=vec_own, dst_ref=vec_landed.at[offset],
            send_sem=vec_ssem.at[offset], recv_sem=vec_rsem.at[offset],
            device_id={"tok": peer(offset)}, device_id_type=MESH,
        )

    def gather(offset):
        return pltpu.make_async_remote_copy(
            src_ref=total.at[rows_of(me)], dst_ref=total.at[rows_of(me)],
            send_sem=out_ssem.at[offset], recv_sem=out_rsem.at[offset],
            device_id={"tok": peer(offset)}, device_id_type=MESH,
        )

    def gathered(offset):
        rows = rows_of(lax.rem(me - offset + blocks, blocks))
        return pltpu.make_async_remote_copy(
            src_ref=total.at[rows], dst_ref=total.at[rows],
            send_sem=out_ssem.at[offset], recv_sem=out_rsem.at[offset],
            device_id={"tok": peer(offset)}, device_id_type=MESH,
        )

    def start(offset, carry):
        scatter(offset).start()
        scatter_vec(offset).start()
        return carry

    lax.fori_loop(1, blocks, start, 0)

    def add(offset, carry):
        scatter(offset).wait_recv()
        return carry + landed[offset].astype(F32)

    chunk_sum = lax.fori_loop(1, blocks, add, own[rows_of(me)])
    total[rows_of(me)] = chunk_sum.astype(BF16)

    def spread(offset, carry):
        gather(offset).start()
        return carry

    lax.fori_loop(1, blocks, spread, 0)

    def add_vec(offset, carry):
        scatter_vec(offset).wait_recv()
        return carry + vec_landed[offset]

    vec_out[...] = lax.fori_loop(1, blocks, add_vec, vec_own[...])

    def arrive(offset, carry):
        gathered(offset).wait_recv()
        return carry

    lax.fori_loop(1, blocks, arrive, 0)
    kv_rows = pl.ds(layout.kv, 2 * layout.tall)
    third = to_sibling(total.at[kv_rows], sib_kv, 2)
    third.start()
    total_out[...] = total[...]

    def drain(offset, carry):
        scatter(offset).wait_send()
        scatter_vec(offset).wait_send()
        gather(offset).wait_send()
        return carry

    lax.fori_loop(1, blocks, drain, 0)
    third.wait()
    kv_out[...] = sib_kv[...]


def run_sum(enc_sums, dec_sums, layout, blocks):
    channels = layout.channels
    rows, chunk, tall = layout.rows, layout.chunk, layout.tall
    dma = pltpu.SemaphoreType.DMA
    vmem = pl.BlockSpec(memory_space=pltpu.VMEM)
    args = [*enc_sums, *dec_sums]
    return pl.pallas_call(
        functools.partial(sum_gradients, layout, blocks),
        in_specs=[vmem] * len(args),
        out_specs=[vmem] * 3,
        out_shape=[
            jax.ShapeDtypeStruct((rows, LANES_A), BF16),
            jax.ShapeDtypeStruct((2 * tall, LANES_A), BF16),
            jax.ShapeDtypeStruct((8, channels), F32),
        ],
        scratch_shapes=[
            pltpu.VMEM((rows, LANES_A), F32),
            pltpu.VMEM((rows, LANES_A), BF16),
            pltpu.VMEM((rows, LANES_A), BF16),
            pltpu.VMEM((rows, LANES_A), BF16),
            pltpu.VMEM((blocks, chunk, LANES_A), BF16),
            pltpu.VMEM((rows, LANES_A), BF16),
            pltpu.VMEM((2 * tall, LANES_A), BF16),
            pltpu.VMEM((8, channels), F32),
            pltpu.VMEM((8, channels), F32),
            pltpu.VMEM((8, channels), F32),
            pltpu.VMEM((blocks, 8, channels), F32),
            dma((3,)),
            dma((3,)),
            *[dma((blocks,))] * 6,
        ],
        compiler_params=pltpu.CompilerParams(
            collective_id=0, has_side_effects=True, vmem_limit_bytes=VMEM_BYTES
        ),
        name="sum_gradients",
    )(*args)


def finish(layout, batches, returns, core_ref, total, sib_kv, vec, *refs):
    returned, refs = refs[:returns], refs[returns + 1 :]
    (
        ends, ln1_gain, ln1_bias, q_weight, q_bias, kv_weight, v_bias, out_weight, out_bias, bias,
        ln2_gain, ln2_bias, up_weight, up_bias, down_weight, down_bias, copy_sem,
    ) = refs
    is_encoder = core_ref[0] == 0
    step = pl.program_id(0)

    def copies():
        return [
            pltpu.make_async_copy(
                ref,
                ends.at[batches - returns + k, pl.ds(WIN, WIN), pl.ds(step * WIN, WIN)],
                copy_sem.at[k],
            )
            for k, ref in enumerate(returned)
        ]

    pl.when(is_encoder)(lambda: start_all(copies()))

    @pl.when(step == 0)
    def _():
        unpack(
            layout, is_encoder, total, sib_kv, vec, ln1_gain, ln1_bias, q_weight, q_bias, kv_weight,
            v_bias, out_weight, out_bias, bias, ln2_gain, ln2_bias, up_weight, up_bias, down_weight,
            down_bias,
        )

    pl.when(is_encoder)(lambda: wait_all(copies()))


def unpack(
    layout, is_encoder, total, sib_kv, vec, ln1_gain, ln1_bias, q_weight, q_bias, kv_weight,
    v_bias, out_weight, out_bias, bias, ln2_gain, ln2_bias, up_weight, up_bias, down_weight, down_bias,
):
    channels, tall, half = layout.channels, layout.tall, LANES_A // 2
    for row, ref in enumerate((ln1_gain, ln1_bias, ln2_gain, ln2_bias, down_bias)):
        ref[...] = vec[row : row + 1]

    def at(start, rows):
        return total[start : start + rows].astype(F32)

    for k in range(layout.tiles):
        cols = slice(k * LANES_A, (k + 1) * LANES_A)
        tile = at(layout.up + k * tall, tall)
        up_weight[:, cols] = tile[:channels]
        up_bias[:, cols] = tile[channels : channels + 1]
        down_weight[cols] = at(layout.down + k * channels, channels).T
    rest = at(layout.rest, tall)
    q = jnp.concatenate([at(layout.q, tall), rest[:, :half]], 1)
    out = jnp.concatenate([at(layout.out, tall), rest[:, half:]], 1)
    q_weight[...] = q[:channels]
    q_bias[...] = q[channels : channels + 1]
    out_weight[...] = out[:channels]
    out_bias[...] = out[channels : channels + 1]
    mine = at(layout.kv, 2 * tall)
    other = sib_kv[...].astype(F32)
    for start, side in ((0, jnp.where(is_encoder, mine, other)), (channels, jnp.where(is_encoder, other, mine))):
        side = jnp.concatenate([side[:tall], side[tall:, :half]], 1)
        kv_weight[:, start : start + channels] = side[:channels]
    v_bias[...] = side[channels : channels + 1]
    for k in range(HEADS * CELLS // LANES_A):
        bias[:, k * LANES_A : (k + 1) * LANES_A] = at(layout.bias + k * CELLS, CELLS)


def run_finish(core, total, sib_kv, vec, returned, ends, layout):
    channels = layout.channels
    hidden = layout.tiles * LANES_A
    _, _, rows_y, rows_z, _ = ends.shape
    any_spec = pl.BlockSpec(memory_space=pl.ANY)
    shapes = [
        (1, channels), (1, channels), (channels, channels), (1, channels), (channels, 2 * channels),
        (1, channels), (channels, channels), (1, channels), (CELLS, HEADS * CELLS),
        (1, channels), (1, channels), (channels, hidden), (1, hidden), (hidden, channels), (1, channels),
    ]
    shapes = [jax.ShapeDtypeStruct(shape, F32) for shape in shapes]
    return pl.pallas_call(
        functools.partial(finish, layout, ends.shape[0], len(returned)),
        grid=(rows_y // WIN,),
        in_specs=[
            pl.BlockSpec(memory_space=pltpu.SMEM),
            *[whole(a) for a in (total, sib_kv, vec)],
            *[pl.BlockSpec((WIN, WIN, rows_z, channels), lambda i: (0, i, 0, 0))] * len(returned),
            any_spec,
        ],
        out_specs=[any_spec, *[whole(a) for a in shapes]],
        out_shape=[jax.ShapeDtypeStruct(ends.shape, F32), *shapes],
        input_output_aliases={4 + len(returned): 0},
        scratch_shapes=[pltpu.SemaphoreType.DMA((len(returned),))],
        compiler_params=params,
        name="finish",
    )(core, total, sib_kv, vec, *returned, ends)


def cell_position(ids):
    x = 2 * (ids // 32) + ids // 4 % 2
    y = 2 * (ids // 16 % 2) + ids // 2 % 2
    z = 2 * (ids // 8 % 2) + ids % 2
    return (x * SPAN + y) * SPAN + z


CENTRE = (WIN - 1) * (SPAN * SPAN + SPAN + 1)
TABLE_ROW = 8


def position_matrix(odd):
    rows = lax.broadcasted_iota(jnp.int32, (256, 2 * CELLS), 0)
    ids = lax.broadcasted_iota(jnp.int32, (256, 2 * CELLS), 1) - (CELLS if odd else 0)
    hit = (ids >= 0) & (ids < CELLS) & (rows == cell_position(ids))
    return jnp.where(hit, 1.0, 0.0).astype(BF16)


def spread_bias(table, shifted):
    for j in range(CELLS):
        turned = pltpu.roll(table, (384 - CENTRE + cell_position(j)) % 384, 1)
        for h in range(HEADS):
            shifted[h, j : j + 1] = turned[h : h + 1, :256]
    even, odd = position_matrix(False), position_matrix(True)
    pairs = [
        nn(shifted[2 * p].astype(BF16), even) + nn(shifted[2 * p + 1].astype(BF16), odd)
        for p in range(HEADS // 2)
    ]
    return jnp.concatenate(pairs, 1) * log2_e


def prepare(
    blocks, q_w, out_w, up_w, down_w, kv_w, v_b, ln1_g, ln1_b, ln2_g, ln2_b, out_b, down_b, q_b, up_b, table,
    vec_e, vec_d, w_qkv, b_qkv, w_q_d, b_q_d, w_out_e, w_out_d, w_up_e, w_up_d, b_up_e, b_up_d,
    w_down_e, w_down_d, bias_e, bias_d,
    small, small_sib, q_sib, out_sib, up_sib, down_sib, shifted, send_sem, recv_sem,
):
    core, block = lax.axis_index("section"), lax.axis_index("tok")
    channels, hidden = up_w.shape
    sibling = {"section": 1 - core}
    barrier = pltpu.get_barrier_semaphore()
    pl.semaphore_signal(barrier, inc=1, device_id=sibling, device_id_type=MESH)
    small[...] = jnp.zeros_like(small)
    for row, ref in enumerate((ln1_g, ln1_b, ln2_g, ln2_b, out_b, down_b, q_b)):
        small[row : row + 1, :channels] = ref[...].astype(F32)
    small[7:8, :hidden] = up_b[...].astype(F32)
    small[TABLE_ROW : TABLE_ROW + HEADS, : SPAN**3] = table[...].astype(F32)
    pl.semaphore_wait(barrier, 1)
    pairs = ((small, small_sib), (q_w, q_sib), (out_w, out_sib), (up_w, up_sib), (down_w, down_sib))
    copies = [
        pltpu.make_async_remote_copy(
            src_ref=source, dst_ref=target, send_sem=send_sem.at[k], recv_sem=recv_sem.at[k],
            device_id=sibling, device_id_type=MESH,
        )
        for k, (source, target) in enumerate(pairs)
    ]
    for copy in copies:
        copy.start()
    for copy in copies:
        copy.wait()

    def place(enc, dec):
        e_small, e_q, e_out, e_up, e_down = enc
        d_small, d_q, d_out, d_up, d_down = dec
        for source, vec, b_up in ((e_small, vec_e, b_up_e), (d_small, vec_d, b_up_d)):
            vec[...] = source[:8, :channels]
            b_up[...] = source[7:8, :hidden]
        w_qkv[...] = jnp.zeros_like(w_qkv)
        b_qkv[...] = jnp.zeros_like(b_qkv)
        w_qkv[:, :channels] = e_q[...]
        w_qkv[:, 256 : 256 + channels] = kv_w[:, :channels]
        w_qkv[:, 512 : 512 + channels] = kv_w[:, channels:]
        b_qkv[:, :channels] = e_small[6:7, :channels]
        b_qkv[:, 512 : 512 + channels] = v_b[...].astype(F32)
        w_q_d[...] = d_q[...]
        b_q_d[...] = d_small[6:7, :channels]
        for target, source in (
            (w_out_e, e_out), (w_out_d, d_out), (w_up_e, e_up), (w_up_d, d_up),
            (w_down_e, e_down), (w_down_d, d_down),
        ):
            target[...] = source[...]
        rows = slice(TABLE_ROW, TABLE_ROW + 8)
        bias_e[...] = spread_bias(e_small[rows, :384], shifted)
        return spread_bias(d_small[rows, :384], shifted)

    own = (small, q_w, out_w, up_w, down_w)
    sib = (small_sib, q_sib, out_sib, up_sib, down_sib)

    def masked(base):
        shape = (CELLS, HEADS * CELLS)
        keys = lax.broadcasted_iota(jnp.int32, shape, 0)
        queries = lax.broadcasted_iota(jnp.int32, shape, 1) % CELLS

        def differ(unit):
            return jnp.where(keys // unit % 2 != queries // unit % 2, 1.0, 0.0)

        last = jnp.where((core == 1) & (block == blocks - 1), 1.0, 0.0)
        for y in range(2):
            for z in range(2):
                apart = jnp.maximum(last * differ(32), jnp.maximum(y * differ(16), z * differ(8)))
                bias_d[y, z] = base + apart * (mask_fill * log2_e)

    @pl.when(core == 0)
    def _():
        masked(place(own, sib))

    @pl.when(core == 1)
    def _():
        masked(place(sib, own))


def run_prepare(blocks, weights, smalls, table, kv_weight, v_bias):
    q_w, out_w, up_w, down_w = weights
    channels, hidden = up_w.shape
    vmem = pl.BlockSpec(memory_space=pltpu.VMEM)
    args = [*weights, kv_weight, v_bias, *smalls, table]
    bias = (CELLS, HEADS * CELLS)
    square = (channels, channels)

    def f32(*shape):
        return jax.ShapeDtypeStruct(shape, F32)

    def bf16(*shape):
        return jax.ShapeDtypeStruct(shape, BF16)

    shapes = [
        f32(8, channels), f32(8, channels), bf16(channels, 768), f32(1, 768), bf16(*square),
        f32(1, channels), bf16(*square), bf16(*square), bf16(channels, hidden), bf16(channels, hidden),
        f32(1, hidden), f32(1, hidden), bf16(hidden, channels), bf16(hidden, channels),
        f32(*bias), f32(2, 2, *bias),
    ]
    return pl.pallas_call(
        functools.partial(prepare, blocks),
        in_specs=[vmem] * len(args),
        out_specs=[vmem] * len(shapes),
        out_shape=shapes,
        scratch_shapes=[
            pltpu.VMEM((TABLE_ROW + 8, hidden), F32),
            pltpu.VMEM((TABLE_ROW + 8, hidden), F32),
            pltpu.VMEM(square, BF16),
            pltpu.VMEM(square, BF16),
            pltpu.VMEM((channels, hidden), BF16),
            pltpu.VMEM((hidden, channels), BF16),
            pltpu.VMEM((HEADS, CELLS, 256), F32),
            pltpu.SemaphoreType.DMA((5,)),
            pltpu.SemaphoreType.DMA((5,)),
        ],
        compiler_params=pltpu.CompilerParams(
            collective_id=1, has_side_effects=True, vmem_limit_bytes=VMEM_BYTES
        ),
        name="prepare",
    )(*args)


def run_encoder(core, tokens, batch, consts, cotangent):
    _, _, rows_y, rows_z, channels = tokens.shape
    groups, size = rows_y // WIN, 4 * rows_z
    cells, windows = 4 * size, rows_z // WIN
    hidden = consts[6].shape[1]
    slab = jax.ShapeDtypeStruct((groups, 2, 3, size * 3 // 2, LANES_A), BF16)
    outs = [
        slab,
        slab,
        jax.ShapeDtypeStruct((groups, cells, channels), F32),
        jax.ShapeDtypeStruct((groups, cells, channels), F32),
        jax.ShapeDtypeStruct((groups, cells, 256), F32),
        jax.ShapeDtypeStruct((groups, cells, 768), BF16),
        jax.ShapeDtypeStruct((groups, windows, CELLS, HEADS * CELLS), F32),
        jax.ShapeDtypeStruct((groups, cells, channels), BF16),
        jax.ShapeDtypeStruct((groups, cells, hidden), BF16),
        jax.ShapeDtypeStruct((groups, cells, hidden), F32),
    ]

    def row(array):
        zeros = (0,) * (array.ndim - 1)
        return pl.BlockSpec((1, *array.shape[1:]), lambda i, c: (i, *zeros))

    batches = tokens.shape[0]
    cut = [] if cotangent is None else [cotangent]
    cut_block = (batches, SHIFT, WIN, rows_z, channels)
    cut_outs = [
        jax.ShapeDtypeStruct((batches, SHIFT, rows_y, rows_z, channels), a.dtype) for a in cut
    ]
    return pl.pallas_call(
        functools.partial(encoder_forward, len(cut)),
        grid_spec=pltpu.PrefetchScalarGridSpec(
            num_scalar_prefetch=1,
            grid=(groups,),
            in_specs=[
                pl.BlockSpec(
                    (1, WIN, WIN, rows_z, channels), lambda i, c: (batch, c[0], i, 0, 0)
                ),
                *[whole(a) for a in consts],
                *[pl.BlockSpec(cut_block, lambda i, c: (0, 2 * c[0], i, 0, 0)) for _ in cut],
            ],
            out_specs=[
                *[row(a) for a in outs],
                *[pl.BlockSpec(cut_block, lambda i, c: (0, 0, i, 0, 0)) for _ in cut],
            ],
        ),
        out_shape=[*outs, *cut_outs],
        compiler_params=params,
        cost_estimate=cost(groups * cells, 466944, groups * cells * 7500),
        name="encoder_forward",
    )(core, tokens, *consts, *cut)


def run_encoder_back(core, batch, own, halo, ys, returned, saved, old, consts, tokens):
    groups, _, _, packed, _ = own.shape
    batches, planes, rows_y, rows_z, channels = tokens.shape
    size = 4 * rows_z
    hidden = consts[4].shape[1]
    first = old is None
    shapes = sums_shapes(channels, hidden, 3)
    outs = [
        jax.ShapeDtypeStruct(tokens.shape, F32),
        jax.ShapeDtypeStruct((WIN, rows_y, rows_z, channels), F32),
        *shapes,
    ]

    def slab(unit):
        def place(i):
            return ((i if unit == 0 else (i + groups - 1) % groups), unit, 0, 0, 0)

        return pl.BlockSpec((1, 1, 3, packed, LANES_A), place)

    def row(array):
        zeros = (0,) * (array.ndim - 1)
        return pl.BlockSpec((1, *array.shape[1:]), lambda i: (i, *zeros))

    any_spec = pl.BlockSpec(memory_space=pl.ANY)
    olds = [] if first else [*old[1], old[0]]
    args = [core, *consts, *ys, own, own, halo, halo, *saved, *returned, *olds]
    return pl.pallas_call(
        functools.partial(encoder_backward, first, batch, len(returned)),
        grid=(groups,),
        in_specs=[
            pl.BlockSpec(memory_space=pltpu.SMEM),
            *[whole(a) for a in consts],
            *[pl.BlockSpec((n, WIN, rows_z, channels), lambda i: (0, i, 0, 0)) for n in (2, 2, 4)],
            slab(0),
            slab(1),
            slab(0),
            slab(1),
            *[row(a) for a in saved],
            *[pl.BlockSpec((WIN, WIN, rows_z, channels), lambda i: (0, i, 0, 0))] * len(returned),
            *[whole(a) for a in olds[:-1]],
            *[any_spec] * (0 if first else 1),
        ],
        out_specs=[any_spec, any_spec, *[whole(a) for a in shapes]],
        out_shape=outs,
        input_output_aliases={} if first else {len(args) - 1: 0},
        scratch_shapes=[
            pltpu.VMEM((3, 4 * size, channels), BF16),
            pltpu.VMEM((2, WIN, WIN, rows_z, channels), F32),
            pltpu.SemaphoreType.DMA((2,)),
            pltpu.SemaphoreType.DMA((8 + batches,)),
        ],
        compiler_params=params,
        cost_estimate=cost(groups * 4 * size, 933888, groups * 4 * size * 9000),
        name="encoder_backward",
    )(*args)


def run_decoder(core, keep, recv, cotangent, cot_recv, batch, old, consts):
    groups, _, _, packed, _ = keep.shape
    rows_z, channels = cotangent.shape[3:]
    size = 4 * rows_z
    hidden = consts[6].shape[1]
    windows = rows_z // WIN
    first = old is None
    shapes = sums_shapes(channels, hidden, 1)
    slab_shape = jax.ShapeDtypeStruct((groups, 2, 3, packed, LANES_A), BF16)
    outs = [
        *[jax.ShapeDtypeStruct((n, groups * WIN, rows_z, channels), F32) for n in (4, 2)],
        slab_shape,
        slab_shape,
        *shapes,
    ]

    def slab(unit):
        def place(i, c):
            return ((i if unit == 1 else (i + 1) % groups), unit, 0, 0, 0)

        return pl.BlockSpec((1, 1, 3, packed, LANES_A), place)

    def cot(unit, own):
        def place(i, c):
            y = 2 * i + 1 if unit == 1 else (2 * i + 2) % (2 * groups)
            return (batch, 2 * c[0] + 1 if own else 0, y, 0, 0)

        return pl.BlockSpec((1, 2, 2, rows_z, channels), place)

    def bias_place(i, c):
        return (i // (groups - 1), 0, 0, 0)

    specs = [whole(a) for a in consts]
    specs[4] = pl.BlockSpec((1, *consts[4].shape[1:]), bias_place)
    olds = [] if first else list(old)
    out_slab = pl.BlockSpec((1, 2, 3, packed, LANES_A), lambda i, c: (i, 0, 0, 0, 0))
    return pl.pallas_call(
        functools.partial(decoder, first),
        grid_spec=pltpu.PrefetchScalarGridSpec(
            num_scalar_prefetch=1,
            grid=(groups,),
            in_specs=[
                *specs,
                slab(1),
                slab(0),
                slab(1),
                slab(0),
                cot(1, True),
                cot(0, True),
                cot(1, False),
                cot(0, False),
                *[whole(a) for a in olds],
            ],
            out_specs=[
                *[pl.BlockSpec((n, WIN, rows_z, channels), lambda i, c: (0, i, 0, 0)) for n in (4, 2)],
                out_slab,
                out_slab,
                *[whole(a) for a in shapes],
            ],
            scratch_shapes=[
                pltpu.VMEM((windows, CELLS, HEADS * CELLS), F32),
                pltpu.VMEM((4 * size, channels), BF16),
                pltpu.VMEM((4 * size, hidden), BF16),
                pltpu.VMEM((4 * size, hidden), F32),
                pltpu.VMEM((3, 4 * size, channels), F32),
            ],
        ),
        out_shape=outs,
        compiler_params=params,
        cost_estimate=cost(groups * 4 * size, 1253376, groups * 4 * size * 4000),
        name="decoder",
    )(core, *consts, keep, keep, recv, recv, cotangent, cotangent, cot_recv, cot_recv, *olds)


def body(
    tokens,
    cotangent,
    ln1_gain,
    ln1_bias,
    q_weight,
    q_bias,
    kv_weight,
    v_bias,
    out_weight,
    out_bias,
    rel_table,
    ln2_gain,
    ln2_bias,
    up_weight,
    up_bias,
    down_weight,
    down_bias,
):
    batches, planes, rows_y, rows_z, channels = tokens.shape
    axes = ("section", "tok")
    core = lax.axis_index("section")
    block = lax.axis_index("tok")
    blocks = lax.axis_size("tok")
    is_encoder = core == 0
    core_arg = core.astype(jnp.int32).reshape(1)

    def device(position):
        position = position % (2 * blocks)
        return (position % 2) * blocks + position // 2

    to_previous = [(device(r), device(r - 1)) for r in range(2 * blocks)]
    to_next = [(device(r), device(r + 1)) for r in range(2 * blocks)]

    (
        vec_e, vec_d, w_qkv, b_qkv, w_q_d, b_q_d, w_out_e, w_out_d, w_up_e, w_up_d, b_up_e, b_up_d,
        w_down_e, w_down_d, bias_e, bias_d,
    ) = run_prepare(
        blocks,
        (q_weight[0], out_weight[0], up_weight[0], down_weight[0]),
        (ln1_gain, ln1_bias, ln2_gain, ln2_bias, out_bias, down_bias, q_bias, up_bias),
        rel_table[0],
        kv_weight,
        v_bias[None],
    )
    one_hot = (
        jnp.asarray(relative_index().reshape(-1))[None, :] == jnp.arange(SPAN**3)[:, None]
    ).astype(F32)
    order = jnp.asarray(order_matrix(rows_z, 0), BF16)
    order_rolled = jnp.asarray(order_matrix(rows_z, 1), BF16)

    enc_consts = (order, vec_e, w_qkv, b_qkv, bias_e, w_out_e, w_up_e, b_up_e, w_down_e)
    enc_back_consts = (order, vec_e, w_qkv, w_out_e, w_up_e, w_down_e)
    dec_consts = (order_rolled, vec_d, w_q_d, b_q_d, bias_d, w_out_d, w_up_d, b_up_d, w_down_d)

    handed, saved = [], []
    for batch in range(batches):
        send, keep, *rest = run_encoder(
            core_arg, tokens, batch, enc_consts, cotangent if batch == 0 else None
        )
        if batch == 0:
            *rest, half = rest
            cot_recv = lax.ppermute(half, axes, to_previous)
        handed.append((keep, lax.ppermute(send, axes, to_previous)))
        saved.append(rest)
    dec_sums = None
    returned, ys = [], []
    to_decoder = [(t, blocks + t) for t in range(blocks)]
    to_encoder = [(blocks + t, t) for t in range(blocks)]
    to_after = [(blocks + t, blocks + (t + 1) % blocks) for t in range(blocks)]
    for batch in range(batches):
        out_all, out_tail, own, halo, *dec_sums = run_decoder(
            core_arg, *handed[batch], cotangent, cot_recv, batch, dec_sums, dec_consts
        )
        returned.append((own, lax.ppermute(halo, axes, to_next)))
        y_halo = lax.ppermute(out_tail, axes, to_after)
        ys.append((out_all, y_halo, lax.ppermute(out_all, axes, to_decoder)))
    old = None
    backs = []
    for batch in range(batches):
        arrived = backs[:1] if batch == batches - 1 else []
        ends, back, *enc_sums = run_encoder_back(
            core_arg, batch, *returned[batch], ys[batch], arrived, saved[batch], old,
            enc_back_consts, tokens,
        )
        old = (ends, enc_sums)
        backs.append(lax.ppermute(back, axes, to_encoder))

    layout = Layout(channels, up_weight.shape[2], blocks)
    total, sib_kv, vec_sum = run_sum(enc_sums, dec_sums, layout, blocks)
    (
        ends, g_ln1_gain, g_ln1_bias, g_q_weight, g_q_bias, g_kv_weight, g_v_bias, g_out_weight,
        g_out_bias, g_bias, g_ln2_gain, g_ln2_bias, g_up_weight, g_up_bias, g_down_weight, g_down_bias,
    ) = run_finish(core_arg, total, sib_kv, vec_sum, backs[1:], ends, layout)
    g_table = jnp.dot(
        g_bias.reshape(CELLS, HEADS, CELLS).transpose(1, 0, 2).reshape(HEADS, -1),
        one_hot.T,
        precision=lax.Precision.HIGHEST,
    )
    return (
        ends[None],
        g_ln1_gain,
        g_ln1_bias,
        g_q_weight[None],
        g_q_bias,
        g_kv_weight[None],
        g_v_bias,
        g_out_weight[None],
        g_out_bias,
        g_table[None],
        g_ln2_gain,
        g_ln2_bias,
        g_up_weight[None],
        g_up_bias,
        g_down_weight[None],
        g_down_bias,
    )


def solution(mesh):
    in_specs = (
        P(None, "tok", None, None, None),
        P(None, "tok", None, None, None),
        P("section", None),
        P("section", None),
        P("section", None, None),
        P("section", None),
        P(),
        P(),
        P("section", None, None),
        P("section", None),
        P("section", None, None),
        P("section", None),
        P("section", None),
        P("section", None, None),
        P("section", None),
        P("section", None, None),
        P("section", None),
    )
    out_specs = (
        P("section", None, "tok", None, None, None),
        P("section", None),
        P("section", None),
        P("section", None, None),
        P("section", None),
        P("section", None, None),
        P("section", None),
        P("section", None, None),
        P("section", None),
        P("section", None, None),
        P("section", None),
        P("section", None),
        P("section", None, None),
        P("section", None),
        P("section", None, None),
        P("section", None),
    )
    return jax.shard_map(body, mesh=mesh, in_specs=in_specs, out_specs=out_specs, check_vma=False)
```

```python
import functools

import jax
import jax.numpy as jnp
import numpy as np
from jax import lax
from jax.experimental import pallas as pl
from jax.experimental.pallas import tpu as pltpu
from jax.sharding import PartitionSpec as P

HEADS = 6
HD = 32
WIN = 4
SHIFT = 2
CELLS = WIN**3
SPAN = 2 * WIN - 1
HEADS_A = 4
LANES_A = HEADS_A * HD
COLS_A = HEADS_A * CELLS

eps_norm = 1e-05
mask_fill = -100.0
log2_e = 1.4426950408889634
root_half = 0.7071067811865476
inv_root_two_pi = 0.3989422804014327
scale = HD ** (-0.5)
VMEM_BYTES = 56 * 1024 * 1024

F32 = jnp.float32
BF16 = jnp.bfloat16


def nn(left, right):
    return lax.dot_general(left, right, (((1,), (0,)), ((), ())), preferred_element_type=F32)


def nt(left, right):
    return lax.dot_general(left, right, (((1,), (1,)), ((), ())), preferred_element_type=F32)


def tn(left, right):
    return lax.dot_general(left, right, (((0,), (0,)), ((), ())), preferred_element_type=F32)


def order_matrix(rows_z, rolled):
    count = 4 * rows_z
    matrix = np.zeros((count, count), np.float32)
    units = rows_z // 2
    for unit in range(units):
        for dx in range(2):
            for dy in range(2):
                for dz in range(2):
                    z = (2 * (unit + rolled) + dz) % rows_z
                    matrix[unit * 8 + dx * 4 + dy * 2 + dz, (dx * 2 + dy) * rows_z + z] = 1.0
    return matrix


def windows_of(pieces):
    count, rows, channels = pieces.shape
    return pieces.reshape(count, rows // 16, 16, channels).transpose(1, 0, 2, 3).reshape(-1, channels)


def pieces_of(windows):
    rows, channels = windows.shape
    return (
        windows.reshape(rows // CELLS, 4, 16, channels)
        .transpose(1, 0, 2, 3)
        .reshape(4, rows // 4, channels)
    )


def roll_rows(pieces, steps):
    return jnp.concatenate([pieces[:, steps:], pieces[:, :steps]], 1)


def pack_slab(pieces):
    half = pieces.shape[1] // 2
    rest = pieces[:, :, LANES_A:]
    return jnp.concatenate(
        [pieces[:, :, :LANES_A], jnp.concatenate([rest[:, :half], rest[:, half:]], 2)], 1
    ).astype(BF16)


def unpack_slab(block):
    size = block.shape[0] * 2 // 3
    half = LANES_A // 2
    rest = jnp.concatenate([block[size:, :half], block[size:, half:]], 0)
    return jnp.concatenate([block[:size], rest], 1)


def normalize(rows):
    mean = jnp.mean(rows, -1, keepdims=True)
    centered = rows - mean
    inv_std = lax.rsqrt(jnp.mean(centered * centered, -1, keepdims=True) + eps_norm)
    return centered * inv_std, inv_std


def norm_back(grad_rows, unit_rows, inv_std, gain):
    scaled = grad_rows * gain
    return inv_std * (
        scaled
        - jnp.mean(scaled, -1, keepdims=True)
        - unit_rows * jnp.mean(scaled * unit_rows, -1, keepdims=True)
    )


def gelu_pair(rows):
    upper = 0.5 * lax.erf(rows * root_half) + 0.5
    bell = jnp.exp2(rows * rows * (-0.5 * log2_e))
    return rows * upper, upper + rows * bell * inv_root_two_pi


def head_masks(width):
    heads = lax.broadcasted_iota(jnp.int32, (1, width), 1) // HD
    return [jnp.where(heads == h, 1.0, 0.0).astype(BF16) for h in range(width // HD)]


def expand(rows):
    masks = head_masks(rows.shape[1])
    return jnp.concatenate([rows * mask for mask in masks], 0)


def collapse(stacked):
    width = stacked.shape[1]
    lanes = lax.broadcasted_iota(jnp.int32, (CELLS, width), 1)
    total = stacked[:CELLS]
    for h in range(1, width // HD):
        total = jnp.where(lanes >= h * HD, stacked[h * CELLS : (h + 1) * CELLS], total)
    return total


def split(rows):
    return rows[:, :LANES_A], rows[:, LANES_A:]


def attend(parts, bias):
    queries, keys, values = zip(*[[split(rows) for rows in part] for part in parts])
    wide = [[expand(half) for half in q] for q in queries]
    scores = [
        jnp.concatenate([nt(k[0], q[0]), nt(k[1], q[1])], 1) for k, q in zip(keys, wide)
    ]
    scores = [s * (scale * log2_e) + b for s, b in zip(scores, bias)]
    exponents = [jnp.exp2(s - jnp.max(s, 0, keepdims=True)) for s in scores]
    probs = [e * (1.0 / jnp.sum(e, 0, keepdims=True)) for e in exponents]
    low = [p.astype(BF16) for p in probs]
    mixed = [
        (tn(p[:, :COLS_A], v[0]), tn(p[:, COLS_A:], v[1])) for p, v in zip(low, values)
    ]
    mixed = [jnp.concatenate([collapse(m[0]), collapse(m[1])], 1).astype(BF16) for m in mixed]
    return mixed, probs


def attend_back(parts):
    queries, keys, values, grads = zip(
        *[[split(rows) for rows in part[:3] + part[4:]] for part in parts]
    )
    probs = [part[3] for part in parts]
    wide_g = [[expand(half) for half in g] for g in grads]
    d_probs = [
        jnp.concatenate([nt(v[0], g[0]), nt(v[1], g[1])], 1) for v, g in zip(values, wide_g)
    ]
    low = [part[3].astype(BF16) for part in parts]
    d_values = [
        jnp.concatenate([nn(p[:, :COLS_A], g[0]), nn(p[:, COLS_A:], g[1])], 1)
        for p, g in zip(low, wide_g)
    ]
    wide_q = [[expand(half) for half in q] for q in queries]
    d_scores = [
        p * (d - jnp.sum(d * p, 0, keepdims=True)) for p, d in zip(probs, d_probs)
    ]
    low_d = [d.astype(BF16) for d in d_scores]
    d_keys = [
        jnp.concatenate([nn(d[:, :COLS_A], q[0]), nn(d[:, COLS_A:], q[1])], 1) * scale
        for d, q in zip(low_d, wide_q)
    ]
    d_queries = [
        (tn(d[:, :COLS_A], k[0]), tn(d[:, COLS_A:], k[1])) for d, k in zip(low_d, keys)
    ]
    d_queries = [
        jnp.concatenate([collapse(d[0]), collapse(d[1])], 1) * scale for d in d_queries
    ]
    table = d_scores[0]
    for d in d_scores[1:]:
        table = table + d
    return d_queries, d_keys, d_values, table


def window_groups(count):
    return [range(k, min(k + TOGETHER, count)) for k in range(0, count, TOGETHER)]


def window_rows(k):
    return slice(k * CELLS, (k + 1) * CELLS)


def with_ones(rows):
    return jnp.concatenate([rows.T, jnp.ones((16, rows.shape[0]), BF16)], 0)


def col_sum(rows):
    return jnp.sum(rows, 0, keepdims=True)


def start_sums(first, old_refs, new_refs):
    @pl.when(pl.program_id(0) == 0)
    def _():
        for k, new in enumerate(new_refs):
            new[...] = jnp.zeros_like(new) if first else old_refs[k][...]


def restore(matrix, rows):
    high = rows.astype(BF16)
    low = (rows - high.astype(F32)).astype(BF16)
    return tn(matrix, high) + tn(matrix, low)


CHUNK = 256
TOGETHER = 4


def encoder_forward(
    cuts, core_ref, tok, order, vec, w_qkv, b_qkv, bias, w_out, w_up, b_up, w_down, *rest,
):
    cut_in, rest = rest[:cuts], rest[cuts:]
    send, keep, n1_out, n2_out, p_out, o_out, a_out, s_out, *cut_out, qkv = rest
    for source, target in zip(cut_in, cut_out):
        target[...] = source[...]
    rows_z = tok.shape[3]
    size = 4 * rows_z
    pieces = []
    for x in range(2):
        for y in range(2):
            part = tok[0, 2 * x : 2 * x + 2, 2 * y : 2 * y + 2].reshape(size, -1)
            pieces.append(nn(order[...], part))
    entry = windows_of(jnp.stack(pieces))
    unit, inv_std = normalize(entry)
    channels = entry.shape[1]
    wide = jnp.broadcast_to(inv_std, (entry.shape[0], 256 - channels))
    n1_out[0, :, :channels] = unit
    n1_out[0, :, channels:] = wide
    left = (unit * vec[0:1] + vec[1:2]).astype(BF16)
    triple = nn(left, w_qkv[...]) + b_qkv[...]
    qkv[...] = triple.astype(BF16)
    for together in window_groups(entry.shape[0] // CELLS):
        parts = [
            [qkv[window_rows(k), 256 * f : 256 * f + 192] for f in range(3)] for k in together
        ]
        mixed, probs = attend(parts, [bias[...]] * len(parts))
        for k, o, p in zip(together, mixed, probs):
            p_out[0, k] = p.astype(BF16)
            o_out[0, window_rows(k)] = o
    middle = entry + nn(o_out[0], w_out[...]) + vec[4:5]
    unit, inv_std = normalize(middle)
    wide = jnp.broadcast_to(inv_std, (entry.shape[0], 256 - channels))
    n2_out[0, :, :channels] = unit
    n2_out[0, :, channels:] = wide
    left = (unit * vec[2:3] + vec[3:4]).astype(BF16)
    results = []
    for k in range(entry.shape[0] // CHUNK):
        rows = slice(k * CHUNK, (k + 1) * CHUNK)
        hidden, slope = gelu_pair(nn(left[rows], w_up[...]) + b_up[...])
        hidden = hidden.astype(BF16)
        a_out[0, rows] = hidden
        s_out[0, rows] = slope.astype(BF16)
        results.append(nn(hidden, w_down[...]))
    result = middle + jnp.concatenate(results, 0) + vec[5:6]
    for field, rows in enumerate((result, triple[:, 256:448], triple[:, 512:704])):
        rolled = pack_slab(roll_rows(pieces_of(rows), 8))
        send[0, :, field] = rolled[:2]
        keep[0, :, field] = rolled[2:]


def mlp_back(grad, grad_low, hidden, slope, left_two, unit, inv_std, w_up, w_down, vec, sums):
    g_up, g_down, g_vec = sums
    backs = []
    total_up = None
    turned = grad_low.T
    ones = with_ones(left_two)
    for k in range(grad.shape[0] // CHUNK):
        rows = slice(k * CHUNK, (k + 1) * CHUNK)
        d_pre = (nt(grad_low[rows], w_down[...]) * slope(rows)).astype(BF16)
        part = nn(ones[:, rows], d_pre)
        total_up = part if total_up is None else total_up + part
        backs.append(nt(d_pre, w_up[...]))
    g_up[...] += total_up
    g_down[...] += nn(turned, hidden)
    d_normed = jnp.concatenate(backs, 0)
    g_vec[2:3] += col_sum(d_normed * unit)
    g_vec[3:4] += col_sum(d_normed)
    g_vec[4:5] += col_sum(grad)
    return grad + norm_back(d_normed, unit, inv_std, vec[2:3])


def start_all(copies):
    for copy in copies:
        copy.start()


def wait_all(copies):
    for copy in copies:
        copy.wait()


def encoder_backward(
    first, batch, returns, core_ref, order, vec, w_qkv, b_qkv, w_out, w_up, w_down,
    y_own, y_halo, y_sib,
    keep_a, keep_b, recv_a, recv_b,
    n1_in, n2_in, p_in, o_in, a_in, s_in, *rest,
):
    returned, rest = rest[:returns], rest[returns:]
    old, rest = ([], rest) if first else (rest[:8], rest[9:])
    ends, back, *sums, qkv, dqkv, buffer, out_sem, copy_sem = rest
    g_up, g_down, g_q, g_k, g_v, g_out, g_vec, g_bias = sums
    step, steps = pl.program_id(0), pl.num_programs(0)
    is_encoder = core_ref[0] == 0
    rows_y = ends.shape[2]
    slot = lax.rem(step, 2)

    def output_copies():
        copies = []
        for start, planes, ref in ((0, 2, y_halo), (2, 4, y_sib), (6, 2, y_own)):
            for half in range(2):
                rows = pl.ds(lax.rem(step * WIN + SHIFT + 2 * half, rows_y), 2)
                target = ends.at[batch, pl.ds(start, planes), rows]
                copies.append((ref.at[:, pl.ds(2 * half, 2)], target))
        return [
            pltpu.make_async_copy(source, target, copy_sem.at[k])
            for k, (source, target) in enumerate(copies)
        ]

    def gradient_copies():
        return [
            pltpu.make_async_copy(
                ref, ends.at[k, pl.ds(WIN, WIN), pl.ds(step * WIN, WIN)], copy_sem.at[8 + k]
            )
            for k, ref in enumerate(returned)
        ]

    def result_copy(index, to_ends):
        target = (
            ends.at[batch, pl.ds(0, WIN), pl.ds(index * WIN, WIN)]
            if to_ends
            else back.at[:, pl.ds(index * WIN, WIN)]
        )
        at = lax.rem(index, 2)
        return pltpu.make_async_copy(buffer.at[at], target, out_sem.at[at])

    def for_core(encoder_work, decoder_work):
        pl.when(is_encoder)(encoder_work)
        pl.when(jnp.logical_not(is_encoder))(decoder_work)

    for_core(lambda: start_all(gradient_copies()), lambda: start_all(output_copies()))
    start_sums(first, old, sums)
    fields = []
    for field in range(3):
        pieces = jnp.stack(
            [unpack_slab(ref[0, 0, field]) for ref in (recv_b, recv_a, keep_b, keep_a)]
        )
        fields.append(windows_of(pieces))
    grad_low, d_key_1, d_value_1 = fields
    grad = grad_low.astype(F32)
    channels = grad.shape[1]
    unit_1, unit_2 = n1_in[0, :, :channels], n2_in[0, :, :channels]
    wide_1, wide_2 = [ref[0, :, channels : channels + 1] for ref in (n1_in, n2_in)]
    left_1 = (unit_1 * vec[0:1] + vec[1:2]).astype(BF16)
    left_2 = (unit_2 * vec[2:3] + vec[3:4]).astype(BF16)
    qkv[...] = (nn(left_1, w_qkv[...]) + b_qkv[...]).astype(BF16)
    d_middle = mlp_back(
        grad, grad_low, a_in[0], lambda rows: s_in[0, rows].astype(F32), left_2, unit_2, wide_2, w_up, w_down, vec,
        (g_up, g_down, g_vec),
    )
    branch = d_middle.astype(BF16)
    g_out[...] += nn(with_ones(o_in[0]), branch)
    d_mixed = nt(branch, w_out[...]).astype(BF16)
    d_table = None
    for together in window_groups(grad.shape[0] // CELLS):
        parts = [
            [qkv[window_rows(k), 256 * f : 256 * f + 192] for f in range(3)]
            + [p_in[0, k].astype(F32), d_mixed[window_rows(k)]]
            for k in together
        ]
        *d_qkv, d_s = attend_back(parts)
        for k, d_q, d_k, d_v in zip(together, *d_qkv):
            rows = window_rows(k)
            dqkv[0, rows] = d_q.astype(BF16)
            dqkv[1, rows] = (d_k + d_key_1[rows].astype(F32)).astype(BF16)
            dqkv[2, rows] = (d_v + d_value_1[rows].astype(F32)).astype(BF16)
        d_table = d_s if d_table is None else d_table + d_s
    g_bias[...] += d_table
    ones = with_ones(left_1)
    d_normed = None
    for field, g_field in enumerate((g_q, g_k, g_v)):
        cols = slice(field * 256, field * 256 + 192)
        g_field[...] += nn(ones, dqkv[field])
        part = nt(dqkv[field], w_qkv[:, cols])
        d_normed = part if d_normed is None else d_normed + part
    g_vec[0:1] += col_sum(d_normed * unit_1)
    g_vec[1:2] += col_sum(d_normed)
    result = pieces_of(d_middle + norm_back(d_normed, unit_1, wide_1, vec[0:1]))
    rows_z = ends.shape[3]

    @pl.when(step >= 2)
    def _():
        for_core(
            lambda: result_copy(step - 2, True).wait(), lambda: result_copy(step - 2, False).wait()
        )

    for x in range(2):
        for y in range(2):
            part = restore(order[...], result[2 * x + y])
            buffer[slot, 2 * x : 2 * x + 2, 2 * y : 2 * y + 2] = part.reshape(2, 2, rows_z, -1)
    for_core(lambda: result_copy(step, True).start(), lambda: result_copy(step, False).start())

    @pl.when(step == steps - 1)
    def _():
        def finish(to_ends):
            result_copy(step - 1, to_ends).wait()
            result_copy(step, to_ends).wait()

        for_core(lambda: finish(True), lambda: finish(False))

    for_core(lambda: wait_all(gradient_copies()), lambda: wait_all(output_copies()))


def decoder(
    first, core_ref, order, vec, w_q, b_q, bias, w_out, w_up, b_up, w_down,
    keep_1, keep_0, recv_1, recv_0, cot_1, cot_0, cot_r1, cot_r0, *rest,
):
    old, new = ([], rest) if first else (rest[:6], rest[6:])
    out_all, out_tail, own, halo, *sums, p_scr, o_scr, a_scr, s_scr, dqkv = new
    g_up, g_down, g_q, g_out, g_vec, g_bias = sums
    start_sums(first, old, sums)
    fields = []
    for field in range(3):
        pieces = jnp.stack([unpack_slab(ref[0, 0, field]) for ref in (keep_1, keep_0, recv_1, recv_0)])
        fields.append(windows_of(pieces))
    entry_low, keys, values = fields
    entry = entry_low.astype(F32)
    unit_1, inv_1 = normalize(entry)
    left_1 = (unit_1 * vec[0:1] + vec[1:2]).astype(BF16)
    queries = (nn(left_1, w_q[...]) + b_q[...]).astype(BF16)
    windows = entry.shape[0] // CELLS
    for together in window_groups(windows):
        parts = [[rows[window_rows(k)] for rows in (queries, keys, values)] for k in together]
        mixed, probs = attend(parts, [bias[0, 1 if k == windows - 1 else 0] for k in together])
        for k, o, p in zip(together, mixed, probs):
            p_scr[k] = p
            o_scr[window_rows(k)] = o
    middle = entry + nn(o_scr[...], w_out[...]) + vec[4:5]
    unit_2, inv_2 = normalize(middle)
    left_2 = (unit_2 * vec[2:3] + vec[3:4]).astype(BF16)
    results = []
    for k in range(entry.shape[0] // CHUNK):
        rows = slice(k * CHUNK, (k + 1) * CHUNK)
        hidden, slope = gelu_pair(nn(left_2[rows], w_up[...]) + b_up[...])
        hidden = hidden.astype(BF16)
        a_scr[rows] = hidden
        s_scr[rows] = slope
        results.append(nn(hidden, w_down[...]))
    result = pieces_of(middle + jnp.concatenate(results, 0) + vec[5:6])
    rows_z = out_all.shape[2]
    size = 4 * rows_z
    for x in range(2):
        for y in range(2):
            part = restore(order[...], result[2 * x + y]).reshape(2, 2, rows_z, -1)
            out_all[2 * x : 2 * x + 2, 2 * y : 2 * y + 2] = part
            if x == 1:
                out_tail[:, 2 * y : 2 * y + 2] = part

    cots = [
        nn(order[...], ref[0].reshape(size, -1)).astype(BF16) for ref in (cot_1, cot_0, cot_r1, cot_r0)
    ]
    grad_low = windows_of(jnp.stack(cots))
    grad = grad_low.astype(F32)
    d_middle = mlp_back(
        grad, grad_low, a_scr[...], lambda rows: s_scr[rows], left_2, unit_2, inv_2, w_up, w_down, vec,
        (g_up, g_down, g_vec),
    )
    branch = d_middle.astype(BF16)
    g_out[...] += nn(with_ones(o_scr[...]), branch)
    d_mixed = nt(branch, w_out[...]).astype(BF16)
    d_table = None
    for together in window_groups(windows):
        parts = [
            [rows[window_rows(k)] for rows in (queries, keys, values)]
            + [p_scr[k], d_mixed[window_rows(k)]]
            for k in together
        ]
        *d_qkv, d_s = attend_back(parts)
        for k, *grads in zip(together, *d_qkv):
            for f in range(3):
                dqkv[f, window_rows(k)] = grads[f]
        d_table = d_s if d_table is None else d_table + d_s
    g_bias[...] += d_table
    d_queries = dqkv[0].astype(BF16)
    g_q[...] += nn(with_ones(left_1), d_queries)
    d_normed = nt(d_queries, w_q[...])
    g_vec[0:1] += col_sum(d_normed * unit_1)
    g_vec[1:2] += col_sum(d_normed)
    d_entry = d_middle + norm_back(d_normed, unit_1, inv_1, vec[0:1])
    for field, rows in enumerate((d_entry, dqkv[1], dqkv[2])):
        turned = pack_slab(roll_rows(pieces_of(rows), size - 8))
        own[0, :, field] = turned[:2]
        halo[0, :, field] = turned[2:]


def whole(array):
    zeros = (0,) * array.ndim
    return pl.BlockSpec(array.shape, lambda *_: zeros)


def sums_shapes(channels, hidden, products):
    return [
        jax.ShapeDtypeStruct(shape, F32)
        for shape in (
            (channels + 16, hidden),
            (channels, hidden),
            *[(channels + 16, channels)] * products,
            (channels + 16, channels),
            (8, channels),
            (CELLS, HEADS * CELLS),
        )
    ]


def cost(cells, per_cell, hbm):
    return pl.CostEstimate(
        flops=2 * cells * per_cell, bytes_accessed=hbm, transcendentals=cells * 1536
    )


params = pltpu.CompilerParams(
    dimension_semantics=("arbitrary",), vmem_limit_bytes=VMEM_BYTES
)


class Layout:
    def __init__(self, channels, hidden, blocks):
        tall = channels + 16
        self.tall, self.channels = tall, channels
        self.tiles = hidden // LANES_A
        self.up = 0
        self.down = self.tiles * tall
        self.q = self.down + self.tiles * channels
        self.out = self.q + tall
        self.rest = self.out + tall
        self.kv = self.rest + tall
        self.bias = self.kv + 2 * tall
        self.end = self.bias + HEADS * CELLS // LANES_A * CELLS
        self.chunk = -(-self.end // (16 * blocks)) * 16
        self.rows = self.chunk * blocks


def fill(buffer, layout, up, down, q, out, kv, bias):
    kind, half = buffer.dtype, LANES_A // 2
    tall, channels = layout.tall, layout.channels
    for k in range(layout.tiles):
        cols = slice(k * LANES_A, (k + 1) * LANES_A)
        buffer[layout.up + k * tall : layout.up + (k + 1) * tall] = up[:, cols].astype(kind)
        buffer[layout.down + k * channels : layout.down + (k + 1) * channels] = down[
            :, cols
        ].astype(kind)
    buffer[layout.q : layout.q + tall] = q[:, :LANES_A].astype(kind)
    buffer[layout.out : layout.out + tall] = out[:, :LANES_A].astype(kind)
    rests = jnp.concatenate([q[:, LANES_A:], out[:, LANES_A:]], 1)
    buffer[layout.rest : layout.rest + tall] = rests.astype(kind)
    buffer[layout.kv : layout.kv + tall] = kv[:, :LANES_A].astype(kind)
    rests = jnp.concatenate([kv[:, LANES_A:], jnp.zeros((tall, half), F32)], 1)
    buffer[layout.kv + tall : layout.kv + 2 * tall] = rests.astype(kind)
    for k in range(HEADS * CELLS // LANES_A):
        start = layout.bias + k * CELLS
        buffer[start : start + CELLS] = bias[:, k * LANES_A : (k + 1) * LANES_A].astype(kind)
    if layout.rows > layout.end:
        buffer[layout.end :] = jnp.zeros((layout.rows - layout.end, LANES_A), kind)


MESH = pl.DeviceIdType.MESH


def sum_gradients(layout, blocks, *refs):
    enc, dec, rest = refs[:8], refs[8:14], refs[14:]
    (
        total_out, kv_out, vec_out,
        own, theirs, from_sib, low, landed, total, sib_kv, vec_send, vec_sib, vec_own, vec_landed,
        sib_send, sib_recv, send_sem, recv_sem, vec_ssem, vec_rsem, out_ssem, out_rsem,
    ) = rest
    core, me = lax.axis_index("section"), lax.axis_index("tok")
    sibling = {"section": 1 - core}

    def peer(offset):
        return lax.rem(me + offset, blocks)

    barrier = pltpu.get_barrier_semaphore()
    pl.semaphore_signal(barrier, inc=1, device_id=sibling, device_id_type=MESH)

    def greet(offset, carry):
        pl.semaphore_signal(
            barrier, inc=1, device_id={"tok": peer(offset)}, device_id_type=MESH
        )
        return carry

    lax.fori_loop(1, blocks, greet, 0)

    e_up, e_down, e_q, e_k, e_v, e_out, e_vec, e_bias = enc
    d_up, d_down, d_q, d_out, d_vec, d_bias = dec

    @pl.when(core == 0)
    def _():
        fill(theirs, layout, d_up, d_down, d_q, d_out, e_v, d_bias)
        fill(own, layout, e_up, e_down, e_q, e_out, e_k, e_bias)
        vec_send[...] = d_vec[...]
        vec_own[...] = e_vec[...]

    @pl.when(core == 1)
    def _():
        fill(theirs, layout, e_up, e_down, e_q, e_out, e_k, e_bias)
        fill(own, layout, d_up, d_down, d_q, d_out, e_v, d_bias)
        vec_send[...] = e_vec[...]
        vec_own[...] = d_vec[...]

    pl.semaphore_wait(barrier, blocks)

    def to_sibling(source, target, k):
        return pltpu.make_async_remote_copy(
            src_ref=source, dst_ref=target, send_sem=sib_send.at[k], recv_sem=sib_recv.at[k],
            device_id=sibling, device_id_type=MESH,
        )

    first = to_sibling(theirs, from_sib, 0)
    second = to_sibling(vec_send, vec_sib, 1)
    first.start()
    second.start()
    first.wait()
    second.wait()
    own[...] += from_sib[...].astype(F32)
    low[...] = own[...].astype(BF16)
    vec_own[...] += vec_sib[...]

    def rows_of(position):
        return pl.ds(pl.multiple_of(position * layout.chunk, 16), layout.chunk)

    def scatter(offset):
        return pltpu.make_async_remote_copy(
            src_ref=low.at[rows_of(peer(offset))], dst_ref=landed.at[offset],
            send_sem=send_sem.at[offset], recv_sem=recv_sem.at[offset],
            device_id={"tok": peer(offset)}, device_id_type=MESH,
        )

    def scatter_vec(offset):
        return pltpu.make_async_remote_copy(
            src_ref=vec_own, dst_ref=vec_landed.at[offset],
            send_sem=vec_ssem.at[offset], recv_sem=vec_rsem.at[offset],
            device_id={"tok": peer(offset)}, device_id_type=MESH,
        )

    def gather(offset):
        return pltpu.make_async_remote_copy(
            src_ref=total.at[rows_of(me)], dst_ref=total.at[rows_of(me)],
            send_sem=out_ssem.at[offset], recv_sem=out_rsem.at[offset],
            device_id={"tok": peer(offset)}, device_id_type=MESH,
        )

    def gathered(offset):
        rows = rows_of(lax.rem(me - offset + blocks, blocks))
        return pltpu.make_async_remote_copy(
            src_ref=total.at[rows], dst_ref=total.at[rows],
            send_sem=out_ssem.at[offset], recv_sem=out_rsem.at[offset],
            device_id={"tok": peer(offset)}, device_id_type=MESH,
        )

    def start(offset, carry):
        scatter(offset).start()
        scatter_vec(offset).start()
        return carry

    lax.fori_loop(1, blocks, start, 0)

    def add(offset, carry):
        scatter(offset).wait_recv()
        return carry + landed[offset].astype(F32)

    chunk_sum = lax.fori_loop(1, blocks, add, own[rows_of(me)])
    total[rows_of(me)] = chunk_sum.astype(BF16)

    def spread(offset, carry):
        gather(offset).start()
        return carry

    lax.fori_loop(1, blocks, spread, 0)

    def add_vec(offset, carry):
        scatter_vec(offset).wait_recv()
        return carry + vec_landed[offset]

    vec_out[...] = lax.fori_loop(1, blocks, add_vec, vec_own[...])

    def arrive(offset, carry):
        gathered(offset).wait_recv()
        return carry

    lax.fori_loop(1, blocks, arrive, 0)
    kv_rows = pl.ds(layout.kv, 2 * layout.tall)
    third = to_sibling(total.at[kv_rows], sib_kv, 2)
    third.start()
    total_out[...] = total[...]

    def drain(offset, carry):
        scatter(offset).wait_send()
        scatter_vec(offset).wait_send()
        gather(offset).wait_send()
        return carry

    lax.fori_loop(1, blocks, drain, 0)
    third.wait()
    kv_out[...] = sib_kv[...]


def run_sum(enc_sums, dec_sums, layout, blocks):
    channels = layout.channels
    rows, chunk, tall = layout.rows, layout.chunk, layout.tall
    dma = pltpu.SemaphoreType.DMA
    vmem = pl.BlockSpec(memory_space=pltpu.VMEM)
    args = [*enc_sums, *dec_sums]
    return pl.pallas_call(
        functools.partial(sum_gradients, layout, blocks),
        in_specs=[vmem] * len(args),
        out_specs=[vmem] * 3,
        out_shape=[
            jax.ShapeDtypeStruct((rows, LANES_A), BF16),
            jax.ShapeDtypeStruct((2 * tall, LANES_A), BF16),
            jax.ShapeDtypeStruct((8, channels), F32),
        ],
        scratch_shapes=[
            pltpu.VMEM((rows, LANES_A), F32),
            pltpu.VMEM((rows, LANES_A), BF16),
            pltpu.VMEM((rows, LANES_A), BF16),
            pltpu.VMEM((rows, LANES_A), BF16),
            pltpu.VMEM((blocks, chunk, LANES_A), BF16),
            pltpu.VMEM((rows, LANES_A), BF16),
            pltpu.VMEM((2 * tall, LANES_A), BF16),
            pltpu.VMEM((8, channels), F32),
            pltpu.VMEM((8, channels), F32),
            pltpu.VMEM((8, channels), F32),
            pltpu.VMEM((blocks, 8, channels), F32),
            dma((3,)),
            dma((3,)),
            *[dma((blocks,))] * 6,
        ],
        compiler_params=pltpu.CompilerParams(
            collective_id=0, has_side_effects=True, vmem_limit_bytes=VMEM_BYTES
        ),
        name="sum_gradients",
    )(*args)


def finish(layout, batches, returns, core_ref, total, sib_kv, vec, *refs):
    returned, refs = refs[:returns], refs[returns + 1 :]
    (
        ends, ln1_gain, ln1_bias, q_weight, q_bias, kv_weight, v_bias, out_weight, out_bias, table,
        ln2_gain, ln2_bias, up_weight, up_bias, down_weight, down_bias, placed, copy_sem,
    ) = refs
    is_encoder = core_ref[0] == 0
    step = pl.program_id(0)

    def copies():
        return [
            pltpu.make_async_copy(
                ref,
                ends.at[batches - returns + k, pl.ds(WIN, WIN), pl.ds(step * WIN, WIN)],
                copy_sem.at[k],
            )
            for k, ref in enumerate(returned)
        ]

    pl.when(is_encoder)(lambda: start_all(copies()))

    @pl.when(step == 0)
    def _():
        unpack(
            layout, is_encoder, total, sib_kv, vec, ln1_gain, ln1_bias, q_weight, q_bias, kv_weight,
            v_bias, out_weight, out_bias, table, ln2_gain, ln2_bias, up_weight, up_bias, down_weight,
            down_bias, placed,
        )

    pl.when(is_encoder)(lambda: wait_all(copies()))


def unpack(
    layout, is_encoder, total, sib_kv, vec, ln1_gain, ln1_bias, q_weight, q_bias, kv_weight,
    v_bias, out_weight, out_bias, table, ln2_gain, ln2_bias, up_weight, up_bias, down_weight, down_bias,
    placed,
):
    channels, tall, half = layout.channels, layout.tall, LANES_A // 2
    for row, ref in enumerate((ln1_gain, ln1_bias, ln2_gain, ln2_bias, down_bias)):
        ref[...] = vec[row : row + 1]

    def at(start, rows):
        return total[start : start + rows].astype(F32)

    for k in range(layout.tiles):
        cols = slice(k * LANES_A, (k + 1) * LANES_A)
        tile = at(layout.up + k * tall, tall)
        up_weight[:, cols] = tile[:channels]
        up_bias[:, cols] = tile[channels : channels + 1]
        down_weight[cols] = at(layout.down + k * channels, channels).T
    rest = at(layout.rest, tall)
    q = jnp.concatenate([at(layout.q, tall), rest[:, :half]], 1)
    out = jnp.concatenate([at(layout.out, tall), rest[:, half:]], 1)
    q_weight[...] = q[:channels]
    q_bias[...] = q[channels : channels + 1]
    out_weight[...] = out[:channels]
    out_bias[...] = out[channels : channels + 1]
    mine = at(layout.kv, 2 * tall)
    other = sib_kv[...].astype(F32)
    for start, side in ((0, jnp.where(is_encoder, mine, other)), (channels, jnp.where(is_encoder, other, mine))):
        side = jnp.concatenate([side[:tall], side[tall:, :half]], 1)
        kv_weight[:, start : start + channels] = side[:channels]
    v_bias[...] = side[channels : channels + 1]
    placed[...] = jnp.zeros_like(placed)
    positions = [position_matrix(False), position_matrix(True)]
    for h in range(HEADS):
        start = layout.bias + h // 2 * CELLS
        placed[h, :, :256] = nt(total[start : start + CELLS], positions[h % 2])
    entries = jnp.zeros((8, 384), F32)
    for j in range(CELLS):
        entries += pltpu.roll(placed[:, j, :], CENTRE - cell_position(j), 1)
    table[...] = entries[:HEADS, : SPAN**3]


def run_finish(core, total, sib_kv, vec, returned, ends, layout):
    channels = layout.channels
    hidden = layout.tiles * LANES_A
    _, _, rows_y, rows_z, _ = ends.shape
    any_spec = pl.BlockSpec(memory_space=pl.ANY)
    shapes = [
        (1, channels), (1, channels), (channels, channels), (1, channels), (channels, 2 * channels),
        (1, channels), (channels, channels), (1, channels), (HEADS, SPAN**3),
        (1, channels), (1, channels), (channels, hidden), (1, hidden), (hidden, channels), (1, channels),
    ]
    shapes = [jax.ShapeDtypeStruct(shape, F32) for shape in shapes]
    return pl.pallas_call(
        functools.partial(finish, layout, ends.shape[0], len(returned)),
        grid_spec=pltpu.PrefetchScalarGridSpec(
            num_scalar_prefetch=1,
            grid=(rows_y // WIN,),
            in_specs=[
                *[whole(a) for a in (total, sib_kv, vec)],
                *[
                    pl.BlockSpec(
                        (WIN, WIN, rows_z, channels), lambda i, c: (0, i * (1 - c[0]), 0, 0)
                    )
                ]
                * len(returned),
                any_spec,
            ],
            out_specs=[any_spec, *[whole(a) for a in shapes]],
            scratch_shapes=[
                pltpu.VMEM((8, CELLS, 384), F32),
                pltpu.SemaphoreType.DMA((len(returned),)),
            ],
        ),
        out_shape=[jax.ShapeDtypeStruct(ends.shape, F32), *shapes],
        input_output_aliases={4 + len(returned): 0},
        compiler_params=params,
        name="finish",
    )(core, total, sib_kv, vec, *returned, ends)


def cell_position(ids):
    x = 2 * (ids // 32) + ids // 4 % 2
    y = 2 * (ids // 16 % 2) + ids // 2 % 2
    z = 2 * (ids // 8 % 2) + ids % 2
    return (x * SPAN + y) * SPAN + z


CENTRE = (WIN - 1) * (SPAN * SPAN + SPAN + 1)
TABLE_ROW = 8


def position_matrix(odd):
    rows = lax.broadcasted_iota(jnp.int32, (256, 2 * CELLS), 0)
    ids = lax.broadcasted_iota(jnp.int32, (256, 2 * CELLS), 1) - (CELLS if odd else 0)
    hit = (ids >= 0) & (ids < CELLS) & (rows == cell_position(ids))
    return jnp.where(hit, 1.0, 0.0).astype(BF16)


def spread_bias(table, shifted):
    for j in range(CELLS):
        turned = pltpu.roll(table, (384 - CENTRE + cell_position(j)) % 384, 1)
        for h in range(HEADS):
            shifted[h, j : j + 1] = turned[h : h + 1, :256]
    even, odd = position_matrix(False), position_matrix(True)
    pairs = [
        nn(shifted[2 * p].astype(BF16), even) + nn(shifted[2 * p + 1].astype(BF16), odd)
        for p in range(HEADS // 2)
    ]
    return jnp.concatenate(pairs, 1) * log2_e


def prepare(
    blocks, q_w, out_w, up_w, down_w, kv_w, v_b, ln1_g, ln1_b, ln2_g, ln2_b, out_b, down_b, q_b, up_b, table,
    vec_e, vec_d, w_qkv, b_qkv, w_q_d, b_q_d, w_out_e, w_out_d, w_up_e, w_up_d, b_up_e, b_up_d,
    w_down_e, w_down_d, bias_e, bias_d,
    small, small_sib, q_sib, out_sib, up_sib, down_sib, shifted, send_sem, recv_sem,
):
    core, block = lax.axis_index("section"), lax.axis_index("tok")
    channels, hidden = up_w.shape
    sibling = {"section": 1 - core}
    barrier = pltpu.get_barrier_semaphore()
    pl.semaphore_signal(barrier, inc=1, device_id=sibling, device_id_type=MESH)
    small[...] = jnp.zeros_like(small)
    for row, ref in enumerate((ln1_g, ln1_b, ln2_g, ln2_b, out_b, down_b, q_b)):
        small[row : row + 1, :channels] = ref[...].astype(F32)
    small[7:8, :hidden] = up_b[...].astype(F32)
    small[TABLE_ROW : TABLE_ROW + HEADS, : SPAN**3] = table[...].astype(F32)
    pl.semaphore_wait(barrier, 1)
    pairs = ((small, small_sib), (q_w, q_sib), (out_w, out_sib), (up_w, up_sib), (down_w, down_sib))
    copies = [
        pltpu.make_async_remote_copy(
            src_ref=source, dst_ref=target, send_sem=send_sem.at[k], recv_sem=recv_sem.at[k],
            device_id=sibling, device_id_type=MESH,
        )
        for k, (source, target) in enumerate(pairs)
    ]
    for copy in copies:
        copy.start()
    for copy in copies:
        copy.wait()

    def place(enc, dec):
        e_small, e_q, e_out, e_up, e_down = enc
        d_small, d_q, d_out, d_up, d_down = dec
        for source, vec, b_up in ((e_small, vec_e, b_up_e), (d_small, vec_d, b_up_d)):
            vec[...] = source[:8, :channels]
            b_up[...] = source[7:8, :hidden]
        w_qkv[...] = jnp.zeros_like(w_qkv)
        b_qkv[...] = jnp.zeros_like(b_qkv)
        w_qkv[:, :channels] = e_q[...]
        w_qkv[:, 256 : 256 + channels] = kv_w[:, :channels]
        w_qkv[:, 512 : 512 + channels] = kv_w[:, channels:]
        b_qkv[:, :channels] = e_small[6:7, :channels]
        b_qkv[:, 512 : 512 + channels] = v_b[...].astype(F32)
        w_q_d[...] = d_q[...]
        b_q_d[...] = d_small[6:7, :channels]
        for target, source in (
            (w_out_e, e_out), (w_out_d, d_out), (w_up_e, e_up), (w_up_d, d_up),
            (w_down_e, e_down), (w_down_d, d_down),
        ):
            target[...] = source[...]
        rows = slice(TABLE_ROW, TABLE_ROW + 8)
        bias_e[...] = spread_bias(e_small[rows, :384], shifted)
        return spread_bias(d_small[rows, :384], shifted)

    own = (small, q_w, out_w, up_w, down_w)
    sib = (small_sib, q_sib, out_sib, up_sib, down_sib)

    def masked(base):
        shape = (CELLS, HEADS * CELLS)
        keys = lax.broadcasted_iota(jnp.int32, shape, 0)
        queries = lax.broadcasted_iota(jnp.int32, shape, 1) % CELLS

        def differ(unit):
            return jnp.where(keys // unit % 2 != queries // unit % 2, 1.0, 0.0)

        last = jnp.where((core == 1) & (block == blocks - 1), 1.0, 0.0)
        for y in range(2):
            for z in range(2):
                apart = jnp.maximum(last * differ(32), jnp.maximum(y * differ(16), z * differ(8)))
                bias_d[y, z] = base + apart * (mask_fill * log2_e)

    @pl.when(core == 0)
    def _():
        masked(place(own, sib))

    @pl.when(core == 1)
    def _():
        masked(place(sib, own))


def run_prepare(blocks, weights, smalls, table, kv_weight, v_bias):
    q_w, out_w, up_w, down_w = weights
    channels, hidden = up_w.shape
    vmem = pl.BlockSpec(memory_space=pltpu.VMEM)
    args = [*weights, kv_weight, v_bias, *smalls, table]
    bias = (CELLS, HEADS * CELLS)
    square = (channels, channels)

    def f32(*shape):
        return jax.ShapeDtypeStruct(shape, F32)

    def bf16(*shape):
        return jax.ShapeDtypeStruct(shape, BF16)

    shapes = [
        f32(8, channels), f32(8, channels), bf16(channels, 768), f32(1, 768), bf16(*square),
        f32(1, channels), bf16(*square), bf16(*square), bf16(channels, hidden), bf16(channels, hidden),
        f32(1, hidden), f32(1, hidden), bf16(hidden, channels), bf16(hidden, channels),
        f32(*bias), f32(2, 2, *bias),
    ]
    return pl.pallas_call(
        functools.partial(prepare, blocks),
        in_specs=[vmem] * len(args),
        out_specs=[vmem] * len(shapes),
        out_shape=shapes,
        scratch_shapes=[
            pltpu.VMEM((TABLE_ROW + 8, hidden), F32),
            pltpu.VMEM((TABLE_ROW + 8, hidden), F32),
            pltpu.VMEM(square, BF16),
            pltpu.VMEM(square, BF16),
            pltpu.VMEM((channels, hidden), BF16),
            pltpu.VMEM((hidden, channels), BF16),
            pltpu.VMEM((HEADS, CELLS, 256), F32),
            pltpu.SemaphoreType.DMA((5,)),
            pltpu.SemaphoreType.DMA((5,)),
        ],
        compiler_params=pltpu.CompilerParams(
            collective_id=1, has_side_effects=True, vmem_limit_bytes=VMEM_BYTES
        ),
        name="prepare",
    )(*args)


def run_encoder(core, tokens, batch, consts, cotangent):
    _, _, rows_y, rows_z, channels = tokens.shape
    groups, size = rows_y // WIN, 4 * rows_z
    cells, windows = 4 * size, rows_z // WIN
    hidden = consts[6].shape[1]
    slab = jax.ShapeDtypeStruct((groups, 2, 3, size * 3 // 2, LANES_A), BF16)
    outs = [
        slab,
        slab,
        jax.ShapeDtypeStruct((groups, cells, 256), F32),
        jax.ShapeDtypeStruct((groups, cells, 256), F32),
        jax.ShapeDtypeStruct((groups, windows, CELLS, HEADS * CELLS), BF16),
        jax.ShapeDtypeStruct((groups, cells, channels), BF16),
        jax.ShapeDtypeStruct((groups, cells, hidden), BF16),
        jax.ShapeDtypeStruct((groups, cells, hidden), BF16),
    ]

    def row(array):
        zeros = (0,) * (array.ndim - 1)
        return pl.BlockSpec((1, *array.shape[1:]), lambda i, c: (i, *zeros))

    batches = tokens.shape[0]
    cut = [] if cotangent is None else [cotangent]
    cut_block = (batches, SHIFT, WIN, rows_z, channels)
    cut_outs = [
        jax.ShapeDtypeStruct((batches, SHIFT, rows_y, rows_z, channels), a.dtype) for a in cut
    ]
    return pl.pallas_call(
        functools.partial(encoder_forward, len(cut)),
        grid_spec=pltpu.PrefetchScalarGridSpec(
            num_scalar_prefetch=1,
            grid=(groups,),
            in_specs=[
                pl.BlockSpec(
                    (1, WIN, WIN, rows_z, channels), lambda i, c: (batch, c[0], i, 0, 0)
                ),
                *[whole(a) for a in consts],
                *[pl.BlockSpec(cut_block, lambda i, c: (0, 2 * c[0], i, 0, 0)) for _ in cut],
            ],
            out_specs=[
                *[row(a) for a in outs],
                *[pl.BlockSpec(cut_block, lambda i, c: (0, 0, i, 0, 0)) for _ in cut],
            ],
            scratch_shapes=[pltpu.VMEM((cells, 768), BF16)],
        ),
        out_shape=[*outs, *cut_outs],
        compiler_params=params,
        cost_estimate=cost(groups * cells, 466944, groups * cells * 7500),
        name="encoder_forward",
    )(core, tokens, *consts, *cut)


def run_encoder_back(core, batch, own, halo, ys, returned, saved, old, consts, tokens):
    groups, _, _, packed, _ = own.shape
    batches, planes, rows_y, rows_z, channels = tokens.shape
    size = 4 * rows_z
    hidden = consts[5].shape[1]
    first = old is None
    shapes = sums_shapes(channels, hidden, 3)
    outs = [
        jax.ShapeDtypeStruct(tokens.shape, F32),
        jax.ShapeDtypeStruct((WIN, rows_y, rows_z, channels), F32),
        *shapes,
    ]

    def slab(unit):
        def place(i, c):
            return ((i if unit == 0 else (i + groups - 1) % groups), unit, 0, 0, 0)

        return pl.BlockSpec((1, 1, 3, packed, LANES_A), place)

    def row(array):
        zeros = (0,) * (array.ndim - 1)
        return pl.BlockSpec((1, *array.shape[1:]), lambda i, c: (i, *zeros))

    def for_core(core, planes_here):
        def place(i, c):
            return (0, i * (c[0] if core == 1 else 1 - c[0]), 0, 0)

        return pl.BlockSpec((planes_here, WIN, rows_z, channels), place)

    any_spec = pl.BlockSpec(memory_space=pl.ANY)
    olds = [] if first else [*old[1], old[0]]
    args = [core, *consts, *ys, own, own, halo, halo, *saved, *returned, *olds]
    return pl.pallas_call(
        functools.partial(encoder_backward, first, batch, len(returned)),
        grid_spec=pltpu.PrefetchScalarGridSpec(
            num_scalar_prefetch=1,
            grid=(groups,),
            in_specs=[
                *[whole(a) for a in consts],
                *[for_core(1, n) for n in (2, 2, 4)],
                slab(0),
                slab(1),
                slab(0),
                slab(1),
                *[row(a) for a in saved],
                *[for_core(0, WIN)] * len(returned),
                *[whole(a) for a in olds[:-1]],
                *[any_spec] * (0 if first else 1),
            ],
            out_specs=[any_spec, any_spec, *[whole(a) for a in shapes]],
            scratch_shapes=[
                pltpu.VMEM((4 * size, 768), BF16),
                pltpu.VMEM((3, 4 * size, channels), BF16),
                pltpu.VMEM((2, WIN, WIN, rows_z, channels), F32),
                pltpu.SemaphoreType.DMA((2,)),
                pltpu.SemaphoreType.DMA((8 + batches,)),
            ],
        ),
        out_shape=outs,
        input_output_aliases={} if first else {len(args) - 1: 0},
        compiler_params=params,
        cost_estimate=cost(groups * 4 * size, 933888, groups * 4 * size * 9000),
        name="encoder_backward",
    )(*args)


def run_decoder(core, keep, recv, cotangent, cot_recv, batch, old, consts):
    groups, _, _, packed, _ = keep.shape
    rows_z, channels = cotangent.shape[3:]
    size = 4 * rows_z
    hidden = consts[6].shape[1]
    windows = rows_z // WIN
    first = old is None
    shapes = sums_shapes(channels, hidden, 1)
    slab_shape = jax.ShapeDtypeStruct((groups, 2, 3, packed, LANES_A), BF16)
    outs = [
        *[jax.ShapeDtypeStruct((n, groups * WIN, rows_z, channels), F32) for n in (4, 2)],
        slab_shape,
        slab_shape,
        *shapes,
    ]

    def slab(unit):
        def place(i, c):
            return ((i if unit == 1 else (i + 1) % groups), unit, 0, 0, 0)

        return pl.BlockSpec((1, 1, 3, packed, LANES_A), place)

    def cot(unit, own):
        def place(i, c):
            y = 2 * i + 1 if unit == 1 else (2 * i + 2) % (2 * groups)
            return (batch, 2 * c[0] + 1 if own else 0, y, 0, 0)

        return pl.BlockSpec((1, 2, 2, rows_z, channels), place)

    def bias_place(i, c):
        return (i // (groups - 1), 0, 0, 0)

    specs = [whole(a) for a in consts]
    specs[4] = pl.BlockSpec((1, *consts[4].shape[1:]), bias_place)
    olds = [] if first else list(old)
    out_slab = pl.BlockSpec((1, 2, 3, packed, LANES_A), lambda i, c: (i, 0, 0, 0, 0))
    return pl.pallas_call(
        functools.partial(decoder, first),
        grid_spec=pltpu.PrefetchScalarGridSpec(
            num_scalar_prefetch=1,
            grid=(groups,),
            in_specs=[
                *specs,
                slab(1),
                slab(0),
                slab(1),
                slab(0),
                cot(1, True),
                cot(0, True),
                cot(1, False),
                cot(0, False),
                *[whole(a) for a in olds],
            ],
            out_specs=[
                *[pl.BlockSpec((n, WIN, rows_z, channels), lambda i, c: (0, i, 0, 0)) for n in (4, 2)],
                out_slab,
                out_slab,
                *[whole(a) for a in shapes],
            ],
            scratch_shapes=[
                pltpu.VMEM((windows, CELLS, HEADS * CELLS), F32),
                pltpu.VMEM((4 * size, channels), BF16),
                pltpu.VMEM((4 * size, hidden), BF16),
                pltpu.VMEM((4 * size, hidden), F32),
                pltpu.VMEM((3, 4 * size, channels), F32),
            ],
        ),
        out_shape=outs,
        compiler_params=params,
        cost_estimate=cost(groups * 4 * size, 1253376, groups * 4 * size * 4000),
        name="decoder",
    )(core, *consts, keep, keep, recv, recv, cotangent, cotangent, cot_recv, cot_recv, *olds)


def body(
    tokens,
    cotangent,
    ln1_gain,
    ln1_bias,
    q_weight,
    q_bias,
    kv_weight,
    v_bias,
    out_weight,
    out_bias,
    rel_table,
    ln2_gain,
    ln2_bias,
    up_weight,
    up_bias,
    down_weight,
    down_bias,
):
    batches, planes, rows_y, rows_z, channels = tokens.shape
    axes = ("section", "tok")
    core = lax.axis_index("section")
    block = lax.axis_index("tok")
    blocks = lax.axis_size("tok")
    is_encoder = core == 0
    core_arg = core.astype(jnp.int32).reshape(1)

    def device(position):
        position = position % (2 * blocks)
        return (position % 2) * blocks + position // 2

    to_previous = [(device(r), device(r - 1)) for r in range(2 * blocks)]
    to_next = [(device(r), device(r + 1)) for r in range(2 * blocks)]

    (
        vec_e, vec_d, w_qkv, b_qkv, w_q_d, b_q_d, w_out_e, w_out_d, w_up_e, w_up_d, b_up_e, b_up_d,
        w_down_e, w_down_d, bias_e, bias_d,
    ) = run_prepare(
        blocks,
        (q_weight[0], out_weight[0], up_weight[0], down_weight[0]),
        (ln1_gain, ln1_bias, ln2_gain, ln2_bias, out_bias, down_bias, q_bias, up_bias),
        rel_table[0],
        kv_weight,
        v_bias[None],
    )
    order = jnp.asarray(order_matrix(rows_z, 0), BF16)
    order_rolled = jnp.asarray(order_matrix(rows_z, 1), BF16)

    enc_consts = (order, vec_e, w_qkv, b_qkv, bias_e, w_out_e, w_up_e, b_up_e, w_down_e)
    enc_back_consts = (order, vec_e, w_qkv, b_qkv, w_out_e, w_up_e, w_down_e)
    dec_consts = (order_rolled, vec_d, w_q_d, b_q_d, bias_d, w_out_d, w_up_d, b_up_d, w_down_d)

    handed, saved = [], []
    for batch in range(batches):
        send, keep, *rest = run_encoder(
            core_arg, tokens, batch, enc_consts, cotangent if batch == 0 else None
        )
        if batch == 0:
            *rest, half = rest
            cot_recv = lax.ppermute(half, axes, to_previous)
        handed.append((keep, lax.ppermute(send, axes, to_previous)))
        saved.append(rest)
    dec_sums = None
    returned, ys = [], []
    to_decoder = [(t, blocks + t) for t in range(blocks)]
    to_encoder = [(blocks + t, t) for t in range(blocks)]
    to_after = [(blocks + t, blocks + (t + 1) % blocks) for t in range(blocks)]
    for batch in range(batches):
        out_all, out_tail, own, halo, *dec_sums = run_decoder(
            core_arg, *handed[batch], cotangent, cot_recv, batch, dec_sums, dec_consts
        )
        returned.append((own, lax.ppermute(halo, axes, to_next)))
        y_halo = lax.ppermute(out_tail, axes, to_after)
        ys.append((out_all, y_halo, lax.ppermute(out_all, axes, to_decoder)))
    old = None
    backs = []
    for batch in range(batches):
        arrived = backs[:1] if batch == batches - 1 else []
        ends, back, *enc_sums = run_encoder_back(
            core_arg, batch, *returned[batch], ys[batch], arrived, saved[batch], old,
            enc_back_consts, tokens,
        )
        old = (ends, enc_sums)
        backs.append(lax.ppermute(back, axes, to_encoder))

    layout = Layout(channels, up_weight.shape[2], blocks)
    total, sib_kv, vec_sum = run_sum(enc_sums, dec_sums, layout, blocks)
    (
        ends, g_ln1_gain, g_ln1_bias, g_q_weight, g_q_bias, g_kv_weight, g_v_bias, g_out_weight,
        g_out_bias, g_table, g_ln2_gain, g_ln2_bias, g_up_weight, g_up_bias, g_down_weight, g_down_bias,
    ) = run_finish(core_arg, total, sib_kv, vec_sum, backs[1:], ends, layout)
    return (
        ends[None],
        g_ln1_gain,
        g_ln1_bias,
        g_q_weight[None],
        g_q_bias,
        g_kv_weight[None],
        g_v_bias,
        g_out_weight[None],
        g_out_bias,
        g_table[None],
        g_ln2_gain,
        g_ln2_bias,
        g_up_weight[None],
        g_up_bias,
        g_down_weight[None],
        g_down_bias,
    )


def solution(mesh):
    in_specs = (
        P(None, "tok", None, None, None),
        P(None, "tok", None, None, None),
        P("section", None),
        P("section", None),
        P("section", None, None),
        P("section", None),
        P(),
        P(),
        P("section", None, None),
        P("section", None),
        P("section", None, None),
        P("section", None),
        P("section", None),
        P("section", None, None),
        P("section", None),
        P("section", None, None),
        P("section", None),
    )
    out_specs = (
        P("section", None, "tok", None, None, None),
        P("section", None),
        P("section", None),
        P("section", None, None),
        P("section", None),
        P("section", None, None),
        P("section", None),
        P("section", None, None),
        P("section", None),
        P("section", None, None),
        P("section", None),
        P("section", None),
        P("section", None, None),
        P("section", None),
        P("section", None, None),
        P("section", None),
    )
    return jax.shard_map(body, mesh=mesh, in_specs=in_specs, out_specs=out_specs, check_vma=False)
```

```python
import functools

import jax
import jax.numpy as jnp
import numpy as np
from jax import lax
from jax.experimental import pallas as pl
from jax.experimental.pallas import tpu as pltpu
from jax.sharding import PartitionSpec as P

HEADS = 6
HD = 32
WIN = 4
SHIFT = 2
CELLS = WIN**3
SPAN = 2 * WIN - 1
HEADS_A = 4
LANES_A = HEADS_A * HD
COLS_A = HEADS_A * CELLS

eps_norm = 1e-05
mask_fill = -100.0
log2_e = 1.4426950408889634
root_half = 0.7071067811865476
inv_root_two_pi = 0.3989422804014327
scale = HD ** (-0.5)
VMEM_BYTES = 56 * 1024 * 1024

F32 = jnp.float32
BF16 = jnp.bfloat16


def nn(left, right):
    return lax.dot_general(left, right, (((1,), (0,)), ((), ())), preferred_element_type=F32)


def nt(left, right):
    return lax.dot_general(left, right, (((1,), (1,)), ((), ())), preferred_element_type=F32)


def tn(left, right):
    return lax.dot_general(left, right, (((0,), (0,)), ((), ())), preferred_element_type=F32)


def order_matrix(rows_z, rolled):
    count = 4 * rows_z
    matrix = np.zeros((count, count), np.float32)
    units = rows_z // 2
    for unit in range(units):
        for dx in range(2):
            for dy in range(2):
                for dz in range(2):
                    z = (2 * (unit + rolled) + dz) % rows_z
                    matrix[unit * 8 + dx * 4 + dy * 2 + dz, (dx * 2 + dy) * rows_z + z] = 1.0
    return matrix


def windows_of(pieces):
    count, rows, channels = pieces.shape
    return pieces.reshape(count, rows // 16, 16, channels).transpose(1, 0, 2, 3).reshape(-1, channels)


def pieces_of(windows):
    rows, channels = windows.shape
    return (
        windows.reshape(rows // CELLS, 4, 16, channels)
        .transpose(1, 0, 2, 3)
        .reshape(4, rows // 4, channels)
    )


def roll_rows(pieces, steps):
    return jnp.concatenate([pieces[:, steps:], pieces[:, :steps]], 1)


def pack_slab(pieces):
    half = pieces.shape[1] // 2
    rest = pieces[:, :, LANES_A:]
    return jnp.concatenate(
        [pieces[:, :, :LANES_A], jnp.concatenate([rest[:, :half], rest[:, half:]], 2)], 1
    ).astype(BF16)


def unpack_slab(block):
    size = block.shape[0] * 2 // 3
    half = LANES_A // 2
    rest = jnp.concatenate([block[size:, :half], block[size:, half:]], 0)
    return jnp.concatenate([block[:size], rest], 1)


def normalize(rows):
    mean = jnp.mean(rows, -1, keepdims=True)
    centered = rows - mean
    inv_std = lax.rsqrt(jnp.mean(centered * centered, -1, keepdims=True) + eps_norm)
    return centered * inv_std, inv_std


def norm_back(grad_rows, unit_rows, inv_std, gain):
    scaled = grad_rows * gain
    return inv_std * (
        scaled
        - jnp.mean(scaled, -1, keepdims=True)
        - unit_rows * jnp.mean(scaled * unit_rows, -1, keepdims=True)
    )


def gelu_pair(rows):
    upper = 0.5 * lax.erf(rows * root_half) + 0.5
    bell = jnp.exp2(rows * rows * (-0.5 * log2_e))
    return rows * upper, upper + rows * bell * inv_root_two_pi


def head_masks(width):
    heads = lax.broadcasted_iota(jnp.int32, (1, width), 1) // HD
    return [jnp.where(heads == h, 1.0, 0.0).astype(BF16) for h in range(width // HD)]


def expand(rows):
    masks = head_masks(rows.shape[1])
    return jnp.concatenate([rows * mask for mask in masks], 0)


def collapse(stacked):
    width = stacked.shape[1]
    lanes = lax.broadcasted_iota(jnp.int32, (CELLS, width), 1)
    total = stacked[:CELLS]
    for h in range(1, width // HD):
        total = jnp.where(lanes >= h * HD, stacked[h * CELLS : (h + 1) * CELLS], total)
    return total


def split(rows):
    return rows[:, :LANES_A], rows[:, LANES_A:]


def attend(parts, bias):
    queries, keys, values = zip(*[[split(rows) for rows in part] for part in parts])
    wide = [[expand(half) for half in q] for q in queries]
    scores = [
        jnp.concatenate([nt(k[0], q[0]), nt(k[1], q[1])], 1) for k, q in zip(keys, wide)
    ]
    scores = [s * (scale * log2_e) + b for s, b in zip(scores, bias)]
    exponents = [jnp.exp2(s - jnp.max(s, 0, keepdims=True)) for s in scores]
    probs = [e * (1.0 / jnp.sum(e, 0, keepdims=True)) for e in exponents]
    low = [p.astype(BF16) for p in probs]
    mixed = [
        (tn(p[:, :COLS_A], v[0]), tn(p[:, COLS_A:], v[1])) for p, v in zip(low, values)
    ]
    mixed = [jnp.concatenate([collapse(m[0]), collapse(m[1])], 1).astype(BF16) for m in mixed]
    return mixed, probs


def attend_back(parts):
    queries, keys, values, grads = zip(
        *[[split(rows) for rows in part[:3] + part[4:]] for part in parts]
    )
    probs = [part[3] for part in parts]
    wide_g = [[expand(half) for half in g] for g in grads]
    d_probs = [
        jnp.concatenate([nt(v[0], g[0]), nt(v[1], g[1])], 1) for v, g in zip(values, wide_g)
    ]
    low = [part[3].astype(BF16) for part in parts]
    d_values = [
        jnp.concatenate([nn(p[:, :COLS_A], g[0]), nn(p[:, COLS_A:], g[1])], 1)
        for p, g in zip(low, wide_g)
    ]
    wide_q = [[expand(half) for half in q] for q in queries]
    d_scores = [
        p * (d - jnp.sum(d * p, 0, keepdims=True)) for p, d in zip(probs, d_probs)
    ]
    low_d = [d.astype(BF16) for d in d_scores]
    d_keys = [
        jnp.concatenate([nn(d[:, :COLS_A], q[0]), nn(d[:, COLS_A:], q[1])], 1) * scale
        for d, q in zip(low_d, wide_q)
    ]
    d_queries = [
        (tn(d[:, :COLS_A], k[0]), tn(d[:, COLS_A:], k[1])) for d, k in zip(low_d, keys)
    ]
    d_queries = [
        jnp.concatenate([collapse(d[0]), collapse(d[1])], 1) * scale for d in d_queries
    ]
    table = d_scores[0]
    for d in d_scores[1:]:
        table = table + d
    return d_queries, d_keys, d_values, table


def window_groups(count):
    return [range(k, min(k + TOGETHER, count)) for k in range(0, count, TOGETHER)]


def window_rows(k):
    return slice(k * CELLS, (k + 1) * CELLS)


def with_ones(rows):
    return jnp.concatenate([rows.T, jnp.ones((16, rows.shape[0]), BF16)], 0)


def col_sum(rows):
    return jnp.sum(rows, 0, keepdims=True)


def start_sums(first, old_refs, new_refs):
    @pl.when(pl.program_id(0) == 0)
    def _():
        for k, new in enumerate(new_refs):
            new[...] = jnp.zeros_like(new) if first else old_refs[k][...]


def restore(matrix, rows):
    high = rows.astype(BF16)
    low = (rows - high.astype(F32)).astype(BF16)
    return tn(matrix, high) + tn(matrix, low)


CHUNK = 256
TOGETHER = 4


def encoder_forward(
    cuts, core_ref, tok, order, vec, w_qkv, b_qkv, bias, w_out, w_up, b_up, w_down, *rest,
):
    cut_in, rest = rest[:cuts], rest[cuts:]
    send, keep, n1_out, n2_out, p_out, o_out, a_out, s_out, *cut_out, qkv = rest
    for source, target in zip(cut_in, cut_out):
        target[...] = source[...]
    rows_z = tok.shape[3]
    size = 4 * rows_z
    pieces = []
    for x in range(2):
        for y in range(2):
            part = tok[0, 2 * x : 2 * x + 2, 2 * y : 2 * y + 2].reshape(size, -1)
            pieces.append(nn(order[...], part))
    entry = windows_of(jnp.stack(pieces))
    unit, inv_std = normalize(entry)
    channels = entry.shape[1]
    wide = jnp.broadcast_to(inv_std, (entry.shape[0], 256 - channels))
    n1_out[0, :, :channels] = unit
    n1_out[0, :, channels:] = wide
    left = (unit * vec[0:1] + vec[1:2]).astype(BF16)
    triple = nn(left, w_qkv[...]) + b_qkv[...]
    qkv[...] = triple.astype(BF16)
    for together in window_groups(entry.shape[0] // CELLS):
        parts = [
            [qkv[window_rows(k), 256 * f : 256 * f + 192] for f in range(3)] for k in together
        ]
        mixed, probs = attend(parts, [bias[...]] * len(parts))
        for k, o, p in zip(together, mixed, probs):
            p_out[0, k] = p.astype(BF16)
            o_out[0, window_rows(k)] = o
    middle = entry + nn(o_out[0], w_out[...]) + vec[4:5]
    unit, inv_std = normalize(middle)
    wide = jnp.broadcast_to(inv_std, (entry.shape[0], 256 - channels))
    n2_out[0, :, :channels] = unit
    n2_out[0, :, channels:] = wide
    left = (unit * vec[2:3] + vec[3:4]).astype(BF16)
    results = []
    for k in range(entry.shape[0] // CHUNK):
        rows = slice(k * CHUNK, (k + 1) * CHUNK)
        hidden, slope = gelu_pair(nn(left[rows], w_up[...]) + b_up[...])
        hidden = hidden.astype(BF16)
        a_out[0, rows] = hidden
        s_out[0, rows] = slope.astype(BF16)
        results.append(nn(hidden, w_down[...]))
    result = middle + jnp.concatenate(results, 0) + vec[5:6]
    for field, rows in enumerate((result, triple[:, 256:448], triple[:, 512:704])):
        rolled = pack_slab(roll_rows(pieces_of(rows), 8))
        send[0, :, field] = rolled[:2]
        keep[0, :, field] = rolled[2:]


def mlp_back(grad, grad_low, hidden, slope, left_two, unit, inv_std, w_up, w_down, vec, sums):
    g_up, g_down, g_vec = sums
    backs = []
    total_up = None
    turned = grad_low.T
    ones = with_ones(left_two)
    for k in range(grad.shape[0] // CHUNK):
        rows = slice(k * CHUNK, (k + 1) * CHUNK)
        d_pre = (nt(grad_low[rows], w_down[...]) * slope(rows)).astype(BF16)
        part = nn(ones[:, rows], d_pre)
        total_up = part if total_up is None else total_up + part
        backs.append(nt(d_pre, w_up[...]))
    g_up[...] += total_up
    g_down[...] += nn(turned, hidden)
    d_normed = jnp.concatenate(backs, 0)
    g_vec[2:3] += col_sum(d_normed * unit)
    g_vec[3:4] += col_sum(d_normed)
    g_vec[4:5] += col_sum(grad)
    return grad + norm_back(d_normed, unit, inv_std, vec[2:3])


def start_all(copies):
    for copy in copies:
        copy.start()


def wait_all(copies):
    for copy in copies:
        copy.wait()


def encoder_backward(
    first, batch, returns, comm, order, vec, w_qkv, b_qkv, w_out, w_up, w_down,
    y_own, y_halo, y_sib,
    keep_a, keep_b, recv_a, recv_b,
    n1_in, n2_in, p_in, o_in, a_in, s_in, *rest,
):
    returned, rest = rest[:returns], rest[returns:]
    old, rest = ([], rest) if first else (rest[:8], rest[9:])
    comm_in, rest = rest[: comm.inputs], rest[comm.inputs :]
    ends, back, *rest = rest
    sums, rest = rest[:8], rest[8:]
    comm_out, rest = rest[: comm.outputs], rest[comm.outputs :]
    qkv, dqkv, buffer, out_sem, copy_sem, *comm_scratch = rest
    comm_begin, comm_end = comm.work(comm_in, comm_out, comm_scratch)
    g_up, g_down, g_q, g_k, g_v, g_out, g_vec, g_bias = sums
    step, steps = pl.program_id(0), pl.num_programs(0)
    is_encoder = lax.axis_index("section") == 0
    rows_y = ends.shape[2]
    slot = lax.rem(step, 2)

    def output_copies():
        copies = []
        for start, planes, ref in ((0, 2, y_halo), (2, 4, y_sib), (6, 2, y_own)):
            for half in range(2):
                rows = pl.ds(lax.rem(step * WIN + SHIFT + 2 * half, rows_y), 2)
                target = ends.at[batch, pl.ds(start, planes), rows]
                copies.append((ref.at[:, pl.ds(2 * half, 2)], target))
        return [
            pltpu.make_async_copy(source, target, copy_sem.at[k])
            for k, (source, target) in enumerate(copies)
        ]

    def gradient_copies():
        return [
            pltpu.make_async_copy(
                ref, ends.at[k, pl.ds(WIN, WIN), pl.ds(step * WIN, WIN)], copy_sem.at[8 + k]
            )
            for k, ref in enumerate(returned)
        ]

    def result_copy(index, to_ends):
        target = (
            ends.at[batch, pl.ds(0, WIN), pl.ds(index * WIN, WIN)]
            if to_ends
            else back.at[:, pl.ds(index * WIN, WIN)]
        )
        at = lax.rem(index, 2)
        return pltpu.make_async_copy(buffer.at[at], target, out_sem.at[at])

    def for_core(encoder_work, decoder_work):
        pl.when(is_encoder)(encoder_work)
        pl.when(jnp.logical_not(is_encoder))(decoder_work)

    for_core(lambda: start_all(gradient_copies()), lambda: start_all(output_copies()))
    comm_begin()
    start_sums(first, old, sums)
    fields = []
    for field in range(3):
        pieces = jnp.stack(
            [unpack_slab(ref[0, 0, field]) for ref in (recv_b, recv_a, keep_b, keep_a)]
        )
        fields.append(windows_of(pieces))
    grad_low, d_key_1, d_value_1 = fields
    grad = grad_low.astype(F32)
    channels = grad.shape[1]
    unit_1, unit_2 = n1_in[0, :, :channels], n2_in[0, :, :channels]
    wide_1, wide_2 = [ref[0, :, channels : channels + 1] for ref in (n1_in, n2_in)]
    left_1 = (unit_1 * vec[0:1] + vec[1:2]).astype(BF16)
    left_2 = (unit_2 * vec[2:3] + vec[3:4]).astype(BF16)
    qkv[...] = (nn(left_1, w_qkv[...]) + b_qkv[...]).astype(BF16)
    d_middle = mlp_back(
        grad, grad_low, a_in[0], lambda rows: s_in[0, rows].astype(F32), left_2, unit_2, wide_2, w_up, w_down, vec,
        (g_up, g_down, g_vec),
    )
    branch = d_middle.astype(BF16)
    g_out[...] += nn(with_ones(o_in[0]), branch)
    d_mixed = nt(branch, w_out[...]).astype(BF16)
    d_table = None
    for together in window_groups(grad.shape[0] // CELLS):
        parts = [
            [qkv[window_rows(k), 256 * f : 256 * f + 192] for f in range(3)]
            + [p_in[0, k].astype(F32), d_mixed[window_rows(k)]]
            for k in together
        ]
        *d_qkv, d_s = attend_back(parts)
        for k, d_q, d_k, d_v in zip(together, *d_qkv):
            rows = window_rows(k)
            dqkv[0, rows] = d_q.astype(BF16)
            dqkv[1, rows] = (d_k + d_key_1[rows].astype(F32)).astype(BF16)
            dqkv[2, rows] = (d_v + d_value_1[rows].astype(F32)).astype(BF16)
        d_table = d_s if d_table is None else d_table + d_s
    g_bias[...] += d_table
    ones = with_ones(left_1)
    d_normed = None
    for field, g_field in enumerate((g_q, g_k, g_v)):
        cols = slice(field * 256, field * 256 + 192)
        g_field[...] += nn(ones, dqkv[field])
        part = nt(dqkv[field], w_qkv[:, cols])
        d_normed = part if d_normed is None else d_normed + part
    g_vec[0:1] += col_sum(d_normed * unit_1)
    g_vec[1:2] += col_sum(d_normed)
    result = pieces_of(d_middle + norm_back(d_normed, unit_1, wide_1, vec[0:1]))
    rows_z = ends.shape[3]

    @pl.when(step >= 2)
    def _():
        for_core(
            lambda: result_copy(step - 2, True).wait(), lambda: result_copy(step - 2, False).wait()
        )

    for x in range(2):
        for y in range(2):
            part = restore(order[...], result[2 * x + y])
            buffer[slot, 2 * x : 2 * x + 2, 2 * y : 2 * y + 2] = part.reshape(2, 2, rows_z, -1)
    for_core(lambda: result_copy(step, True).start(), lambda: result_copy(step, False).start())

    @pl.when(step == steps - 1)
    def _():
        def finish(to_ends):
            result_copy(step - 1, to_ends).wait()
            result_copy(step, to_ends).wait()

        for_core(lambda: finish(True), lambda: finish(False))

    for_core(lambda: wait_all(gradient_copies()), lambda: wait_all(output_copies()))
    comm_end()


def decoder(
    first, core_ref, order, vec, w_q, b_q, bias, w_out, w_up, b_up, w_down,
    keep_1, keep_0, recv_1, recv_0, cot_1, cot_0, cot_r1, cot_r0, *rest,
):
    old, new = ([], rest) if first else (rest[:6], rest[6:])
    out_all, out_tail, own, halo, *sums, p_scr, o_scr, a_scr, s_scr, dqkv = new
    g_up, g_down, g_q, g_out, g_vec, g_bias = sums
    start_sums(first, old, sums)
    fields = []
    for field in range(3):
        pieces = jnp.stack([unpack_slab(ref[0, 0, field]) for ref in (keep_1, keep_0, recv_1, recv_0)])
        fields.append(windows_of(pieces))
    entry_low, keys, values = fields
    entry = entry_low.astype(F32)
    unit_1, inv_1 = normalize(entry)
    left_1 = (unit_1 * vec[0:1] + vec[1:2]).astype(BF16)
    queries = (nn(left_1, w_q[...]) + b_q[...]).astype(BF16)
    windows = entry.shape[0] // CELLS
    for together in window_groups(windows):
        parts = [[rows[window_rows(k)] for rows in (queries, keys, values)] for k in together]
        mixed, probs = attend(parts, [bias[0, 1 if k == windows - 1 else 0] for k in together])
        for k, o, p in zip(together, mixed, probs):
            p_scr[k] = p
            o_scr[window_rows(k)] = o
    middle = entry + nn(o_scr[...], w_out[...]) + vec[4:5]
    unit_2, inv_2 = normalize(middle)
    left_2 = (unit_2 * vec[2:3] + vec[3:4]).astype(BF16)
    results = []
    for k in range(entry.shape[0] // CHUNK):
        rows = slice(k * CHUNK, (k + 1) * CHUNK)
        hidden, slope = gelu_pair(nn(left_2[rows], w_up[...]) + b_up[...])
        hidden = hidden.astype(BF16)
        a_scr[rows] = hidden
        s_scr[rows] = slope
        results.append(nn(hidden, w_down[...]))
    result = pieces_of(middle + jnp.concatenate(results, 0) + vec[5:6])
    rows_z = out_all.shape[2]
    size = 4 * rows_z
    for x in range(2):
        for y in range(2):
            part = restore(order[...], result[2 * x + y]).reshape(2, 2, rows_z, -1)
            out_all[2 * x : 2 * x + 2, 2 * y : 2 * y + 2] = part
            if x == 1:
                out_tail[:, 2 * y : 2 * y + 2] = part

    cots = [
        nn(order[...], ref[0].reshape(size, -1)).astype(BF16) for ref in (cot_1, cot_0, cot_r1, cot_r0)
    ]
    grad_low = windows_of(jnp.stack(cots))
    grad = grad_low.astype(F32)
    d_middle = mlp_back(
        grad, grad_low, a_scr[...], lambda rows: s_scr[rows], left_2, unit_2, inv_2, w_up, w_down, vec,
        (g_up, g_down, g_vec),
    )
    branch = d_middle.astype(BF16)
    g_out[...] += nn(with_ones(o_scr[...]), branch)
    d_mixed = nt(branch, w_out[...]).astype(BF16)
    d_table = None
    for together in window_groups(windows):
        parts = [
            [rows[window_rows(k)] for rows in (queries, keys, values)]
            + [p_scr[k], d_mixed[window_rows(k)]]
            for k in together
        ]
        *d_qkv, d_s = attend_back(parts)
        for k, *grads in zip(together, *d_qkv):
            for f in range(3):
                dqkv[f, window_rows(k)] = grads[f]
        d_table = d_s if d_table is None else d_table + d_s
    g_bias[...] += d_table
    d_queries = dqkv[0].astype(BF16)
    g_q[...] += nn(with_ones(left_1), d_queries)
    d_normed = nt(d_queries, w_q[...])
    g_vec[0:1] += col_sum(d_normed * unit_1)
    g_vec[1:2] += col_sum(d_normed)
    d_entry = d_middle + norm_back(d_normed, unit_1, inv_1, vec[0:1])
    for field, rows in enumerate((d_entry, dqkv[1], dqkv[2])):
        turned = pack_slab(roll_rows(pieces_of(rows), size - 8))
        own[0, :, field] = turned[:2]
        halo[0, :, field] = turned[2:]


def whole(array):
    zeros = (0,) * array.ndim
    return pl.BlockSpec(array.shape, lambda *_: zeros)


def sums_shapes(channels, hidden, products):
    return [
        jax.ShapeDtypeStruct(shape, F32)
        for shape in (
            (channels + 16, hidden),
            (channels, hidden),
            *[(channels + 16, channels)] * products,
            (channels + 16, channels),
            (8, channels),
            (CELLS, HEADS * CELLS),
        )
    ]


def cost(cells, per_cell, hbm):
    return pl.CostEstimate(
        flops=2 * cells * per_cell, bytes_accessed=hbm, transcendentals=cells * 1536
    )


params = pltpu.CompilerParams(
    dimension_semantics=("arbitrary",), vmem_limit_bytes=VMEM_BYTES
)


class Layout:
    def __init__(self, channels, hidden, devices, encoder):
        tall = channels + 16
        self.tall, self.channels = tall, channels
        self.tiles = hidden // LANES_A
        self.up = 0
        self.down = self.tiles * tall
        self.pair = self.down + self.tiles * channels
        self.bias = self.pair + 3 * tall
        self.kv = self.bias + HEADS * CELLS // LANES_A * CELLS
        self.end = self.kv + (3 * tall if encoder else 0)
        self.chunk = -(-self.end // (16 * devices)) * 16
        self.rows = self.chunk * devices


def fill(buffer, layout, up, down, q, out, bias, kv=None):
    tall, channels = layout.tall, layout.channels

    def put(start, rows):
        buffer[start : start + rows.shape[0]] = rows.astype(buffer.dtype)

    def put_pair(start, left, right):
        put(start, left[:, :LANES_A])
        put(start + tall, right[:, :LANES_A])
        put(start + 2 * tall, jnp.concatenate([left[:, LANES_A:], right[:, LANES_A:]], 1))

    for k in range(layout.tiles):
        cols = slice(k * LANES_A, (k + 1) * LANES_A)
        put(layout.up + k * tall, up[:, cols])
        put(layout.down + k * channels, down[:, cols])
    put_pair(layout.pair, q, out)
    for k in range(HEADS * CELLS // LANES_A):
        put(layout.bias + k * CELLS, bias[:, k * LANES_A : (k + 1) * LANES_A])
    if kv is not None:
        put_pair(layout.kv, *kv)
    if layout.rows > layout.end:
        put(layout.end, jnp.zeros((layout.rows - layout.end, LANES_A), F32))


class NoComm:
    inputs = outputs = 0
    args = ()

    def out_shapes(self):
        return []

    def scratch(self):
        return []

    def params(self):
        return params

    def work(self, ins, outs, scratch):
        return (lambda: None), (lambda: None)


def comm_params(collective_id):
    return pltpu.CompilerParams(
        dimension_semantics=("arbitrary",),
        vmem_limit_bytes=VMEM_BYTES,
        collective_id=collective_id,
        has_side_effects=True,
    )


class Scatter:
    inputs, outputs = 5, 1

    def __init__(self, layout, blocks, args):
        self.layout, self.blocks, self.args = layout, blocks, args

    def out_shapes(self):
        return [jax.ShapeDtypeStruct((self.layout.chunk, LANES_A), BF16)]

    def scratch(self):
        devices = 2 * self.blocks
        return [
            *[pltpu.VMEM(a.shape, F32) for a in self.args],
            pltpu.VMEM((self.layout.rows, LANES_A), BF16),
            pltpu.VMEM((devices, self.layout.chunk, LANES_A), BF16),
            pltpu.SemaphoreType.DMA((5,)),
            pltpu.SemaphoreType.DMA((devices,)),
            pltpu.SemaphoreType.DMA((devices,)),
        ]

    def params(self):
        return comm_params(2)

    def work(self, ins, outs, scratch):
        local, (low, landed, load_sem, send_sem, recv_sem) = scratch[:5], scratch[5:]
        layout, blocks = self.layout, self.blocks
        devices = 2 * blocks
        step, steps = pl.program_id(0), pl.num_programs(0)
        me = lax.axis_index("section") * blocks + lax.axis_index("tok")

        def peer(offset):
            return lax.rem(me + offset, devices)

        def place(index):
            return {"section": lax.div(index, blocks), "tok": lax.rem(index, blocks)}

        def rows_of(index):
            return pl.ds(pl.multiple_of(index * layout.chunk, 16), layout.chunk)

        def loads():
            return [
                pltpu.make_async_copy(source, target, load_sem.at[k])
                for k, (source, target) in enumerate(zip(ins, local))
            ]

        def copy(offset):
            return pltpu.make_async_remote_copy(
                src_ref=low.at[rows_of(peer(offset))], dst_ref=landed.at[offset],
                send_sem=send_sem.at[offset], recv_sem=recv_sem.at[offset],
                device_id=place(peer(offset)), device_id_type=MESH,
            )

        def begin():
            @pl.when(step == 0)
            def _():
                barrier = pltpu.get_barrier_semaphore()

                def greet(offset, carry):
                    pl.semaphore_signal(
                        barrier, inc=1, device_id=place(peer(offset)), device_id_type=MESH
                    )
                    return carry

                lax.fori_loop(1, devices, greet, 0)
                start_all(loads())

            @pl.when(step == 1)
            def _():
                wait_all(loads())
                fill(low, layout, *local)
                pl.semaphore_wait(pltpu.get_barrier_semaphore(), devices - 1)

                def send(offset, carry):
                    copy(offset).start()
                    return carry

                lax.fori_loop(1, devices, send, 0)

        def end():
            @pl.when(step == steps - 1)
            def _():
                def add(offset, carry):
                    copy(offset).wait_recv()
                    return carry + landed[offset].astype(F32)

                total = lax.fori_loop(1, devices, add, low[rows_of(me)].astype(F32))
                outs[0][...] = total.astype(BF16)

                def drain(offset, carry):
                    copy(offset).wait_send()
                    return carry

                lax.fori_loop(1, devices, drain, 0)

        return begin, end


class Gather:
    inputs = outputs = 1

    def __init__(self, layout, blocks, chunk):
        self.layout, self.blocks, self.args = layout, blocks, (chunk,)

    def out_shapes(self):
        return [jax.ShapeDtypeStruct((self.layout.rows, LANES_A), BF16)]

    def scratch(self):
        return [
            pltpu.VMEM((self.layout.chunk, LANES_A), BF16),
            pltpu.VMEM((self.layout.rows, LANES_A), BF16),
            pltpu.SemaphoreType.DMA((1,)),
            pltpu.SemaphoreType.DMA((self.blocks,)),
            pltpu.SemaphoreType.DMA((2, self.blocks)),
        ]

    def params(self):
        return comm_params(3)

    def work(self, ins, outs, scratch):
        chunk, whole_rows, load_sem, send_sem, recv_sem = scratch
        layout, blocks = self.layout, self.blocks
        step, steps = pl.program_id(0), pl.num_programs(0)
        core, block = lax.axis_index("section"), lax.axis_index("tok")

        def load():
            return pltpu.make_async_copy(ins[0], chunk, load_sem.at[0])

        def rows_of(section, position):
            start = (section * blocks + position) * layout.chunk
            return pl.ds(pl.multiple_of(start, 16), layout.chunk)

        def send(offset):
            return pltpu.make_async_remote_copy(
                src_ref=chunk, dst_ref=whole_rows.at[rows_of(core, block)],
                send_sem=send_sem.at[offset], recv_sem=recv_sem.at[core, offset],
                device_id={"section": 1, "tok": lax.rem(block + offset, blocks)}, device_id_type=MESH,
            )

        def arrival(section, offset):
            source = lax.rem(block + blocks - offset, blocks)
            return pltpu.make_async_remote_copy(
                src_ref=chunk, dst_ref=whole_rows.at[rows_of(section, source)],
                send_sem=send_sem.at[offset], recv_sem=recv_sem.at[section, offset],
                device_id={"section": 1, "tok": lax.rem(block + offset, blocks)}, device_id_type=MESH,
            )

        def each(work, start):
            def run(offset, carry):
                work(offset)
                return carry

            lax.fori_loop(start, blocks, run, 0)

        def for_targets(work):
            pl.when(core == 0)(lambda: each(work, 0))
            pl.when(core == 1)(lambda: each(work, 1))

        def greet(section, offset):
            pl.semaphore_signal(
                pltpu.get_barrier_semaphore(), inc=1,
                device_id={"section": section, "tok": lax.rem(block + offset, blocks)},
                device_id_type=MESH,
            )

        def begin():
            @pl.when(step == 0)
            def _():
                @pl.when(core == 1)
                def _():
                    each(lambda offset: greet(0, offset), 0)
                    each(lambda offset: greet(1, offset), 1)

                load().start()

            @pl.when(step == 1)
            def _():
                load().wait()
                barrier = pltpu.get_barrier_semaphore()
                pl.when(core == 0)(lambda: pl.semaphore_wait(barrier, blocks))
                pl.when(core == 1)(lambda: pl.semaphore_wait(barrier, blocks - 1))
                for_targets(lambda offset: send(offset).start())

        def end():
            @pl.when(step == steps - 1)
            def _():
                @pl.when(core == 1)
                def _():
                    whole_rows[rows_of(1, block)] = chunk[...]
                    each(lambda offset: arrival(0, offset).wait_recv(), 0)
                    each(lambda offset: arrival(1, offset).wait_recv(), 1)
                    outs[0][...] = whole_rows[...]

                @pl.when(core == 0)
                def _():
                    outs[0][...] = jnp.zeros_like(outs[0])

                for_targets(lambda offset: send(offset).wait_send())

        return begin, end


MESH = pl.DeviceIdType.MESH


def sum_gradients(layout, blocks, *refs):
    enc, (d_vec, *rest) = refs[:8], refs[8:]
    (
        total_out, kv_out, vec_out,
        low, from_sib, half, landed, chunk, total, sib_kv, vec_send, vec_sib, vec_own, vec_landed,
        sib_send, sib_recv, send_sem, recv_sem, vec_ssem, vec_rsem, out_ssem, out_rsem,
    ) = rest
    e_up, e_down, e_q, e_k, e_v, e_out, e_vec, e_bias = enc
    core, me = lax.axis_index("section"), lax.axis_index("tok")
    sibling = {"section": 1 - core}
    half_rows = layout.rows // 2

    def peer(offset):
        return lax.rem(me + offset, blocks)

    def each(work, start=1):
        def run(offset, carry):
            work(offset)
            return carry

        lax.fori_loop(start, blocks, run, 0)

    barrier = pltpu.get_barrier_semaphore()
    pl.semaphore_signal(barrier, inc=1, device_id=sibling, device_id_type=MESH)

    def greet(offset):
        pl.semaphore_signal(
            barrier, inc=1, device_id={"tok": peer(offset)}, device_id_type=MESH
        )

    each(greet)

    @pl.when(core == 0)
    def _():
        def greet_other(offset):
            pl.semaphore_signal(
                barrier, inc=1, device_id={"section": 1, "tok": peer(offset)}, device_id_type=MESH
            )

        each(greet_other)

    fill(low, layout, e_up, e_down, e_q, e_out, e_bias, (e_k, e_v))

    @pl.when(core == 0)
    def _():
        vec_send[...] = d_vec[...]
        vec_own[...] = e_vec[...]

    @pl.when(core == 1)
    def _():
        vec_send[...] = e_vec[...]
        vec_own[...] = d_vec[...]

    pl.when(core == 0)(lambda: pl.semaphore_wait(barrier, blocks))
    pl.when(core == 1)(lambda: pl.semaphore_wait(barrier, 2 * blocks - 1))

    def half_of(section):
        return pl.ds(pl.multiple_of(section * half_rows, 16), half_rows)

    def to_sibling(source, target, k):
        return pltpu.make_async_remote_copy(
            src_ref=source, dst_ref=target, send_sem=sib_send.at[k], recv_sem=sib_recv.at[k],
            device_id=sibling, device_id_type=MESH,
        )

    first = to_sibling(low.at[half_of(1 - core)], from_sib, 0)
    second = to_sibling(vec_send, vec_sib, 1)
    first.start()
    second.start()
    first.wait()
    second.wait()
    half[...] = (low[half_of(core)].astype(F32) + from_sib[...].astype(F32)).astype(BF16)
    vec_own[...] += vec_sib[...]

    def chunk_of(position):
        return pl.ds(pl.multiple_of(position * layout.chunk, 16), layout.chunk)

    def rows_of(section, position):
        start = section * half_rows + position * layout.chunk
        return pl.ds(pl.multiple_of(start, 16), layout.chunk)

    def scatter(offset):
        return pltpu.make_async_remote_copy(
            src_ref=half.at[chunk_of(peer(offset))], dst_ref=landed.at[offset],
            send_sem=send_sem.at[offset], recv_sem=recv_sem.at[offset],
            device_id={"tok": peer(offset)}, device_id_type=MESH,
        )

    def scatter_vec(offset):
        return pltpu.make_async_remote_copy(
            src_ref=vec_own, dst_ref=vec_landed.at[offset],
            send_sem=vec_ssem.at[offset], recv_sem=vec_rsem.at[offset],
            device_id={"tok": peer(offset)}, device_id_type=MESH,
        )

    def gather(offset):
        return pltpu.make_async_remote_copy(
            src_ref=chunk, dst_ref=total.at[rows_of(core, me)],
            send_sem=out_ssem.at[offset], recv_sem=out_rsem.at[core, offset],
            device_id={"section": 0, "tok": peer(offset)}, device_id_type=MESH,
        )

    def gathered(section, offset):
        source = lax.rem(me + blocks - offset, blocks)
        return pltpu.make_async_remote_copy(
            src_ref=chunk, dst_ref=total.at[rows_of(section, source)],
            send_sem=out_ssem.at[offset], recv_sem=out_rsem.at[section, offset],
            device_id={"section": 0, "tok": peer(offset)}, device_id_type=MESH,
        )

    def start(offset):
        scatter(offset).start()
        scatter_vec(offset).start()

    each(start)

    def add(offset, carry):
        scatter(offset).wait_recv()
        return carry + landed[offset].astype(F32)

    chunk_sum = lax.fori_loop(1, blocks, add, half[chunk_of(me)].astype(F32))
    chunk[...] = chunk_sum.astype(BF16)

    @pl.when(core == 0)
    def _():
        total[rows_of(0, me)] = chunk[...]
        each(lambda offset: gather(offset).start())

    @pl.when(core == 1)
    def _():
        each(lambda offset: gather(offset).start(), 0)

    def add_vec(offset, carry):
        scatter_vec(offset).wait_recv()
        return carry + vec_landed[offset]

    vec_out[...] = lax.fori_loop(1, blocks, add_vec, vec_own[...])
    third = to_sibling(total.at[pl.ds(layout.kv, 3 * layout.tall)], sib_kv, 2)

    @pl.when(core == 0)
    def _():
        each(lambda offset: gathered(0, offset).wait_recv())
        each(lambda offset: gathered(1, offset).wait_recv(), 0)
        third.start()
        total_out[...] = total[...]
        kv_out[...] = total[pl.ds(layout.kv, 3 * layout.tall)]
        each(lambda offset: gather(offset).wait_send())
        third.wait_send()

    @pl.when(core == 1)
    def _():
        total_out[...] = jnp.zeros_like(total_out)
        each(lambda offset: gather(offset).wait_send(), 0)
        third.wait_recv()
        kv_out[...] = sib_kv[...]

    def drain(offset):
        scatter(offset).wait_send()
        scatter_vec(offset).wait_send()

    each(drain)


def run_sum(enc_sums, dec_vec, layout, blocks):
    channels = layout.channels
    rows, chunk, kv = layout.rows, layout.chunk, 3 * layout.tall
    dma = pltpu.SemaphoreType.DMA
    vmem = pl.BlockSpec(memory_space=pltpu.VMEM)
    args = [*enc_sums, dec_vec]
    return pl.pallas_call(
        functools.partial(sum_gradients, layout, blocks),
        in_specs=[vmem] * len(args),
        out_specs=[vmem] * 3,
        out_shape=[
            jax.ShapeDtypeStruct((rows, LANES_A), BF16),
            jax.ShapeDtypeStruct((kv, LANES_A), BF16),
            jax.ShapeDtypeStruct((8, channels), F32),
        ],
        scratch_shapes=[
            pltpu.VMEM((rows, LANES_A), BF16),
            pltpu.VMEM((rows // 2, LANES_A), BF16),
            pltpu.VMEM((rows // 2, LANES_A), BF16),
            pltpu.VMEM((blocks, chunk, LANES_A), BF16),
            pltpu.VMEM((chunk, LANES_A), BF16),
            pltpu.VMEM((rows, LANES_A), BF16),
            pltpu.VMEM((kv, LANES_A), BF16),
            pltpu.VMEM((8, channels), F32),
            pltpu.VMEM((8, channels), F32),
            pltpu.VMEM((8, channels), F32),
            pltpu.VMEM((blocks, 8, channels), F32),
            dma((3,)),
            dma((3,)),
            *[dma((blocks,))] * 5,
            dma((2, blocks)),
        ],
        compiler_params=pltpu.CompilerParams(
            collective_id=0, has_side_effects=True, vmem_limit_bytes=VMEM_BYTES
        ),
        name="sum_gradients",
    )(*args)


def finish(layout, batches, returns, core_ref, enc_total, dec_total, kv, vec, *refs):
    returned, refs = refs[:returns], refs[returns + 1 :]
    (
        ends, ln1_gain, ln1_bias, q_weight, q_bias, kv_weight, v_bias, out_weight, out_bias, table,
        ln2_gain, ln2_bias, up_weight, up_bias, down_weight, down_bias, placed, copy_sem,
    ) = refs
    is_encoder = core_ref[0] == 0
    step = pl.program_id(0)

    def copies():
        return [
            pltpu.make_async_copy(
                ref,
                ends.at[batches - returns + k, pl.ds(WIN, WIN), pl.ds(step * WIN, WIN)],
                copy_sem.at[k],
            )
            for k, ref in enumerate(returned)
        ]

    pl.when(is_encoder)(lambda: start_all(copies()))

    def spread(total):
        unpack(
            layout, total, kv, vec, ln1_gain, ln1_bias, q_weight, q_bias, kv_weight,
            v_bias, out_weight, out_bias, table, ln2_gain, ln2_bias, up_weight, up_bias, down_weight,
            down_bias, placed,
        )

    pl.when((step == 0) & is_encoder)(lambda: spread(enc_total))
    pl.when((step == 0) & jnp.logical_not(is_encoder))(lambda: spread(dec_total))
    pl.when(is_encoder)(lambda: wait_all(copies()))


def unpack(
    layout, total, kv, vec, ln1_gain, ln1_bias, q_weight, q_bias, kv_weight,
    v_bias, out_weight, out_bias, table, ln2_gain, ln2_bias, up_weight, up_bias, down_weight, down_bias,
    placed,
):
    channels, tall, half = layout.channels, layout.tall, LANES_A // 2
    for row, ref in enumerate((ln1_gain, ln1_bias, ln2_gain, ln2_bias, down_bias)):
        ref[...] = vec[row : row + 1]

    def at(start, rows):
        return total[start : start + rows].astype(F32)

    for k in range(layout.tiles):
        cols = slice(k * LANES_A, (k + 1) * LANES_A)
        tile = at(layout.up + k * tall, tall)
        up_weight[:, cols] = tile[:channels]
        up_bias[:, cols] = tile[channels : channels + 1]
        down_weight[cols] = at(layout.down + k * channels, channels).T

    def pair(rows):
        rest = rows[2 * tall :]
        left = jnp.concatenate([rows[:tall], rest[:, :half]], 1)
        return left, jnp.concatenate([rows[tall : 2 * tall], rest[:, half:]], 1)

    q, out = pair(at(layout.pair, 3 * tall))
    q_weight[...] = q[:channels]
    q_bias[...] = q[channels : channels + 1]
    out_weight[...] = out[:channels]
    out_bias[...] = out[channels : channels + 1]
    k, v = pair(kv[...].astype(F32))
    kv_weight[:, :channels] = k[:channels]
    kv_weight[:, channels:] = v[:channels]
    v_bias[...] = v[channels : channels + 1]
    placed[...] = jnp.zeros_like(placed)
    positions = [position_matrix(False), position_matrix(True)]
    for h in range(HEADS):
        start = layout.bias + h // 2 * CELLS
        placed[h, :, :256] = nt(total[start : start + CELLS], positions[h % 2])
    entries = jnp.zeros((8, 384), F32)
    for j in range(CELLS):
        entries += pltpu.roll(placed[:, j, :], CENTRE - cell_position(j), 1)
    table[...] = entries[:HEADS, : SPAN**3]


def run_finish(core, totals, returned, ends, layout):
    channels = layout.channels
    hidden = layout.tiles * LANES_A
    _, _, rows_y, rows_z, _ = ends.shape
    any_spec = pl.BlockSpec(memory_space=pl.ANY)
    shapes = [
        (1, channels), (1, channels), (channels, channels), (1, channels), (channels, 2 * channels),
        (1, channels), (channels, channels), (1, channels), (HEADS, SPAN**3),
        (1, channels), (1, channels), (channels, hidden), (1, hidden), (hidden, channels), (1, channels),
    ]
    shapes = [jax.ShapeDtypeStruct(shape, F32) for shape in shapes]
    return pl.pallas_call(
        functools.partial(finish, layout, ends.shape[0], len(returned)),
        grid_spec=pltpu.PrefetchScalarGridSpec(
            num_scalar_prefetch=1,
            grid=(rows_y // WIN,),
            in_specs=[
                *[whole(a) for a in totals],
                *[
                    pl.BlockSpec(
                        (WIN, WIN, rows_z, channels), lambda i, c: (0, i * (1 - c[0]), 0, 0)
                    )
                ]
                * len(returned),
                any_spec,
            ],
            out_specs=[any_spec, *[whole(a) for a in shapes]],
            scratch_shapes=[
                pltpu.VMEM((8, CELLS, 384), F32),
                pltpu.SemaphoreType.DMA((len(returned),)),
            ],
        ),
        out_shape=[jax.ShapeDtypeStruct(ends.shape, F32), *shapes],
        input_output_aliases={1 + len(totals) + len(returned): 0},
        compiler_params=params,
        name="finish",
    )(core, *totals, *returned, ends)


def cell_position(ids):
    x = 2 * (ids // 32) + ids // 4 % 2
    y = 2 * (ids // 16 % 2) + ids // 2 % 2
    z = 2 * (ids // 8 % 2) + ids % 2
    return (x * SPAN + y) * SPAN + z


CENTRE = (WIN - 1) * (SPAN * SPAN + SPAN + 1)
TABLE_ROW = 8


def position_matrix(odd):
    rows = lax.broadcasted_iota(jnp.int32, (256, 2 * CELLS), 0)
    ids = lax.broadcasted_iota(jnp.int32, (256, 2 * CELLS), 1) - (CELLS if odd else 0)
    hit = (ids >= 0) & (ids < CELLS) & (rows == cell_position(ids))
    return jnp.where(hit, 1.0, 0.0).astype(BF16)


def spread_bias(table, shifted):
    for j in range(CELLS):
        turned = pltpu.roll(table, (384 - CENTRE + cell_position(j)) % 384, 1)
        for h in range(HEADS):
            shifted[h, j : j + 1] = turned[h : h + 1, :256]
    even, odd = position_matrix(False), position_matrix(True)
    pairs = [
        nn(shifted[2 * p].astype(BF16), even) + nn(shifted[2 * p + 1].astype(BF16), odd)
        for p in range(HEADS // 2)
    ]
    return jnp.concatenate(pairs, 1) * log2_e


def prepare(
    blocks, q_w, out_w, up_w, down_w, kv_w, v_b, ln1_g, ln1_b, ln2_g, ln2_b, out_b, down_b, q_b, up_b, table,
    vec_e, vec_d, w_qkv, b_qkv, w_q_d, b_q_d, w_out_e, w_out_d, w_up_e, w_up_d, b_up_e, b_up_d,
    w_down_e, w_down_d, bias_e, bias_d,
    small, small_sib, q_sib, out_sib, up_sib, down_sib, shifted, send_sem, recv_sem,
):
    core, block = lax.axis_index("section"), lax.axis_index("tok")
    channels, hidden = up_w.shape
    sibling = {"section": 1 - core}
    barrier = pltpu.get_barrier_semaphore()
    pl.semaphore_signal(barrier, inc=1, device_id=sibling, device_id_type=MESH)
    small[...] = jnp.zeros_like(small)
    for row, ref in enumerate((ln1_g, ln1_b, ln2_g, ln2_b, out_b, down_b, q_b)):
        small[row : row + 1, :channels] = ref[...].astype(F32)
    small[7:8, :hidden] = up_b[...].astype(F32)
    small[TABLE_ROW : TABLE_ROW + HEADS, : SPAN**3] = table[...].astype(F32)
    pl.semaphore_wait(barrier, 1)
    pairs = ((small, small_sib), (q_w, q_sib), (out_w, out_sib), (up_w, up_sib), (down_w, down_sib))
    copies = [
        pltpu.make_async_remote_copy(
            src_ref=source, dst_ref=target, send_sem=send_sem.at[k], recv_sem=recv_sem.at[k],
            device_id=sibling, device_id_type=MESH,
        )
        for k, (source, target) in enumerate(pairs)
    ]
    for copy in copies:
        copy.start()
    for copy in copies:
        copy.wait()

    def place(enc, dec):
        e_small, e_q, e_out, e_up, e_down = enc
        d_small, d_q, d_out, d_up, d_down = dec
        for source, vec, b_up in ((e_small, vec_e, b_up_e), (d_small, vec_d, b_up_d)):
            vec[...] = source[:8, :channels]
            b_up[...] = source[7:8, :hidden]
        w_qkv[...] = jnp.zeros_like(w_qkv)
        b_qkv[...] = jnp.zeros_like(b_qkv)
        w_qkv[:, :channels] = e_q[...]
        w_qkv[:, 256 : 256 + channels] = kv_w[:, :channels]
        w_qkv[:, 512 : 512 + channels] = kv_w[:, channels:]
        b_qkv[:, :channels] = e_small[6:7, :channels]
        b_qkv[:, 512 : 512 + channels] = v_b[...].astype(F32)
        w_q_d[...] = d_q[...]
        b_q_d[...] = d_small[6:7, :channels]
        for target, source in (
            (w_out_e, e_out), (w_out_d, d_out), (w_up_e, e_up), (w_up_d, d_up),
            (w_down_e, e_down), (w_down_d, d_down),
        ):
            target[...] = source[...]
        rows = slice(TABLE_ROW, TABLE_ROW + 8)
        bias_e[...] = spread_bias(e_small[rows, :384], shifted)
        return spread_bias(d_small[rows, :384], shifted)

    own = (small, q_w, out_w, up_w, down_w)
    sib = (small_sib, q_sib, out_sib, up_sib, down_sib)

    def masked(base):
        shape = (CELLS, HEADS * CELLS)
        keys = lax.broadcasted_iota(jnp.int32, shape, 0)
        queries = lax.broadcasted_iota(jnp.int32, shape, 1) % CELLS

        def differ(unit):
            return jnp.where(keys // unit % 2 != queries // unit % 2, 1.0, 0.0)

        last = jnp.where((core == 1) & (block == blocks - 1), 1.0, 0.0)
        for y in range(2):
            for z in range(2):
                apart = jnp.maximum(last * differ(32), jnp.maximum(y * differ(16), z * differ(8)))
                bias_d[y, z] = base + apart * (mask_fill * log2_e)

    @pl.when(core == 0)
    def _():
        masked(place(own, sib))

    @pl.when(core == 1)
    def _():
        masked(place(sib, own))


def run_prepare(blocks, weights, smalls, table, kv_weight, v_bias):
    q_w, out_w, up_w, down_w = weights
    channels, hidden = up_w.shape
    vmem = pl.BlockSpec(memory_space=pltpu.VMEM)
    args = [*weights, kv_weight, v_bias, *smalls, table]
    bias = (CELLS, HEADS * CELLS)
    square = (channels, channels)

    def f32(*shape):
        return jax.ShapeDtypeStruct(shape, F32)

    def bf16(*shape):
        return jax.ShapeDtypeStruct(shape, BF16)

    shapes = [
        f32(8, channels), f32(8, channels), bf16(channels, 768), f32(1, 768), bf16(*square),
        f32(1, channels), bf16(*square), bf16(*square), bf16(channels, hidden), bf16(channels, hidden),
        f32(1, hidden), f32(1, hidden), bf16(hidden, channels), bf16(hidden, channels),
        f32(*bias), f32(2, 2, *bias),
    ]
    return pl.pallas_call(
        functools.partial(prepare, blocks),
        in_specs=[vmem] * len(args),
        out_specs=[vmem] * len(shapes),
        out_shape=shapes,
        scratch_shapes=[
            pltpu.VMEM((TABLE_ROW + 8, hidden), F32),
            pltpu.VMEM((TABLE_ROW + 8, hidden), F32),
            pltpu.VMEM(square, BF16),
            pltpu.VMEM(square, BF16),
            pltpu.VMEM((channels, hidden), BF16),
            pltpu.VMEM((hidden, channels), BF16),
            pltpu.VMEM((HEADS, CELLS, 256), F32),
            pltpu.SemaphoreType.DMA((5,)),
            pltpu.SemaphoreType.DMA((5,)),
        ],
        compiler_params=pltpu.CompilerParams(
            collective_id=1, has_side_effects=True, vmem_limit_bytes=VMEM_BYTES
        ),
        name="prepare",
    )(*args)


def run_encoder(core, tokens, batch, consts, cotangent):
    _, _, rows_y, rows_z, channels = tokens.shape
    groups, size = rows_y // WIN, 4 * rows_z
    cells, windows = 4 * size, rows_z // WIN
    hidden = consts[6].shape[1]
    slab = jax.ShapeDtypeStruct((groups, 2, 3, size * 3 // 2, LANES_A), BF16)
    outs = [
        slab,
        slab,
        jax.ShapeDtypeStruct((groups, cells, 256), F32),
        jax.ShapeDtypeStruct((groups, cells, 256), F32),
        jax.ShapeDtypeStruct((groups, windows, CELLS, HEADS * CELLS), BF16),
        jax.ShapeDtypeStruct((groups, cells, channels), BF16),
        jax.ShapeDtypeStruct((groups, cells, hidden), BF16),
        jax.ShapeDtypeStruct((groups, cells, hidden), BF16),
    ]

    def row(array):
        zeros = (0,) * (array.ndim - 1)
        return pl.BlockSpec((1, *array.shape[1:]), lambda i, c: (i, *zeros))

    batches = tokens.shape[0]
    cut = [] if cotangent is None else [cotangent]
    cut_block = (batches, SHIFT, WIN, rows_z, channels)
    cut_outs = [
        jax.ShapeDtypeStruct((batches, SHIFT, rows_y, rows_z, channels), a.dtype) for a in cut
    ]
    return pl.pallas_call(
        functools.partial(encoder_forward, len(cut)),
        grid_spec=pltpu.PrefetchScalarGridSpec(
            num_scalar_prefetch=1,
            grid=(groups,),
            in_specs=[
                pl.BlockSpec(
                    (1, WIN, WIN, rows_z, channels), lambda i, c: (batch, c[0], i, 0, 0)
                ),
                *[whole(a) for a in consts],
                *[pl.BlockSpec(cut_block, lambda i, c: (0, 2 * c[0], i, 0, 0)) for _ in cut],
            ],
            out_specs=[
                *[row(a) for a in outs],
                *[pl.BlockSpec(cut_block, lambda i, c: (0, 0, i, 0, 0)) for _ in cut],
            ],
            scratch_shapes=[pltpu.VMEM((cells, 768), BF16)],
        ),
        out_shape=[*outs, *cut_outs],
        compiler_params=params,
        cost_estimate=cost(groups * cells, 466944, groups * cells * 7500),
        name="encoder_forward",
    )(core, tokens, *consts, *cut)


def run_encoder_back(batch, own, halo, ys, returned, saved, old, consts, tokens, comm):
    groups, _, _, packed, _ = own.shape
    batches, planes, rows_y, rows_z, channels = tokens.shape
    size = 4 * rows_z
    hidden = consts[5].shape[1]
    first = old is None
    shapes = sums_shapes(channels, hidden, 3)
    outs = [
        jax.ShapeDtypeStruct(tokens.shape, F32),
        jax.ShapeDtypeStruct((WIN, rows_y, rows_z, channels), F32),
        *shapes,
        *comm.out_shapes(),
    ]

    def slab(unit):
        def place(i):
            return ((i if unit == 0 else (i + groups - 1) % groups), unit, 0, 0, 0)

        return pl.BlockSpec((1, 1, 3, packed, LANES_A), place)

    def row(array):
        zeros = (0,) * (array.ndim - 1)
        return pl.BlockSpec((1, *array.shape[1:]), lambda i: (i, *zeros))

    def strip(planes_here):
        return pl.BlockSpec((planes_here, WIN, rows_z, channels), lambda i: (0, i, 0, 0))

    any_spec = pl.BlockSpec(memory_space=pl.ANY)
    olds = [] if first else [*old[1], old[0]]
    args = [*consts, *ys, own, own, halo, halo, *saved, *returned, *olds]
    alias = {} if first else {len(args) - 1: 0}
    return pl.pallas_call(
        functools.partial(encoder_backward, first, batch, len(returned), comm),
        grid=(groups,),
        in_specs=[
            *[whole(a) for a in consts],
            *[strip(n) for n in (2, 2, 4)],
            slab(0),
            slab(1),
            slab(0),
            slab(1),
            *[row(a) for a in saved],
            *[strip(WIN)] * len(returned),
            *[whole(a) for a in olds[:-1]],
            *[any_spec] * (0 if first else 1),
            *[any_spec] * comm.inputs,
        ],
        out_specs=[
            any_spec,
            any_spec,
            *[whole(a) for a in shapes],
            *[whole(a) for a in comm.out_shapes()],
        ],
        out_shape=outs,
        input_output_aliases=alias,
        scratch_shapes=[
            pltpu.VMEM((4 * size, 768), BF16),
            pltpu.VMEM((3, 4 * size, channels), BF16),
            pltpu.VMEM((2, WIN, WIN, rows_z, channels), F32),
            pltpu.SemaphoreType.DMA((2,)),
            pltpu.SemaphoreType.DMA((8 + batches,)),
            *comm.scratch(),
        ],
        compiler_params=comm.params(),
        cost_estimate=cost(groups * 4 * size, 933888, groups * 4 * size * 9000),
        name="encoder_backward",
    )(*args, *comm.args)


def run_decoder(core, keep, recv, cotangent, cot_recv, batch, old, consts):
    groups, _, _, packed, _ = keep.shape
    rows_z, channels = cotangent.shape[3:]
    size = 4 * rows_z
    hidden = consts[6].shape[1]
    windows = rows_z // WIN
    first = old is None
    shapes = sums_shapes(channels, hidden, 1)
    slab_shape = jax.ShapeDtypeStruct((groups, 2, 3, packed, LANES_A), BF16)
    outs = [
        *[jax.ShapeDtypeStruct((n, groups * WIN, rows_z, channels), F32) for n in (4, 2)],
        slab_shape,
        slab_shape,
        *shapes,
    ]

    def slab(unit):
        def place(i, c):
            return ((i if unit == 1 else (i + 1) % groups), unit, 0, 0, 0)

        return pl.BlockSpec((1, 1, 3, packed, LANES_A), place)

    def cot(unit, own):
        def place(i, c):
            y = 2 * i + 1 if unit == 1 else (2 * i + 2) % (2 * groups)
            return (batch, 2 * c[0] + 1 if own else 0, y, 0, 0)

        return pl.BlockSpec((1, 2, 2, rows_z, channels), place)

    def bias_place(i, c):
        return (i // (groups - 1), 0, 0, 0)

    specs = [whole(a) for a in consts]
    specs[4] = pl.BlockSpec((1, *consts[4].shape[1:]), bias_place)
    olds = [] if first else list(old)
    out_slab = pl.BlockSpec((1, 2, 3, packed, LANES_A), lambda i, c: (i, 0, 0, 0, 0))
    return pl.pallas_call(
        functools.partial(decoder, first),
        grid_spec=pltpu.PrefetchScalarGridSpec(
            num_scalar_prefetch=1,
            grid=(groups,),
            in_specs=[
                *specs,
                slab(1),
                slab(0),
                slab(1),
                slab(0),
                cot(1, True),
                cot(0, True),
                cot(1, False),
                cot(0, False),
                *[whole(a) for a in olds],
            ],
            out_specs=[
                *[pl.BlockSpec((n, WIN, rows_z, channels), lambda i, c: (0, i, 0, 0)) for n in (4, 2)],
                out_slab,
                out_slab,
                *[whole(a) for a in shapes],
            ],
            scratch_shapes=[
                pltpu.VMEM((windows, CELLS, HEADS * CELLS), F32),
                pltpu.VMEM((4 * size, channels), BF16),
                pltpu.VMEM((4 * size, hidden), BF16),
                pltpu.VMEM((4 * size, hidden), F32),
                pltpu.VMEM((3, 4 * size, channels), F32),
            ],
        ),
        out_shape=outs,
        compiler_params=params,
        cost_estimate=cost(groups * 4 * size, 1253376, groups * 4 * size * 4000),
        name="decoder",
    )(core, *consts, keep, keep, recv, recv, cotangent, cotangent, cot_recv, cot_recv, *olds)


def body(
    tokens,
    cotangent,
    ln1_gain,
    ln1_bias,
    q_weight,
    q_bias,
    kv_weight,
    v_bias,
    out_weight,
    out_bias,
    rel_table,
    ln2_gain,
    ln2_bias,
    up_weight,
    up_bias,
    down_weight,
    down_bias,
):
    batches, planes, rows_y, rows_z, channels = tokens.shape
    axes = ("section", "tok")
    core = lax.axis_index("section")
    block = lax.axis_index("tok")
    blocks = lax.axis_size("tok")
    is_encoder = core == 0
    core_arg = core.astype(jnp.int32).reshape(1)

    def device(position):
        position = position % (2 * blocks)
        return (position % 2) * blocks + position // 2

    to_previous = [(device(r), device(r - 1)) for r in range(2 * blocks)]
    to_next = [(device(r), device(r + 1)) for r in range(2 * blocks)]

    (
        vec_e, vec_d, w_qkv, b_qkv, w_q_d, b_q_d, w_out_e, w_out_d, w_up_e, w_up_d, b_up_e, b_up_d,
        w_down_e, w_down_d, bias_e, bias_d,
    ) = run_prepare(
        blocks,
        (q_weight[0], out_weight[0], up_weight[0], down_weight[0]),
        (ln1_gain, ln1_bias, ln2_gain, ln2_bias, out_bias, down_bias, q_bias, up_bias),
        rel_table[0],
        kv_weight,
        v_bias[None],
    )
    order = jnp.asarray(order_matrix(rows_z, 0), BF16)
    order_rolled = jnp.asarray(order_matrix(rows_z, 1), BF16)

    enc_consts = (order, vec_e, w_qkv, b_qkv, bias_e, w_out_e, w_up_e, b_up_e, w_down_e)
    enc_back_consts = (order, vec_e, w_qkv, b_qkv, w_out_e, w_up_e, w_down_e)
    dec_consts = (order_rolled, vec_d, w_q_d, b_q_d, bias_d, w_out_d, w_up_d, b_up_d, w_down_d)

    handed, saved = [], []
    for batch in range(batches):
        send, keep, *rest = run_encoder(
            core_arg, tokens, batch, enc_consts, cotangent if batch == 0 else None
        )
        if batch == 0:
            *rest, half = rest
            cot_recv = lax.ppermute(half, axes, to_previous)
        handed.append((keep, lax.ppermute(send, axes, to_previous)))
        saved.append(rest)
    dec_sums = None
    returned, ys = [], []
    to_decoder = [(t, blocks + t) for t in range(blocks)]
    to_encoder = [(blocks + t, t) for t in range(blocks)]
    to_after = [(blocks + t, blocks + (t + 1) % blocks) for t in range(blocks)]
    for batch in range(batches):
        out_all, out_tail, own, halo, *dec_sums = run_decoder(
            core_arg, *handed[batch], cotangent, cot_recv, batch, dec_sums, dec_consts
        )
        returned.append((own, lax.ppermute(halo, axes, to_next)))
        y_halo = lax.ppermute(out_tail, axes, to_after)
        ys.append((out_all, y_halo, lax.ppermute(out_all, axes, to_decoder)))
    old = None
    backs = []
    hidden = up_weight.shape[2]
    enc_layout = Layout(channels, hidden, 2 * blocks, True)
    dec_layout = Layout(channels, hidden, 2 * blocks, False)
    d_up, d_down, d_q, d_out, d_vec, d_bias = dec_sums
    comm = Scatter(dec_layout, blocks, (d_up, d_down, d_q, d_out, d_bias))
    for batch in range(batches):
        arrived = backs[:1] if batch == batches - 1 else []
        ends, back, *enc_sums = run_encoder_back(
            batch, *returned[batch], ys[batch], arrived, saved[batch], old, enc_back_consts, tokens,
            comm,
        )
        enc_sums, result = enc_sums[:8], enc_sums[8:]
        if batch == 0:
            comm = Gather(dec_layout, blocks, result[0])
        elif batch == 1:
            comm, dec_total = NoComm(), result[0]
        old = (ends, enc_sums)
        backs.append(lax.ppermute(back, axes, to_encoder))

    enc_total, kv_total, vec_sum = run_sum(enc_sums, d_vec, enc_layout, blocks)
    (
        ends, g_ln1_gain, g_ln1_bias, g_q_weight, g_q_bias, g_kv_weight, g_v_bias, g_out_weight,
        g_out_bias, g_table, g_ln2_gain, g_ln2_bias, g_up_weight, g_up_bias, g_down_weight, g_down_bias,
    ) = run_finish(core_arg, (enc_total, dec_total, kv_total, vec_sum), backs[1:], ends, enc_layout)
    return (
        ends[None],
        g_ln1_gain,
        g_ln1_bias,
        g_q_weight[None],
        g_q_bias,
        g_kv_weight[None],
        g_v_bias,
        g_out_weight[None],
        g_out_bias,
        g_table[None],
        g_ln2_gain,
        g_ln2_bias,
        g_up_weight[None],
        g_up_bias,
        g_down_weight[None],
        g_down_bias,
    )


def solution(mesh):
    in_specs = (
        P(None, "tok", None, None, None),
        P(None, "tok", None, None, None),
        P("section", None),
        P("section", None),
        P("section", None, None),
        P("section", None),
        P(),
        P(),
        P("section", None, None),
        P("section", None),
        P("section", None, None),
        P("section", None),
        P("section", None),
        P("section", None, None),
        P("section", None),
        P("section", None, None),
        P("section", None),
    )
    out_specs = (
        P("section", None, "tok", None, None, None),
        P("section", None),
        P("section", None),
        P("section", None, None),
        P("section", None),
        P("section", None, None),
        P("section", None),
        P("section", None, None),
        P("section", None),
        P("section", None, None),
        P("section", None),
        P("section", None),
        P("section", None, None),
        P("section", None),
        P("section", None, None),
        P("section", None),
    )
    return jax.shard_map(body, mesh=mesh, in_specs=in_specs, out_specs=out_specs, check_vma=False)
```

```python
import functools

import jax
import jax.numpy as jnp
import numpy as np
from jax import lax
from jax.experimental import pallas as pl
from jax.experimental.pallas import tpu as pltpu
from jax.sharding import PartitionSpec as P

HEADS = 6
HD = 32
WIN = 4
SHIFT = 2
CELLS = WIN**3
SPAN = 2 * WIN - 1
HEADS_A = 4
LANES_A = HEADS_A * HD
COLS_A = HEADS_A * CELLS

eps_norm = 1e-05
mask_fill = -100.0
log2_e = 1.4426950408889634
root_half = 0.7071067811865476
inv_root_two_pi = 0.3989422804014327
scale = HD ** (-0.5)
VMEM_BYTES = 63 * 1024 * 1024

F32 = jnp.float32
BF16 = jnp.bfloat16


def nn(left, right):
    return lax.dot_general(left, right, (((1,), (0,)), ((), ())), preferred_element_type=F32)


def nt(left, right):
    return lax.dot_general(left, right, (((1,), (1,)), ((), ())), preferred_element_type=F32)


def tn(left, right):
    return lax.dot_general(left, right, (((0,), (0,)), ((), ())), preferred_element_type=F32)


def order_matrix(rows_z, rolled):
    count = 4 * rows_z
    matrix = np.zeros((count, count), np.float32)
    units = rows_z // 2
    for unit in range(units):
        for dx in range(2):
            for dy in range(2):
                for dz in range(2):
                    z = (2 * (unit + rolled) + dz) % rows_z
                    matrix[unit * 8 + dx * 4 + dy * 2 + dz, (dx * 2 + dy) * rows_z + z] = 1.0
    return matrix


def windows_of(pieces):
    count, rows, channels = pieces.shape
    return pieces.reshape(count, rows // 16, 16, channels).transpose(1, 0, 2, 3).reshape(-1, channels)


def pieces_of(windows):
    rows, channels = windows.shape
    return (
        windows.reshape(rows // CELLS, 4, 16, channels)
        .transpose(1, 0, 2, 3)
        .reshape(4, rows // 4, channels)
    )


def roll_rows(pieces, steps):
    return jnp.concatenate([pieces[:, steps:], pieces[:, :steps]], 1)


def pack_slab(pieces):
    half = pieces.shape[1] // 2
    rest = pieces[:, :, LANES_A:]
    return jnp.concatenate(
        [pieces[:, :, :LANES_A], jnp.concatenate([rest[:, :half], rest[:, half:]], 2)], 1
    ).astype(BF16)


def unpack_slab(block):
    size = block.shape[0] * 2 // 3
    half = LANES_A // 2
    rest = jnp.concatenate([block[size:, :half], block[size:, half:]], 0)
    return jnp.concatenate([block[:size], rest], 1)


def normalize(rows):
    mean = jnp.mean(rows, -1, keepdims=True)
    centered = rows - mean
    inv_std = lax.rsqrt(jnp.mean(centered * centered, -1, keepdims=True) + eps_norm)
    return centered * inv_std, inv_std


def norm_back(grad_rows, unit_rows, inv_std, gain):
    scaled = grad_rows * gain
    return inv_std * (
        scaled
        - jnp.mean(scaled, -1, keepdims=True)
        - unit_rows * jnp.mean(scaled * unit_rows, -1, keepdims=True)
    )


def gelu_pair(rows):
    upper = 0.5 * lax.erf(rows * root_half) + 0.5
    bell = jnp.exp2(rows * rows * (-0.5 * log2_e))
    return rows * upper, upper + rows * bell * inv_root_two_pi


def head_masks(width):
    heads = lax.broadcasted_iota(jnp.int32, (1, width), 1) // HD
    return [jnp.where(heads == h, 1.0, 0.0).astype(BF16) for h in range(width // HD)]


def expand(rows):
    masks = head_masks(rows.shape[1])
    return jnp.concatenate([rows * mask for mask in masks], 0)


def collapse(stacked):
    width = stacked.shape[1]
    lanes = lax.broadcasted_iota(jnp.int32, (CELLS, width), 1)
    total = stacked[:CELLS]
    for h in range(1, width // HD):
        total = jnp.where(lanes >= h * HD, stacked[h * CELLS : (h + 1) * CELLS], total)
    return total


def split(rows):
    return rows[:, :LANES_A], rows[:, LANES_A:]


def attend(parts, bias):
    queries, keys, values = zip(*[[split(rows) for rows in part] for part in parts])
    wide = [[expand(half) for half in q] for q in queries]
    scores = [
        jnp.concatenate([nt(k[0], q[0]), nt(k[1], q[1])], 1) for k, q in zip(keys, wide)
    ]
    scores = [s * (scale * log2_e) + b for s, b in zip(scores, bias)]
    exponents = [jnp.exp2(s - jnp.max(s, 0, keepdims=True)) for s in scores]
    probs = [e * (1.0 / jnp.sum(e, 0, keepdims=True)) for e in exponents]
    low = [p.astype(BF16) for p in probs]
    mixed = [
        (tn(p[:, :COLS_A], v[0]), tn(p[:, COLS_A:], v[1])) for p, v in zip(low, values)
    ]
    mixed = [jnp.concatenate([collapse(m[0]), collapse(m[1])], 1).astype(BF16) for m in mixed]
    return mixed, probs


def attend_back(parts):
    queries, keys, values, grads = zip(
        *[[split(rows) for rows in part[:3] + part[4:]] for part in parts]
    )
    probs = [part[3] for part in parts]
    wide_g = [[expand(half) for half in g] for g in grads]
    d_probs = [
        jnp.concatenate([nt(v[0], g[0]), nt(v[1], g[1])], 1) for v, g in zip(values, wide_g)
    ]
    low = [part[3].astype(BF16) for part in parts]
    d_values = [
        jnp.concatenate([nn(p[:, :COLS_A], g[0]), nn(p[:, COLS_A:], g[1])], 1)
        for p, g in zip(low, wide_g)
    ]
    wide_q = [[expand(half) for half in q] for q in queries]
    d_scores = [
        p * (d - jnp.sum(d * p, 0, keepdims=True)) for p, d in zip(probs, d_probs)
    ]
    low_d = [d.astype(BF16) for d in d_scores]
    d_keys = [
        jnp.concatenate([nn(d[:, :COLS_A], q[0]), nn(d[:, COLS_A:], q[1])], 1) * scale
        for d, q in zip(low_d, wide_q)
    ]
    d_queries = [
        (tn(d[:, :COLS_A], k[0]), tn(d[:, COLS_A:], k[1])) for d, k in zip(low_d, keys)
    ]
    d_queries = [
        jnp.concatenate([collapse(d[0]), collapse(d[1])], 1) * scale for d in d_queries
    ]
    table = d_scores[0]
    for d in d_scores[1:]:
        table = table + d
    return d_queries, d_keys, d_values, table


def window_groups(count):
    return [range(k, min(k + TOGETHER, count)) for k in range(0, count, TOGETHER)]


def window_rows(k):
    return slice(k * CELLS, (k + 1) * CELLS)


def with_ones(rows):
    return jnp.concatenate([rows.T, jnp.ones((16, rows.shape[0]), BF16)], 0)


def col_sum(rows):
    return jnp.sum(rows, 0, keepdims=True)


def start_sums(first, old_refs, new_refs):
    @pl.when(pl.program_id(0) == 0)
    def _():
        for k, new in enumerate(new_refs):
            new[...] = jnp.zeros_like(new) if first else old_refs[k][...]


def restore(matrix, rows):
    high = rows.astype(BF16)
    low = (rows - high.astype(F32)).astype(BF16)
    return tn(matrix, high) + tn(matrix, low)


CHUNK = 256
TOGETHER = 8


def encoder_forward(
    cuts, core_ref, tok, order, vec, w_qkv, b_qkv, bias, w_out, w_up, b_up, w_down, *rest,
):
    cut_in, rest = rest[:cuts], rest[cuts:]
    send, keep, n1_out, n2_out, p_out, o_out, a_out, s_out, *cut_out, qkv = rest
    for source, target in zip(cut_in, cut_out):
        target[...] = source[...]
    rows_z = tok.shape[3]
    size = 4 * rows_z
    pieces = []
    for x in range(2):
        for y in range(2):
            part = tok[0, 2 * x : 2 * x + 2, 2 * y : 2 * y + 2].reshape(size, -1)
            pieces.append(nn(order[...], part))
    entry = windows_of(jnp.stack(pieces))
    unit, inv_std = normalize(entry)
    channels = entry.shape[1]
    wide = jnp.broadcast_to(inv_std, (entry.shape[0], 256 - channels))
    n1_out[0, :, :channels] = unit
    n1_out[0, :, channels:] = wide
    left = (unit * vec[0:1] + vec[1:2]).astype(BF16)
    triple = nn(left, w_qkv[...]) + b_qkv[...]
    qkv[...] = triple.astype(BF16)
    for together in window_groups(entry.shape[0] // CELLS):
        parts = [
            [qkv[window_rows(k), 256 * f : 256 * f + 192] for f in range(3)] for k in together
        ]
        mixed, probs = attend(parts, [bias[...]] * len(parts))
        for k, o, p in zip(together, mixed, probs):
            p_out[0, k] = p.astype(BF16)
            o_out[0, window_rows(k)] = o
    middle = entry + nn(o_out[0], w_out[...]) + vec[4:5]
    unit, inv_std = normalize(middle)
    wide = jnp.broadcast_to(inv_std, (entry.shape[0], 256 - channels))
    n2_out[0, :, :channels] = unit
    n2_out[0, :, channels:] = wide
    left = (unit * vec[2:3] + vec[3:4]).astype(BF16)
    results = []
    for k in range(entry.shape[0] // CHUNK):
        rows = slice(k * CHUNK, (k + 1) * CHUNK)
        hidden, slope = gelu_pair(nn(left[rows], w_up[...]) + b_up[...])
        hidden = hidden.astype(BF16)
        a_out[0, rows] = hidden
        s_out[0, rows] = slope.astype(BF16)
        results.append(nt(hidden, w_down[...]))
    result = middle + jnp.concatenate(results, 0) + vec[5:6]
    for field, rows in enumerate((result, triple[:, 256:448], triple[:, 512:704])):
        rolled = pack_slab(roll_rows(pieces_of(rows), 8))
        send[0, :, field] = rolled[:2]
        keep[0, :, field] = rolled[2:]


def mlp_back(grad, grad_low, hidden, slope, left_two, unit, inv_std, w_up, w_down, vec, sums):
    g_up, g_down, g_vec = sums
    backs = []
    total_up = None
    turned = grad_low.T
    ones = with_ones(left_two)
    for k in range(grad.shape[0] // CHUNK):
        rows = slice(k * CHUNK, (k + 1) * CHUNK)
        d_pre = (nn(grad_low[rows], w_down[...]) * slope(rows)).astype(BF16)
        part = nn(ones[:, rows], d_pre)
        total_up = part if total_up is None else total_up + part
        backs.append(nt(d_pre, w_up[...]))
    g_up[...] += total_up
    g_down[...] += nn(turned, hidden)
    d_normed = jnp.concatenate(backs, 0)
    g_vec[2:3] += col_sum(d_normed * unit)
    g_vec[3:4] += col_sum(d_normed)
    g_vec[4:5] += col_sum(grad)
    return grad + norm_back(d_normed, unit, inv_std, vec[2:3])


def start_all(copies):
    for copy in copies:
        copy.start()


def wait_all(copies):
    for copy in copies:
        copy.wait()


def encoder_backward(
    first, batch, returns, core_ref, order, vec, w_qkv, b_qkv, w_out, w_up, w_down,
    y_own, y_halo, y_sib,
    keep_a, keep_b, recv_a, recv_b,
    n1_in, n2_in, p_in, o_in, a_in, s_in, *rest,
):
    returned, rest = rest[:returns], rest[returns:]
    old, rest = ([], rest) if first else (rest[:8], rest[9:])
    ends, back, *sums, qkv, dqkv, buffer, out_sem, copy_sem = rest
    g_up, g_down, g_q, g_k, g_v, g_out, g_vec, g_bias = sums
    step, steps = pl.program_id(0), pl.num_programs(0)
    is_encoder = core_ref[0] == 0
    rows_y = ends.shape[2]
    slot = lax.rem(step, 2)

    def output_copies():
        copies = []
        for start, planes, ref in ((0, 2, y_halo), (2, 4, y_sib), (6, 2, y_own)):
            for half in range(2):
                rows = pl.ds(lax.rem(step * WIN + SHIFT + 2 * half, rows_y), 2)
                target = ends.at[batch, pl.ds(start, planes), rows]
                copies.append((ref.at[:, pl.ds(2 * half, 2)], target))
        return [
            pltpu.make_async_copy(source, target, copy_sem.at[k])
            for k, (source, target) in enumerate(copies)
        ]

    def gradient_copies():
        return [
            pltpu.make_async_copy(
                ref, ends.at[k, pl.ds(WIN, WIN), pl.ds(step * WIN, WIN)], copy_sem.at[8 + k]
            )
            for k, ref in enumerate(returned)
        ]

    def result_copy(index, to_ends):
        target = (
            ends.at[batch, pl.ds(0, WIN), pl.ds(index * WIN, WIN)]
            if to_ends
            else back.at[:, pl.ds(index * WIN, WIN)]
        )
        at = lax.rem(index, 2)
        return pltpu.make_async_copy(buffer.at[at], target, out_sem.at[at])

    def for_core(encoder_work, decoder_work):
        pl.when(is_encoder)(encoder_work)
        pl.when(jnp.logical_not(is_encoder))(decoder_work)

    for_core(lambda: start_all(gradient_copies()), lambda: start_all(output_copies()))
    start_sums(first, old, sums)
    fields = []
    for field in range(3):
        pieces = jnp.stack(
            [unpack_slab(ref[0, 0, field]) for ref in (recv_b, recv_a, keep_b, keep_a)]
        )
        fields.append(windows_of(pieces))
    grad_low, d_key_1, d_value_1 = fields
    grad = grad_low.astype(F32)
    channels = grad.shape[1]
    unit_1, unit_2 = n1_in[0, :, :channels], n2_in[0, :, :channels]
    wide_1, wide_2 = [ref[0, :, channels : channels + 1] for ref in (n1_in, n2_in)]
    left_1 = (unit_1 * vec[0:1] + vec[1:2]).astype(BF16)
    left_2 = (unit_2 * vec[2:3] + vec[3:4]).astype(BF16)
    qkv[...] = (nn(left_1, w_qkv[...]) + b_qkv[...]).astype(BF16)
    d_middle = mlp_back(
        grad, grad_low, a_in[0], lambda rows: s_in[0, rows].astype(F32), left_2, unit_2, wide_2, w_up, w_down, vec,
        (g_up, g_down, g_vec),
    )
    branch = d_middle.astype(BF16)
    g_out[...] += nn(with_ones(o_in[0]), branch)
    d_mixed = nt(branch, w_out[...]).astype(BF16)
    d_table = None
    for together in window_groups(grad.shape[0] // CELLS):
        parts = [
            [qkv[window_rows(k), 256 * f : 256 * f + 192] for f in range(3)]
            + [p_in[0, k].astype(F32), d_mixed[window_rows(k)]]
            for k in together
        ]
        *d_qkv, d_s = attend_back(parts)
        for k, d_q, d_k, d_v in zip(together, *d_qkv):
            rows = window_rows(k)
            dqkv[0, rows] = d_q.astype(BF16)
            dqkv[1, rows] = (d_k + d_key_1[rows].astype(F32)).astype(BF16)
            dqkv[2, rows] = (d_v + d_value_1[rows].astype(F32)).astype(BF16)
        d_table = d_s if d_table is None else d_table + d_s
    g_bias[...] += d_table
    ones = with_ones(left_1)
    d_normed = None
    for field, g_field in enumerate((g_q, g_k, g_v)):
        cols = slice(field * 256, field * 256 + 192)
        g_field[...] += nn(ones, dqkv[field])
        part = nt(dqkv[field], w_qkv[:, cols])
        d_normed = part if d_normed is None else d_normed + part
    g_vec[0:1] += col_sum(d_normed * unit_1)
    g_vec[1:2] += col_sum(d_normed)
    result = pieces_of(d_middle + norm_back(d_normed, unit_1, wide_1, vec[0:1]))
    rows_z = ends.shape[3]

    @pl.when(step >= 2)
    def _():
        for_core(
            lambda: result_copy(step - 2, True).wait(), lambda: result_copy(step - 2, False).wait()
        )

    for x in range(2):
        for y in range(2):
            part = restore(order[...], result[2 * x + y])
            buffer[slot, 2 * x : 2 * x + 2, 2 * y : 2 * y + 2] = part.reshape(2, 2, rows_z, -1)
    for_core(lambda: result_copy(step, True).start(), lambda: result_copy(step, False).start())

    @pl.when(step == steps - 1)
    def _():
        def finish(to_ends):
            result_copy(step - 1, to_ends).wait()
            result_copy(step, to_ends).wait()

        for_core(lambda: finish(True), lambda: finish(False))

    for_core(lambda: wait_all(gradient_copies()), lambda: wait_all(output_copies()))


def decoder(
    first, core_ref, order, vec, w_q, b_q, bias, w_out, w_up, b_up, w_down,
    keep_1, keep_0, recv_1, recv_0, cot_1, cot_0, cot_r1, cot_r0, *rest,
):
    old, new = ([], rest) if first else (rest[:6], rest[6:])
    out_all, out_tail, own, halo, *sums, p_scr, o_scr, a_scr, s_scr, dqkv = new
    g_up, g_down, g_q, g_out, g_vec, g_bias = sums
    start_sums(first, old, sums)
    fields = []
    for field in range(3):
        pieces = jnp.stack([unpack_slab(ref[0, 0, field]) for ref in (keep_1, keep_0, recv_1, recv_0)])
        fields.append(windows_of(pieces))
    entry_low, keys, values = fields
    entry = entry_low.astype(F32)
    unit_1, inv_1 = normalize(entry)
    left_1 = (unit_1 * vec[0:1] + vec[1:2]).astype(BF16)
    queries = (nn(left_1, w_q[...]) + b_q[...]).astype(BF16)
    windows = entry.shape[0] // CELLS
    for together in window_groups(windows):
        parts = [[rows[window_rows(k)] for rows in (queries, keys, values)] for k in together]
        mixed, probs = attend(parts, [bias[0, 1 if k == windows - 1 else 0] for k in together])
        for k, o, p in zip(together, mixed, probs):
            p_scr[k] = p
            o_scr[window_rows(k)] = o
    middle = entry + nn(o_scr[...], w_out[...]) + vec[4:5]
    unit_2, inv_2 = normalize(middle)
    left_2 = (unit_2 * vec[2:3] + vec[3:4]).astype(BF16)
    results = []
    for k in range(entry.shape[0] // CHUNK):
        rows = slice(k * CHUNK, (k + 1) * CHUNK)
        hidden, slope = gelu_pair(nn(left_2[rows], w_up[...]) + b_up[...])
        hidden = hidden.astype(BF16)
        a_scr[rows] = hidden
        s_scr[rows] = slope
        results.append(nt(hidden, w_down[...]))
    result = pieces_of(middle + jnp.concatenate(results, 0) + vec[5:6])
    rows_z = out_all.shape[2]
    size = 4 * rows_z
    for x in range(2):
        for y in range(2):
            part = restore(order[...], result[2 * x + y]).reshape(2, 2, rows_z, -1)
            out_all[2 * x : 2 * x + 2, 2 * y : 2 * y + 2] = part
            if x == 1:
                out_tail[:, 2 * y : 2 * y + 2] = part

    cots = [
        nn(order[...], ref[0].reshape(size, -1)).astype(BF16) for ref in (cot_1, cot_0, cot_r1, cot_r0)
    ]
    grad_low = windows_of(jnp.stack(cots))
    grad = grad_low.astype(F32)
    d_middle = mlp_back(
        grad, grad_low, a_scr[...], lambda rows: s_scr[rows], left_2, unit_2, inv_2, w_up, w_down, vec,
        (g_up, g_down, g_vec),
    )
    branch = d_middle.astype(BF16)
    g_out[...] += nn(with_ones(o_scr[...]), branch)
    d_mixed = nt(branch, w_out[...]).astype(BF16)
    d_table = None
    for together in window_groups(windows):
        parts = [
            [rows[window_rows(k)] for rows in (queries, keys, values)]
            + [p_scr[k], d_mixed[window_rows(k)]]
            for k in together
        ]
        *d_qkv, d_s = attend_back(parts)
        for k, *grads in zip(together, *d_qkv):
            for f in range(3):
                dqkv[f, window_rows(k)] = grads[f]
        d_table = d_s if d_table is None else d_table + d_s
    g_bias[...] += d_table
    d_queries = dqkv[0].astype(BF16)
    g_q[...] += nn(with_ones(left_1), d_queries)
    d_normed = nt(d_queries, w_q[...])
    g_vec[0:1] += col_sum(d_normed * unit_1)
    g_vec[1:2] += col_sum(d_normed)
    d_entry = d_middle + norm_back(d_normed, unit_1, inv_1, vec[0:1])
    for field, rows in enumerate((d_entry, dqkv[1], dqkv[2])):
        turned = pack_slab(roll_rows(pieces_of(rows), size - 8))
        own[0, :, field] = turned[:2]
        halo[0, :, field] = turned[2:]


def whole(array):
    zeros = (0,) * array.ndim
    return pl.BlockSpec(array.shape, lambda *_: zeros)


def sums_shapes(channels, hidden, products):
    return [
        jax.ShapeDtypeStruct(shape, F32)
        for shape in (
            (channels + 16, hidden),
            (channels, hidden),
            *[(channels + 16, channels)] * products,
            (channels + 16, channels),
            (8, channels),
            (CELLS, HEADS * CELLS),
        )
    ]


def cost(cells, per_cell, hbm):
    return pl.CostEstimate(
        flops=2 * cells * per_cell, bytes_accessed=hbm, transcendentals=cells * 1536
    )


params = pltpu.CompilerParams(
    dimension_semantics=("arbitrary",), vmem_limit_bytes=VMEM_BYTES
)


class Layout:
    def __init__(self, channels, hidden, blocks):
        tall = channels + 16
        self.tall, self.channels = tall, channels
        self.tiles = hidden // LANES_A
        self.up = 0
        self.down = self.tiles * tall
        self.q = self.down + self.tiles * channels
        self.out = self.q + tall
        self.rest = self.out + tall
        self.kv = self.rest + tall
        self.bias = self.kv + 2 * tall
        self.vec = self.bias + HEADS * CELLS // LANES_A * CELLS
        self.end = self.vec + 16
        self.chunk = -(-self.end // (16 * blocks)) * 16
        self.rows = self.chunk * blocks


def fill(buffer, layout, up, down, q, out, kv, bias, vec):
    kind, half = buffer.dtype, LANES_A // 2
    tall, channels = layout.tall, layout.channels
    for k in range(layout.tiles):
        cols = slice(k * LANES_A, (k + 1) * LANES_A)
        buffer[layout.up + k * tall : layout.up + (k + 1) * tall] = up[:, cols].astype(kind)
        buffer[layout.down + k * channels : layout.down + (k + 1) * channels] = down[
            :, cols
        ].astype(kind)
    buffer[layout.q : layout.q + tall] = q[:, :LANES_A].astype(kind)
    buffer[layout.out : layout.out + tall] = out[:, :LANES_A].astype(kind)
    rests = jnp.concatenate([q[:, LANES_A:], out[:, LANES_A:]], 1)
    buffer[layout.rest : layout.rest + tall] = rests.astype(kind)
    buffer[layout.kv : layout.kv + tall] = kv[:, :LANES_A].astype(kind)
    rests = jnp.concatenate([kv[:, LANES_A:], jnp.zeros((tall, half), F32)], 1)
    buffer[layout.kv + tall : layout.kv + 2 * tall] = rests.astype(kind)
    for k in range(HEADS * CELLS // LANES_A):
        start = layout.bias + k * CELLS
        buffer[start : start + CELLS] = bias[:, k * LANES_A : (k + 1) * LANES_A].astype(kind)
    rests = jnp.concatenate([vec[:, LANES_A:], jnp.zeros((8, half), F32)], 1)
    both = jnp.concatenate([vec[:, :LANES_A], rests], 0)
    buffer[layout.vec : layout.vec + 16] = both.astype(kind)
    if layout.rows > layout.end:
        buffer[layout.end :] = jnp.zeros((layout.rows - layout.end, LANES_A), kind)


MESH = pl.DeviceIdType.MESH


def sum_gradients(layout, blocks, *refs):
    enc, dec, rest = refs[:8], refs[8:14], refs[14:]
    (
        total_out, kv_out, own, theirs, from_sib, low, landed, total, sib_kv,
        sib_send, sib_recv, send_sem, recv_sem, out_ssem, out_rsem,
    ) = rest
    core, me = lax.axis_index("section"), lax.axis_index("tok")
    sibling = {"section": 1 - core}

    def peer(offset):
        return lax.rem(me + offset, blocks)

    barrier = pltpu.get_barrier_semaphore()
    pl.semaphore_signal(barrier, inc=1, device_id=sibling, device_id_type=MESH)

    def greet(offset, carry):
        pl.semaphore_signal(
            barrier, inc=1, device_id={"tok": peer(offset)}, device_id_type=MESH
        )
        return carry

    lax.fori_loop(1, blocks, greet, 0)

    e_up, e_down, e_q, e_k, e_v, e_out, e_vec, e_bias = enc
    d_up, d_down, d_q, d_out, d_vec, d_bias = dec

    @pl.when(core == 0)
    def _():
        fill(theirs, layout, d_up, d_down, d_q, d_out, e_v, d_bias, d_vec)
        fill(own, layout, e_up, e_down, e_q, e_out, e_k, e_bias, e_vec)

    @pl.when(core == 1)
    def _():
        fill(theirs, layout, e_up, e_down, e_q, e_out, e_k, e_bias, e_vec)
        fill(own, layout, d_up, d_down, d_q, d_out, e_v, d_bias, d_vec)

    pl.semaphore_wait(barrier, blocks)

    def to_sibling(source, target, k):
        return pltpu.make_async_remote_copy(
            src_ref=source, dst_ref=target, send_sem=sib_send.at[k], recv_sem=sib_recv.at[k],
            device_id=sibling, device_id_type=MESH,
        )

    first = to_sibling(theirs, from_sib, 0)
    first.start()
    first.wait()
    own[...] += from_sib[...].astype(F32)
    low[...] = own[...].astype(BF16)

    def rows_of(position):
        return pl.ds(pl.multiple_of(position * layout.chunk, 16), layout.chunk)

    def scatter(offset):
        return pltpu.make_async_remote_copy(
            src_ref=low.at[rows_of(peer(offset))], dst_ref=landed.at[offset],
            send_sem=send_sem.at[offset], recv_sem=recv_sem.at[offset],
            device_id={"tok": peer(offset)}, device_id_type=MESH,
        )

    def gather(offset):
        return pltpu.make_async_remote_copy(
            src_ref=total.at[rows_of(me)], dst_ref=total.at[rows_of(me)],
            send_sem=out_ssem.at[offset], recv_sem=out_rsem.at[offset],
            device_id={"tok": peer(offset)}, device_id_type=MESH,
        )

    def gathered(offset):
        rows = rows_of(lax.rem(me - offset + blocks, blocks))
        return pltpu.make_async_remote_copy(
            src_ref=total.at[rows], dst_ref=total.at[rows],
            send_sem=out_ssem.at[offset], recv_sem=out_rsem.at[offset],
            device_id={"tok": peer(offset)}, device_id_type=MESH,
        )

    def start(offset, carry):
        scatter(offset).start()
        return carry

    lax.fori_loop(1, blocks, start, 0)

    def add(offset, carry):
        scatter(offset).wait_recv()
        return carry + landed[offset].astype(F32)

    chunk_sum = lax.fori_loop(1, blocks, add, own[rows_of(me)])
    total[rows_of(me)] = chunk_sum.astype(BF16)

    def spread(offset, carry):
        gather(offset).start()
        return carry

    lax.fori_loop(1, blocks, spread, 0)

    def arrive(offset, carry):
        gathered(offset).wait_recv()
        return carry

    lax.fori_loop(1, blocks, arrive, 0)
    kv_rows = pl.ds(layout.kv, 2 * layout.tall)
    third = to_sibling(total.at[kv_rows], sib_kv, 1)
    third.start()
    total_out[...] = total[...]

    def drain(offset, carry):
        scatter(offset).wait_send()
        gather(offset).wait_send()
        return carry

    lax.fori_loop(1, blocks, drain, 0)
    third.wait()
    kv_out[...] = sib_kv[...]


def run_sum(enc_sums, dec_sums, layout, blocks):
    rows, chunk, tall = layout.rows, layout.chunk, layout.tall
    dma = pltpu.SemaphoreType.DMA
    vmem = pl.BlockSpec(memory_space=pltpu.VMEM)
    args = [*enc_sums, *dec_sums]
    return pl.pallas_call(
        functools.partial(sum_gradients, layout, blocks),
        in_specs=[vmem] * len(args),
        out_specs=[vmem] * 2,
        out_shape=[
            jax.ShapeDtypeStruct((rows, LANES_A), BF16),
            jax.ShapeDtypeStruct((2 * tall, LANES_A), BF16),
        ],
        scratch_shapes=[
            pltpu.VMEM((rows, LANES_A), F32),
            pltpu.VMEM((rows, LANES_A), BF16),
            pltpu.VMEM((rows, LANES_A), BF16),
            pltpu.VMEM((rows, LANES_A), BF16),
            pltpu.VMEM((blocks, chunk, LANES_A), BF16),
            pltpu.VMEM((rows, LANES_A), BF16),
            pltpu.VMEM((2 * tall, LANES_A), BF16),
            dma((2,)),
            dma((2,)),
            *[dma((blocks,))] * 4,
        ],
        compiler_params=pltpu.CompilerParams(
            collective_id=0, has_side_effects=True, vmem_limit_bytes=VMEM_BYTES
        ),
        name="sum_gradients",
    )(*args)


def finish(layout, batches, returns, core_ref, total, sib_kv, *refs):
    returned, refs = refs[:returns], refs[returns + 1 :]
    (
        ends, ln1_gain, ln1_bias, q_weight, q_bias, kv_weight, v_bias, out_weight, out_bias, table,
        ln2_gain, ln2_bias, up_weight, up_bias, down_weight, down_bias, placed, copy_sem,
    ) = refs
    is_encoder = core_ref[0] == 0
    step = pl.program_id(0)

    def copies():
        return [
            pltpu.make_async_copy(
                ref,
                ends.at[batches - returns + k, pl.ds(WIN, WIN), pl.ds(step * WIN, WIN)],
                copy_sem.at[k],
            )
            for k, ref in enumerate(returned)
        ]

    pl.when(is_encoder)(lambda: start_all(copies()))

    @pl.when(step == 0)
    def _():
        unpack(
            layout, is_encoder, total, sib_kv, ln1_gain, ln1_bias, q_weight, q_bias, kv_weight,
            v_bias, out_weight, out_bias, table, ln2_gain, ln2_bias, up_weight, up_bias, down_weight,
            down_bias, placed,
        )

    pl.when(is_encoder)(lambda: wait_all(copies()))


def unpack(
    layout, is_encoder, total, sib_kv, ln1_gain, ln1_bias, q_weight, q_bias, kv_weight,
    v_bias, out_weight, out_bias, table, ln2_gain, ln2_bias, up_weight, up_bias, down_weight, down_bias,
    placed,
):
    channels, tall, half = layout.channels, layout.tall, LANES_A // 2

    def at(start, rows):
        return total[start : start + rows].astype(F32)

    vec = at(layout.vec, 16)
    vec = jnp.concatenate([vec[:8], vec[8:, :half]], 1)
    for row, ref in enumerate((ln1_gain, ln1_bias, ln2_gain, ln2_bias, down_bias)):
        ref[...] = vec[row : row + 1]

    for k in range(layout.tiles):
        cols = slice(k * LANES_A, (k + 1) * LANES_A)
        tile = at(layout.up + k * tall, tall)
        up_weight[:, cols] = tile[:channels]
        up_bias[:, cols] = tile[channels : channels + 1]
        down_weight[:, cols] = at(layout.down + k * channels, channels)
    rest = at(layout.rest, tall)
    q = jnp.concatenate([at(layout.q, tall), rest[:, :half]], 1)
    out = jnp.concatenate([at(layout.out, tall), rest[:, half:]], 1)
    q_weight[...] = q[:channels]
    q_bias[...] = q[channels : channels + 1]
    out_weight[...] = out[:channels]
    out_bias[...] = out[channels : channels + 1]
    mine = at(layout.kv, 2 * tall)
    other = sib_kv[...].astype(F32)
    for start, side in ((0, jnp.where(is_encoder, mine, other)), (channels, jnp.where(is_encoder, other, mine))):
        side = jnp.concatenate([side[:tall], side[tall:, :half]], 1)
        kv_weight[:, start : start + channels] = side[:channels]
    v_bias[...] = side[channels : channels + 1]
    placed[...] = jnp.zeros_like(placed)
    positions = [position_matrix(False), position_matrix(True)]
    for h in range(HEADS):
        start = layout.bias + h // 2 * CELLS
        placed[h, :, :256] = nt(total[start : start + CELLS], positions[h % 2])
    entries = jnp.zeros((8, 384), F32)
    for j in range(CELLS):
        entries += pltpu.roll(placed[:, j, :], CENTRE - cell_position(j), 1)
    table[...] = entries[:HEADS, : SPAN**3][:, None]


def run_finish(core, total, sib_kv, returned, ends, layout):
    channels = layout.channels
    hidden = layout.tiles * LANES_A
    _, _, rows_y, rows_z, _ = ends.shape
    any_spec = pl.BlockSpec(memory_space=pl.ANY)
    shapes = [
        (1, channels), (1, channels), (channels, channels), (1, channels), (channels, 2 * channels),
        (1, channels), (channels, channels), (1, channels), (HEADS, 1, SPAN**3),
        (1, channels), (1, channels), (channels, hidden), (1, hidden), (channels, hidden), (1, channels),
    ]
    shapes = [jax.ShapeDtypeStruct(shape, F32) for shape in shapes]
    return pl.pallas_call(
        functools.partial(finish, layout, ends.shape[0], len(returned)),
        grid_spec=pltpu.PrefetchScalarGridSpec(
            num_scalar_prefetch=1,
            grid=(rows_y // WIN,),
            in_specs=[
                *[whole(a) for a in (total, sib_kv)],
                *[
                    pl.BlockSpec(
                        (WIN, WIN, rows_z, channels), lambda i, c: (0, i * (1 - c[0]), 0, 0)
                    )
                ]
                * len(returned),
                any_spec,
            ],
            out_specs=[any_spec, *[whole(a) for a in shapes]],
            scratch_shapes=[
                pltpu.VMEM((8, CELLS, 384), F32),
                pltpu.SemaphoreType.DMA((len(returned),)),
            ],
        ),
        out_shape=[jax.ShapeDtypeStruct(ends.shape, F32), *shapes],
        input_output_aliases={3 + len(returned): 0},
        compiler_params=params,
        name="finish",
    )(core, total, sib_kv, *returned, ends)


def cell_position(ids):
    x = 2 * (ids // 32) + ids // 4 % 2
    y = 2 * (ids // 16 % 2) + ids // 2 % 2
    z = 2 * (ids // 8 % 2) + ids % 2
    return (x * SPAN + y) * SPAN + z


CENTRE = (WIN - 1) * (SPAN * SPAN + SPAN + 1)
TABLE_ROW = 8


def position_matrix(odd):
    rows = lax.broadcasted_iota(jnp.int32, (256, 2 * CELLS), 0)
    ids = lax.broadcasted_iota(jnp.int32, (256, 2 * CELLS), 1) - (CELLS if odd else 0)
    hit = (ids >= 0) & (ids < CELLS) & (rows == cell_position(ids))
    return jnp.where(hit, 1.0, 0.0).astype(BF16)


def spread_bias(table, shifted):
    for j in range(CELLS):
        turned = pltpu.roll(table, (384 - CENTRE + cell_position(j)) % 384, 1)
        for h in range(HEADS):
            shifted[h, j : j + 1] = turned[h : h + 1, :256]
    even, odd = position_matrix(False), position_matrix(True)
    pairs = [
        nn(shifted[2 * p].astype(BF16), even) + nn(shifted[2 * p + 1].astype(BF16), odd)
        for p in range(HEADS // 2)
    ]
    return jnp.concatenate(pairs, 1) * log2_e


def prepare(
    blocks, q_w, out_w, up_w, down_w, kv_w, v_b, ln1_g, ln1_b, ln2_g, ln2_b, out_b, down_b, q_b, up_b, table,
    vec_e, vec_d, w_qkv, b_qkv, w_q_d, b_q_d, w_out_e, w_out_d, w_up_e, w_up_d, b_up_e, b_up_d,
    w_down_e, w_down_d, bias_e, bias_d,
    small, small_sib, q_sib, out_sib, up_sib, down_sib, shifted, send_sem, recv_sem,
):
    core, block = lax.axis_index("section"), lax.axis_index("tok")
    channels, hidden = up_w.shape
    sibling = {"section": 1 - core}
    barrier = pltpu.get_barrier_semaphore()
    pl.semaphore_signal(barrier, inc=1, device_id=sibling, device_id_type=MESH)
    small[...] = jnp.zeros_like(small)
    for row, ref in enumerate((ln1_g, ln1_b, ln2_g, ln2_b, out_b, down_b, q_b)):
        small[row : row + 1, :channels] = ref[...].astype(F32)
    small[7:8, :hidden] = up_b[...].astype(F32)
    small[TABLE_ROW : TABLE_ROW + HEADS, : SPAN**3] = table[...].astype(F32)
    pl.semaphore_wait(barrier, 1)
    pairs = ((small, small_sib), (q_w, q_sib), (out_w, out_sib), (up_w, up_sib), (down_w, down_sib))
    copies = [
        pltpu.make_async_remote_copy(
            src_ref=source, dst_ref=target, send_sem=send_sem.at[k], recv_sem=recv_sem.at[k],
            device_id=sibling, device_id_type=MESH,
        )
        for k, (source, target) in enumerate(pairs)
    ]
    for copy in copies:
        copy.start()
    for copy in copies:
        copy.wait()

    def place(enc, dec):
        e_small, e_q, e_out, e_up, e_down = enc
        d_small, d_q, d_out, d_up, d_down = dec
        for source, vec, b_up in ((e_small, vec_e, b_up_e), (d_small, vec_d, b_up_d)):
            vec[...] = source[:8, :channels]
            b_up[...] = source[7:8, :hidden]
        w_qkv[...] = jnp.zeros_like(w_qkv)
        b_qkv[...] = jnp.zeros_like(b_qkv)
        w_qkv[:, :channels] = e_q[...]
        w_qkv[:, 256 : 256 + channels] = kv_w[:, :channels]
        w_qkv[:, 512 : 512 + channels] = kv_w[:, channels:]
        b_qkv[:, :channels] = e_small[6:7, :channels]
        b_qkv[:, 512 : 512 + channels] = v_b[...].astype(F32)
        w_q_d[...] = d_q[...]
        b_q_d[...] = d_small[6:7, :channels]
        for target, source in (
            (w_out_e, e_out), (w_out_d, d_out), (w_up_e, e_up), (w_up_d, d_up),
            (w_down_e, e_down), (w_down_d, d_down),
        ):
            target[...] = source[...]
        rows = slice(TABLE_ROW, TABLE_ROW + 8)
        bias_e[...] = spread_bias(e_small[rows, :384], shifted)
        return spread_bias(d_small[rows, :384], shifted)

    own = (small, q_w, out_w, up_w, down_w)
    sib = (small_sib, q_sib, out_sib, up_sib, down_sib)

    def masked(base):
        shape = (CELLS, HEADS * CELLS)
        keys = lax.broadcasted_iota(jnp.int32, shape, 0)
        queries = lax.broadcasted_iota(jnp.int32, shape, 1) % CELLS

        def differ(unit):
            return jnp.where(keys // unit % 2 != queries // unit % 2, 1.0, 0.0)

        last = jnp.where((core == 1) & (block == blocks - 1), 1.0, 0.0)
        for y in range(2):
            for z in range(2):
                apart = jnp.maximum(last * differ(32), jnp.maximum(y * differ(16), z * differ(8)))
                bias_d[y, z] = base + apart * (mask_fill * log2_e)

    @pl.when(core == 0)
    def _():
        masked(place(own, sib))

    @pl.when(core == 1)
    def _():
        masked(place(sib, own))


def run_prepare(blocks, weights, smalls, table, kv_weight, v_bias):
    q_w, out_w, up_w, down_w = weights
    channels, hidden = up_w.shape
    vmem = pl.BlockSpec(memory_space=pltpu.VMEM)
    args = [*weights, kv_weight, v_bias, *smalls, table]
    bias = (CELLS, HEADS * CELLS)
    square = (channels, channels)

    def f32(*shape):
        return jax.ShapeDtypeStruct(shape, F32)

    def bf16(*shape):
        return jax.ShapeDtypeStruct(shape, BF16)

    shapes = [
        f32(8, channels), f32(8, channels), bf16(channels, 768), f32(1, 768), bf16(*square),
        f32(1, channels), bf16(*square), bf16(*square), bf16(channels, hidden), bf16(channels, hidden),
        f32(1, hidden), f32(1, hidden), bf16(channels, hidden), bf16(channels, hidden),
        f32(*bias), f32(2, 2, *bias),
    ]
    return pl.pallas_call(
        functools.partial(prepare, blocks),
        in_specs=[vmem] * len(args),
        out_specs=[vmem] * len(shapes),
        out_shape=shapes,
        scratch_shapes=[
            pltpu.VMEM((TABLE_ROW + 8, hidden), F32),
            pltpu.VMEM((TABLE_ROW + 8, hidden), F32),
            pltpu.VMEM(square, BF16),
            pltpu.VMEM(square, BF16),
            pltpu.VMEM((channels, hidden), BF16),
            pltpu.VMEM((channels, hidden), BF16),
            pltpu.VMEM((HEADS, CELLS, 256), F32),
            pltpu.SemaphoreType.DMA((5,)),
            pltpu.SemaphoreType.DMA((5,)),
        ],
        compiler_params=pltpu.CompilerParams(
            collective_id=1, has_side_effects=True, vmem_limit_bytes=VMEM_BYTES
        ),
        name="prepare",
    )(*args)


def run_encoder(core, tokens, batch, consts, cotangent):
    _, _, rows_y, rows_z, channels = tokens.shape
    groups, size = rows_y // WIN, 4 * rows_z
    cells, windows = 4 * size, rows_z // WIN
    hidden = consts[6].shape[1]
    slab = jax.ShapeDtypeStruct((groups, 2, 3, size * 3 // 2, LANES_A), BF16)
    outs = [
        slab,
        slab,
        jax.ShapeDtypeStruct((groups, cells, 256), F32),
        jax.ShapeDtypeStruct((groups, cells, 256), F32),
        jax.ShapeDtypeStruct((groups, windows, CELLS, HEADS * CELLS), BF16),
        jax.ShapeDtypeStruct((groups, cells, channels), BF16),
        jax.ShapeDtypeStruct((groups, cells, hidden), BF16),
        jax.ShapeDtypeStruct((groups, cells, hidden), BF16),
    ]

    def row(array):
        zeros = (0,) * (array.ndim - 1)
        return pl.BlockSpec((1, *array.shape[1:]), lambda i, c: (i, *zeros))

    batches = tokens.shape[0]
    cut = [] if cotangent is None else [cotangent]
    cut_block = (batches, SHIFT, WIN, rows_z, channels)
    cut_outs = [
        jax.ShapeDtypeStruct((batches, SHIFT, rows_y, rows_z, channels), a.dtype) for a in cut
    ]
    return pl.pallas_call(
        functools.partial(encoder_forward, len(cut)),
        grid_spec=pltpu.PrefetchScalarGridSpec(
            num_scalar_prefetch=1,
            grid=(groups,),
            in_specs=[
                pl.BlockSpec(
                    (1, WIN, WIN, rows_z, channels), lambda i, c: (batch, c[0], i, 0, 0)
                ),
                *[whole(a) for a in consts],
                *[pl.BlockSpec(cut_block, lambda i, c: (0, 2 * c[0], i, 0, 0)) for _ in cut],
            ],
            out_specs=[
                *[row(a) for a in outs],
                *[pl.BlockSpec(cut_block, lambda i, c: (0, 0, i, 0, 0)) for _ in cut],
            ],
            scratch_shapes=[pltpu.VMEM((cells, 768), BF16)],
        ),
        out_shape=[*outs, *cut_outs],
        compiler_params=params,
        cost_estimate=cost(groups * cells, 466944, groups * cells * 7500),
        name="encoder_forward",
    )(core, tokens, *consts, *cut)


def run_encoder_back(core, batch, own, halo, ys, returned, saved, old, consts, tokens):
    groups, _, _, packed, _ = own.shape
    batches, planes, rows_y, rows_z, channels = tokens.shape
    size = 4 * rows_z
    hidden = consts[5].shape[1]
    first = old is None
    shapes = sums_shapes(channels, hidden, 3)
    outs = [
        jax.ShapeDtypeStruct(tokens.shape, F32),
        jax.ShapeDtypeStruct((WIN, rows_y, rows_z, channels), F32),
        *shapes,
    ]

    def slab(unit):
        def place(i, c):
            return ((i if unit == 0 else (i + groups - 1) % groups), unit, 0, 0, 0)

        return pl.BlockSpec((1, 1, 3, packed, LANES_A), place)

    def row(array):
        zeros = (0,) * (array.ndim - 1)
        return pl.BlockSpec((1, *array.shape[1:]), lambda i, c: (i, *zeros))

    def for_core(core, planes_here):
        def place(i, c):
            return (0, i * (c[0] if core == 1 else 1 - c[0]), 0, 0)

        return pl.BlockSpec((planes_here, WIN, rows_z, channels), place)

    any_spec = pl.BlockSpec(memory_space=pl.ANY)
    olds = [] if first else [*old[1], old[0]]
    args = [core, *consts, *ys, own, own, halo, halo, *saved, *returned, *olds]
    return pl.pallas_call(
        functools.partial(encoder_backward, first, batch, len(returned)),
        grid_spec=pltpu.PrefetchScalarGridSpec(
            num_scalar_prefetch=1,
            grid=(groups,),
            in_specs=[
                *[whole(a) for a in consts],
                *[for_core(1, n) for n in (2, 2, 4)],
                slab(0),
                slab(1),
                slab(0),
                slab(1),
                *[row(a) for a in saved],
                *[for_core(0, WIN)] * len(returned),
                *[whole(a) for a in olds[:-1]],
                *[any_spec] * (0 if first else 1),
            ],
            out_specs=[any_spec, any_spec, *[whole(a) for a in shapes]],
            scratch_shapes=[
                pltpu.VMEM((4 * size, 768), BF16),
                pltpu.VMEM((3, 4 * size, channels), BF16),
                pltpu.VMEM((2, WIN, WIN, rows_z, channels), F32),
                pltpu.SemaphoreType.DMA((2,)),
                pltpu.SemaphoreType.DMA((8 + batches,)),
            ],
        ),
        out_shape=outs,
        input_output_aliases={} if first else {len(args) - 1: 0},
        compiler_params=params,
        cost_estimate=cost(groups * 4 * size, 933888, groups * 4 * size * 9000),
        name="encoder_backward",
    )(*args)


def run_decoder(core, keep, recv, cotangent, cot_recv, batch, old, consts):
    groups, _, _, packed, _ = keep.shape
    rows_z, channels = cotangent.shape[3:]
    size = 4 * rows_z
    hidden = consts[6].shape[1]
    windows = rows_z // WIN
    first = old is None
    shapes = sums_shapes(channels, hidden, 1)
    slab_shape = jax.ShapeDtypeStruct((groups, 2, 3, packed, LANES_A), BF16)
    outs = [
        *[jax.ShapeDtypeStruct((n, groups * WIN, rows_z, channels), F32) for n in (4, 2)],
        slab_shape,
        slab_shape,
        *shapes,
    ]

    def slab(unit):
        def place(i, c):
            return ((i if unit == 1 else (i + 1) % groups), unit, 0, 0, 0)

        return pl.BlockSpec((1, 1, 3, packed, LANES_A), place)

    def cot(unit, own):
        def place(i, c):
            y = 2 * i + 1 if unit == 1 else (2 * i + 2) % (2 * groups)
            return (batch, 2 * c[0] + 1 if own else 0, y, 0, 0)

        return pl.BlockSpec((1, 2, 2, rows_z, channels), place)

    def bias_place(i, c):
        return (i // (groups - 1), 0, 0, 0)

    specs = [whole(a) for a in consts]
    specs[4] = pl.BlockSpec((1, *consts[4].shape[1:]), bias_place)
    olds = [] if first else list(old)
    out_slab = pl.BlockSpec((1, 2, 3, packed, LANES_A), lambda i, c: (i, 0, 0, 0, 0))
    return pl.pallas_call(
        functools.partial(decoder, first),
        grid_spec=pltpu.PrefetchScalarGridSpec(
            num_scalar_prefetch=1,
            grid=(groups,),
            in_specs=[
                *specs,
                slab(1),
                slab(0),
                slab(1),
                slab(0),
                cot(1, True),
                cot(0, True),
                cot(1, False),
                cot(0, False),
                *[whole(a) for a in olds],
            ],
            out_specs=[
                *[pl.BlockSpec((n, WIN, rows_z, channels), lambda i, c: (0, i, 0, 0)) for n in (4, 2)],
                out_slab,
                out_slab,
                *[whole(a) for a in shapes],
            ],
            scratch_shapes=[
                pltpu.VMEM((windows, CELLS, HEADS * CELLS), F32),
                pltpu.VMEM((4 * size, channels), BF16),
                pltpu.VMEM((4 * size, hidden), BF16),
                pltpu.VMEM((4 * size, hidden), F32),
                pltpu.VMEM((3, 4 * size, channels), F32),
            ],
        ),
        out_shape=outs,
        compiler_params=params,
        cost_estimate=cost(groups * 4 * size, 1253376, groups * 4 * size * 4000),
        name="decoder",
    )(core, *consts, keep, keep, recv, recv, cotangent, cotangent, cot_recv, cot_recv, *olds)


def body(
    tokens,
    cotangent,
    ln1_gain,
    ln1_bias,
    q_weight,
    q_bias,
    kv_weight,
    v_bias,
    out_weight,
    out_bias,
    rel_table,
    ln2_gain,
    ln2_bias,
    up_weight,
    up_bias,
    down_weight,
    down_bias,
):
    batches, planes, rows_y, rows_z, channels = tokens.shape
    axes = ("section", "tok")
    core = lax.axis_index("section")
    block = lax.axis_index("tok")
    blocks = lax.axis_size("tok")
    is_encoder = core == 0
    core_arg = core.astype(jnp.int32).reshape(1)

    def device(position):
        position = position % (2 * blocks)
        return (position % 2) * blocks + position // 2

    to_previous = [(device(r), device(r - 1)) for r in range(2 * blocks)]
    to_next = [(device(r), device(r + 1)) for r in range(2 * blocks)]

    (
        vec_e, vec_d, w_qkv, b_qkv, w_q_d, b_q_d, w_out_e, w_out_d, w_up_e, w_up_d, b_up_e, b_up_d,
        w_down_e, w_down_d, bias_e, bias_d,
    ) = run_prepare(
        blocks,
        (q_weight[0], out_weight[0], up_weight[0], down_weight[0].T),
        (ln1_gain, ln1_bias, ln2_gain, ln2_bias, out_bias, down_bias, q_bias, up_bias),
        rel_table[0],
        kv_weight,
        v_bias[None],
    )
    order = jnp.asarray(order_matrix(rows_z, 0), BF16)
    order_rolled = jnp.asarray(order_matrix(rows_z, 1), BF16)

    enc_consts = (order, vec_e, w_qkv, b_qkv, bias_e, w_out_e, w_up_e, b_up_e, w_down_e)
    enc_back_consts = (order, vec_e, w_qkv, b_qkv, w_out_e, w_up_e, w_down_e)
    dec_consts = (order_rolled, vec_d, w_q_d, b_q_d, bias_d, w_out_d, w_up_d, b_up_d, w_down_d)

    handed, saved = [], []
    for batch in range(batches):
        send, keep, *rest = run_encoder(
            core_arg, tokens, batch, enc_consts, cotangent if batch == 0 else None
        )
        if batch == 0:
            *rest, half = rest
            cot_recv = lax.ppermute(half, axes, to_previous)
        handed.append((keep, lax.ppermute(send, axes, to_previous)))
        saved.append(rest)
    dec_sums = None
    returned, ys = [], []
    to_decoder = [(t, blocks + t) for t in range(blocks)]
    to_encoder = [(blocks + t, t) for t in range(blocks)]
    to_after = [(blocks + t, blocks + (t + 1) % blocks) for t in range(blocks)]
    for batch in range(batches):
        out_all, out_tail, own, halo, *dec_sums = run_decoder(
            core_arg, *handed[batch], cotangent, cot_recv, batch, dec_sums, dec_consts
        )
        returned.append((own, lax.ppermute(halo, axes, to_next)))
        y_halo = lax.ppermute(out_tail, axes, to_after)
        ys.append((out_all, y_halo, lax.ppermute(out_all, axes, to_decoder)))
    old = None
    backs = []
    for batch in range(batches):
        arrived = backs[:1] if batch == batches - 1 else []
        ends, back, *enc_sums = run_encoder_back(
            core_arg, batch, *returned[batch], ys[batch], arrived, saved[batch], old,
            enc_back_consts, tokens,
        )
        old = (ends, enc_sums)
        backs.append(lax.ppermute(back, axes, to_encoder))

    layout = Layout(channels, up_weight.shape[2], blocks)
    total, sib_kv = run_sum(enc_sums, dec_sums, layout, blocks)
    (
        ends, g_ln1_gain, g_ln1_bias, g_q_weight, g_q_bias, g_kv_weight, g_v_bias, g_out_weight,
        g_out_bias, g_table, g_ln2_gain, g_ln2_bias, g_up_weight, g_up_bias, g_down_weight, g_down_bias,
    ) = run_finish(core_arg, total, sib_kv, backs[1:], ends, layout)
    return (
        ends[None],
        g_ln1_gain,
        g_ln1_bias,
        g_q_weight[None],
        g_q_bias,
        g_kv_weight[None],
        g_v_bias,
        g_out_weight[None],
        g_out_bias,
        g_table.transpose(1, 0, 2),
        g_ln2_gain,
        g_ln2_bias,
        g_up_weight[None],
        g_up_bias,
        g_down_weight.T[None],
        g_down_bias,
    )


def solution(mesh):
    in_specs = (
        P(None, "tok", None, None, None),
        P(None, "tok", None, None, None),
        P("section", None),
        P("section", None),
        P("section", None, None),
        P("section", None),
        P(),
        P(),
        P("section", None, None),
        P("section", None),
        P("section", None, None),
        P("section", None),
        P("section", None),
        P("section", None, None),
        P("section", None),
        P("section", None, None),
        P("section", None),
    )
    out_specs = (
        P("section", None, "tok", None, None, None),
        P("section", None),
        P("section", None),
        P("section", None, None),
        P("section", None),
        P("section", None, None),
        P("section", None),
        P("section", None, None),
        P("section", None),
        P("section", None, None),
        P("section", None),
        P("section", None),
        P("section", None, None),
        P("section", None),
        P("section", None, None),
        P("section", None),
    )
    return jax.shard_map(body, mesh=mesh, in_specs=in_specs, out_specs=out_specs, check_vma=False)
```

```python
import functools

import jax
import jax.numpy as jnp
import numpy as np
from jax import lax
from jax.experimental import pallas as pl
from jax.experimental.pallas import tpu as pltpu
from jax.sharding import PartitionSpec as P

HEADS = 6
HD = 32
WIN = 4
SHIFT = 2
CELLS = WIN**3
SPAN = 2 * WIN - 1
HEADS_A = 4
LANES_A = HEADS_A * HD
COLS_A = HEADS_A * CELLS

eps_norm = 1e-05
mask_fill = -100.0
log2_e = 1.4426950408889634
root_half = 0.7071067811865476
inv_root_two_pi = 0.3989422804014327
scale = HD ** (-0.5)
VMEM_BYTES = 63 * 1024 * 1024

F32 = jnp.float32
BF16 = jnp.bfloat16


def nn(left, right):
    return lax.dot_general(left, right, (((1,), (0,)), ((), ())), preferred_element_type=F32)


def nt(left, right):
    return lax.dot_general(left, right, (((1,), (1,)), ((), ())), preferred_element_type=F32)


def tn(left, right):
    return lax.dot_general(left, right, (((0,), (0,)), ((), ())), preferred_element_type=F32)


def order_matrix(rows_z, rolled):
    count = 4 * rows_z
    matrix = np.zeros((count, count), np.float32)
    units = rows_z // 2
    for unit in range(units):
        for dx in range(2):
            for dy in range(2):
                for dz in range(2):
                    z = (2 * (unit + rolled) + dz) % rows_z
                    matrix[unit * 8 + dx * 4 + dy * 2 + dz, (dx * 2 + dy) * rows_z + z] = 1.0
    return matrix


def windows_of(pieces):
    count, rows, channels = pieces.shape
    return pieces.reshape(count, rows // 16, 16, channels).transpose(1, 0, 2, 3).reshape(-1, channels)


def pieces_of(windows):
    rows, channels = windows.shape
    return (
        windows.reshape(rows // CELLS, 4, 16, channels)
        .transpose(1, 0, 2, 3)
        .reshape(4, rows // 4, channels)
    )


def roll_rows(pieces, steps):
    return jnp.concatenate([pieces[:, steps:], pieces[:, :steps]], 1)


def pack_slab(pieces):
    half = pieces.shape[1] // 2
    rest = pieces[:, :, LANES_A:]
    return jnp.concatenate(
        [pieces[:, :, :LANES_A], jnp.concatenate([rest[:, :half], rest[:, half:]], 2)], 1
    ).astype(BF16)


def unpack_slab(block):
    size = block.shape[0] * 2 // 3
    half = LANES_A // 2
    rest = jnp.concatenate([block[size:, :half], block[size:, half:]], 0)
    return jnp.concatenate([block[:size], rest], 1)


def normalize(rows):
    mean = jnp.mean(rows, -1, keepdims=True)
    centered = rows - mean
    inv_std = lax.rsqrt(jnp.mean(centered * centered, -1, keepdims=True) + eps_norm)
    return centered * inv_std, inv_std


def norm_back(grad_rows, unit_rows, inv_std, gain):
    scaled = grad_rows * gain
    return inv_std * (
        scaled
        - jnp.mean(scaled, -1, keepdims=True)
        - unit_rows * jnp.mean(scaled * unit_rows, -1, keepdims=True)
    )


def gelu_pair(rows):
    upper = 0.5 * lax.erf(rows * root_half) + 0.5
    bell = jnp.exp2(rows * rows * (-0.5 * log2_e))
    return rows * upper, upper + rows * bell * inv_root_two_pi


def head_masks(width):
    heads = lax.broadcasted_iota(jnp.int32, (1, width), 1) // HD
    return [jnp.where(heads == h, 1.0, 0.0).astype(BF16) for h in range(width // HD)]


def expand(rows):
    masks = head_masks(rows.shape[1])
    return jnp.concatenate([rows * mask for mask in masks], 0)


def collapse(stacked):
    width = stacked.shape[1]
    lanes = lax.broadcasted_iota(jnp.int32, (CELLS, width), 1)
    total = stacked[:CELLS]
    for h in range(1, width // HD):
        total = jnp.where(lanes >= h * HD, stacked[h * CELLS : (h + 1) * CELLS], total)
    return total


def split(rows):
    return rows[:, :LANES_A], rows[:, LANES_A:]


def attend(parts, bias):
    queries, keys, values = zip(*[[split(rows) for rows in part] for part in parts])
    wide = [[expand(half) for half in q] for q in queries]
    scores = [
        jnp.concatenate([nt(k[0], q[0]), nt(k[1], q[1])], 1) for k, q in zip(keys, wide)
    ]
    scores = [s * (scale * log2_e) + b for s, b in zip(scores, bias)]
    exponents = [jnp.exp2(s - jnp.max(s, 0, keepdims=True)) for s in scores]
    probs = [e * (1.0 / jnp.sum(e, 0, keepdims=True)) for e in exponents]
    low = [p.astype(BF16) for p in probs]
    mixed = [
        (tn(p[:, :COLS_A], v[0]), tn(p[:, COLS_A:], v[1])) for p, v in zip(low, values)
    ]
    mixed = [jnp.concatenate([collapse(m[0]), collapse(m[1])], 1).astype(BF16) for m in mixed]
    return mixed, probs


def attend_back(parts):
    queries, keys, values, grads = zip(
        *[[split(rows) for rows in part[:3] + part[4:]] for part in parts]
    )
    probs = [part[3] for part in parts]
    wide_g = [[expand(half) for half in g] for g in grads]
    d_probs = [
        jnp.concatenate([nt(v[0], g[0]), nt(v[1], g[1])], 1) for v, g in zip(values, wide_g)
    ]
    low = [part[3].astype(BF16) for part in parts]
    d_values = [
        jnp.concatenate([nn(p[:, :COLS_A], g[0]), nn(p[:, COLS_A:], g[1])], 1)
        for p, g in zip(low, wide_g)
    ]
    wide_q = [[expand(half) for half in q] for q in queries]
    d_scores = [
        p * (d - jnp.sum(d * p, 0, keepdims=True)) for p, d in zip(probs, d_probs)
    ]
    low_d = [d.astype(BF16) for d in d_scores]
    d_keys = [
        jnp.concatenate([nn(d[:, :COLS_A], q[0]), nn(d[:, COLS_A:], q[1])], 1) * scale
        for d, q in zip(low_d, wide_q)
    ]
    d_queries = [
        (tn(d[:, :COLS_A], k[0]), tn(d[:, COLS_A:], k[1])) for d, k in zip(low_d, keys)
    ]
    d_queries = [
        jnp.concatenate([collapse(d[0]), collapse(d[1])], 1) * scale for d in d_queries
    ]
    table = d_scores[0]
    for d in d_scores[1:]:
        table = table + d
    return d_queries, d_keys, d_values, table


def window_groups(count):
    return [range(k, min(k + TOGETHER, count)) for k in range(0, count, TOGETHER)]


def window_rows(k):
    return slice(k * CELLS, (k + 1) * CELLS)


def with_ones(rows):
    return jnp.concatenate([rows.T, jnp.ones((16, rows.shape[0]), BF16)], 0)


def col_sum(rows):
    return jnp.sum(rows, 0, keepdims=True)


def start_sums(old, new):
    @pl.when(pl.program_id(0) == 0)
    def _():
        new[...] = jnp.zeros_like(new) if old is None else old[...]


def restore(matrix, rows):
    high = rows.astype(BF16)
    low = (rows - high.astype(F32)).astype(BF16)
    return tn(matrix, high) + tn(matrix, low)


CHUNK = 256
BLOCK = 256
TOGETHER = 8


class View:
    def __init__(self, ref, row, rows, col, cols):
        self.ref, self.row, self.col, self.shape = ref, row, col, (rows, cols)

    def place(self, key):
        key = (slice(None), slice(None)) if key is Ellipsis else key
        key = key if isinstance(key, tuple) else (key, slice(None))
        return tuple(
            slice(start + part.indices(size)[0], start + part.indices(size)[1])
            for part, start, size in zip(key, (self.row, self.col), self.shape)
        )

    def __getitem__(self, key):
        return self.ref[self.place(key)]

    def __setitem__(self, key, value):
        self.ref[self.place(key)] = value

    def first_columns(self, cols):
        return View(self.ref, self.row, self.shape[0], self.col, cols)


def layer_views(weights, vectors):
    hidden = weights.shape[1]
    channels = weights.shape[0] // 4
    q_cols = 768

    def rows(k, cols):
        return View(weights, k * channels, channels, 0, cols)

    return (
        View(vectors, 0, 8, 0, channels),
        View(vectors, 8, 1, 0, hidden),
        View(vectors, 9, 1, 0, q_cols),
        rows(0, hidden),
        rows(1, hidden),
        rows(2, q_cols),
        rows(3, channels),
    )


def sum_rows(channels, encoder):
    tall = channels + 16
    return 2 * tall + channels + (tall if encoder else 0)


def sum_views(sums, channels, encoder):
    tall = channels + 16
    base = tall + channels

    def view(row, rows, col, cols):
        return View(sums, row, rows, col, cols)

    fields = [view(base, tall, 256 * k, channels) for k in range(3 if encoder else 2)]
    last = base + (tall if encoder else 0)
    side = 256 if encoder else 512
    out = view(last, tall, 0, channels) if encoder else fields[1]
    bias = (view(last, CELLS, side, COLS_A), view(last + CELLS, CELLS, side, 2 * CELLS))
    vec = view(last + 2 * CELLS, 8, side, channels)
    return (
        view(0, tall, 0, sums.shape[1]),
        view(tall, channels, 0, sums.shape[1]),
        fields[:3] if encoder else fields[:1],
        out,
        vec,
        bias,
    )


def add_bias(views, table):
    views[0][...] += table[:, :COLS_A]
    views[1][...] += table[:, COLS_A:]


def encoder_forward(cuts, core_ref, tok, order, weights, vectors, bias, *rest):
    vec, b_up, b_qkv, w_up, w_down, w_qkv, w_out = layer_views(weights, vectors)
    cut_in, rest = rest[:cuts], rest[cuts:]
    send, keep, wide_out, low_out, *cut_out, qkv = rest
    hidden_cols = w_up.shape[1]
    s_start, p_start, o_start = hidden_cols, 2 * hidden_cols, 2 * hidden_cols + HEADS * CELLS
    for source, target in zip(cut_in, cut_out):
        target[...] = source[...]
    rows_z = tok.shape[3]
    size = 4 * rows_z
    pieces = []
    for x in range(2):
        for y in range(2):
            part = tok[0, 2 * x : 2 * x + 2, 2 * y : 2 * y + 2].reshape(size, -1)
            pieces.append(nn(order[...], part))
    entry = windows_of(jnp.stack(pieces))
    unit, inv_std = normalize(entry)
    channels = entry.shape[1]
    wide = jnp.broadcast_to(inv_std, (entry.shape[0], 256 - channels))
    wide_out[0, :, :channels] = unit
    wide_out[0, :, channels:256] = wide
    left = (unit * vec[0:1] + vec[1:2]).astype(BF16)
    triple = nn(left, w_qkv[...]) + b_qkv[...]
    qkv[...] = triple.astype(BF16)
    for together in window_groups(entry.shape[0] // CELLS):
        parts = [
            [qkv[window_rows(k), 256 * f : 256 * f + 192] for f in range(3)] for k in together
        ]
        mixed, probs = attend(parts, [bias[...]] * len(parts))
        for k, o, p in zip(together, mixed, probs):
            low_out[0, window_rows(k), p_start:o_start] = p.astype(BF16)
            low_out[0, window_rows(k), o_start : o_start + channels] = o
    mixed = low_out[0, :, o_start : o_start + channels]
    middle = entry + nn(mixed, w_out[...]) + vec[4:5]
    unit, inv_std = normalize(middle)
    wide = jnp.broadcast_to(inv_std, (entry.shape[0], 256 - channels))
    wide_out[0, :, 256 : 256 + channels] = unit
    wide_out[0, :, 256 + channels :] = wide
    left = (unit * vec[2:3] + vec[3:4]).astype(BF16)
    results = []
    for k in range(entry.shape[0] // CHUNK):
        rows = slice(k * CHUNK, (k + 1) * CHUNK)
        hidden, slope = gelu_pair(nn(left[rows], w_up[...]) + b_up[...])
        hidden = hidden.astype(BF16)
        low_out[0, rows, :s_start] = hidden
        low_out[0, rows, s_start:p_start] = slope.astype(BF16)
        results.append(nt(hidden, w_down[...]))
    result = middle + jnp.concatenate(results, 0) + vec[5:6]
    for field, rows in enumerate((result, triple[:, 256:448], triple[:, 512:704])):
        rolled = pack_slab(roll_rows(pieces_of(rows), 8))
        send[0, :, field] = rolled[:2]
        keep[0, :, field] = rolled[2:]


def run_together(*works):
    works = list(works)
    while works:
        for work in list(works):
            try:
                next(work)
            except StopIteration:
                works.remove(work)


def row_blocks(count, size):
    return [slice(k, k + size) for k in range(0, count, size)]


def norm_back_steps(rows_grad, base, unit, inv_std, gain, g_vec, row, results):
    sums = [None, None]
    for rows in row_blocks(base.shape[0], BLOCK):
        grad = rows_grad(rows)
        found = (col_sum(grad * unit[rows]), col_sum(grad))
        sums = [f if total is None else total + f for f, total in zip(found, sums)]
        results.append(base[rows] + norm_back(grad, unit[rows], inv_std[rows], gain))
        yield
    g_vec[row : row + 1] += sums[0]
    g_vec[row + 1 : row + 2] += sums[1]


def product_steps(products):
    for target, cols, left, right in products:
        target[:, cols] += nn(left, right)
        yield


def mlp_back(grad, grad_low, hidden, slope, left_two, unit, inv_std, w_up, w_down, vec, sums):
    g_up, g_down, g_vec = sums
    backs, pres = [], []
    for rows in row_blocks(grad.shape[0], CHUNK):
        d_pre = (nn(grad_low[rows], w_down[...]) * slope(rows)).astype(BF16)
        pres.append(d_pre)
        backs.append(nt(d_pre, w_up[...]))
    d_pre = jnp.concatenate(pres, 0)
    d_normed = jnp.concatenate(backs, 0)
    ones, turned = with_ones(left_two), grad_low.T
    tiles = row_blocks(w_up.shape[1], 256)
    products = [(g_up, cols, ones, d_pre[:, cols]) for cols in tiles]
    products += [(g_down, cols, turned, hidden[:, cols]) for cols in tiles]
    results = []
    run_together(
        norm_back_steps(
            lambda rows: d_normed[rows], grad, unit, inv_std, vec[2:3], g_vec, 2, results
        ),
        product_steps(products),
    )
    g_vec[4:5] += col_sum(grad)
    return jnp.concatenate(results, 0)


def start_all(copies):
    for copy in copies:
        copy.start()


def wait_all(copies):
    for copy in copies:
        copy.wait()


def encoder_backward(
    first, batch, returns, core_ref, order, weights, vectors,
    y_own, y_halo, y_sib,
    keep_a, keep_b, recv_a, recv_b,
    wide_in, low_in, *rest,
):
    vec, _, b_qkv, w_up, w_down, w_qkv, w_out = layer_views(weights, vectors)
    channels, hidden_cols = w_up.shape
    s_start, p_start, o_start = hidden_cols, 2 * hidden_cols, 2 * hidden_cols + HEADS * CELLS
    returned, rest = rest[:returns], rest[returns:]
    old, rest = (None, rest) if first else (rest[0], rest[2:])
    ends, back, sums, qkv, dqkv, buffer, out_sem, copy_sem = rest
    g_up, g_down, g_fields, g_out, g_vec, g_bias = sum_views(sums, channels, True)
    step, steps = pl.program_id(0), pl.num_programs(0)
    is_encoder = core_ref[0] == 0
    rows_y = ends.shape[2]
    slot = lax.rem(step, 2)

    def output_copies():
        copies = []
        for start, planes, ref in ((0, 2, y_halo), (2, 4, y_sib), (6, 2, y_own)):
            for half in range(2):
                rows = pl.ds(lax.rem(step * WIN + SHIFT + 2 * half, rows_y), 2)
                target = ends.at[batch, pl.ds(start, planes), rows]
                copies.append((ref.at[:, pl.ds(2 * half, 2)], target))
        return [
            pltpu.make_async_copy(source, target, copy_sem.at[k])
            for k, (source, target) in enumerate(copies)
        ]

    def gradient_copies():
        return [
            pltpu.make_async_copy(
                ref, ends.at[k, pl.ds(WIN, WIN), pl.ds(step * WIN, WIN)], copy_sem.at[8 + k]
            )
            for k, ref in enumerate(returned)
        ]

    def result_copy(index, to_ends):
        target = (
            ends.at[batch, pl.ds(0, WIN), pl.ds(index * WIN, WIN)]
            if to_ends
            else back.at[:, pl.ds(index * WIN, WIN)]
        )
        at = lax.rem(index, 2)
        return pltpu.make_async_copy(buffer.at[at], target, out_sem.at[at])

    def for_core(encoder_work, decoder_work):
        pl.when(is_encoder)(encoder_work)
        pl.when(jnp.logical_not(is_encoder))(decoder_work)

    for_core(lambda: start_all(gradient_copies()), lambda: start_all(output_copies()))

    @pl.when(step >= 2)
    def _():
        for_core(
            lambda: result_copy(step - 2, True).wait(), lambda: result_copy(step - 2, False).wait()
        )

    start_sums(old, sums)
    fields = []
    for field in range(3):
        pieces = jnp.stack(
            [unpack_slab(ref[0, 0, field]) for ref in (recv_b, recv_a, keep_b, keep_a)]
        )
        fields.append(windows_of(pieces))
    grad_low, d_key_1, d_value_1 = fields
    grad = grad_low.astype(F32)
    unit_1, unit_2 = wide_in[0, :, :channels], wide_in[0, :, 256 : 256 + channels]
    wide_1, wide_2 = [wide_in[0, :, k + channels : k + channels + 1] for k in (0, 256)]
    left_1 = (unit_1 * vec[0:1] + vec[1:2]).astype(BF16)
    left_2 = (unit_2 * vec[2:3] + vec[3:4]).astype(BF16)
    qkv[...] = (nn(left_1, w_qkv[...]) + b_qkv[...]).astype(BF16)
    d_middle = mlp_back(
        grad, grad_low, low_in[0, :, :s_start], lambda rows: low_in[0, rows, s_start:p_start].astype(F32),
        left_2, unit_2, wide_2, w_up, w_down, vec,
        (g_up, g_down, g_vec),
    )
    branch = d_middle.astype(BF16)
    d_mixed = nt(branch, w_out[...]).astype(BF16)
    d_table = None
    for together in window_groups(grad.shape[0] // CELLS):
        parts = [
            [qkv[window_rows(k), 256 * f : 256 * f + 192] for f in range(3)]
            + [low_in[0, window_rows(k), p_start:o_start].astype(F32), d_mixed[window_rows(k)]]
            for k in together
        ]
        *d_qkv, d_s = attend_back(parts)
        for k, d_q, d_k, d_v in zip(together, *d_qkv):
            rows = window_rows(k)
            dqkv[0, rows] = d_q.astype(BF16)
            dqkv[1, rows] = (d_k + d_key_1[rows].astype(F32)).astype(BF16)
            dqkv[2, rows] = (d_v + d_value_1[rows].astype(F32)).astype(BF16)
        d_table = d_s if d_table is None else d_table + d_s
    add_bias(g_bias, d_table)
    ones = with_ones(left_1)
    every = slice(None)
    mixed = with_ones(low_in[0, :, o_start : o_start + channels])
    products = [(g_field, every, ones, dqkv[k]) for k, g_field in enumerate(g_fields)]
    products.append((g_out, every, mixed, branch))

    def rows_grad(rows):
        parts = [
            nt(dqkv[k, rows], w_qkv[:, 256 * k : 256 * k + channels]) for k in range(3)
        ]
        return parts[0] + parts[1] + parts[2]

    results = []
    run_together(
        norm_back_steps(rows_grad, d_middle, unit_1, wide_1, vec[0:1], g_vec, 0, results),
        product_steps(products),
    )
    result = pieces_of(jnp.concatenate(results, 0))
    rows_z = ends.shape[3]
    for x in range(2):
        for y in range(2):
            part = restore(order[...], result[2 * x + y])
            buffer[slot, 2 * x : 2 * x + 2, 2 * y : 2 * y + 2] = part.reshape(2, 2, rows_z, -1)
    for_core(lambda: result_copy(step, True).start(), lambda: result_copy(step, False).start())

    @pl.when(step == steps - 1)
    def _():
        def finish(to_ends):
            result_copy(step - 1, to_ends).wait()
            result_copy(step, to_ends).wait()

        for_core(lambda: finish(True), lambda: finish(False))

    for_core(lambda: wait_all(gradient_copies()), lambda: wait_all(output_copies()))


def decoder(
    first, core_ref, order, weights, vectors, bias,
    keep_1, keep_0, recv_1, recv_0, cot_1, cot_0, cot_r1, cot_r0, *rest,
):
    vec, b_up, b_qkv, w_up, w_down, w_qkv, w_out = layer_views(weights, vectors)
    channels = w_up.shape[0]
    w_q, b_q = w_qkv.first_columns(channels), b_qkv.first_columns(channels)
    old, new = (None, rest) if first else (rest[0], rest[1:])
    out_all, out_tail, own, halo, sums, p_scr, o_scr, a_scr, s_scr, dqkv = new
    g_up, g_down, (g_q,), g_out, g_vec, g_bias = sum_views(sums, channels, False)
    start_sums(old, sums)
    fields = []
    for field in range(3):
        pieces = jnp.stack([unpack_slab(ref[0, 0, field]) for ref in (keep_1, keep_0, recv_1, recv_0)])
        fields.append(windows_of(pieces))
    entry_low, keys, values = fields
    entry = entry_low.astype(F32)
    unit_1, inv_1 = normalize(entry)
    left_1 = (unit_1 * vec[0:1] + vec[1:2]).astype(BF16)
    queries = (nn(left_1, w_q[...]) + b_q[...]).astype(BF16)
    windows = entry.shape[0] // CELLS
    for together in window_groups(windows):
        parts = [[rows[window_rows(k)] for rows in (queries, keys, values)] for k in together]
        mixed, probs = attend(parts, [bias[0, 1 if k == windows - 1 else 0] for k in together])
        for k, o, p in zip(together, mixed, probs):
            p_scr[k] = p
            o_scr[window_rows(k)] = o
    middle = entry + nn(o_scr[...], w_out[...]) + vec[4:5]
    unit_2, inv_2 = normalize(middle)
    left_2 = (unit_2 * vec[2:3] + vec[3:4]).astype(BF16)
    results = []
    for k in range(entry.shape[0] // CHUNK):
        rows = slice(k * CHUNK, (k + 1) * CHUNK)
        hidden, slope = gelu_pair(nn(left_2[rows], w_up[...]) + b_up[...])
        hidden = hidden.astype(BF16)
        a_scr[rows] = hidden
        s_scr[rows] = slope
        results.append(nt(hidden, w_down[...]))
    result = pieces_of(middle + jnp.concatenate(results, 0) + vec[5:6])
    rows_z = out_all.shape[2]
    size = 4 * rows_z
    for x in range(2):
        for y in range(2):
            part = restore(order[...], result[2 * x + y]).reshape(2, 2, rows_z, -1)
            out_all[2 * x : 2 * x + 2, 2 * y : 2 * y + 2] = part
            if x == 1:
                out_tail[:, 2 * y : 2 * y + 2] = part

    cots = [
        nn(order[...], ref[0].reshape(size, -1)).astype(BF16) for ref in (cot_1, cot_0, cot_r1, cot_r0)
    ]
    grad_low = windows_of(jnp.stack(cots))
    grad = grad_low.astype(F32)
    d_middle = mlp_back(
        grad, grad_low, a_scr[...], lambda rows: s_scr[rows], left_2, unit_2, inv_2, w_up, w_down, vec,
        (g_up, g_down, g_vec),
    )
    branch = d_middle.astype(BF16)
    d_mixed = nt(branch, w_out[...]).astype(BF16)
    d_table = None
    for together in window_groups(windows):
        parts = [
            [rows[window_rows(k)] for rows in (queries, keys, values)]
            + [p_scr[k], d_mixed[window_rows(k)]]
            for k in together
        ]
        *d_qkv, d_s = attend_back(parts)
        for k, *grads in zip(together, *d_qkv):
            for f in range(3):
                dqkv[f, window_rows(k)] = grads[f]
        d_table = d_s if d_table is None else d_table + d_s
    add_bias(g_bias, d_table)
    d_queries = dqkv[0].astype(BF16)
    every = slice(None)
    products = [
        (g_q, every, with_ones(left_1), d_queries),
        (g_out, every, with_ones(o_scr[...]), branch),
    ]
    results = []
    run_together(
        norm_back_steps(
            lambda rows: nt(d_queries[rows], w_q[...]), d_middle, unit_1, inv_1, vec[0:1], g_vec, 0,
            results,
        ),
        product_steps(products),
    )
    d_entry = jnp.concatenate(results, 0)
    for field, rows in enumerate((d_entry, dqkv[1], dqkv[2])):
        turned = pack_slab(roll_rows(pieces_of(rows), size - 8))
        own[0, :, field] = turned[:2]
        halo[0, :, field] = turned[2:]


def whole(array):
    zeros = (0,) * array.ndim
    return pl.BlockSpec(array.shape, lambda *_: zeros)


def cost(cells, per_cell, hbm):
    return pl.CostEstimate(
        flops=2 * cells * per_cell, bytes_accessed=hbm, transcendentals=cells * 1536
    )


params = pltpu.CompilerParams(
    dimension_semantics=("arbitrary",), vmem_limit_bytes=VMEM_BYTES
)


class Layout:
    def __init__(self, channels, hidden, blocks):
        tall = channels + 16
        self.tall, self.channels = tall, channels
        self.tiles = hidden // LANES_A
        self.up = 0
        self.down = self.tiles * tall
        self.q = self.down + self.tiles * channels
        self.out = self.q + tall
        self.rest = self.out + tall
        self.kv = self.rest + tall
        self.bias = self.kv + 2 * tall
        self.vec = self.bias + HEADS * CELLS // LANES_A * CELLS
        self.end = self.vec + 16
        self.chunk = -(-self.end // (16 * blocks)) * 16
        self.rows = self.chunk * blocks


def fill(buffer, layout, up, down, q, out, kv, bias, vec):
    kind, half = buffer.dtype, LANES_A // 2
    tall, channels = layout.tall, layout.channels
    for k in range(layout.tiles):
        cols = slice(k * LANES_A, (k + 1) * LANES_A)
        buffer[layout.up + k * tall : layout.up + (k + 1) * tall] = up[:, cols].astype(kind)
        buffer[layout.down + k * channels : layout.down + (k + 1) * channels] = down[
            :, cols
        ].astype(kind)
    buffer[layout.q : layout.q + tall] = q[:, :LANES_A].astype(kind)
    buffer[layout.out : layout.out + tall] = out[:, :LANES_A].astype(kind)
    rests = jnp.concatenate([q[:, LANES_A:], out[:, LANES_A:]], 1)
    buffer[layout.rest : layout.rest + tall] = rests.astype(kind)
    buffer[layout.kv : layout.kv + tall] = kv[:, :LANES_A].astype(kind)
    rests = jnp.concatenate([kv[:, LANES_A:], jnp.zeros((tall, half), F32)], 1)
    buffer[layout.kv + tall : layout.kv + 2 * tall] = rests.astype(kind)
    tiles = [bias[0][:, :LANES_A], bias[0][:, LANES_A:], bias[1][...]]
    for k, tile in enumerate(tiles):
        start = layout.bias + k * CELLS
        buffer[start : start + CELLS] = tile.astype(kind)
    rests = jnp.concatenate([vec[:, LANES_A:], jnp.zeros((8, half), F32)], 1)
    both = jnp.concatenate([vec[:, :LANES_A], rests], 0)
    buffer[layout.vec : layout.vec + 16] = both.astype(kind)
    if layout.rows > layout.end:
        buffer[layout.end :] = jnp.zeros((layout.rows - layout.end, LANES_A), kind)


MESH = pl.DeviceIdType.MESH


def groups_of(blocks):
    near = 4 if blocks % 4 == 0 else blocks
    return near, blocks // near


def sum_gradients(layout, blocks, *refs):
    enc, dec, *rest = refs
    (
        total_out, kv_out, own, theirs, from_sib, low, landed, near_low, far_landed, total, sib_kv,
        sib_send, sib_recv, send_sem, recv_sem,
    ) = rest
    core, me = lax.axis_index("section"), lax.axis_index("tok")
    sibling = {"section": 1 - core}

    near, far = groups_of(blocks)
    inner, outer = lax.rem(me, near), lax.div(me, near)
    quarter = far * layout.chunk

    def near_peer(offset):
        return lax.rem(inner + offset, near)

    def far_peer(offset):
        return lax.rem(outer + offset, far)

    def near_device(offset):
        return {"tok": outer * near + near_peer(offset)}

    def far_device(offset):
        return {"tok": far_peer(offset) * near + inner}

    barrier = pltpu.get_barrier_semaphore()
    pl.semaphore_signal(barrier, inc=1, device_id=sibling, device_id_type=MESH)
    for count, device in ((near, near_device), (far, far_device)):

        def greet(offset, carry, device=device):
            pl.semaphore_signal(barrier, inc=1, device_id=device(offset), device_id_type=MESH)
            return carry

        lax.fori_loop(1, count, greet, 0)

    channels = layout.channels
    e_up, e_down, (e_q, e_k, e_v), e_out, e_vec, e_bias = sum_views(enc, channels, True)
    d_up, d_down, (d_q,), d_out, d_vec, d_bias = sum_views(dec, channels, False)

    @pl.when(core == 0)
    def _():
        fill(theirs, layout, d_up, d_down, d_q, d_out, e_v, d_bias, d_vec)
        fill(own, layout, e_up, e_down, e_q, e_out, e_k, e_bias, e_vec)

    @pl.when(core == 1)
    def _():
        fill(theirs, layout, e_up, e_down, e_q, e_out, e_k, e_bias, e_vec)
        fill(own, layout, d_up, d_down, d_q, d_out, e_v, d_bias, d_vec)

    pl.semaphore_wait(barrier, near + far - 1)

    def to_sibling(source, target, k):
        return pltpu.make_async_remote_copy(
            src_ref=source, dst_ref=target, send_sem=sib_send.at[k], recv_sem=sib_recv.at[k],
            device_id=sibling, device_id_type=MESH,
        )

    first = to_sibling(theirs, from_sib, 0)
    first.start()
    first.wait()
    own[...] += from_sib[...].astype(F32)
    low[...] = own[...].astype(BF16)

    def quarter_of(position):
        return pl.ds(pl.multiple_of(position * quarter, 16), quarter)

    def chunk_of(position):
        return pl.ds(pl.multiple_of(position * layout.chunk, 16), layout.chunk)

    def rows_of(position):
        start = inner * quarter + position * layout.chunk
        return pl.ds(pl.multiple_of(start, 16), layout.chunk)

    def exchange(stage, offset, source, target, device):
        return pltpu.make_async_remote_copy(
            src_ref=source, dst_ref=target,
            send_sem=send_sem.at[stage, offset], recv_sem=recv_sem.at[stage, offset],
            device_id=device(offset), device_id_type=MESH,
        )

    def near_scatter(offset):
        source = low.at[quarter_of(near_peer(offset))]
        return exchange(0, offset, source, landed.at[offset], near_device)

    def far_scatter(offset):
        source = near_low.at[chunk_of(far_peer(offset))]
        return exchange(1, offset, source, far_landed.at[offset], far_device)

    def far_gather(offset, owner):
        rows = rows_of(owner)
        return exchange(2, offset, total.at[rows], total.at[rows], far_device)

    def near_gather(offset, owner):
        rows = quarter_of(owner)
        return exchange(3, offset, total.at[rows], total.at[rows], near_device)

    def each(count, work):
        def run(offset, carry):
            work(offset)
            return carry

        lax.fori_loop(1, count, run, 0)

    def reduced(count, copy, landing, start):
        def add(offset, carry):
            copy(offset).wait_recv()
            return carry + landing[offset].astype(F32)

        return lax.fori_loop(1, count, add, start)

    each(near, lambda offset: near_scatter(offset).start())
    near_sum = reduced(near, near_scatter, landed, own[quarter_of(inner)])
    own[quarter_of(inner)] = near_sum
    near_low[...] = near_sum.astype(BF16)
    each(far, lambda offset: far_scatter(offset).start())
    total[rows_of(outer)] = reduced(far, far_scatter, far_landed, own[rows_of(outer)]).astype(BF16)
    each(far, lambda offset: far_gather(offset, outer).start())
    each(far, lambda offset: far_gather(offset, lax.rem(outer + far - offset, far)).wait_recv())
    each(near, lambda offset: near_gather(offset, inner).start())
    each(near, lambda offset: near_gather(offset, lax.rem(inner + near - offset, near)).wait_recv())
    kv_rows = pl.ds(layout.kv, 2 * layout.tall)
    third = to_sibling(total.at[kv_rows], sib_kv, 1)
    third.start()
    total_out[...] = total[...]

    each(near, lambda offset: near_scatter(offset).wait_send())
    each(far, lambda offset: far_scatter(offset).wait_send())
    each(far, lambda offset: far_gather(offset, outer).wait_send())
    each(near, lambda offset: near_gather(offset, inner).wait_send())
    third.wait()
    kv_out[...] = sib_kv[...]


def run_sum(enc_sums, dec_sums, layout, blocks):
    rows, chunk, tall = layout.rows, layout.chunk, layout.tall
    near, far = groups_of(blocks)
    dma = pltpu.SemaphoreType.DMA
    vmem = pl.BlockSpec(memory_space=pltpu.VMEM)
    args = [enc_sums, dec_sums]
    return pl.pallas_call(
        functools.partial(sum_gradients, layout, blocks),
        in_specs=[vmem] * len(args),
        out_specs=[vmem] * 2,
        out_shape=[
            jax.ShapeDtypeStruct((rows, LANES_A), BF16),
            jax.ShapeDtypeStruct((2 * tall, LANES_A), BF16),
        ],
        scratch_shapes=[
            pltpu.VMEM((rows, LANES_A), F32),
            pltpu.VMEM((rows, LANES_A), BF16),
            pltpu.VMEM((rows, LANES_A), BF16),
            pltpu.VMEM((rows, LANES_A), BF16),
            pltpu.VMEM((near, far * chunk, LANES_A), BF16),
            pltpu.VMEM((far * chunk, LANES_A), BF16),
            pltpu.VMEM((far, chunk, LANES_A), BF16),
            pltpu.VMEM((rows, LANES_A), BF16),
            pltpu.VMEM((2 * tall, LANES_A), BF16),
            dma((2,)),
            dma((2,)),
            *[dma((4, max(near, far)))] * 2,
        ],
        compiler_params=pltpu.CompilerParams(
            collective_id=0, has_side_effects=True, vmem_limit_bytes=VMEM_BYTES
        ),
        name="sum_gradients",
    )(*args)


def finish(layout, batches, returns, core_ref, total, sib_kv, *refs):
    returned, refs = refs[:returns], refs[returns + 1 :]
    (
        ends, ln1_gain, ln1_bias, q_weight, q_bias, kv_weight, v_bias, out_weight, out_bias, table,
        ln2_gain, ln2_bias, up_weight, up_bias, down_weight, down_bias, placed, copy_sem,
    ) = refs
    is_encoder = core_ref[0] == 0
    step = pl.program_id(0)

    def copies():
        return [
            pltpu.make_async_copy(
                ref,
                ends.at[batches - returns + k, pl.ds(WIN, WIN), pl.ds(step * WIN, WIN)],
                copy_sem.at[k],
            )
            for k, ref in enumerate(returned)
        ]

    pl.when(is_encoder)(lambda: start_all(copies()))

    @pl.when(step == 0)
    def _():
        unpack(
            layout, is_encoder, total, sib_kv, ln1_gain, ln1_bias, q_weight, q_bias, kv_weight,
            v_bias, out_weight, out_bias, table, ln2_gain, ln2_bias, up_weight, up_bias, down_weight,
            down_bias, placed,
        )

    pl.when(is_encoder)(lambda: wait_all(copies()))


def unpack(
    layout, is_encoder, total, sib_kv, ln1_gain, ln1_bias, q_weight, q_bias, kv_weight,
    v_bias, out_weight, out_bias, table, ln2_gain, ln2_bias, up_weight, up_bias, down_weight, down_bias,
    placed,
):
    channels, tall, half = layout.channels, layout.tall, LANES_A // 2

    def at(start, rows):
        return total[start : start + rows].astype(F32)

    vec = at(layout.vec, 16)
    vec = jnp.concatenate([vec[:8], vec[8:, :half]], 1)
    for row, ref in enumerate((ln1_gain, ln1_bias, ln2_gain, ln2_bias, down_bias)):
        ref[...] = vec[row : row + 1]

    for k in range(layout.tiles):
        cols = slice(k * LANES_A, (k + 1) * LANES_A)
        tile = at(layout.up + k * tall, tall)
        up_weight[:, cols] = tile[:channels]
        up_bias[:, cols] = tile[channels : channels + 1]
        down_weight[:, cols] = at(layout.down + k * channels, channels)
    rest = at(layout.rest, tall)
    q = jnp.concatenate([at(layout.q, tall), rest[:, :half]], 1)
    out = jnp.concatenate([at(layout.out, tall), rest[:, half:]], 1)
    q_weight[...] = q[:channels]
    q_bias[...] = q[channels : channels + 1]
    out_weight[...] = out[:channels]
    out_bias[...] = out[channels : channels + 1]
    mine = at(layout.kv, 2 * tall)
    other = sib_kv[...].astype(F32)
    for start, side in ((0, jnp.where(is_encoder, mine, other)), (channels, jnp.where(is_encoder, other, mine))):
        side = jnp.concatenate([side[:tall], side[tall:, :half]], 1)
        kv_weight[:, start : start + channels] = side[:channels]
    v_bias[...] = side[channels : channels + 1]
    placed[...] = jnp.zeros_like(placed)
    positions = [position_matrix(False), position_matrix(True)]
    for h in range(HEADS):
        start = layout.bias + h // 2 * CELLS
        placed[h, :, :256] = nt(total[start : start + CELLS], positions[h % 2])
    entries = jnp.zeros((8, 384), F32)
    for j in range(CELLS):
        entries += pltpu.roll(placed[:, j, :], CENTRE - cell_position(j), 1)
    table[...] = entries[:HEADS, : SPAN**3][:, None]


def run_finish(core, total, sib_kv, returned, ends, layout):
    channels = layout.channels
    hidden = layout.tiles * LANES_A
    _, _, rows_y, rows_z, _ = ends.shape
    any_spec = pl.BlockSpec(memory_space=pl.ANY)
    shapes = [
        (1, channels), (1, channels), (channels, channels), (1, channels), (channels, 2 * channels),
        (1, channels), (channels, channels), (1, channels), (HEADS, 1, SPAN**3),
        (1, channels), (1, channels), (channels, hidden), (1, hidden), (channels, hidden), (1, channels),
    ]
    shapes = [jax.ShapeDtypeStruct(shape, F32) for shape in shapes]
    return pl.pallas_call(
        functools.partial(finish, layout, ends.shape[0], len(returned)),
        grid_spec=pltpu.PrefetchScalarGridSpec(
            num_scalar_prefetch=1,
            grid=(rows_y // WIN,),
            in_specs=[
                *[whole(a) for a in (total, sib_kv)],
                *[
                    pl.BlockSpec(
                        (WIN, WIN, rows_z, channels), lambda i, c: (0, i * (1 - c[0]), 0, 0)
                    )
                ]
                * len(returned),
                any_spec,
            ],
            out_specs=[any_spec, *[whole(a) for a in shapes]],
            scratch_shapes=[
                pltpu.VMEM((8, CELLS, 384), F32),
                pltpu.SemaphoreType.DMA((len(returned),)),
            ],
        ),
        out_shape=[jax.ShapeDtypeStruct(ends.shape, F32), *shapes],
        input_output_aliases={3 + len(returned): 0},
        compiler_params=params,
        name="finish",
    )(core, total, sib_kv, *returned, ends)


def cell_position(ids):
    x = 2 * (ids // 32) + ids // 4 % 2
    y = 2 * (ids // 16 % 2) + ids // 2 % 2
    z = 2 * (ids // 8 % 2) + ids % 2
    return (x * SPAN + y) * SPAN + z


CENTRE = (WIN - 1) * (SPAN * SPAN + SPAN + 1)
TABLE_ROW = 8


def position_matrix(odd):
    rows = lax.broadcasted_iota(jnp.int32, (256, 2 * CELLS), 0)
    ids = lax.broadcasted_iota(jnp.int32, (256, 2 * CELLS), 1) - (CELLS if odd else 0)
    hit = (ids >= 0) & (ids < CELLS) & (rows == cell_position(ids))
    return jnp.where(hit, 1.0, 0.0).astype(BF16)


def spread_bias(table, shifted):
    for j in range(CELLS):
        turned = pltpu.roll(table, (384 - CENTRE + cell_position(j)) % 384, 1)
        for h in range(HEADS):
            shifted[h, j : j + 1] = turned[h : h + 1, :256]
    even, odd = position_matrix(False), position_matrix(True)
    pairs = [
        nn(shifted[2 * p].astype(BF16), even) + nn(shifted[2 * p + 1].astype(BF16), odd)
        for p in range(HEADS // 2)
    ]
    return jnp.concatenate(pairs, 1) * log2_e


def prepare(
    blocks, q_w, out_w, up_w, down_w, kv_w, v_b, ln1_g, ln1_b, ln2_g, ln2_b, out_b, down_b, q_b, up_b, table,
    weights_e, vectors_e, bias_e, weights_d, vectors_d, bias_d,
    small, small_sib, q_sib, out_sib, up_sib, down_sib, shifted, send_sem, recv_sem,
):
    core, block = lax.axis_index("section"), lax.axis_index("tok")
    channels, hidden = up_w.shape
    sibling = {"section": 1 - core}
    barrier = pltpu.get_barrier_semaphore()
    pl.semaphore_signal(barrier, inc=1, device_id=sibling, device_id_type=MESH)
    small[...] = jnp.zeros_like(small)
    for row, ref in enumerate((ln1_g, ln1_b, ln2_g, ln2_b, out_b, down_b, q_b)):
        small[row : row + 1, :channels] = ref[...].astype(F32)
    small[7:8, :hidden] = up_b[...].astype(F32)
    small[TABLE_ROW : TABLE_ROW + HEADS, : SPAN**3] = table[...].astype(F32)
    pl.semaphore_wait(barrier, 1)
    pairs = ((small, small_sib), (q_w, q_sib), (out_w, out_sib), (up_w, up_sib), (down_w, down_sib))
    copies = [
        pltpu.make_async_remote_copy(
            src_ref=source, dst_ref=target, send_sem=send_sem.at[k], recv_sem=recv_sem.at[k],
            device_id=sibling, device_id_type=MESH,
        )
        for k, (source, target) in enumerate(pairs)
    ]
    for copy in copies:
        copy.start()
    for copy in copies:
        copy.wait()

    def place(enc, dec):
        e_small, d_small = enc[0], dec[0]
        for weights, vectors, (source, q, out, up, down) in (
            (weights_e, vectors_e, enc), (weights_d, vectors_d, dec),
        ):
            weights[2 * channels :] = jnp.zeros((2 * channels, hidden), BF16)
            weights[:channels] = up[...]
            weights[channels : 2 * channels] = down[...]
            weights[2 * channels : 3 * channels, :channels] = q[...]
            weights[3 * channels :, :channels] = out[...]
            vectors[...] = jnp.zeros_like(vectors)
            vectors[:8, :channels] = source[:8, :channels]
            vectors[8:9, :hidden] = source[7:8, :hidden]
            vectors[9:10, :channels] = source[6:7, :channels]
        weights_e[2 * channels : 3 * channels, 256 : 256 + channels] = kv_w[:, :channels]
        weights_e[2 * channels : 3 * channels, 512 : 512 + channels] = kv_w[:, channels:]
        vectors_e[9:10, 512 : 512 + channels] = v_b[...].astype(F32)
        rows = slice(TABLE_ROW, TABLE_ROW + 8)
        bias_e[...] = spread_bias(e_small[rows, :384], shifted)
        return spread_bias(d_small[rows, :384], shifted)

    own = (small, q_w, out_w, up_w, down_w)
    sib = (small_sib, q_sib, out_sib, up_sib, down_sib)

    def masked(base):
        shape = (CELLS, HEADS * CELLS)
        keys = lax.broadcasted_iota(jnp.int32, shape, 0)
        queries = lax.broadcasted_iota(jnp.int32, shape, 1) % CELLS

        def differ(unit):
            return jnp.where(keys // unit % 2 != queries // unit % 2, 1.0, 0.0)

        last = jnp.where((core == 1) & (block == blocks - 1), 1.0, 0.0)
        for y in range(2):
            for z in range(2):
                apart = jnp.maximum(last * differ(32), jnp.maximum(y * differ(16), z * differ(8)))
                bias_d[y, z] = base + apart * (mask_fill * log2_e)

    @pl.when(core == 0)
    def _():
        masked(place(own, sib))

    @pl.when(core == 1)
    def _():
        masked(place(sib, own))


def run_prepare(blocks, weights, smalls, table, kv_weight, v_bias):
    q_w, out_w, up_w, down_w = weights
    channels, hidden = up_w.shape
    vmem = pl.BlockSpec(memory_space=pltpu.VMEM)
    args = [*weights, kv_weight, v_bias, *smalls, table]
    bias = (CELLS, HEADS * CELLS)
    square = (channels, channels)
    layer = [
        jax.ShapeDtypeStruct((4 * channels, hidden), BF16),
        jax.ShapeDtypeStruct((16, hidden), F32),
    ]
    shapes = [
        *layer,
        jax.ShapeDtypeStruct(bias, F32),
        *layer,
        jax.ShapeDtypeStruct((2, 2, *bias), F32),
    ]
    return pl.pallas_call(
        functools.partial(prepare, blocks),
        in_specs=[vmem] * len(args),
        out_specs=[vmem] * len(shapes),
        out_shape=shapes,
        scratch_shapes=[
            pltpu.VMEM((TABLE_ROW + 8, hidden), F32),
            pltpu.VMEM((TABLE_ROW + 8, hidden), F32),
            pltpu.VMEM(square, BF16),
            pltpu.VMEM(square, BF16),
            pltpu.VMEM((channels, hidden), BF16),
            pltpu.VMEM((channels, hidden), BF16),
            pltpu.VMEM((HEADS, CELLS, 256), F32),
            pltpu.SemaphoreType.DMA((5,)),
            pltpu.SemaphoreType.DMA((5,)),
        ],
        compiler_params=pltpu.CompilerParams(
            collective_id=1, has_side_effects=True, vmem_limit_bytes=VMEM_BYTES
        ),
        name="prepare",
    )(*args)


def run_encoder(core, tokens, batch, consts, cotangent):
    _, _, rows_y, rows_z, channels = tokens.shape
    groups, size = rows_y // WIN, 4 * rows_z
    cells = 4 * size
    hidden = consts[1].shape[1]
    slab = jax.ShapeDtypeStruct((groups, 2, 3, size * 3 // 2, LANES_A), BF16)
    outs = [
        slab,
        slab,
        jax.ShapeDtypeStruct((groups, cells, 512), F32),
        jax.ShapeDtypeStruct((groups, cells, 2 * hidden + HEADS * CELLS + 256), BF16),
    ]

    def row(array):
        zeros = (0,) * (array.ndim - 1)
        return pl.BlockSpec((1, *array.shape[1:]), lambda i, c: (i, *zeros))

    batches = tokens.shape[0]
    cut = [] if cotangent is None else [cotangent]
    cut_block = (batches, SHIFT, WIN, rows_z, channels)
    cut_outs = [
        jax.ShapeDtypeStruct((batches, SHIFT, rows_y, rows_z, channels), a.dtype) for a in cut
    ]
    return pl.pallas_call(
        functools.partial(encoder_forward, len(cut)),
        grid_spec=pltpu.PrefetchScalarGridSpec(
            num_scalar_prefetch=1,
            grid=(groups,),
            in_specs=[
                pl.BlockSpec(
                    (1, WIN, WIN, rows_z, channels), lambda i, c: (batch, c[0], i, 0, 0)
                ),
                *[whole(a) for a in consts],
                *[pl.BlockSpec(cut_block, lambda i, c: (0, 2 * c[0], i, 0, 0)) for _ in cut],
            ],
            out_specs=[
                *[row(a) for a in outs],
                *[pl.BlockSpec(cut_block, lambda i, c: (0, 0, i, 0, 0)) for _ in cut],
            ],
            scratch_shapes=[pltpu.VMEM((cells, 768), BF16)],
        ),
        out_shape=[*outs, *cut_outs],
        compiler_params=params,
        cost_estimate=cost(groups * cells, 466944, groups * cells * 7500),
        name="encoder_forward",
    )(core, tokens, *consts, *cut)


def run_encoder_back(core, batch, own, halo, ys, returned, saved, old, consts, tokens):
    groups, _, _, packed, _ = own.shape
    batches, planes, rows_y, rows_z, channels = tokens.shape
    size = 4 * rows_z
    hidden = consts[1].shape[1]
    first = old is None
    sums = jax.ShapeDtypeStruct((sum_rows(channels, True), hidden), F32)
    outs = [
        jax.ShapeDtypeStruct(tokens.shape, F32),
        jax.ShapeDtypeStruct((WIN, rows_y, rows_z, channels), F32),
        sums,
    ]

    def slab(unit):
        def place(i, c):
            return ((i if unit == 0 else (i + groups - 1) % groups), unit, 0, 0, 0)

        return pl.BlockSpec((1, 1, 3, packed, LANES_A), place)

    def row(array):
        zeros = (0,) * (array.ndim - 1)
        return pl.BlockSpec((1, *array.shape[1:]), lambda i, c: (i, *zeros))

    def for_core(core, planes_here):
        def place(i, c):
            return (0, i * (c[0] if core == 1 else 1 - c[0]), 0, 0)

        return pl.BlockSpec((planes_here, WIN, rows_z, channels), place)

    any_spec = pl.BlockSpec(memory_space=pl.ANY)
    olds = [] if first else [old[1], old[0]]
    args = [core, *consts, *ys, own, own, halo, halo, *saved, *returned, *olds]
    return pl.pallas_call(
        functools.partial(encoder_backward, first, batch, len(returned)),
        grid_spec=pltpu.PrefetchScalarGridSpec(
            num_scalar_prefetch=1,
            grid=(groups,),
            in_specs=[
                *[whole(a) for a in consts],
                *[for_core(1, n) for n in (2, 2, 4)],
                slab(0),
                slab(1),
                slab(0),
                slab(1),
                *[row(a) for a in saved],
                *[for_core(0, WIN)] * len(returned),
                *[whole(a) for a in olds[:-1]],
                *[any_spec] * (0 if first else 1),
            ],
            out_specs=[any_spec, any_spec, whole(sums)],
            scratch_shapes=[
                pltpu.VMEM((4 * size, 768), BF16),
                pltpu.VMEM((3, 4 * size, channels), BF16),
                pltpu.VMEM((2, WIN, WIN, rows_z, channels), F32),
                pltpu.SemaphoreType.DMA((2,)),
                pltpu.SemaphoreType.DMA((8 + batches,)),
            ],
        ),
        out_shape=outs,
        input_output_aliases={} if first else {len(args) - 1: 0},
        compiler_params=params,
        cost_estimate=cost(groups * 4 * size, 933888, groups * 4 * size * 9000),
        name="encoder_backward",
    )(*args)


def run_decoder(core, keep, recv, cotangent, cot_recv, batch, old, consts):
    groups, _, _, packed, _ = keep.shape
    rows_z, channels = cotangent.shape[3:]
    size = 4 * rows_z
    hidden = consts[1].shape[1]
    windows = rows_z // WIN
    first = old is None
    sums = jax.ShapeDtypeStruct((sum_rows(channels, False), hidden), F32)
    slab_shape = jax.ShapeDtypeStruct((groups, 2, 3, packed, LANES_A), BF16)
    outs = [
        *[jax.ShapeDtypeStruct((n, groups * WIN, rows_z, channels), F32) for n in (4, 2)],
        slab_shape,
        slab_shape,
        sums,
    ]

    def slab(unit):
        def place(i, c):
            return ((i if unit == 1 else (i + 1) % groups), unit, 0, 0, 0)

        return pl.BlockSpec((1, 1, 3, packed, LANES_A), place)

    def cot(unit, own):
        def place(i, c):
            y = 2 * i + 1 if unit == 1 else (2 * i + 2) % (2 * groups)
            return (batch, 2 * c[0] + 1 if own else 0, y, 0, 0)

        return pl.BlockSpec((1, 2, 2, rows_z, channels), place)

    def bias_place(i, c):
        return (i // (groups - 1), 0, 0, 0)

    specs = [whole(a) for a in consts]
    specs[3] = pl.BlockSpec((1, *consts[3].shape[1:]), bias_place)
    olds = [] if first else [old]
    out_slab = pl.BlockSpec((1, 2, 3, packed, LANES_A), lambda i, c: (i, 0, 0, 0, 0))
    return pl.pallas_call(
        functools.partial(decoder, first),
        grid_spec=pltpu.PrefetchScalarGridSpec(
            num_scalar_prefetch=1,
            grid=(groups,),
            in_specs=[
                *specs,
                slab(1),
                slab(0),
                slab(1),
                slab(0),
                cot(1, True),
                cot(0, True),
                cot(1, False),
                cot(0, False),
                *[whole(a) for a in olds],
            ],
            out_specs=[
                *[pl.BlockSpec((n, WIN, rows_z, channels), lambda i, c: (0, i, 0, 0)) for n in (4, 2)],
                out_slab,
                out_slab,
                whole(sums),
            ],
            scratch_shapes=[
                pltpu.VMEM((windows, CELLS, HEADS * CELLS), F32),
                pltpu.VMEM((4 * size, channels), BF16),
                pltpu.VMEM((4 * size, hidden), BF16),
                pltpu.VMEM((4 * size, hidden), F32),
                pltpu.VMEM((3, 4 * size, channels), F32),
            ],
        ),
        out_shape=outs,
        compiler_params=params,
        cost_estimate=cost(groups * 4 * size, 1253376, groups * 4 * size * 4000),
        name="decoder",
    )(core, *consts, keep, keep, recv, recv, cotangent, cotangent, cot_recv, cot_recv, *olds)


def body(
    tokens,
    cotangent,
    ln1_gain,
    ln1_bias,
    q_weight,
    q_bias,
    kv_weight,
    v_bias,
    out_weight,
    out_bias,
    rel_table,
    ln2_gain,
    ln2_bias,
    up_weight,
    up_bias,
    down_weight,
    down_bias,
):
    batches, planes, rows_y, rows_z, channels = tokens.shape
    axes = ("section", "tok")
    core = lax.axis_index("section")
    block = lax.axis_index("tok")
    blocks = lax.axis_size("tok")
    is_encoder = core == 0
    core_arg = core.astype(jnp.int32).reshape(1)

    def device(position):
        position = position % (2 * blocks)
        return (position % 2) * blocks + position // 2

    to_previous = [(device(r), device(r - 1)) for r in range(2 * blocks)]
    to_next = [(device(r), device(r + 1)) for r in range(2 * blocks)]

    weights_e, vectors_e, bias_e, weights_d, vectors_d, bias_d = run_prepare(
        blocks,
        (q_weight[0], out_weight[0], up_weight[0], down_weight[0].T),
        (ln1_gain, ln1_bias, ln2_gain, ln2_bias, out_bias, down_bias, q_bias, up_bias),
        rel_table[0],
        kv_weight,
        v_bias[None],
    )
    order = jnp.asarray(order_matrix(rows_z, 0), BF16)
    order_rolled = jnp.asarray(order_matrix(rows_z, 1), BF16)

    enc_consts = (order, weights_e, vectors_e, bias_e)
    enc_back_consts = (order, weights_e, vectors_e)
    dec_consts = (order_rolled, weights_d, vectors_d, bias_d)

    handed, saved = [], []
    for batch in range(batches):
        send, keep, *rest = run_encoder(
            core_arg, tokens, batch, enc_consts, cotangent if batch == 0 else None
        )
        if batch == 0:
            *rest, half = rest
            cot_recv = lax.ppermute(half, axes, to_previous)
        handed.append((keep, lax.ppermute(send, axes, to_previous)))
        saved.append(rest)
    dec_sums = None
    returned, ys = [], []
    to_decoder = [(t, blocks + t) for t in range(blocks)]
    to_encoder = [(blocks + t, t) for t in range(blocks)]
    to_after = [(blocks + t, blocks + (t + 1) % blocks) for t in range(blocks)]
    for batch in range(batches):
        out_all, out_tail, own, halo, dec_sums = run_decoder(
            core_arg, *handed[batch], cotangent, cot_recv, batch, dec_sums, dec_consts
        )
        returned.append((own, lax.ppermute(halo, axes, to_next)))
        y_halo = lax.ppermute(out_tail, axes, to_after)
        ys.append((out_all, y_halo, lax.ppermute(out_all, axes, to_decoder)))
    old = None
    backs = []
    for batch in range(batches):
        arrived = backs[:1] if batch == batches - 1 else []
        ends, back, enc_sums = run_encoder_back(
            core_arg, batch, *returned[batch], ys[batch], arrived, saved[batch], old,
            enc_back_consts, tokens,
        )
        old = (ends, enc_sums)
        backs.append(lax.ppermute(back, axes, to_encoder))

    layout = Layout(channels, up_weight.shape[2], blocks)
    total, sib_kv = run_sum(enc_sums, dec_sums, layout, blocks)
    (
        ends, g_ln1_gain, g_ln1_bias, g_q_weight, g_q_bias, g_kv_weight, g_v_bias, g_out_weight,
        g_out_bias, g_table, g_ln2_gain, g_ln2_bias, g_up_weight, g_up_bias, g_down_weight, g_down_bias,
    ) = run_finish(core_arg, total, sib_kv, backs[1:], ends, layout)
    return (
        ends[None],
        g_ln1_gain,
        g_ln1_bias,
        g_q_weight[None],
        g_q_bias,
        g_kv_weight[None],
        g_v_bias,
        g_out_weight[None],
        g_out_bias,
        g_table.transpose(1, 0, 2),
        g_ln2_gain,
        g_ln2_bias,
        g_up_weight[None],
        g_up_bias,
        g_down_weight.T[None],
        g_down_bias,
    )


def solution(mesh):
    in_specs = (
        P(None, "tok", None, None, None),
        P(None, "tok", None, None, None),
        P("section", None),
        P("section", None),
        P("section", None, None),
        P("section", None),
        P(),
        P(),
        P("section", None, None),
        P("section", None),
        P("section", None, None),
        P("section", None),
        P("section", None),
        P("section", None, None),
        P("section", None),
        P("section", None, None),
        P("section", None),
    )
    out_specs = (
        P("section", None, "tok", None, None, None),
        P("section", None),
        P("section", None),
        P("section", None, None),
        P("section", None),
        P("section", None, None),
        P("section", None),
        P("section", None, None),
        P("section", None),
        P("section", None, None),
        P("section", None),
        P("section", None),
        P("section", None, None),
        P("section", None),
        P("section", None, None),
        P("section", None),
    )
    return jax.shard_map(body, mesh=mesh, in_specs=in_specs, out_specs=out_specs, check_vma=False)
```

```python
import functools

import jax
import jax.numpy as jnp
import numpy as np
from jax import lax
from jax.experimental import pallas as pl
from jax.experimental.pallas import tpu as pltpu
from jax.sharding import PartitionSpec as P

HEADS = 6
HD = 32
WIN = 4
SHIFT = 2
CELLS = WIN**3
SPAN = 2 * WIN - 1
HEADS_A = 4
LANES_A = HEADS_A * HD
COLS_A = HEADS_A * CELLS

eps_norm = 1e-05
mask_fill = -100.0
log2_e = 1.4426950408889634
root_half = 0.7071067811865476
inv_root_two_pi = 0.3989422804014327
scale = HD ** (-0.5)
VMEM_BYTES = 63 * 1024 * 1024

F32 = jnp.float32
MESH = pl.DeviceIdType.MESH
BF16 = jnp.bfloat16


def nn(left, right):
    return lax.dot_general(left, right, (((1,), (0,)), ((), ())), preferred_element_type=F32)


def nt(left, right):
    return lax.dot_general(left, right, (((1,), (1,)), ((), ())), preferred_element_type=F32)


def tn(left, right):
    return lax.dot_general(left, right, (((0,), (0,)), ((), ())), preferred_element_type=F32)


def order_matrix(rows_z, rolled):
    count = 4 * rows_z
    matrix = np.zeros((count, count), np.float32)
    units = rows_z // 2
    for unit in range(units):
        for dx in range(2):
            for dy in range(2):
                for dz in range(2):
                    z = (2 * (unit + rolled) + dz) % rows_z
                    matrix[unit * 8 + dx * 4 + dy * 2 + dz, (dx * 2 + dy) * rows_z + z] = 1.0
    return matrix


def windows_of(pieces):
    count, rows, channels = pieces.shape
    return pieces.reshape(count, rows // 16, 16, channels).transpose(1, 0, 2, 3).reshape(-1, channels)


def pieces_of(windows):
    rows, channels = windows.shape
    return (
        windows.reshape(rows // CELLS, 4, 16, channels)
        .transpose(1, 0, 2, 3)
        .reshape(4, rows // 4, channels)
    )


def roll_rows(pieces, steps):
    return jnp.concatenate([pieces[:, steps:], pieces[:, :steps]], 1)


def pack_slab(pieces):
    half = pieces.shape[1] // 2
    rest = pieces[:, :, LANES_A:]
    return jnp.concatenate(
        [pieces[:, :, :LANES_A], jnp.concatenate([rest[:, :half], rest[:, half:]], 2)], 1
    ).astype(BF16)


def unpack_slab(block):
    size = block.shape[0] * 2 // 3
    half = LANES_A // 2
    rest = jnp.concatenate([block[size:, :half], block[size:, half:]], 0)
    return jnp.concatenate([block[:size], rest], 1)


def normalize(rows):
    mean = jnp.mean(rows, -1, keepdims=True)
    centered = rows - mean
    inv_std = lax.rsqrt(jnp.mean(centered * centered, -1, keepdims=True) + eps_norm)
    return centered * inv_std, inv_std


def norm_back(grad_rows, unit_rows, inv_std, gain):
    scaled = grad_rows * gain
    return inv_std * (
        scaled
        - jnp.mean(scaled, -1, keepdims=True)
        - unit_rows * jnp.mean(scaled * unit_rows, -1, keepdims=True)
    )


def gelu_pair(rows):
    upper = 0.5 * lax.erf(rows * root_half) + 0.5
    bell = jnp.exp2(rows * rows * (-0.5 * log2_e))
    return rows * upper, upper + rows * bell * inv_root_two_pi


def head_masks(width):
    heads = lax.broadcasted_iota(jnp.int32, (1, width), 1) // HD
    return [jnp.where(heads == h, 1.0, 0.0).astype(BF16) for h in range(width // HD)]


def expand(rows):
    masks = head_masks(rows.shape[1])
    return jnp.concatenate([rows * mask for mask in masks], 0)


def collapse(stacked):
    width = stacked.shape[1]
    lanes = lax.broadcasted_iota(jnp.int32, (CELLS, width), 1)
    total = stacked[:CELLS]
    for h in range(1, width // HD):
        total = jnp.where(lanes >= h * HD, stacked[h * CELLS : (h + 1) * CELLS], total)
    return total


def split(rows):
    return rows[:, :LANES_A], rows[:, LANES_A:]


def attend(parts, bias):
    queries, keys, values = zip(*[[split(rows) for rows in part] for part in parts])
    wide = [[expand(half) for half in q] for q in queries]
    scores = [
        jnp.concatenate([nt(k[0], q[0]), nt(k[1], q[1])], 1) for k, q in zip(keys, wide)
    ]
    scores = [s * (scale * log2_e) + b for s, b in zip(scores, bias)]
    exponents = [jnp.exp2(s - jnp.max(s, 0, keepdims=True)) for s in scores]
    probs = [e * (1.0 / jnp.sum(e, 0, keepdims=True)) for e in exponents]
    low = [p.astype(BF16) for p in probs]
    mixed = [
        (tn(p[:, :COLS_A], v[0]), tn(p[:, COLS_A:], v[1])) for p, v in zip(low, values)
    ]
    mixed = [jnp.concatenate([collapse(m[0]), collapse(m[1])], 1).astype(BF16) for m in mixed]
    return mixed, probs


def attend_back(parts):
    queries, keys, values, grads = zip(
        *[[split(rows) for rows in part[:3] + part[4:]] for part in parts]
    )
    probs = [part[3] for part in parts]
    wide_g = [[expand(half) for half in g] for g in grads]
    d_probs = [
        jnp.concatenate([nt(v[0], g[0]), nt(v[1], g[1])], 1) for v, g in zip(values, wide_g)
    ]
    low = [part[3].astype(BF16) for part in parts]
    d_values = [
        jnp.concatenate([nn(p[:, :COLS_A], g[0]), nn(p[:, COLS_A:], g[1])], 1)
        for p, g in zip(low, wide_g)
    ]
    wide_q = [[expand(half) for half in q] for q in queries]
    d_scores = [
        p * (d - jnp.sum(d * p, 0, keepdims=True)) for p, d in zip(probs, d_probs)
    ]
    low_d = [d.astype(BF16) for d in d_scores]
    d_keys = [
        jnp.concatenate([nn(d[:, :COLS_A], q[0]), nn(d[:, COLS_A:], q[1])], 1) * scale
        for d, q in zip(low_d, wide_q)
    ]
    d_queries = [
        (tn(d[:, :COLS_A], k[0]), tn(d[:, COLS_A:], k[1])) for d, k in zip(low_d, keys)
    ]
    d_queries = [
        jnp.concatenate([collapse(d[0]), collapse(d[1])], 1) * scale for d in d_queries
    ]
    table = d_scores[0]
    for d in d_scores[1:]:
        table = table + d
    return d_queries, d_keys, d_values, table


def window_groups(count):
    return [range(k, min(k + TOGETHER, count)) for k in range(0, count, TOGETHER)]


def window_rows(k):
    return slice(k * CELLS, (k + 1) * CELLS)


def with_ones(rows):
    return jnp.concatenate([rows.T, jnp.ones((16, rows.shape[0]), BF16)], 0)


def col_sum(rows):
    return jnp.sum(rows, 0, keepdims=True)


def start_sums(old, new):
    @pl.when(pl.program_id(0) == 0)
    def _():
        new[...] = jnp.zeros_like(new) if old is None else old[...]


def restore(matrix, rows):
    high = rows.astype(BF16)
    low = (rows - high.astype(F32)).astype(BF16)
    return tn(matrix, high) + tn(matrix, low)


CHUNK = 256
BLOCK = 256
TOGETHER = 8


class View:
    def __init__(self, ref, row, rows, col, cols):
        self.ref, self.row, self.col, self.shape = ref, row, col, (rows, cols)

    def place(self, key):
        key = (slice(None), slice(None)) if key is Ellipsis else key
        key = key if isinstance(key, tuple) else (key, slice(None))
        return tuple(
            slice(start + part.indices(size)[0], start + part.indices(size)[1])
            for part, start, size in zip(key, (self.row, self.col), self.shape)
        )

    def __getitem__(self, key):
        return self.ref[self.place(key)]

    def __setitem__(self, key, value):
        self.ref[self.place(key)] = value

    def first_columns(self, cols):
        return View(self.ref, self.row, self.shape[0], self.col, cols)


def layer_views(weights, vectors):
    hidden = weights.shape[1]
    channels = weights.shape[0] // 4
    q_cols = 768

    def rows(k, cols):
        return View(weights, k * channels, channels, 0, cols)

    return (
        View(vectors, 0, 8, 0, channels),
        View(vectors, 8, 1, 0, hidden),
        View(vectors, 9, 1, 0, q_cols),
        rows(0, hidden),
        rows(1, hidden),
        rows(2, q_cols),
        rows(3, channels),
    )


def sum_rows(channels, encoder):
    tall = channels + 16
    return 2 * tall + channels + (tall if encoder else 0)


def sum_views(sums, channels, encoder):
    tall = channels + 16
    base = tall + channels

    def view(row, rows, col, cols):
        return View(sums, row, rows, col, cols)

    fields = [view(base, tall, 256 * k, channels) for k in range(3 if encoder else 2)]
    last = base + (tall if encoder else 0)
    side = 256 if encoder else 512
    out = view(last, tall, 0, channels) if encoder else fields[1]
    bias = (view(last, CELLS, side, COLS_A), view(last + CELLS, CELLS, side, 2 * CELLS))
    vec = view(last + 2 * CELLS, 8, side, channels)
    return (
        view(0, tall, 0, sums.shape[1]),
        view(tall, channels, 0, sums.shape[1]),
        fields[:3] if encoder else fields[:1],
        out,
        vec,
        bias,
    )


def add_bias(views, table):
    views[0][...] += table[:, :COLS_A]
    views[1][...] += table[:, COLS_A:]


def encoder_forward(cuts, core_ref, tok, order, weights, vectors, bias, *rest):
    vec, b_up, b_qkv, w_up, w_down, w_qkv, w_out = layer_views(weights, vectors)
    cut_in, rest = rest[:cuts], rest[cuts:]
    send, keep, wide_out, low_out, *cut_out, qkv = rest
    hidden_cols = w_up.shape[1]
    s_start, p_start, o_start = hidden_cols, 2 * hidden_cols, 2 * hidden_cols + HEADS * CELLS
    for source, target in zip(cut_in, cut_out):
        target[...] = source[...]
    rows_z = tok.shape[3]
    size = 4 * rows_z
    pieces = []
    for x in range(2):
        for y in range(2):
            part = tok[0, 2 * x : 2 * x + 2, 2 * y : 2 * y + 2].reshape(size, -1)
            pieces.append(nn(order[...], part))
    entry = windows_of(jnp.stack(pieces))
    unit, inv_std = normalize(entry)
    channels = entry.shape[1]
    wide = jnp.broadcast_to(inv_std, (entry.shape[0], 256 - channels))
    wide_out[0, :, :channels] = unit
    wide_out[0, :, channels:256] = wide
    left = (unit * vec[0:1] + vec[1:2]).astype(BF16)
    triple = nn(left, w_qkv[...]) + b_qkv[...]
    qkv[...] = triple.astype(BF16)
    for together in window_groups(entry.shape[0] // CELLS):
        parts = [
            [qkv[window_rows(k), 256 * f : 256 * f + 192] for f in range(3)] for k in together
        ]
        mixed, probs = attend(parts, [bias[...]] * len(parts))
        for k, o, p in zip(together, mixed, probs):
            low_out[0, window_rows(k), p_start:o_start] = p.astype(BF16)
            low_out[0, window_rows(k), o_start : o_start + channels] = o
    mixed = low_out[0, :, o_start : o_start + channels]
    middle = entry + nn(mixed, w_out[...]) + vec[4:5]
    unit, inv_std = normalize(middle)
    wide = jnp.broadcast_to(inv_std, (entry.shape[0], 256 - channels))
    wide_out[0, :, 256 : 256 + channels] = unit
    wide_out[0, :, 256 + channels :] = wide
    left = (unit * vec[2:3] + vec[3:4]).astype(BF16)
    results = []
    for k in range(entry.shape[0] // CHUNK):
        rows = slice(k * CHUNK, (k + 1) * CHUNK)
        hidden, slope = gelu_pair(nn(left[rows], w_up[...]) + b_up[...])
        hidden = hidden.astype(BF16)
        low_out[0, rows, :s_start] = hidden
        low_out[0, rows, s_start:p_start] = slope.astype(BF16)
        results.append(nt(hidden, w_down[...]))
    result = middle + jnp.concatenate(results, 0) + vec[5:6]
    for field, rows in enumerate((result, triple[:, 256:448], triple[:, 512:704])):
        rolled = pack_slab(roll_rows(pieces_of(rows), 8))
        send[0, :, field] = rolled[:2]
        keep[0, :, field] = rolled[2:]


def run_together(*works):
    works = list(works)
    while works:
        for work in list(works):
            try:
                next(work)
            except StopIteration:
                works.remove(work)


def row_blocks(count, size):
    return [slice(k, k + size) for k in range(0, count, size)]


def norm_back_steps(rows_grad, base, unit, inv_std, gain, g_vec, row, results):
    sums = [None, None]
    for rows in row_blocks(base.shape[0], BLOCK):
        grad = rows_grad(rows)
        found = (col_sum(grad * unit[rows]), col_sum(grad))
        sums = [f if total is None else total + f for f, total in zip(found, sums)]
        results.append(base[rows] + norm_back(grad, unit[rows], inv_std[rows], gain))
        yield
    g_vec[row : row + 1] += sums[0]
    g_vec[row + 1 : row + 2] += sums[1]


def product_steps(products):
    for target, cols, left, right in products:
        target[:, cols] += nn(left, right)
        yield


def mlp_back(grad, grad_low, hidden, slope, left_two, unit, inv_std, w_up, w_down, vec, sums):
    g_up, g_down, g_vec = sums
    backs, pres = [], []
    for rows in row_blocks(grad.shape[0], CHUNK):
        d_pre = (nn(grad_low[rows], w_down[...]) * slope(rows)).astype(BF16)
        pres.append(d_pre)
        backs.append(nt(d_pre, w_up[...]))
    d_pre = jnp.concatenate(pres, 0)
    d_normed = jnp.concatenate(backs, 0)
    ones, turned = with_ones(left_two), grad_low.T
    tiles = row_blocks(w_up.shape[1], 256)
    products = [(g_up, cols, ones, d_pre[:, cols]) for cols in tiles]
    products += [(g_down, cols, turned, hidden[:, cols]) for cols in tiles]
    results = []
    run_together(
        norm_back_steps(
            lambda rows: d_normed[rows], grad, unit, inv_std, vec[2:3], g_vec, 2, results
        ),
        product_steps(products),
    )
    g_vec[4:5] += col_sum(grad)
    return jnp.concatenate(results, 0)


def start_all(copies):
    for copy in copies:
        copy.start()


def wait_all(copies):
    for copy in copies:
        copy.wait()


def encoder_backward(
    first, batch, returns, core_ref, order, weights, vectors,
    y_own, y_halo, y_sib,
    keep_a, keep_b, recv_a, recv_b,
    wide_in, low_in, *rest,
):
    vec, _, b_qkv, w_up, w_down, w_qkv, w_out = layer_views(weights, vectors)
    channels, hidden_cols = w_up.shape
    s_start, p_start, o_start = hidden_cols, 2 * hidden_cols, 2 * hidden_cols + HEADS * CELLS
    returned, rest = rest[:returns], rest[returns:]
    old, rest = (None, rest) if first else (rest[0], rest[2:])
    ends, back, sums, qkv, dqkv, buffer, out_sem, copy_sem = rest
    g_up, g_down, g_fields, g_out, g_vec, g_bias = sum_views(sums, channels, True)
    step, steps = pl.program_id(0), pl.num_programs(0)
    is_encoder = core_ref[0] == 0
    rows_y = ends.shape[2]
    slot = lax.rem(step, 2)

    def output_copies():
        copies = []
        for start, planes, ref in ((0, 2, y_halo), (2, 4, y_sib), (6, 2, y_own)):
            for half in range(2):
                rows = pl.ds(lax.rem(step * WIN + SHIFT + 2 * half, rows_y), 2)
                target = ends.at[batch, pl.ds(start, planes), rows]
                copies.append((ref.at[:, pl.ds(2 * half, 2)], target))
        return [
            pltpu.make_async_copy(source, target, copy_sem.at[k])
            for k, (source, target) in enumerate(copies)
        ]

    def gradient_copies():
        return [
            pltpu.make_async_copy(
                ref, ends.at[k, pl.ds(WIN, WIN), pl.ds(step * WIN, WIN)], copy_sem.at[8 + k]
            )
            for k, ref in enumerate(returned)
        ]

    def result_copy(index, to_ends):
        target = (
            ends.at[batch, pl.ds(0, WIN), pl.ds(index * WIN, WIN)]
            if to_ends
            else back.at[:, pl.ds(index * WIN, WIN)]
        )
        at = lax.rem(index, 2)
        return pltpu.make_async_copy(buffer.at[at], target, out_sem.at[at])

    def for_core(encoder_work, decoder_work):
        pl.when(is_encoder)(encoder_work)
        pl.when(jnp.logical_not(is_encoder))(decoder_work)

    for_core(lambda: start_all(gradient_copies()), lambda: start_all(output_copies()))

    @pl.when(step >= 2)
    def _():
        for_core(
            lambda: result_copy(step - 2, True).wait(), lambda: result_copy(step - 2, False).wait()
        )

    start_sums(old, sums)
    fields = []
    for field in range(3):
        pieces = jnp.stack(
            [unpack_slab(ref[0, 0, field]) for ref in (recv_b, recv_a, keep_b, keep_a)]
        )
        fields.append(windows_of(pieces))
    grad_low, d_key_1, d_value_1 = fields
    grad = grad_low.astype(F32)
    unit_1, unit_2 = wide_in[0, :, :channels], wide_in[0, :, 256 : 256 + channels]
    wide_1, wide_2 = [wide_in[0, :, k + channels : k + channels + 1] for k in (0, 256)]
    left_1 = (unit_1 * vec[0:1] + vec[1:2]).astype(BF16)
    left_2 = (unit_2 * vec[2:3] + vec[3:4]).astype(BF16)
    qkv[...] = (nn(left_1, w_qkv[...]) + b_qkv[...]).astype(BF16)
    d_middle = mlp_back(
        grad, grad_low, low_in[0, :, :s_start], lambda rows: low_in[0, rows, s_start:p_start].astype(F32),
        left_2, unit_2, wide_2, w_up, w_down, vec,
        (g_up, g_down, g_vec),
    )
    branch = d_middle.astype(BF16)
    d_mixed = nt(branch, w_out[...]).astype(BF16)
    d_table = None
    for together in window_groups(grad.shape[0] // CELLS):
        parts = [
            [qkv[window_rows(k), 256 * f : 256 * f + 192] for f in range(3)]
            + [low_in[0, window_rows(k), p_start:o_start].astype(F32), d_mixed[window_rows(k)]]
            for k in together
        ]
        *d_qkv, d_s = attend_back(parts)
        for k, d_q, d_k, d_v in zip(together, *d_qkv):
            rows = window_rows(k)
            dqkv[0, rows] = d_q.astype(BF16)
            dqkv[1, rows] = (d_k + d_key_1[rows].astype(F32)).astype(BF16)
            dqkv[2, rows] = (d_v + d_value_1[rows].astype(F32)).astype(BF16)
        d_table = d_s if d_table is None else d_table + d_s
    add_bias(g_bias, d_table)
    ones = with_ones(left_1)
    every = slice(None)
    mixed = with_ones(low_in[0, :, o_start : o_start + channels])
    products = [(g_field, every, ones, dqkv[k]) for k, g_field in enumerate(g_fields)]
    products.append((g_out, every, mixed, branch))

    def rows_grad(rows):
        parts = [
            nt(dqkv[k, rows], w_qkv[:, 256 * k : 256 * k + channels]) for k in range(3)
        ]
        return parts[0] + parts[1] + parts[2]

    results = []
    run_together(
        norm_back_steps(rows_grad, d_middle, unit_1, wide_1, vec[0:1], g_vec, 0, results),
        product_steps(products),
    )
    result = pieces_of(jnp.concatenate(results, 0))
    rows_z = ends.shape[3]
    for x in range(2):
        for y in range(2):
            part = restore(order[...], result[2 * x + y])
            buffer[slot, 2 * x : 2 * x + 2, 2 * y : 2 * y + 2] = part.reshape(2, 2, rows_z, -1)
    for_core(lambda: result_copy(step, True).start(), lambda: result_copy(step, False).start())

    @pl.when(step == steps - 1)
    def _():
        def finish(to_ends):
            result_copy(step - 1, to_ends).wait()
            result_copy(step, to_ends).wait()

        for_core(lambda: finish(True), lambda: finish(False))

    for_core(lambda: wait_all(gradient_copies()), lambda: wait_all(output_copies()))


def decoder(
    first, order, weights, vectors, bias,
    keep_1, keep_0, recv_1, recv_0, cot_1, cot_0, cot_r1, cot_r0, *rest,
):
    vec, b_up, b_qkv, w_up, w_down, w_qkv, w_out = layer_views(weights, vectors)
    channels = w_up.shape[0]
    w_q, b_q = w_qkv.first_columns(channels), b_qkv.first_columns(channels)
    old, new = (None, rest) if first else (rest[0], rest[1:])
    (
        out_own, y_sib, y_halo, own, halo, sums, p_scr, o_scr, a_scr, s_scr, dqkv, y_buffer, send_sem, recv_sem,
    ) = new
    step, steps = pl.program_id(0), pl.num_programs(0)
    core, block, blocks = lax.axis_index("section"), lax.axis_index("tok"), lax.axis_size("tok")
    slot = lax.rem(step, 2)

    def to_sibling(index):
        return pltpu.make_async_remote_copy(
            src_ref=y_buffer.at[lax.rem(index, 2)], dst_ref=y_sib.at[:, pl.ds(index * WIN, WIN)],
            send_sem=send_sem.at[lax.rem(index, 2)], recv_sem=recv_sem.at[0, index],
            device_id={"section": 1 - core}, device_id_type=MESH,
        )

    def to_after(index):
        return pltpu.make_async_remote_copy(
            src_ref=y_buffer.at[lax.rem(index, 2), pl.ds(SHIFT, SHIFT)],
            dst_ref=y_halo.at[:, pl.ds(index * WIN, WIN)],
            send_sem=send_sem.at[lax.rem(index, 2)], recv_sem=recv_sem.at[1, index],
            device_id={"tok": lax.rem(block + 1, blocks)}, device_id_type=MESH,
        )

    def for_core(first_work, second_work):
        pl.when(core == 0)(first_work)
        pl.when(core == 1)(second_work)

    @pl.when((step == 0) & (core == 1))
    def _():
        barrier = pltpu.get_barrier_semaphore()
        before = lax.rem(block + blocks - 1, blocks)
        pl.semaphore_signal(
            barrier, inc=1, device_id={"section": 1 - core}, device_id_type=MESH
        )
        pl.semaphore_signal(barrier, inc=1, device_id={"tok": before}, device_id_type=MESH)

    @pl.when(step >= 2)
    def _():
        for_core(lambda: to_sibling(step - 2).wait_send(), lambda: to_after(step - 2).wait_send())

    g_up, g_down, (g_q,), g_out, g_vec, g_bias = sum_views(sums, channels, False)
    start_sums(old, sums)
    fields = []
    for field in range(3):
        pieces = jnp.stack([unpack_slab(ref[0, 0, field]) for ref in (keep_1, keep_0, recv_1, recv_0)])
        fields.append(windows_of(pieces))
    entry_low, keys, values = fields
    entry = entry_low.astype(F32)
    unit_1, inv_1 = normalize(entry)
    left_1 = (unit_1 * vec[0:1] + vec[1:2]).astype(BF16)
    queries = (nn(left_1, w_q[...]) + b_q[...]).astype(BF16)
    windows = entry.shape[0] // CELLS
    for together in window_groups(windows):
        parts = [[rows[window_rows(k)] for rows in (queries, keys, values)] for k in together]
        mixed, probs = attend(parts, [bias[0, 1 if k == windows - 1 else 0] for k in together])
        for k, o, p in zip(together, mixed, probs):
            p_scr[k] = p
            o_scr[window_rows(k)] = o
    middle = entry + nn(o_scr[...], w_out[...]) + vec[4:5]
    unit_2, inv_2 = normalize(middle)
    left_2 = (unit_2 * vec[2:3] + vec[3:4]).astype(BF16)
    results = []
    for k in range(entry.shape[0] // CHUNK):
        rows = slice(k * CHUNK, (k + 1) * CHUNK)
        hidden, slope = gelu_pair(nn(left_2[rows], w_up[...]) + b_up[...])
        hidden = hidden.astype(BF16)
        a_scr[rows] = hidden
        s_scr[rows] = slope
        results.append(nt(hidden, w_down[...]))
    result = pieces_of(middle + jnp.concatenate(results, 0) + vec[5:6])
    rows_z = out_own.shape[2]
    size = 4 * rows_z
    for x in range(2):
        for y in range(2):
            part = restore(order[...], result[2 * x + y]).reshape(2, 2, rows_z, -1)
            y_buffer[slot, 2 * x : 2 * x + 2, 2 * y : 2 * y + 2] = part
            if x == 0:
                out_own[:, 2 * y : 2 * y + 2] = part

    @pl.when(step == 0)
    def _():
        pl.semaphore_wait(pltpu.get_barrier_semaphore(), 1)

    for_core(lambda: to_sibling(step).start(), lambda: to_after(step).start())

    cots = [
        nn(order[...], ref[0].reshape(size, -1)).astype(BF16) for ref in (cot_1, cot_0, cot_r1, cot_r0)
    ]
    grad_low = windows_of(jnp.stack(cots))
    grad = grad_low.astype(F32)
    d_middle = mlp_back(
        grad, grad_low, a_scr[...], lambda rows: s_scr[rows], left_2, unit_2, inv_2, w_up, w_down, vec,
        (g_up, g_down, g_vec),
    )
    branch = d_middle.astype(BF16)
    d_mixed = nt(branch, w_out[...]).astype(BF16)
    d_table = None
    for together in window_groups(windows):
        parts = [
            [rows[window_rows(k)] for rows in (queries, keys, values)]
            + [p_scr[k], d_mixed[window_rows(k)]]
            for k in together
        ]
        *d_qkv, d_s = attend_back(parts)
        for k, *grads in zip(together, *d_qkv):
            for f in range(3):
                dqkv[f, window_rows(k)] = grads[f]
        d_table = d_s if d_table is None else d_table + d_s
    add_bias(g_bias, d_table)
    d_queries = dqkv[0].astype(BF16)
    every = slice(None)
    products = [
        (g_q, every, with_ones(left_1), d_queries),
        (g_out, every, with_ones(o_scr[...]), branch),
    ]
    results = []
    run_together(
        norm_back_steps(
            lambda rows: nt(d_queries[rows], w_q[...]), d_middle, unit_1, inv_1, vec[0:1], g_vec, 0,
            results,
        ),
        product_steps(products),
    )
    d_entry = jnp.concatenate(results, 0)
    for field, rows in enumerate((d_entry, dqkv[1], dqkv[2])):
        turned = pack_slab(roll_rows(pieces_of(rows), size - 8))
        own[0, :, field] = turned[:2]
        halo[0, :, field] = turned[2:]

    @pl.when(step == steps - 1)
    def _():
        def finish_second():
            to_after(step - 1).wait_send()
            to_after(step).wait_send()

            def arrive(index, carry):
                to_sibling(index).wait_recv()
                to_after(index).wait_recv()
                return carry

            lax.fori_loop(0, steps, arrive, 0)

        def finish_first():
            to_sibling(step - 1).wait_send()
            to_sibling(step).wait_send()

        for_core(finish_first, finish_second)


def whole(array):
    zeros = (0,) * array.ndim
    return pl.BlockSpec(array.shape, lambda *_: zeros)


def cost(cells, per_cell, hbm):
    return pl.CostEstimate(
        flops=2 * cells * per_cell, bytes_accessed=hbm, transcendentals=cells * 1536
    )


params = pltpu.CompilerParams(
    dimension_semantics=("arbitrary",), vmem_limit_bytes=VMEM_BYTES
)


class Layout:
    def __init__(self, channels, hidden, blocks):
        tall = channels + 16
        self.tall, self.channels = tall, channels
        self.tiles = hidden // LANES_A
        self.up = 0
        self.down = self.tiles * tall
        self.q = self.down + self.tiles * channels
        self.out = self.q + tall
        self.rest = self.out + tall
        self.kv = self.rest + tall
        self.bias = self.kv + 2 * tall
        self.vec = self.bias + HEADS * CELLS // LANES_A * CELLS
        self.end = self.vec + 16
        self.chunk = -(-self.end // (16 * blocks)) * 16
        self.rows = self.chunk * blocks


def fill(buffer, layout, up, down, q, out, kv, bias, vec):
    kind, half = buffer.dtype, LANES_A // 2
    tall, channels = layout.tall, layout.channels
    for k in range(layout.tiles):
        cols = slice(k * LANES_A, (k + 1) * LANES_A)
        buffer[layout.up + k * tall : layout.up + (k + 1) * tall] = up[:, cols].astype(kind)
        buffer[layout.down + k * channels : layout.down + (k + 1) * channels] = down[
            :, cols
        ].astype(kind)
    buffer[layout.q : layout.q + tall] = q[:, :LANES_A].astype(kind)
    buffer[layout.out : layout.out + tall] = out[:, :LANES_A].astype(kind)
    rests = jnp.concatenate([q[:, LANES_A:], out[:, LANES_A:]], 1)
    buffer[layout.rest : layout.rest + tall] = rests.astype(kind)
    buffer[layout.kv : layout.kv + tall] = kv[:, :LANES_A].astype(kind)
    rests = jnp.concatenate([kv[:, LANES_A:], jnp.zeros((tall, half), F32)], 1)
    buffer[layout.kv + tall : layout.kv + 2 * tall] = rests.astype(kind)
    tiles = [bias[0][:, :LANES_A], bias[0][:, LANES_A:], bias[1][...]]
    for k, tile in enumerate(tiles):
        start = layout.bias + k * CELLS
        buffer[start : start + CELLS] = tile.astype(kind)
    rests = jnp.concatenate([vec[:, LANES_A:], jnp.zeros((8, half), F32)], 1)
    both = jnp.concatenate([vec[:, :LANES_A], rests], 0)
    buffer[layout.vec : layout.vec + 16] = both.astype(kind)
    if layout.rows > layout.end:
        buffer[layout.end :] = jnp.zeros((layout.rows - layout.end, LANES_A), kind)


def groups_of(blocks):
    near = 4 if blocks % 4 == 0 else blocks
    return near, blocks // near


def sum_gradients(layout, blocks, *refs):
    enc, dec, *rest = refs
    (
        total_out, kv_out, own, theirs, from_sib, low, landed, near_low, far_landed, total, sib_kv,
        sib_send, sib_recv, send_sem, recv_sem,
    ) = rest
    core, me = lax.axis_index("section"), lax.axis_index("tok")
    sibling = {"section": 1 - core}

    near, far = groups_of(blocks)
    inner, outer = lax.rem(me, near), lax.div(me, near)
    quarter = far * layout.chunk

    def near_peer(offset):
        return lax.rem(inner + offset, near)

    def far_peer(offset):
        return lax.rem(outer + offset, far)

    def near_device(offset):
        return {"tok": outer * near + near_peer(offset)}

    def far_device(offset):
        return {"tok": far_peer(offset) * near + inner}

    barrier = pltpu.get_barrier_semaphore()
    pl.semaphore_signal(barrier, inc=1, device_id=sibling, device_id_type=MESH)
    for count, device in ((near, near_device), (far, far_device)):

        def greet(offset, carry, device=device):
            pl.semaphore_signal(barrier, inc=1, device_id=device(offset), device_id_type=MESH)
            return carry

        lax.fori_loop(1, count, greet, 0)

    channels = layout.channels
    e_up, e_down, (e_q, e_k, e_v), e_out, e_vec, e_bias = sum_views(enc, channels, True)
    d_up, d_down, (d_q,), d_out, d_vec, d_bias = sum_views(dec, channels, False)

    @pl.when(core == 0)
    def _():
        fill(theirs, layout, d_up, d_down, d_q, d_out, e_v, d_bias, d_vec)
        fill(own, layout, e_up, e_down, e_q, e_out, e_k, e_bias, e_vec)

    @pl.when(core == 1)
    def _():
        fill(theirs, layout, e_up, e_down, e_q, e_out, e_k, e_bias, e_vec)
        fill(own, layout, d_up, d_down, d_q, d_out, e_v, d_bias, d_vec)

    pl.semaphore_wait(barrier, near + far - 1)

    def to_sibling(source, target, k):
        return pltpu.make_async_remote_copy(
            src_ref=source, dst_ref=target, send_sem=sib_send.at[k], recv_sem=sib_recv.at[k],
            device_id=sibling, device_id_type=MESH,
        )

    first = to_sibling(theirs, from_sib, 0)
    first.start()
    first.wait()
    own[...] += from_sib[...].astype(F32)
    low[...] = own[...].astype(BF16)

    def quarter_of(position):
        return pl.ds(pl.multiple_of(position * quarter, 16), quarter)

    def chunk_of(position):
        return pl.ds(pl.multiple_of(position * layout.chunk, 16), layout.chunk)

    def rows_of(position):
        start = inner * quarter + position * layout.chunk
        return pl.ds(pl.multiple_of(start, 16), layout.chunk)

    def exchange(stage, offset, source, target, device):
        return pltpu.make_async_remote_copy(
            src_ref=source, dst_ref=target,
            send_sem=send_sem.at[stage, offset], recv_sem=recv_sem.at[stage, offset],
            device_id=device(offset), device_id_type=MESH,
        )

    def near_scatter(offset):
        source = low.at[quarter_of(near_peer(offset))]
        return exchange(0, offset, source, landed.at[offset], near_device)

    def far_scatter(offset):
        source = near_low.at[chunk_of(far_peer(offset))]
        return exchange(1, offset, source, far_landed.at[offset], far_device)

    def far_gather(offset, owner):
        rows = rows_of(owner)
        return exchange(2, offset, total.at[rows], total.at[rows], far_device)

    def near_gather(offset, owner):
        rows = quarter_of(owner)
        return exchange(3, offset, total.at[rows], total.at[rows], near_device)

    def each(count, work):
        def run(offset, carry):
            work(offset)
            return carry

        lax.fori_loop(1, count, run, 0)

    def reduced(count, copy, landing, start):
        def add(offset, carry):
            copy(offset).wait_recv()
            return carry + landing[offset].astype(F32)

        return lax.fori_loop(1, count, add, start)

    each(near, lambda offset: near_scatter(offset).start())
    near_sum = reduced(near, near_scatter, landed, own[quarter_of(inner)])
    own[quarter_of(inner)] = near_sum
    near_low[...] = near_sum.astype(BF16)
    each(far, lambda offset: far_scatter(offset).start())
    total[rows_of(outer)] = reduced(far, far_scatter, far_landed, own[rows_of(outer)]).astype(BF16)
    each(far, lambda offset: far_gather(offset, outer).start())
    each(far, lambda offset: far_gather(offset, lax.rem(outer + far - offset, far)).wait_recv())
    each(near, lambda offset: near_gather(offset, inner).start())
    each(near, lambda offset: near_gather(offset, lax.rem(inner + near - offset, near)).wait_recv())
    kv_rows = pl.ds(layout.kv, 2 * layout.tall)
    third = to_sibling(total.at[kv_rows], sib_kv, 1)
    third.start()
    total_out[...] = total[...]

    each(near, lambda offset: near_scatter(offset).wait_send())
    each(far, lambda offset: far_scatter(offset).wait_send())
    each(far, lambda offset: far_gather(offset, outer).wait_send())
    each(near, lambda offset: near_gather(offset, inner).wait_send())
    third.wait()
    kv_out[...] = sib_kv[...]


def run_sum(enc_sums, dec_sums, layout, blocks):
    rows, chunk, tall = layout.rows, layout.chunk, layout.tall
    near, far = groups_of(blocks)
    dma = pltpu.SemaphoreType.DMA
    vmem = pl.BlockSpec(memory_space=pltpu.VMEM)
    args = [enc_sums, dec_sums]
    return pl.pallas_call(
        functools.partial(sum_gradients, layout, blocks),
        in_specs=[vmem] * len(args),
        out_specs=[vmem] * 2,
        out_shape=[
            jax.ShapeDtypeStruct((rows, LANES_A), BF16),
            jax.ShapeDtypeStruct((2 * tall, LANES_A), BF16),
        ],
        scratch_shapes=[
            pltpu.VMEM((rows, LANES_A), F32),
            pltpu.VMEM((rows, LANES_A), BF16),
            pltpu.VMEM((rows, LANES_A), BF16),
            pltpu.VMEM((rows, LANES_A), BF16),
            pltpu.VMEM((near, far * chunk, LANES_A), BF16),
            pltpu.VMEM((far * chunk, LANES_A), BF16),
            pltpu.VMEM((far, chunk, LANES_A), BF16),
            pltpu.VMEM((rows, LANES_A), BF16),
            pltpu.VMEM((2 * tall, LANES_A), BF16),
            dma((2,)),
            dma((2,)),
            *[dma((4, max(near, far)))] * 2,
        ],
        compiler_params=pltpu.CompilerParams(
            collective_id=0, has_side_effects=True, vmem_limit_bytes=VMEM_BYTES
        ),
        name="sum_gradients",
    )(*args)


def finish(layout, batches, returns, core_ref, total, sib_kv, *refs):
    returned, refs = refs[:returns], refs[returns + 1 :]
    (
        ends, ln1_gain, ln1_bias, q_weight, q_bias, kv_weight, v_bias, out_weight, out_bias, table,
        ln2_gain, ln2_bias, up_weight, up_bias, down_weight, down_bias, placed, copy_sem,
    ) = refs
    is_encoder = core_ref[0] == 0
    step = pl.program_id(0)

    def copies():
        return [
            pltpu.make_async_copy(
                ref,
                ends.at[batches - returns + k, pl.ds(WIN, WIN), pl.ds(step * WIN, WIN)],
                copy_sem.at[k],
            )
            for k, ref in enumerate(returned)
        ]

    pl.when(is_encoder)(lambda: start_all(copies()))

    @pl.when(step == 0)
    def _():
        unpack(
            layout, is_encoder, total, sib_kv, ln1_gain, ln1_bias, q_weight, q_bias, kv_weight,
            v_bias, out_weight, out_bias, table, ln2_gain, ln2_bias, up_weight, up_bias, down_weight,
            down_bias, placed,
        )

    pl.when(is_encoder)(lambda: wait_all(copies()))


def unpack(
    layout, is_encoder, total, sib_kv, ln1_gain, ln1_bias, q_weight, q_bias, kv_weight,
    v_bias, out_weight, out_bias, table, ln2_gain, ln2_bias, up_weight, up_bias, down_weight, down_bias,
    placed,
):
    channels, tall, half = layout.channels, layout.tall, LANES_A // 2

    def at(start, rows):
        return total[start : start + rows].astype(F32)

    vec = at(layout.vec, 16)
    vec = jnp.concatenate([vec[:8], vec[8:, :half]], 1)
    for row, ref in enumerate((ln1_gain, ln1_bias, ln2_gain, ln2_bias, down_bias)):
        ref[...] = vec[row : row + 1]

    for k in range(layout.tiles):
        cols = slice(k * LANES_A, (k + 1) * LANES_A)
        tile = at(layout.up + k * tall, tall)
        up_weight[:, cols] = tile[:channels]
        up_bias[:, cols] = tile[channels : channels + 1]
        down_weight[:, cols] = at(layout.down + k * channels, channels)
    rest = at(layout.rest, tall)
    q = jnp.concatenate([at(layout.q, tall), rest[:, :half]], 1)
    out = jnp.concatenate([at(layout.out, tall), rest[:, half:]], 1)
    q_weight[...] = q[:channels]
    q_bias[...] = q[channels : channels + 1]
    out_weight[...] = out[:channels]
    out_bias[...] = out[channels : channels + 1]
    mine = at(layout.kv, 2 * tall)
    other = sib_kv[...].astype(F32)
    for start, side in ((0, jnp.where(is_encoder, mine, other)), (channels, jnp.where(is_encoder, other, mine))):
        side = jnp.concatenate([side[:tall], side[tall:, :half]], 1)
        kv_weight[:, start : start + channels] = side[:channels]
    v_bias[...] = side[channels : channels + 1]
    placed[...] = jnp.zeros_like(placed)
    positions = [position_matrix(False), position_matrix(True)]
    for h in range(HEADS):
        start = layout.bias + h // 2 * CELLS
        placed[h, :, :256] = nt(total[start : start + CELLS], positions[h % 2])
    entries = jnp.zeros((8, 384), F32)
    for j in range(CELLS):
        entries += pltpu.roll(placed[:, j, :], CENTRE - cell_position(j), 1)
    table[...] = entries[:HEADS, : SPAN**3][:, None]


def run_finish(core, total, sib_kv, returned, ends, layout):
    channels = layout.channels
    hidden = layout.tiles * LANES_A
    _, _, rows_y, rows_z, _ = ends.shape
    any_spec = pl.BlockSpec(memory_space=pl.ANY)
    shapes = [
        (1, channels), (1, channels), (channels, channels), (1, channels), (channels, 2 * channels),
        (1, channels), (channels, channels), (1, channels), (HEADS, 1, SPAN**3),
        (1, channels), (1, channels), (channels, hidden), (1, hidden), (channels, hidden), (1, channels),
    ]
    shapes = [jax.ShapeDtypeStruct(shape, F32) for shape in shapes]
    return pl.pallas_call(
        functools.partial(finish, layout, ends.shape[0], len(returned)),
        grid_spec=pltpu.PrefetchScalarGridSpec(
            num_scalar_prefetch=1,
            grid=(rows_y // WIN,),
            in_specs=[
                *[whole(a) for a in (total, sib_kv)],
                *[
                    pl.BlockSpec(
                        (WIN, WIN, rows_z, channels), lambda i, c: (0, i * (1 - c[0]), 0, 0)
                    )
                ]
                * len(returned),
                any_spec,
            ],
            out_specs=[any_spec, *[whole(a) for a in shapes]],
            scratch_shapes=[
                pltpu.VMEM((8, CELLS, 384), F32),
                pltpu.SemaphoreType.DMA((len(returned),)),
            ],
        ),
        out_shape=[jax.ShapeDtypeStruct(ends.shape, F32), *shapes],
        input_output_aliases={3 + len(returned): 0},
        compiler_params=params,
        name="finish",
    )(core, total, sib_kv, *returned, ends)


def cell_position(ids):
    x = 2 * (ids // 32) + ids // 4 % 2
    y = 2 * (ids // 16 % 2) + ids // 2 % 2
    z = 2 * (ids // 8 % 2) + ids % 2
    return (x * SPAN + y) * SPAN + z


CENTRE = (WIN - 1) * (SPAN * SPAN + SPAN + 1)
TABLE_ROW = 8


def position_matrix(odd):
    rows = lax.broadcasted_iota(jnp.int32, (256, 2 * CELLS), 0)
    ids = lax.broadcasted_iota(jnp.int32, (256, 2 * CELLS), 1) - (CELLS if odd else 0)
    hit = (ids >= 0) & (ids < CELLS) & (rows == cell_position(ids))
    return jnp.where(hit, 1.0, 0.0).astype(BF16)


def spread_bias(table, shifted):
    for j in range(CELLS):
        turned = pltpu.roll(table, (384 - CENTRE + cell_position(j)) % 384, 1)
        for h in range(HEADS):
            shifted[h, j : j + 1] = turned[h : h + 1, :256]
    even, odd = position_matrix(False), position_matrix(True)
    pairs = [
        nn(shifted[2 * p].astype(BF16), even) + nn(shifted[2 * p + 1].astype(BF16), odd)
        for p in range(HEADS // 2)
    ]
    return jnp.concatenate(pairs, 1) * log2_e


def prepare(
    blocks, q_w, out_w, up_w, down_w, kv_w, v_b, ln1_g, ln1_b, ln2_g, ln2_b, out_b, down_b, q_b, up_b, table,
    weights_e, vectors_e, bias_e, weights_d, vectors_d, bias_d,
    small, small_sib, q_sib, out_sib, up_sib, down_sib, shifted, send_sem, recv_sem,
):
    core, block = lax.axis_index("section"), lax.axis_index("tok")
    channels, hidden = up_w.shape
    sibling = {"section": 1 - core}
    barrier = pltpu.get_barrier_semaphore()
    pl.semaphore_signal(barrier, inc=1, device_id=sibling, device_id_type=MESH)
    small[...] = jnp.zeros_like(small)
    for row, ref in enumerate((ln1_g, ln1_b, ln2_g, ln2_b, out_b, down_b, q_b)):
        small[row : row + 1, :channels] = ref[...].astype(F32)
    small[7:8, :hidden] = up_b[...].astype(F32)
    small[TABLE_ROW : TABLE_ROW + HEADS, : SPAN**3] = table[...].astype(F32)
    pl.semaphore_wait(barrier, 1)
    pairs = ((small, small_sib), (q_w, q_sib), (out_w, out_sib), (up_w, up_sib), (down_w, down_sib))
    copies = [
        pltpu.make_async_remote_copy(
            src_ref=source, dst_ref=target, send_sem=send_sem.at[k], recv_sem=recv_sem.at[k],
            device_id=sibling, device_id_type=MESH,
        )
        for k, (source, target) in enumerate(pairs)
    ]
    for copy in copies:
        copy.start()
    for copy in copies:
        copy.wait()

    def place(enc, dec):
        e_small, d_small = enc[0], dec[0]
        for weights, vectors, (source, q, out, up, down) in (
            (weights_e, vectors_e, enc), (weights_d, vectors_d, dec),
        ):
            weights[2 * channels :] = jnp.zeros((2 * channels, hidden), BF16)
            weights[:channels] = up[...]
            weights[channels : 2 * channels] = down[...]
            weights[2 * channels : 3 * channels, :channels] = q[...]
            weights[3 * channels :, :channels] = out[...]
            vectors[...] = jnp.zeros_like(vectors)
            vectors[:8, :channels] = source[:8, :channels]
            vectors[8:9, :hidden] = source[7:8, :hidden]
            vectors[9:10, :channels] = source[6:7, :channels]
        weights_e[2 * channels : 3 * channels, 256 : 256 + channels] = kv_w[:, :channels]
        weights_e[2 * channels : 3 * channels, 512 : 512 + channels] = kv_w[:, channels:]
        vectors_e[9:10, 512 : 512 + channels] = v_b[...].astype(F32)
        rows = slice(TABLE_ROW, TABLE_ROW + 8)
        bias_e[...] = spread_bias(e_small[rows, :384], shifted)
        return spread_bias(d_small[rows, :384], shifted)

    own = (small, q_w, out_w, up_w, down_w)
    sib = (small_sib, q_sib, out_sib, up_sib, down_sib)

    def masked(base):
        shape = (CELLS, HEADS * CELLS)
        keys = lax.broadcasted_iota(jnp.int32, shape, 0)
        queries = lax.broadcasted_iota(jnp.int32, shape, 1) % CELLS

        def differ(unit):
            return jnp.where(keys // unit % 2 != queries // unit % 2, 1.0, 0.0)

        last = jnp.where((core == 1) & (block == blocks - 1), 1.0, 0.0)
        for y in range(2):
            for z in range(2):
                apart = jnp.maximum(last * differ(32), jnp.maximum(y * differ(16), z * differ(8)))
                bias_d[y, z] = base + apart * (mask_fill * log2_e)

    @pl.when(core == 0)
    def _():
        masked(place(own, sib))

    @pl.when(core == 1)
    def _():
        masked(place(sib, own))


def run_prepare(blocks, weights, smalls, table, kv_weight, v_bias):
    q_w, out_w, up_w, down_w = weights
    channels, hidden = up_w.shape
    vmem = pl.BlockSpec(memory_space=pltpu.VMEM)
    args = [*weights, kv_weight, v_bias, *smalls, table]
    bias = (CELLS, HEADS * CELLS)
    square = (channels, channels)
    layer = [
        jax.ShapeDtypeStruct((4 * channels, hidden), BF16),
        jax.ShapeDtypeStruct((16, hidden), F32),
    ]
    shapes = [
        *layer,
        jax.ShapeDtypeStruct(bias, F32),
        *layer,
        jax.ShapeDtypeStruct((2, 2, *bias), F32),
    ]
    return pl.pallas_call(
        functools.partial(prepare, blocks),
        in_specs=[vmem] * len(args),
        out_specs=[vmem] * len(shapes),
        out_shape=shapes,
        scratch_shapes=[
            pltpu.VMEM((TABLE_ROW + 8, hidden), F32),
            pltpu.VMEM((TABLE_ROW + 8, hidden), F32),
            pltpu.VMEM(square, BF16),
            pltpu.VMEM(square, BF16),
            pltpu.VMEM((channels, hidden), BF16),
            pltpu.VMEM((channels, hidden), BF16),
            pltpu.VMEM((HEADS, CELLS, 256), F32),
            pltpu.SemaphoreType.DMA((5,)),
            pltpu.SemaphoreType.DMA((5,)),
        ],
        compiler_params=pltpu.CompilerParams(
            collective_id=1, has_side_effects=True, vmem_limit_bytes=VMEM_BYTES
        ),
        name="prepare",
    )(*args)


def run_encoder(core, tokens, batch, consts, cotangent):
    _, _, rows_y, rows_z, channels = tokens.shape
    groups, size = rows_y // WIN, 4 * rows_z
    cells = 4 * size
    hidden = consts[1].shape[1]
    slab = jax.ShapeDtypeStruct((groups, 2, 3, size * 3 // 2, LANES_A), BF16)
    outs = [
        slab,
        slab,
        jax.ShapeDtypeStruct((groups, cells, 512), F32),
        jax.ShapeDtypeStruct((groups, cells, 2 * hidden + HEADS * CELLS + 256), BF16),
    ]

    def row(array):
        zeros = (0,) * (array.ndim - 1)
        return pl.BlockSpec((1, *array.shape[1:]), lambda i, c: (i, *zeros))

    batches = tokens.shape[0]
    cut = [] if cotangent is None else [cotangent] * 2
    cut_block = (batches, SHIFT, WIN, rows_z, channels)
    cut_outs = [
        jax.ShapeDtypeStruct((batches, SHIFT, rows_y, rows_z, channels), a.dtype) for a in cut
    ]
    return pl.pallas_call(
        functools.partial(encoder_forward, len(cut)),
        grid_spec=pltpu.PrefetchScalarGridSpec(
            num_scalar_prefetch=1,
            grid=(groups,),
            in_specs=[
                pl.BlockSpec(
                    (1, WIN, WIN, rows_z, channels), lambda i, c: (batch, c[0], i, 0, 0)
                ),
                *[whole(a) for a in consts],
                *[
                    pl.BlockSpec(cut_block, lambda i, c, half=half: (0, 2 * c[0] + half, i, 0, 0))
                    for half in range(len(cut))
                ],
            ],
            out_specs=[
                *[row(a) for a in outs],
                *[pl.BlockSpec(cut_block, lambda i, c: (0, 0, i, 0, 0)) for _ in cut],
            ],
            scratch_shapes=[pltpu.VMEM((cells, 768), BF16)],
        ),
        out_shape=[*outs, *cut_outs],
        compiler_params=params,
        cost_estimate=cost(groups * cells, 466944, groups * cells * 7500),
        name="encoder_forward",
    )(core, tokens, *consts, *cut)


def run_encoder_back(core, batch, own, halo, ys, returned, saved, old, consts, tokens):
    groups, _, _, packed, _ = own.shape
    batches, planes, rows_y, rows_z, channels = tokens.shape
    size = 4 * rows_z
    hidden = consts[1].shape[1]
    first = old is None
    sums = jax.ShapeDtypeStruct((sum_rows(channels, True), hidden), F32)
    outs = [
        jax.ShapeDtypeStruct(tokens.shape, F32),
        jax.ShapeDtypeStruct((WIN, rows_y, rows_z, channels), F32),
        sums,
    ]

    def slab(unit):
        def place(i, c):
            return ((i if unit == 0 else (i + groups - 1) % groups), unit, 0, 0, 0)

        return pl.BlockSpec((1, 1, 3, packed, LANES_A), place)

    def row(array):
        zeros = (0,) * (array.ndim - 1)
        return pl.BlockSpec((1, *array.shape[1:]), lambda i, c: (i, *zeros))

    def for_core(core, planes_here):
        def place(i, c):
            return (0, i * (c[0] if core == 1 else 1 - c[0]), 0, 0)

        return pl.BlockSpec((planes_here, WIN, rows_z, channels), place)

    any_spec = pl.BlockSpec(memory_space=pl.ANY)
    olds = [] if first else [old[1], old[0]]
    args = [core, *consts, *ys, own, own, halo, halo, *saved, *returned, *olds]
    return pl.pallas_call(
        functools.partial(encoder_backward, first, batch, len(returned)),
        grid_spec=pltpu.PrefetchScalarGridSpec(
            num_scalar_prefetch=1,
            grid=(groups,),
            in_specs=[
                *[whole(a) for a in consts],
                *[for_core(1, n) for n in (2, 2, 4)],
                slab(0),
                slab(1),
                slab(0),
                slab(1),
                *[row(a) for a in saved],
                *[for_core(0, WIN)] * len(returned),
                *[whole(a) for a in olds[:-1]],
                *[any_spec] * (0 if first else 1),
            ],
            out_specs=[any_spec, any_spec, whole(sums)],
            scratch_shapes=[
                pltpu.VMEM((4 * size, 768), BF16),
                pltpu.VMEM((3, 4 * size, channels), BF16),
                pltpu.VMEM((2, WIN, WIN, rows_z, channels), F32),
                pltpu.SemaphoreType.DMA((2,)),
                pltpu.SemaphoreType.DMA((8 + batches,)),
            ],
        ),
        out_shape=outs,
        input_output_aliases={} if first else {len(args) - 1: 0},
        compiler_params=params,
        cost_estimate=cost(groups * 4 * size, 933888, groups * 4 * size * 9000),
        name="encoder_backward",
    )(*args)


def run_decoder(keep, recv, cot_own, cot_recv, batch, old, consts):
    groups, _, _, packed, _ = keep.shape
    rows_z, channels = cot_own.shape[3:]
    size = 4 * rows_z
    hidden = consts[1].shape[1]
    windows = rows_z // WIN
    first = old is None
    sums = jax.ShapeDtypeStruct((sum_rows(channels, False), hidden), F32)
    slab_shape = jax.ShapeDtypeStruct((groups, 2, 3, packed, LANES_A), BF16)
    outs = [
        *[jax.ShapeDtypeStruct((n, groups * WIN, rows_z, channels), F32) for n in (2, 4, 2)],
        slab_shape,
        slab_shape,
        sums,
    ]

    def slab(unit):
        def place(i):
            return ((i if unit == 1 else (i + 1) % groups), unit, 0, 0, 0)

        return pl.BlockSpec((1, 1, 3, packed, LANES_A), place)

    def cot(unit):
        def place(i):
            return (batch, 0, 2 * i + 1 if unit == 1 else (2 * i + 2) % (2 * groups), 0, 0)

        return pl.BlockSpec((1, 2, 2, rows_z, channels), place)

    def bias_place(i):
        return (i // (groups - 1), 0, 0, 0)

    specs = [whole(a) for a in consts]
    specs[3] = pl.BlockSpec((1, *consts[3].shape[1:]), bias_place)
    olds = [] if first else [old]
    out_slab = pl.BlockSpec((1, 2, 3, packed, LANES_A), lambda i: (i, 0, 0, 0, 0))
    any_spec = pl.BlockSpec(memory_space=pl.ANY)
    return pl.pallas_call(
        functools.partial(decoder, first),
        grid=(groups,),
        in_specs=[
            *specs,
            slab(1),
            slab(0),
            slab(1),
            slab(0),
            cot(1),
            cot(0),
            cot(1),
            cot(0),
            *[whole(a) for a in olds],
        ],
        out_specs=[
            pl.BlockSpec((2, WIN, rows_z, channels), lambda i: (0, i, 0, 0)),
            any_spec,
            any_spec,
            out_slab,
            out_slab,
            whole(sums),
        ],
        scratch_shapes=[
            pltpu.VMEM((windows, CELLS, HEADS * CELLS), F32),
            pltpu.VMEM((4 * size, channels), BF16),
            pltpu.VMEM((4 * size, hidden), BF16),
            pltpu.VMEM((4 * size, hidden), F32),
            pltpu.VMEM((3, 4 * size, channels), F32),
            pltpu.VMEM((2, WIN, WIN, rows_z, channels), F32),
            pltpu.SemaphoreType.DMA((2,)),
            pltpu.SemaphoreType.DMA((2, groups)),
        ],
        out_shape=outs,
        compiler_params=pltpu.CompilerParams(
            dimension_semantics=("arbitrary",),
            vmem_limit_bytes=VMEM_BYTES,
            collective_id=2 + batch,
            has_side_effects=True,
        ),
        cost_estimate=cost(groups * 4 * size, 1253376, groups * 4 * size * 4000),
        name="decoder",
    )(*consts, keep, keep, recv, recv, cot_own, cot_own, cot_recv, cot_recv, *olds)


def body(
    tokens,
    cotangent,
    ln1_gain,
    ln1_bias,
    q_weight,
    q_bias,
    kv_weight,
    v_bias,
    out_weight,
    out_bias,
    rel_table,
    ln2_gain,
    ln2_bias,
    up_weight,
    up_bias,
    down_weight,
    down_bias,
):
    batches, planes, rows_y, rows_z, channels = tokens.shape
    axes = ("section", "tok")
    core = lax.axis_index("section")
    block = lax.axis_index("tok")
    blocks = lax.axis_size("tok")
    is_encoder = core == 0
    core_arg = core.astype(jnp.int32).reshape(1)

    def device(position):
        position = position % (2 * blocks)
        return (position % 2) * blocks + position // 2

    to_previous = [(device(r), device(r - 1)) for r in range(2 * blocks)]
    to_next = [(device(r), device(r + 1)) for r in range(2 * blocks)]

    weights_e, vectors_e, bias_e, weights_d, vectors_d, bias_d = run_prepare(
        blocks,
        (q_weight[0], out_weight[0], up_weight[0], down_weight[0].T),
        (ln1_gain, ln1_bias, ln2_gain, ln2_bias, out_bias, down_bias, q_bias, up_bias),
        rel_table[0],
        kv_weight,
        v_bias[None],
    )
    order = jnp.asarray(order_matrix(rows_z, 0), BF16)
    order_rolled = jnp.asarray(order_matrix(rows_z, 1), BF16)

    enc_consts = (order, weights_e, vectors_e, bias_e)
    enc_back_consts = (order, weights_e, vectors_e)
    dec_consts = (order_rolled, weights_d, vectors_d, bias_d)

    handed, saved = [], []
    for batch in range(batches):
        send, keep, *rest = run_encoder(
            core_arg, tokens, batch, enc_consts, cotangent if batch == 0 else None
        )
        if batch == 0:
            *rest, cot_first, cot_own = rest
            cot_recv = lax.ppermute(cot_first, axes, to_previous)
        handed.append((keep, lax.ppermute(send, axes, to_previous)))
        saved.append(rest)
    dec_sums = None
    returned, ys = [], []
    to_encoder = [(blocks + t, t) for t in range(blocks)]
    for batch in range(batches):
        y_own, y_sib, y_halo, own, halo, dec_sums = run_decoder(
            *handed[batch], cot_own, cot_recv, batch, dec_sums, dec_consts
        )
        returned.append((own, lax.ppermute(halo, axes, to_next)))
        ys.append((y_own, y_halo, y_sib))
    old = None
    backs = []
    for batch in range(batches):
        arrived = backs[:1] if batch == batches - 1 else []
        ends, back, enc_sums = run_encoder_back(
            core_arg, batch, *returned[batch], ys[batch], arrived, saved[batch], old,
            enc_back_consts, tokens,
        )
        old = (ends, enc_sums)
        backs.append(lax.ppermute(back, axes, to_encoder))

    layout = Layout(channels, up_weight.shape[2], blocks)
    total, sib_kv = run_sum(enc_sums, dec_sums, layout, blocks)
    (
        ends, g_ln1_gain, g_ln1_bias, g_q_weight, g_q_bias, g_kv_weight, g_v_bias, g_out_weight,
        g_out_bias, g_table, g_ln2_gain, g_ln2_bias, g_up_weight, g_up_bias, g_down_weight, g_down_bias,
    ) = run_finish(core_arg, total, sib_kv, backs[1:], ends, layout)
    return (
        ends[None],
        g_ln1_gain,
        g_ln1_bias,
        g_q_weight[None],
        g_q_bias,
        g_kv_weight[None],
        g_v_bias,
        g_out_weight[None],
        g_out_bias,
        g_table.transpose(1, 0, 2),
        g_ln2_gain,
        g_ln2_bias,
        g_up_weight[None],
        g_up_bias,
        g_down_weight.T[None],
        g_down_bias,
    )


def solution(mesh):
    in_specs = (
        P(None, "tok", None, None, None),
        P(None, "tok", None, None, None),
        P("section", None),
        P("section", None),
        P("section", None, None),
        P("section", None),
        P(),
        P(),
        P("section", None, None),
        P("section", None),
        P("section", None, None),
        P("section", None),
        P("section", None),
        P("section", None, None),
        P("section", None),
        P("section", None, None),
        P("section", None),
    )
    out_specs = (
        P("section", None, "tok", None, None, None),
        P("section", None),
        P("section", None),
        P("section", None, None),
        P("section", None),
        P("section", None, None),
        P("section", None),
        P("section", None, None),
        P("section", None),
        P("section", None, None),
        P("section", None),
        P("section", None),
        P("section", None, None),
        P("section", None),
        P("section", None, None),
        P("section", None),
    )
    return jax.shard_map(body, mesh=mesh, in_specs=in_specs, out_specs=out_specs, check_vma=False)
```

```python
import functools

import jax
import jax.numpy as jnp
import numpy as np
from jax import lax
from jax.experimental import pallas as pl
from jax.experimental.pallas import tpu as pltpu
from jax.sharding import PartitionSpec as P

HEADS = 6
HD = 32
WIN = 4
SHIFT = 2
CELLS = WIN**3
SPAN = 2 * WIN - 1
HEADS_A = 4
LANES_A = HEADS_A * HD
COLS_A = HEADS_A * CELLS

eps_norm = 1e-05
mask_fill = -100.0
log2_e = 1.4426950408889634
root_half = 0.7071067811865476
inv_root_two_pi = 0.3989422804014327
scale = HD ** (-0.5)
VMEM_BYTES = 63 * 1024 * 1024

F32 = jnp.float32
BF16 = jnp.bfloat16


def nn(left, right):
    return lax.dot_general(left, right, (((1,), (0,)), ((), ())), preferred_element_type=F32)


def nt(left, right):
    return lax.dot_general(left, right, (((1,), (1,)), ((), ())), preferred_element_type=F32)


def tn(left, right):
    return lax.dot_general(left, right, (((0,), (0,)), ((), ())), preferred_element_type=F32)


def order_matrix(rows_z, rolled):
    count = 4 * rows_z
    matrix = np.zeros((count, count), np.float32)
    units = rows_z // 2
    for unit in range(units):
        for dx in range(2):
            for dy in range(2):
                for dz in range(2):
                    z = (2 * (unit + rolled) + dz) % rows_z
                    matrix[unit * 8 + dx * 4 + dy * 2 + dz, (dx * 2 + dy) * rows_z + z] = 1.0
    return matrix


def windows_of(pieces):
    count, rows, channels = pieces.shape
    return pieces.reshape(count, rows // 16, 16, channels).transpose(1, 0, 2, 3).reshape(-1, channels)


def pieces_of(windows):
    rows, channels = windows.shape
    return (
        windows.reshape(rows // CELLS, 4, 16, channels)
        .transpose(1, 0, 2, 3)
        .reshape(4, rows // 4, channels)
    )


def roll_rows(pieces, steps):
    return jnp.concatenate([pieces[:, steps:], pieces[:, :steps]], 1)


def pack_slab(pieces):
    half = pieces.shape[1] // 2
    rest = pieces[:, :, LANES_A:]
    return jnp.concatenate(
        [pieces[:, :, :LANES_A], jnp.concatenate([rest[:, :half], rest[:, half:]], 2)], 1
    ).astype(BF16)


def unpack_slab(block):
    size = block.shape[0] * 2 // 3
    half = LANES_A // 2
    rest = jnp.concatenate([block[size:, :half], block[size:, half:]], 0)
    return jnp.concatenate([block[:size], rest], 1)


def normalize(rows):
    mean = jnp.mean(rows, -1, keepdims=True)
    centered = rows - mean
    inv_std = lax.rsqrt(jnp.mean(centered * centered, -1, keepdims=True) + eps_norm)
    return centered * inv_std, inv_std


def norm_back(grad_rows, unit_rows, inv_std, gain):
    scaled = grad_rows * gain
    return inv_std * (
        scaled
        - jnp.mean(scaled, -1, keepdims=True)
        - unit_rows * jnp.mean(scaled * unit_rows, -1, keepdims=True)
    )


def gelu_pair(rows):
    upper = 0.5 * lax.erf(rows * root_half) + 0.5
    bell = jnp.exp2(rows * rows * (-0.5 * log2_e))
    return rows * upper, upper + rows * bell * inv_root_two_pi


def head_masks(width):
    heads = lax.broadcasted_iota(jnp.int32, (1, width), 1) // HD
    return [jnp.where(heads == h, 1.0, 0.0).astype(BF16) for h in range(width // HD)]


def expand(rows):
    masks = head_masks(rows.shape[1])
    return jnp.concatenate([rows * mask for mask in masks], 0)


def collapse(stacked):
    width = stacked.shape[1]
    lanes = lax.broadcasted_iota(jnp.int32, (CELLS, width), 1)
    total = stacked[:CELLS]
    for h in range(1, width // HD):
        total = jnp.where(lanes >= h * HD, stacked[h * CELLS : (h + 1) * CELLS], total)
    return total


def split(rows):
    return rows[:, :LANES_A], rows[:, LANES_A:]


def attend(parts, bias):
    queries, keys, values = zip(*[[split(rows) for rows in part] for part in parts])
    wide = [[expand(half) for half in q] for q in queries]
    scores = [
        jnp.concatenate([nt(k[0], q[0]), nt(k[1], q[1])], 1) for k, q in zip(keys, wide)
    ]
    scores = [s * (scale * log2_e) + b for s, b in zip(scores, bias)]
    exponents = [jnp.exp2(s - jnp.max(s, 0, keepdims=True)) for s in scores]
    probs = [e * (1.0 / jnp.sum(e, 0, keepdims=True)) for e in exponents]
    low = [p.astype(BF16) for p in probs]
    mixed = [
        (tn(p[:, :COLS_A], v[0]), tn(p[:, COLS_A:], v[1])) for p, v in zip(low, values)
    ]
    mixed = [jnp.concatenate([collapse(m[0]), collapse(m[1])], 1).astype(BF16) for m in mixed]
    return mixed, probs


def attend_back(parts):
    queries, keys, values, grads = zip(
        *[[split(rows) for rows in part[:3] + part[4:]] for part in parts]
    )
    probs = [part[3] for part in parts]
    wide_g = [[expand(half) for half in g] for g in grads]
    d_probs = [
        jnp.concatenate([nt(v[0], g[0]), nt(v[1], g[1])], 1) for v, g in zip(values, wide_g)
    ]
    low = [part[3].astype(BF16) for part in parts]
    d_values = [
        jnp.concatenate([nn(p[:, :COLS_A], g[0]), nn(p[:, COLS_A:], g[1])], 1)
        for p, g in zip(low, wide_g)
    ]
    wide_q = [[expand(half) for half in q] for q in queries]
    d_scores = [
        p * (d - jnp.sum(d * p, 0, keepdims=True)) for p, d in zip(probs, d_probs)
    ]
    low_d = [d.astype(BF16) for d in d_scores]
    d_keys = [
        jnp.concatenate([nn(d[:, :COLS_A], q[0]), nn(d[:, COLS_A:], q[1])], 1) * scale
        for d, q in zip(low_d, wide_q)
    ]
    d_queries = [
        (tn(d[:, :COLS_A], k[0]), tn(d[:, COLS_A:], k[1])) for d, k in zip(low_d, keys)
    ]
    d_queries = [
        jnp.concatenate([collapse(d[0]), collapse(d[1])], 1) * scale for d in d_queries
    ]
    table = d_scores[0]
    for d in d_scores[1:]:
        table = table + d
    return d_queries, d_keys, d_values, table


def window_groups(count):
    return [range(k, min(k + TOGETHER, count)) for k in range(0, count, TOGETHER)]


def window_rows(k):
    return slice(k * CELLS, (k + 1) * CELLS)


def with_ones(rows):
    return jnp.concatenate([rows.T, jnp.ones((16, rows.shape[0]), BF16)], 0)


def col_sum(rows):
    return jnp.sum(rows, 0, keepdims=True)


def start_sums(old, new):
    @pl.when(pl.program_id(0) == 0)
    def _():
        new[...] = jnp.zeros_like(new) if old is None else old[...]


def restore(matrix, rows):
    high = rows.astype(BF16)
    low = (rows - high.astype(F32)).astype(BF16)
    return tn(matrix, high) + tn(matrix, low)


CHUNK = 256
BLOCK = 256
TOGETHER = 8


class View:
    def __init__(self, ref, row, rows, col, cols):
        self.ref, self.row, self.col, self.shape = ref, row, col, (rows, cols)

    def place(self, key):
        key = (slice(None), slice(None)) if key is Ellipsis else key
        key = key if isinstance(key, tuple) else (key, slice(None))
        return tuple(
            slice(start + part.indices(size)[0], start + part.indices(size)[1])
            for part, start, size in zip(key, (self.row, self.col), self.shape)
        )

    def __getitem__(self, key):
        return self.ref[self.place(key)]

    def __setitem__(self, key, value):
        self.ref[self.place(key)] = value

    def first_columns(self, cols):
        return View(self.ref, self.row, self.shape[0], self.col, cols)


def layer_views(weights, vectors):
    hidden = weights.shape[1]
    channels = weights.shape[0] // 4
    q_cols = 768

    def rows(k, cols):
        return View(weights, k * channels, channels, 0, cols)

    return (
        View(vectors, 0, 8, 0, channels),
        View(vectors, 8, 1, 0, hidden),
        View(vectors, 9, 1, 0, q_cols),
        rows(0, hidden),
        rows(1, hidden),
        rows(2, q_cols),
        rows(3, channels),
    )


def sum_rows(channels, encoder):
    tall = channels + 16
    return 2 * tall + channels + (tall if encoder else 0)


def sum_views(sums, channels, encoder):
    tall = channels + 16
    base = tall + channels

    def view(row, rows, col, cols):
        return View(sums, row, rows, col, cols)

    fields = [view(base, tall, 256 * k, channels) for k in range(3 if encoder else 2)]
    last = base + (tall if encoder else 0)
    side = 256 if encoder else 512
    out = view(last, tall, 0, channels) if encoder else fields[1]
    bias = (view(last, CELLS, side, COLS_A), view(last + CELLS, CELLS, side, 2 * CELLS))
    vec = view(last + 2 * CELLS, 8, side, channels)
    return (
        view(0, tall, 0, sums.shape[1]),
        view(tall, channels, 0, sums.shape[1]),
        fields[:3] if encoder else fields[:1],
        out,
        vec,
        bias,
    )


def add_bias(views, table):
    views[0][...] += table[:, :COLS_A]
    views[1][...] += table[:, COLS_A:]


def encoder_forward(cuts, core_ref, tok, order, weights, vectors, bias, *rest):
    vec, b_up, b_qkv, w_up, w_down, w_qkv, w_out = layer_views(weights, vectors)
    cut_in, rest = rest[:cuts], rest[cuts:]
    send, keep, wide_out, low_out, *cut_out, qkv = rest
    hidden_cols = w_up.shape[1]
    s_start, p_start, o_start = hidden_cols, 2 * hidden_cols, 2 * hidden_cols + HEADS * CELLS
    for source, target in zip(cut_in, cut_out):
        target[...] = source[...]
    rows_z = tok.shape[3]
    size = 4 * rows_z
    pieces = []
    for x in range(2):
        for y in range(2):
            part = tok[0, 2 * x : 2 * x + 2, 2 * y : 2 * y + 2].reshape(size, -1)
            pieces.append(nn(order[...], part))
    entry = windows_of(jnp.stack(pieces))
    unit, inv_std = normalize(entry)
    channels = entry.shape[1]
    wide = jnp.broadcast_to(inv_std, (entry.shape[0], 256 - channels))
    wide_out[0, :, :channels] = unit
    wide_out[0, :, channels:256] = wide
    left = (unit * vec[0:1] + vec[1:2]).astype(BF16)
    triple = nn(left, w_qkv[...]) + b_qkv[...]
    qkv[...] = triple.astype(BF16)
    for together in window_groups(entry.shape[0] // CELLS):
        parts = [
            [qkv[window_rows(k), 256 * f : 256 * f + 192] for f in range(3)] for k in together
        ]
        mixed, probs = attend(parts, [bias[...]] * len(parts))
        for k, o, p in zip(together, mixed, probs):
            low_out[0, window_rows(k), p_start:o_start] = p.astype(BF16)
            low_out[0, window_rows(k), o_start : o_start + channels] = o
    mixed = low_out[0, :, o_start : o_start + channels]
    middle = entry + nn(mixed, w_out[...]) + vec[4:5]
    unit, inv_std = normalize(middle)
    wide = jnp.broadcast_to(inv_std, (entry.shape[0], 256 - channels))
    wide_out[0, :, 256 : 256 + channels] = unit
    wide_out[0, :, 256 + channels :] = wide
    left = (unit * vec[2:3] + vec[3:4]).astype(BF16)
    results = []
    for k in range(entry.shape[0] // CHUNK):
        rows = slice(k * CHUNK, (k + 1) * CHUNK)
        hidden, slope = gelu_pair(nn(left[rows], w_up[...]) + b_up[...])
        hidden = hidden.astype(BF16)
        low_out[0, rows, :s_start] = hidden
        low_out[0, rows, s_start:p_start] = slope.astype(BF16)
        results.append(nt(hidden, w_down[...]))
    result = middle + jnp.concatenate(results, 0) + vec[5:6]
    for field, rows in enumerate((result, triple[:, 256:448], triple[:, 512:704])):
        rolled = pack_slab(roll_rows(pieces_of(rows), 8))
        send[0, :, field] = rolled[:2]
        keep[0, :, field] = rolled[2:]


def run_together(*works):
    works = list(works)
    while works:
        for work in list(works):
            try:
                next(work)
            except StopIteration:
                works.remove(work)


def row_blocks(count, size):
    return [slice(k, k + size) for k in range(0, count, size)]


def norm_back_steps(rows_grad, base, unit, inv_std, gain, g_vec, row, results):
    sums = [None, None]
    for rows in row_blocks(base.shape[0], BLOCK):
        grad = rows_grad(rows)
        found = (col_sum(grad * unit[rows]), col_sum(grad))
        sums = [f if total is None else total + f for f, total in zip(found, sums)]
        results.append(base[rows] + norm_back(grad, unit[rows], inv_std[rows], gain))
        yield
    g_vec[row : row + 1] += sums[0]
    g_vec[row + 1 : row + 2] += sums[1]


def product_steps(products):
    for target, cols, left, right in products:
        target[:, cols] += nn(left, right)
        yield


def mlp_back(grad, grad_low, hidden, slope, left_two, unit, inv_std, w_up, w_down, vec, sums):
    g_up, g_down, g_vec = sums
    backs, pres = [], []
    for rows in row_blocks(grad.shape[0], CHUNK):
        d_pre = (nn(grad_low[rows], w_down[...]) * slope(rows)).astype(BF16)
        pres.append(d_pre)
        backs.append(nt(d_pre, w_up[...]))
    d_pre = jnp.concatenate(pres, 0)
    d_normed = jnp.concatenate(backs, 0)
    ones, turned = with_ones(left_two), grad_low.T
    tiles = row_blocks(w_up.shape[1], 256)
    products = [(g_up, cols, ones, d_pre[:, cols]) for cols in tiles]
    products += [(g_down, cols, turned, hidden[:, cols]) for cols in tiles]
    results = []
    run_together(
        norm_back_steps(
            lambda rows: d_normed[rows], grad, unit, inv_std, vec[2:3], g_vec, 2, results
        ),
        product_steps(products),
    )
    g_vec[4:5] += col_sum(grad)
    return jnp.concatenate(results, 0)


def start_all(copies):
    for copy in copies:
        copy.start()


def wait_all(copies):
    for copy in copies:
        copy.wait()


def encoder_backward(
    first, batch, returns, core_ref, order, weights, vectors,
    y_own, y_halo, y_sib,
    keep_a, keep_b, recv_a, recv_b,
    wide_in, low_in, *rest,
):
    vec, _, b_qkv, w_up, w_down, w_qkv, w_out = layer_views(weights, vectors)
    channels, hidden_cols = w_up.shape
    s_start, p_start, o_start = hidden_cols, 2 * hidden_cols, 2 * hidden_cols + HEADS * CELLS
    returned, rest = rest[:returns], rest[returns:]
    old, rest = (None, rest) if first else (rest[0], rest[2:])
    ends, back, sums, qkv, dqkv, buffer, out_sem, copy_sem = rest
    g_up, g_down, g_fields, g_out, g_vec, g_bias = sum_views(sums, channels, True)
    step, steps = pl.program_id(0), pl.num_programs(0)
    is_encoder = core_ref[0] == 0
    rows_y = ends.shape[2]
    slot = lax.rem(step, 2)

    def output_copies():
        copies = []
        for start, planes, ref in ((0, 2, y_halo), (2, 4, y_sib), (6, 2, y_own)):
            for half in range(2):
                rows = pl.ds(lax.rem(step * WIN + SHIFT + 2 * half, rows_y), 2)
                target = ends.at[batch, pl.ds(start, planes), rows]
                copies.append((ref.at[:, pl.ds(2 * half, 2)], target))
        return [
            pltpu.make_async_copy(source, target, copy_sem.at[k])
            for k, (source, target) in enumerate(copies)
        ]

    def gradient_copies():
        return [
            pltpu.make_async_copy(
                ref, ends.at[k, pl.ds(WIN, WIN), pl.ds(step * WIN, WIN)], copy_sem.at[8 + k]
            )
            for k, ref in enumerate(returned)
        ]

    def result_copy(index, to_ends):
        target = (
            ends.at[batch, pl.ds(0, WIN), pl.ds(index * WIN, WIN)]
            if to_ends
            else back.at[:, pl.ds(index * WIN, WIN)]
        )
        at = lax.rem(index, 2)
        return pltpu.make_async_copy(buffer.at[at], target, out_sem.at[at])

    def for_core(encoder_work, decoder_work):
        pl.when(is_encoder)(encoder_work)
        pl.when(jnp.logical_not(is_encoder))(decoder_work)

    for_core(lambda: start_all(gradient_copies()), lambda: start_all(output_copies()))

    @pl.when(step >= 2)
    def _():
        for_core(
            lambda: result_copy(step - 2, True).wait(), lambda: result_copy(step - 2, False).wait()
        )

    start_sums(old, sums)
    fields = []
    for field in range(3):
        pieces = jnp.stack(
            [unpack_slab(ref[0, 0, field]) for ref in (recv_b, recv_a, keep_b, keep_a)]
        )
        fields.append(windows_of(pieces))
    grad_low, d_key_1, d_value_1 = fields
    grad = grad_low.astype(F32)
    unit_1, unit_2 = wide_in[0, :, :channels], wide_in[0, :, 256 : 256 + channels]
    wide_1, wide_2 = [wide_in[0, :, k + channels : k + channels + 1] for k in (0, 256)]
    left_1 = (unit_1 * vec[0:1] + vec[1:2]).astype(BF16)
    left_2 = (unit_2 * vec[2:3] + vec[3:4]).astype(BF16)
    qkv[...] = (nn(left_1, w_qkv[...]) + b_qkv[...]).astype(BF16)
    d_middle = mlp_back(
        grad, grad_low, low_in[0, :, :s_start], lambda rows: low_in[0, rows, s_start:p_start].astype(F32),
        left_2, unit_2, wide_2, w_up, w_down, vec,
        (g_up, g_down, g_vec),
    )
    branch = d_middle.astype(BF16)
    d_mixed = nt(branch, w_out[...]).astype(BF16)
    d_table = None
    for together in window_groups(grad.shape[0] // CELLS):
        parts = [
            [qkv[window_rows(k), 256 * f : 256 * f + 192] for f in range(3)]
            + [low_in[0, window_rows(k), p_start:o_start].astype(F32), d_mixed[window_rows(k)]]
            for k in together
        ]
        *d_qkv, d_s = attend_back(parts)
        for k, d_q, d_k, d_v in zip(together, *d_qkv):
            rows = window_rows(k)
            dqkv[0, rows] = d_q.astype(BF16)
            dqkv[1, rows] = (d_k + d_key_1[rows].astype(F32)).astype(BF16)
            dqkv[2, rows] = (d_v + d_value_1[rows].astype(F32)).astype(BF16)
        d_table = d_s if d_table is None else d_table + d_s
    add_bias(g_bias, d_table)
    ones = with_ones(left_1)
    every = slice(None)
    mixed = with_ones(low_in[0, :, o_start : o_start + channels])
    products = [(g_field, every, ones, dqkv[k]) for k, g_field in enumerate(g_fields)]
    products.append((g_out, every, mixed, branch))

    def rows_grad(rows):
        parts = [
            nt(dqkv[k, rows], w_qkv[:, 256 * k : 256 * k + channels]) for k in range(3)
        ]
        return parts[0] + parts[1] + parts[2]

    results = []
    run_together(
        norm_back_steps(rows_grad, d_middle, unit_1, wide_1, vec[0:1], g_vec, 0, results),
        product_steps(products),
    )
    result = pieces_of(jnp.concatenate(results, 0))
    rows_z = ends.shape[3]
    for x in range(2):
        for y in range(2):
            part = restore(order[...], result[2 * x + y])
            buffer[slot, 2 * x : 2 * x + 2, 2 * y : 2 * y + 2] = part.reshape(2, 2, rows_z, -1)
    for_core(lambda: result_copy(step, True).start(), lambda: result_copy(step, False).start())

    @pl.when(step == steps - 1)
    def _():
        def finish(to_ends):
            result_copy(step - 1, to_ends).wait()
            result_copy(step, to_ends).wait()

        for_core(lambda: finish(True), lambda: finish(False))

    for_core(lambda: wait_all(gradient_copies()), lambda: wait_all(output_copies()))


def decoder(
    first, core_ref, order, weights, vectors, bias,
    keep_1, keep_0, recv_1, recv_0, cot_1, cot_0, cot_r1, cot_r0, *rest,
):
    vec, b_up, b_qkv, w_up, w_down, w_qkv, w_out = layer_views(weights, vectors)
    channels = w_up.shape[0]
    w_q, b_q = w_qkv.first_columns(channels), b_qkv.first_columns(channels)
    old, new = (None, rest) if first else (rest[0], rest[1:])
    out_all, out_tail, own, halo, sums, p_scr, o_scr, a_scr, s_scr, dqkv = new
    g_up, g_down, (g_q,), g_out, g_vec, g_bias = sum_views(sums, channels, False)
    start_sums(old, sums)
    fields = []
    for field in range(3):
        pieces = jnp.stack([unpack_slab(ref[0, 0, field]) for ref in (keep_1, keep_0, recv_1, recv_0)])
        fields.append(windows_of(pieces))
    entry_low, keys, values = fields
    entry = entry_low.astype(F32)
    unit_1, inv_1 = normalize(entry)
    left_1 = (unit_1 * vec[0:1] + vec[1:2]).astype(BF16)
    queries = (nn(left_1, w_q[...]) + b_q[...]).astype(BF16)
    windows = entry.shape[0] // CELLS
    for together in window_groups(windows):
        parts = [[rows[window_rows(k)] for rows in (queries, keys, values)] for k in together]
        mixed, probs = attend(parts, [bias[0, 1 if k == windows - 1 else 0] for k in together])
        for k, o, p in zip(together, mixed, probs):
            p_scr[k] = p
            o_scr[window_rows(k)] = o
    middle = entry + nn(o_scr[...], w_out[...]) + vec[4:5]
    unit_2, inv_2 = normalize(middle)
    left_2 = (unit_2 * vec[2:3] + vec[3:4]).astype(BF16)
    results = []
    for k in range(entry.shape[0] // CHUNK):
        rows = slice(k * CHUNK, (k + 1) * CHUNK)
        hidden, slope = gelu_pair(nn(left_2[rows], w_up[...]) + b_up[...])
        hidden = hidden.astype(BF16)
        a_scr[rows] = hidden
        s_scr[rows] = slope
        results.append(nt(hidden, w_down[...]))
    result = pieces_of(middle + jnp.concatenate(results, 0) + vec[5:6])
    rows_z = out_all.shape[2]
    size = 4 * rows_z
    for x in range(2):
        for y in range(2):
            part = restore(order[...], result[2 * x + y]).reshape(2, 2, rows_z, -1)
            out_all[2 * x : 2 * x + 2, 2 * y : 2 * y + 2] = part
            if x == 1:
                out_tail[:, 2 * y : 2 * y + 2] = part

    cots = [
        nn(order[...], ref[0].reshape(size, -1)).astype(BF16) for ref in (cot_1, cot_0, cot_r1, cot_r0)
    ]
    grad_low = windows_of(jnp.stack(cots))
    grad = grad_low.astype(F32)
    d_middle = mlp_back(
        grad, grad_low, a_scr[...], lambda rows: s_scr[rows], left_2, unit_2, inv_2, w_up, w_down, vec,
        (g_up, g_down, g_vec),
    )
    branch = d_middle.astype(BF16)
    d_mixed = nt(branch, w_out[...]).astype(BF16)
    d_table = None
    for together in window_groups(windows):
        parts = [
            [rows[window_rows(k)] for rows in (queries, keys, values)]
            + [p_scr[k], d_mixed[window_rows(k)]]
            for k in together
        ]
        *d_qkv, d_s = attend_back(parts)
        for k, *grads in zip(together, *d_qkv):
            for f in range(3):
                dqkv[f, window_rows(k)] = grads[f]
        d_table = d_s if d_table is None else d_table + d_s
    add_bias(g_bias, d_table)
    d_queries = dqkv[0].astype(BF16)
    every = slice(None)
    products = [
        (g_q, every, with_ones(left_1), d_queries),
        (g_out, every, with_ones(o_scr[...]), branch),
    ]
    results = []
    run_together(
        norm_back_steps(
            lambda rows: nt(d_queries[rows], w_q[...]), d_middle, unit_1, inv_1, vec[0:1], g_vec, 0,
            results,
        ),
        product_steps(products),
    )
    d_entry = jnp.concatenate(results, 0)
    for field, rows in enumerate((d_entry, dqkv[1], dqkv[2])):
        turned = pack_slab(roll_rows(pieces_of(rows), size - 8))
        own[0, :, field] = turned[:2]
        halo[0, :, field] = turned[2:]


def whole(array):
    zeros = (0,) * array.ndim
    return pl.BlockSpec(array.shape, lambda *_: zeros)


def cost(cells, per_cell, hbm):
    return pl.CostEstimate(
        flops=2 * cells * per_cell, bytes_accessed=hbm, transcendentals=cells * 1536
    )


params = pltpu.CompilerParams(
    dimension_semantics=("arbitrary",), vmem_limit_bytes=VMEM_BYTES
)


class Layout:
    def __init__(self, channels, hidden, blocks):
        tall = channels + 16
        self.tall, self.channels = tall, channels
        self.tiles = hidden // LANES_A
        self.up = 0
        self.down = self.tiles * tall
        self.q = self.down + self.tiles * channels
        self.out = self.q + tall
        self.rest = self.out + tall
        self.kv = self.rest + tall
        self.bias = self.kv + 2 * tall
        self.vec = self.bias + HEADS * CELLS // LANES_A * CELLS
        self.end = self.vec + 16
        units = -(-self.end // (16 * blocks))
        self.chunks = (units // 2 * 16, (units - units // 2) * 16)
        self.starts = (0, self.chunks[0] * blocks)
        self.rows = units * 16 * blocks


def fill(buffer, layout, up, down, q, out, kv, bias, vec):
    kind, half = buffer.dtype, LANES_A // 2
    tall, channels = layout.tall, layout.channels
    for k in range(layout.tiles):
        cols = slice(k * LANES_A, (k + 1) * LANES_A)
        buffer[layout.up + k * tall : layout.up + (k + 1) * tall] = up[:, cols].astype(kind)
        buffer[layout.down + k * channels : layout.down + (k + 1) * channels] = down[
            :, cols
        ].astype(kind)
    buffer[layout.q : layout.q + tall] = q[:, :LANES_A].astype(kind)
    buffer[layout.out : layout.out + tall] = out[:, :LANES_A].astype(kind)
    rests = jnp.concatenate([q[:, LANES_A:], out[:, LANES_A:]], 1)
    buffer[layout.rest : layout.rest + tall] = rests.astype(kind)
    buffer[layout.kv : layout.kv + tall] = kv[:, :LANES_A].astype(kind)
    rests = jnp.concatenate([kv[:, LANES_A:], jnp.zeros((tall, half), F32)], 1)
    buffer[layout.kv + tall : layout.kv + 2 * tall] = rests.astype(kind)
    tiles = [bias[0][:, :LANES_A], bias[0][:, LANES_A:], bias[1][...]]
    for k, tile in enumerate(tiles):
        start = layout.bias + k * CELLS
        buffer[start : start + CELLS] = tile.astype(kind)
    rests = jnp.concatenate([vec[:, LANES_A:], jnp.zeros((8, half), F32)], 1)
    both = jnp.concatenate([vec[:, :LANES_A], rests], 0)
    buffer[layout.vec : layout.vec + 16] = both.astype(kind)
    if layout.rows > layout.end:
        buffer[layout.end :] = jnp.zeros((layout.rows - layout.end, LANES_A), kind)


MESH = pl.DeviceIdType.MESH


def groups_of(blocks):
    near = 4 if blocks % 4 == 0 else blocks
    return near, blocks // near


def sum_gradients(layout, blocks, *refs):
    (
        enc_in, dec_in, total_out, kv_out,
        enc, dec, own, theirs, from_sib, low, total, sib_kv, landed_0, landed_1, near_low_0, near_low_1,
        far_landed_0, far_landed_1, load_sem, sib_send, sib_recv, send_sem, recv_sem,
    ) = refs
    landed, near_low = (landed_0, landed_1), (near_low_0, near_low_1)
    far_landed = (far_landed_0, far_landed_1)
    core, me = lax.axis_index("section"), lax.axis_index("tok")
    sibling = {"section": 1 - core}
    near, far = groups_of(blocks)
    inner, outer = lax.rem(me, near), lax.div(me, near)

    def near_peer(offset):
        return lax.rem(inner + offset, near)

    def far_peer(offset):
        return lax.rem(outer + offset, far)

    def near_device(offset):
        return {"tok": outer * near + near_peer(offset)}

    def far_device(offset):
        return {"tok": far_peer(offset) * near + inner}

    def each(count, work):
        def run(offset, carry):
            work(offset)
            return carry

        lax.fori_loop(1, count, run, 0)

    enc_load = pltpu.make_async_copy(enc_in, enc, load_sem.at[0])
    dec_load = pltpu.make_async_copy(dec_in, dec, load_sem.at[1])
    enc_load.start()
    dec_load.start()
    barrier = pltpu.get_barrier_semaphore()
    pl.semaphore_signal(barrier, inc=1, device_id=sibling, device_id_type=MESH)
    for count, device in ((near, near_device), (far, far_device)):
        each(
            count,
            lambda offset, device=device: pl.semaphore_signal(
                barrier, inc=1, device_id=device(offset), device_id_type=MESH
            ),
        )
    enc_load.wait()
    dec_load.wait()
    channels = layout.channels
    e_up, e_down, (e_q, e_k, e_v), e_out, e_vec, e_bias = sum_views(enc, channels, True)
    d_up, d_down, (d_q,), d_out, d_vec, d_bias = sum_views(dec, channels, False)

    def fill_enc(buffer, kv):
        fill(buffer, layout, e_up, e_down, e_q, e_out, kv, e_bias, e_vec)

    def fill_dec(buffer, kv):
        fill(buffer, layout, d_up, d_down, d_q, d_out, kv, d_bias, d_vec)

    pl.when(core == 0)(lambda: fill_dec(theirs, e_v))
    pl.when(core == 1)(lambda: fill_enc(theirs, e_k))
    pl.semaphore_wait(barrier, near + far - 1)

    def to_sibling(source, target, k):
        return pltpu.make_async_remote_copy(
            src_ref=source, dst_ref=target, send_sem=sib_send.at[k], recv_sem=sib_recv.at[k],
            device_id=sibling, device_id_type=MESH,
        )

    def piece_rows(p):
        return slice(layout.starts[p], layout.starts[p] + layout.chunks[p] * blocks)

    swaps = [to_sibling(theirs.at[piece_rows(p)], from_sib.at[piece_rows(p)], p) for p in range(2)]
    start_all(swaps)
    pl.when(core == 0)(lambda: fill_enc(own, e_k))
    pl.when(core == 1)(lambda: fill_dec(own, e_v))

    def quarter_of(p, position):
        size = far * layout.chunks[p]
        return pl.ds(pl.multiple_of(layout.starts[p] + position * size, 16), size)

    def chunk_of(p, position):
        return pl.ds(pl.multiple_of(position * layout.chunks[p], 16), layout.chunks[p])

    def rows_of(p, position):
        start = layout.starts[p] + (inner * far + position) * layout.chunks[p]
        return pl.ds(pl.multiple_of(start, 16), layout.chunks[p])

    def exchange(p, stage, offset, source, target, device):
        return pltpu.make_async_remote_copy(
            src_ref=source, dst_ref=target,
            send_sem=send_sem.at[p, stage, offset], recv_sem=recv_sem.at[p, stage, offset],
            device_id=device(offset), device_id_type=MESH,
        )

    def near_scatter(p, offset):
        source = low.at[quarter_of(p, near_peer(offset))]
        return exchange(p, 0, offset, source, landed[p].at[offset], near_device)

    def far_scatter(p, offset):
        source = near_low[p].at[chunk_of(p, far_peer(offset))]
        return exchange(p, 1, offset, source, far_landed[p].at[offset], far_device)

    def far_gather(p, offset, owner):
        rows = rows_of(p, owner)
        return exchange(p, 2, offset, total.at[rows], total.at[rows], far_device)

    def near_gather(p, offset, owner):
        rows = quarter_of(p, owner)
        return exchange(p, 3, offset, total.at[rows], total.at[rows], near_device)

    def reduced(count, copy, landing, start):
        def add(offset, carry):
            copy(offset).wait_recv()
            return carry + landing[offset].astype(F32)

        return lax.fori_loop(1, count, add, start)

    def send_near(p):
        swaps[p].wait()
        rows = piece_rows(p)
        own[rows] += from_sib[rows].astype(F32)
        low[rows] = own[rows].astype(BF16)
        each(near, lambda offset: near_scatter(p, offset).start())

    def send_far(p):
        rows = quarter_of(p, inner)
        near_sum = reduced(near, lambda o: near_scatter(p, o), landed[p], own[rows])
        own[rows] = near_sum
        near_low[p][...] = near_sum.astype(BF16)
        each(far, lambda offset: far_scatter(p, offset).start())

    def return_far(p):
        rows = rows_of(p, outer)
        far_sum = reduced(far, lambda o: far_scatter(p, o), far_landed[p], own[rows])
        total[rows] = far_sum.astype(BF16)
        each(far, lambda offset: far_gather(p, offset, outer).start())

    def return_near(p):
        each(far, lambda o: far_gather(p, o, lax.rem(outer + far - o, far)).wait_recv())
        each(near, lambda offset: near_gather(p, offset, inner).start())

    def arrive(p):
        each(near, lambda o: near_gather(p, o, lax.rem(inner + near - o, near)).wait_recv())

    send_near(0)
    send_near(1)
    send_far(0)
    return_far(0)
    send_far(1)
    return_near(0)
    return_far(1)
    return_near(1)
    arrive(0)
    arrive(1)
    third = to_sibling(total.at[layout.kv : layout.kv + 2 * layout.tall], sib_kv, 2)
    third.start()
    total_out[...] = total[...]
    for p in range(2):
        each(near, lambda offset, p=p: near_scatter(p, offset).wait_send())
        each(far, lambda offset, p=p: far_scatter(p, offset).wait_send())
        each(far, lambda offset, p=p: far_gather(p, offset, outer).wait_send())
        each(near, lambda offset, p=p: near_gather(p, offset, inner).wait_send())
    third.wait()
    kv_out[...] = sib_kv[...]


def run_sum(enc_sums, dec_sums, layout, blocks):
    rows, tall = layout.rows, layout.tall
    near, far = groups_of(blocks)
    dma = pltpu.SemaphoreType.DMA
    vmem = pl.BlockSpec(memory_space=pltpu.VMEM)
    args = [enc_sums, dec_sums]

    def buffers(*shape):
        return [pltpu.VMEM((*shape, far * c, LANES_A), BF16) for c in layout.chunks]

    return pl.pallas_call(
        functools.partial(sum_gradients, layout, blocks),
        in_specs=[pl.BlockSpec(memory_space=pl.ANY)] * len(args),
        out_specs=[vmem] * 2,
        out_shape=[
            jax.ShapeDtypeStruct((rows, LANES_A), BF16),
            jax.ShapeDtypeStruct((2 * tall, LANES_A), BF16),
        ],
        scratch_shapes=[
            *[pltpu.VMEM(a.shape, F32) for a in args],
            pltpu.VMEM((rows, LANES_A), F32),
            *[pltpu.VMEM((rows, LANES_A), BF16)] * 4,
            pltpu.VMEM((2 * tall, LANES_A), BF16),
            *buffers(near),
            *buffers(),
            *[pltpu.VMEM((far, c, LANES_A), BF16) for c in layout.chunks],
            dma((2,)),
            dma((3,)),
            dma((3,)),
            *[dma((2, 4, max(near, far)))] * 2,
        ],
        compiler_params=pltpu.CompilerParams(
            collective_id=0, has_side_effects=True, vmem_limit_bytes=VMEM_BYTES
        ),
        name="sum_gradients",
    )(*args)


def finish(layout, batches, returns, core_ref, total, sib_kv, *refs):
    returned, refs = refs[:returns], refs[returns + 1 :]
    (
        ends, ln1_gain, ln1_bias, q_weight, q_bias, kv_weight, v_bias, out_weight, out_bias, table,
        ln2_gain, ln2_bias, up_weight, up_bias, down_weight, down_bias, placed, copy_sem,
    ) = refs
    is_encoder = core_ref[0] == 0
    step = pl.program_id(0)

    def copies():
        return [
            pltpu.make_async_copy(
                ref,
                ends.at[batches - returns + k, pl.ds(WIN, WIN), pl.ds(step * WIN, WIN)],
                copy_sem.at[k],
            )
            for k, ref in enumerate(returned)
        ]

    pl.when(is_encoder)(lambda: start_all(copies()))

    @pl.when(step == 0)
    def _():
        unpack(
            layout, is_encoder, total, sib_kv, ln1_gain, ln1_bias, q_weight, q_bias, kv_weight,
            v_bias, out_weight, out_bias, table, ln2_gain, ln2_bias, up_weight, up_bias, down_weight,
            down_bias, placed,
        )

    pl.when(is_encoder)(lambda: wait_all(copies()))


def unpack(
    layout, is_encoder, total, sib_kv, ln1_gain, ln1_bias, q_weight, q_bias, kv_weight,
    v_bias, out_weight, out_bias, table, ln2_gain, ln2_bias, up_weight, up_bias, down_weight, down_bias,
    placed,
):
    channels, tall, half = layout.channels, layout.tall, LANES_A // 2

    def at(start, rows):
        return total[start : start + rows].astype(F32)

    vec = at(layout.vec, 16)
    vec = jnp.concatenate([vec[:8], vec[8:, :half]], 1)
    for row, ref in enumerate((ln1_gain, ln1_bias, ln2_gain, ln2_bias, down_bias)):
        ref[...] = vec[row : row + 1]

    for k in range(layout.tiles):
        cols = slice(k * LANES_A, (k + 1) * LANES_A)
        tile = at(layout.up + k * tall, tall)
        up_weight[:, cols] = tile[:channels]
        up_bias[:, cols] = tile[channels : channels + 1]
        down_weight[:, cols] = at(layout.down + k * channels, channels)
    rest = at(layout.rest, tall)
    q = jnp.concatenate([at(layout.q, tall), rest[:, :half]], 1)
    out = jnp.concatenate([at(layout.out, tall), rest[:, half:]], 1)
    q_weight[...] = q[:channels]
    q_bias[...] = q[channels : channels + 1]
    out_weight[...] = out[:channels]
    out_bias[...] = out[channels : channels + 1]
    mine = at(layout.kv, 2 * tall)
    other = sib_kv[...].astype(F32)
    for start, side in ((0, jnp.where(is_encoder, mine, other)), (channels, jnp.where(is_encoder, other, mine))):
        side = jnp.concatenate([side[:tall], side[tall:, :half]], 1)
        kv_weight[:, start : start + channels] = side[:channels]
    v_bias[...] = side[channels : channels + 1]
    placed[...] = jnp.zeros_like(placed)
    positions = [position_matrix(False), position_matrix(True)]
    for h in range(HEADS):
        start = layout.bias + h // 2 * CELLS
        placed[h, :, :256] = nt(total[start : start + CELLS], positions[h % 2])
    entries = jnp.zeros((8, 384), F32)
    for j in range(CELLS):
        entries += pltpu.roll(placed[:, j, :], CENTRE - cell_position(j), 1)
    table[...] = entries[:HEADS, : SPAN**3][:, None]


def run_finish(core, total, sib_kv, returned, ends, layout):
    channels = layout.channels
    hidden = layout.tiles * LANES_A
    _, _, rows_y, rows_z, _ = ends.shape
    any_spec = pl.BlockSpec(memory_space=pl.ANY)
    shapes = [
        (1, channels), (1, channels), (channels, channels), (1, channels), (channels, 2 * channels),
        (1, channels), (channels, channels), (1, channels), (HEADS, 1, SPAN**3),
        (1, channels), (1, channels), (channels, hidden), (1, hidden), (channels, hidden), (1, channels),
    ]
    shapes = [jax.ShapeDtypeStruct(shape, F32) for shape in shapes]
    return pl.pallas_call(
        functools.partial(finish, layout, ends.shape[0], len(returned)),
        grid_spec=pltpu.PrefetchScalarGridSpec(
            num_scalar_prefetch=1,
            grid=(rows_y // WIN,),
            in_specs=[
                *[whole(a) for a in (total, sib_kv)],
                *[
                    pl.BlockSpec(
                        (WIN, WIN, rows_z, channels), lambda i, c: (0, i * (1 - c[0]), 0, 0)
                    )
                ]
                * len(returned),
                any_spec,
            ],
            out_specs=[any_spec, *[whole(a) for a in shapes]],
            scratch_shapes=[
                pltpu.VMEM((8, CELLS, 384), F32),
                pltpu.SemaphoreType.DMA((len(returned),)),
            ],
        ),
        out_shape=[jax.ShapeDtypeStruct(ends.shape, F32), *shapes],
        input_output_aliases={3 + len(returned): 0},
        compiler_params=params,
        name="finish",
    )(core, total, sib_kv, *returned, ends)


def cell_position(ids):
    x = 2 * (ids // 32) + ids // 4 % 2
    y = 2 * (ids // 16 % 2) + ids // 2 % 2
    z = 2 * (ids // 8 % 2) + ids % 2
    return (x * SPAN + y) * SPAN + z


CENTRE = (WIN - 1) * (SPAN * SPAN + SPAN + 1)
TABLE_ROW = 8


def position_matrix(odd):
    rows = lax.broadcasted_iota(jnp.int32, (256, 2 * CELLS), 0)
    ids = lax.broadcasted_iota(jnp.int32, (256, 2 * CELLS), 1) - (CELLS if odd else 0)
    hit = (ids >= 0) & (ids < CELLS) & (rows == cell_position(ids))
    return jnp.where(hit, 1.0, 0.0).astype(BF16)


def spread_bias(table, shifted):
    for j in range(CELLS):
        turned = pltpu.roll(table, (384 - CENTRE + cell_position(j)) % 384, 1)
        for h in range(HEADS):
            shifted[h, j : j + 1] = turned[h : h + 1, :256]
    even, odd = position_matrix(False), position_matrix(True)
    pairs = [
        nn(shifted[2 * p].astype(BF16), even) + nn(shifted[2 * p + 1].astype(BF16), odd)
        for p in range(HEADS // 2)
    ]
    return jnp.concatenate(pairs, 1) * log2_e


def prepare(
    blocks, q_w, out_w, up_w, down_w, kv_w, v_b, ln1_g, ln1_b, ln2_g, ln2_b, out_b, down_b, q_b, up_b, table,
    weights_e, vectors_e, bias_e, weights_d, vectors_d, bias_d,
    small, small_sib, q_sib, out_sib, up_sib, down_sib, shifted, send_sem, recv_sem,
):
    core, block = lax.axis_index("section"), lax.axis_index("tok")
    channels, hidden = up_w.shape
    sibling = {"section": 1 - core}
    barrier = pltpu.get_barrier_semaphore()
    pl.semaphore_signal(barrier, inc=1, device_id=sibling, device_id_type=MESH)
    small[...] = jnp.zeros_like(small)
    for row, ref in enumerate((ln1_g, ln1_b, ln2_g, ln2_b, out_b, down_b, q_b)):
        small[row : row + 1, :channels] = ref[...].astype(F32)
    small[7:8, :hidden] = up_b[...].astype(F32)
    small[TABLE_ROW : TABLE_ROW + HEADS, : SPAN**3] = table[...].astype(F32)
    pl.semaphore_wait(barrier, 1)
    pairs = ((small, small_sib), (q_w, q_sib), (out_w, out_sib), (up_w, up_sib), (down_w, down_sib))
    copies = [
        pltpu.make_async_remote_copy(
            src_ref=source, dst_ref=target, send_sem=send_sem.at[k], recv_sem=recv_sem.at[k],
            device_id=sibling, device_id_type=MESH,
        )
        for k, (source, target) in enumerate(pairs)
    ]
    for copy in copies:
        copy.start()
    for copy in copies:
        copy.wait()

    def place(enc, dec):
        e_small, d_small = enc[0], dec[0]
        for weights, vectors, (source, q, out, up, down) in (
            (weights_e, vectors_e, enc), (weights_d, vectors_d, dec),
        ):
            weights[2 * channels :] = jnp.zeros((2 * channels, hidden), BF16)
            weights[:channels] = up[...]
            weights[channels : 2 * channels] = down[...]
            weights[2 * channels : 3 * channels, :channels] = q[...]
            weights[3 * channels :, :channels] = out[...]
            vectors[...] = jnp.zeros_like(vectors)
            vectors[:8, :channels] = source[:8, :channels]
            vectors[8:9, :hidden] = source[7:8, :hidden]
            vectors[9:10, :channels] = source[6:7, :channels]
        weights_e[2 * channels : 3 * channels, 256 : 256 + channels] = kv_w[:, :channels]
        weights_e[2 * channels : 3 * channels, 512 : 512 + channels] = kv_w[:, channels:]
        vectors_e[9:10, 512 : 512 + channels] = v_b[...].astype(F32)
        rows = slice(TABLE_ROW, TABLE_ROW + 8)
        bias_e[...] = spread_bias(e_small[rows, :384], shifted)
        return spread_bias(d_small[rows, :384], shifted)

    own = (small, q_w, out_w, up_w, down_w)
    sib = (small_sib, q_sib, out_sib, up_sib, down_sib)

    def masked(base):
        shape = (CELLS, HEADS * CELLS)
        keys = lax.broadcasted_iota(jnp.int32, shape, 0)
        queries = lax.broadcasted_iota(jnp.int32, shape, 1) % CELLS

        def differ(unit):
            return jnp.where(keys // unit % 2 != queries // unit % 2, 1.0, 0.0)

        last = jnp.where((core == 1) & (block == blocks - 1), 1.0, 0.0)
        for y in range(2):
            for z in range(2):
                apart = jnp.maximum(last * differ(32), jnp.maximum(y * differ(16), z * differ(8)))
                bias_d[y, z] = base + apart * (mask_fill * log2_e)

    @pl.when(core == 0)
    def _():
        masked(place(own, sib))

    @pl.when(core == 1)
    def _():
        masked(place(sib, own))


def run_prepare(blocks, weights, smalls, table, kv_weight, v_bias):
    q_w, out_w, up_w, down_w = weights
    channels, hidden = up_w.shape
    vmem = pl.BlockSpec(memory_space=pltpu.VMEM)
    args = [*weights, kv_weight, v_bias, *smalls, table]
    bias = (CELLS, HEADS * CELLS)
    square = (channels, channels)
    layer = [
        jax.ShapeDtypeStruct((4 * channels, hidden), BF16),
        jax.ShapeDtypeStruct((16, hidden), F32),
    ]
    shapes = [
        *layer,
        jax.ShapeDtypeStruct(bias, F32),
        *layer,
        jax.ShapeDtypeStruct((2, 2, *bias), F32),
    ]
    return pl.pallas_call(
        functools.partial(prepare, blocks),
        in_specs=[vmem] * len(args),
        out_specs=[vmem] * len(shapes),
        out_shape=shapes,
        scratch_shapes=[
            pltpu.VMEM((TABLE_ROW + 8, hidden), F32),
            pltpu.VMEM((TABLE_ROW + 8, hidden), F32),
            pltpu.VMEM(square, BF16),
            pltpu.VMEM(square, BF16),
            pltpu.VMEM((channels, hidden), BF16),
            pltpu.VMEM((channels, hidden), BF16),
            pltpu.VMEM((HEADS, CELLS, 256), F32),
            pltpu.SemaphoreType.DMA((5,)),
            pltpu.SemaphoreType.DMA((5,)),
        ],
        compiler_params=pltpu.CompilerParams(
            collective_id=1, has_side_effects=True, vmem_limit_bytes=VMEM_BYTES
        ),
        name="prepare",
    )(*args)


def run_encoder(core, tokens, batch, consts, cotangent):
    _, _, rows_y, rows_z, channels = tokens.shape
    groups, size = rows_y // WIN, 4 * rows_z
    cells = 4 * size
    hidden = consts[1].shape[1]
    slab = jax.ShapeDtypeStruct((groups, 2, 3, size * 3 // 2, LANES_A), BF16)
    outs = [
        slab,
        slab,
        jax.ShapeDtypeStruct((groups, cells, 512), F32),
        jax.ShapeDtypeStruct((groups, cells, 2 * hidden + HEADS * CELLS + 256), BF16),
    ]

    def row(array):
        zeros = (0,) * (array.ndim - 1)
        return pl.BlockSpec((1, *array.shape[1:]), lambda i, c: (i, *zeros))

    batches = tokens.shape[0]
    cut = [] if cotangent is None else [cotangent]
    cut_block = (batches, SHIFT, WIN, rows_z, channels)
    cut_outs = [
        jax.ShapeDtypeStruct((batches, SHIFT, rows_y, rows_z, channels), a.dtype) for a in cut
    ]
    return pl.pallas_call(
        functools.partial(encoder_forward, len(cut)),
        grid_spec=pltpu.PrefetchScalarGridSpec(
            num_scalar_prefetch=1,
            grid=(groups,),
            in_specs=[
                pl.BlockSpec(
                    (1, WIN, WIN, rows_z, channels), lambda i, c: (batch, c[0], i, 0, 0)
                ),
                *[whole(a) for a in consts],
                *[pl.BlockSpec(cut_block, lambda i, c: (0, 2 * c[0], i, 0, 0)) for _ in cut],
            ],
            out_specs=[
                *[row(a) for a in outs],
                *[pl.BlockSpec(cut_block, lambda i, c: (0, 0, i, 0, 0)) for _ in cut],
            ],
            scratch_shapes=[pltpu.VMEM((cells, 768), BF16)],
        ),
        out_shape=[*outs, *cut_outs],
        compiler_params=params,
        cost_estimate=cost(groups * cells, 466944, groups * cells * 7500),
        name="encoder_forward",
    )(core, tokens, *consts, *cut)


def run_encoder_back(core, batch, own, halo, ys, returned, saved, old, consts, tokens):
    groups, _, _, packed, _ = own.shape
    batches, planes, rows_y, rows_z, channels = tokens.shape
    size = 4 * rows_z
    hidden = consts[1].shape[1]
    first = old is None
    sums = jax.ShapeDtypeStruct((sum_rows(channels, True), hidden), F32)
    outs = [
        jax.ShapeDtypeStruct(tokens.shape, F32),
        jax.ShapeDtypeStruct((WIN, rows_y, rows_z, channels), F32),
        sums,
    ]

    def slab(unit):
        def place(i, c):
            return ((i if unit == 0 else (i + groups - 1) % groups), unit, 0, 0, 0)

        return pl.BlockSpec((1, 1, 3, packed, LANES_A), place)

    def row(array):
        zeros = (0,) * (array.ndim - 1)
        return pl.BlockSpec((1, *array.shape[1:]), lambda i, c: (i, *zeros))

    def for_core(core, planes_here):
        def place(i, c):
            return (0, i * (c[0] if core == 1 else 1 - c[0]), 0, 0)

        return pl.BlockSpec((planes_here, WIN, rows_z, channels), place)

    any_spec = pl.BlockSpec(memory_space=pl.ANY)
    olds = [] if first else [old[1], old[0]]
    args = [core, *consts, *ys, own, own, halo, halo, *saved, *returned, *olds]
    return pl.pallas_call(
        functools.partial(encoder_backward, first, batch, len(returned)),
        grid_spec=pltpu.PrefetchScalarGridSpec(
            num_scalar_prefetch=1,
            grid=(groups,),
            in_specs=[
                *[whole(a) for a in consts],
                *[for_core(1, n) for n in (2, 2, 4)],
                slab(0),
                slab(1),
                slab(0),
                slab(1),
                *[row(a) for a in saved],
                *[for_core(0, WIN)] * len(returned),
                *[whole(a) for a in olds[:-1]],
                *[any_spec] * (0 if first else 1),
            ],
            out_specs=[any_spec, any_spec, whole(sums)],
            scratch_shapes=[
                pltpu.VMEM((4 * size, 768), BF16),
                pltpu.VMEM((3, 4 * size, channels), BF16),
                pltpu.VMEM((2, WIN, WIN, rows_z, channels), F32),
                pltpu.SemaphoreType.DMA((2,)),
                pltpu.SemaphoreType.DMA((8 + batches,)),
            ],
        ),
        out_shape=outs,
        input_output_aliases={} if first else {len(args) - 1: 0},
        compiler_params=params,
        cost_estimate=cost(groups * 4 * size, 933888, groups * 4 * size * 9000),
        name="encoder_backward",
    )(*args)


def run_decoder(core, keep, recv, cotangent, cot_recv, batch, old, consts):
    groups, _, _, packed, _ = keep.shape
    rows_z, channels = cotangent.shape[3:]
    size = 4 * rows_z
    hidden = consts[1].shape[1]
    windows = rows_z // WIN
    first = old is None
    sums = jax.ShapeDtypeStruct((sum_rows(channels, False), hidden), F32)
    slab_shape = jax.ShapeDtypeStruct((groups, 2, 3, packed, LANES_A), BF16)
    outs = [
        *[jax.ShapeDtypeStruct((n, groups * WIN, rows_z, channels), F32) for n in (4, 2)],
        slab_shape,
        slab_shape,
        sums,
    ]

    def slab(unit):
        def place(i, c):
            return ((i if unit == 1 else (i + 1) % groups), unit, 0, 0, 0)

        return pl.BlockSpec((1, 1, 3, packed, LANES_A), place)

    def cot(unit, own):
        def place(i, c):
            y = 2 * i + 1 if unit == 1 else (2 * i + 2) % (2 * groups)
            return (batch, 2 * c[0] + 1 if own else 0, y, 0, 0)

        return pl.BlockSpec((1, 2, 2, rows_z, channels), place)

    def bias_place(i, c):
        return (i // (groups - 1), 0, 0, 0)

    specs = [whole(a) for a in consts]
    specs[3] = pl.BlockSpec((1, *consts[3].shape[1:]), bias_place)
    olds = [] if first else [old]
    out_slab = pl.BlockSpec((1, 2, 3, packed, LANES_A), lambda i, c: (i, 0, 0, 0, 0))
    return pl.pallas_call(
        functools.partial(decoder, first),
        grid_spec=pltpu.PrefetchScalarGridSpec(
            num_scalar_prefetch=1,
            grid=(groups,),
            in_specs=[
                *specs,
                slab(1),
                slab(0),
                slab(1),
                slab(0),
                cot(1, True),
                cot(0, True),
                cot(1, False),
                cot(0, False),
                *[whole(a) for a in olds],
            ],
            out_specs=[
                *[pl.BlockSpec((n, WIN, rows_z, channels), lambda i, c: (0, i, 0, 0)) for n in (4, 2)],
                out_slab,
                out_slab,
                whole(sums),
            ],
            scratch_shapes=[
                pltpu.VMEM((windows, CELLS, HEADS * CELLS), F32),
                pltpu.VMEM((4 * size, channels), BF16),
                pltpu.VMEM((4 * size, hidden), BF16),
                pltpu.VMEM((4 * size, hidden), F32),
                pltpu.VMEM((3, 4 * size, channels), F32),
            ],
        ),
        out_shape=outs,
        compiler_params=params,
        cost_estimate=cost(groups * 4 * size, 1253376, groups * 4 * size * 4000),
        name="decoder",
    )(core, *consts, keep, keep, recv, recv, cotangent, cotangent, cot_recv, cot_recv, *olds)


def body(
    tokens,
    cotangent,
    ln1_gain,
    ln1_bias,
    q_weight,
    q_bias,
    kv_weight,
    v_bias,
    out_weight,
    out_bias,
    rel_table,
    ln2_gain,
    ln2_bias,
    up_weight,
    up_bias,
    down_weight,
    down_bias,
):
    batches, planes, rows_y, rows_z, channels = tokens.shape
    axes = ("section", "tok")
    core = lax.axis_index("section")
    block = lax.axis_index("tok")
    blocks = lax.axis_size("tok")
    is_encoder = core == 0
    core_arg = core.astype(jnp.int32).reshape(1)

    def device(position):
        position = position % (2 * blocks)
        return (position % 2) * blocks + position // 2

    to_previous = [(device(r), device(r - 1)) for r in range(2 * blocks)]
    to_next = [(device(r), device(r + 1)) for r in range(2 * blocks)]

    weights_e, vectors_e, bias_e, weights_d, vectors_d, bias_d = run_prepare(
        blocks,
        (q_weight[0], out_weight[0], up_weight[0], down_weight[0].T),
        (ln1_gain, ln1_bias, ln2_gain, ln2_bias, out_bias, down_bias, q_bias, up_bias),
        rel_table[0],
        kv_weight,
        v_bias[None],
    )
    order = jnp.asarray(order_matrix(rows_z, 0), BF16)
    order_rolled = jnp.asarray(order_matrix(rows_z, 1), BF16)

    enc_consts = (order, weights_e, vectors_e, bias_e)
    enc_back_consts = (order, weights_e, vectors_e)
    dec_consts = (order_rolled, weights_d, vectors_d, bias_d)

    handed, saved = [], []
    for batch in range(batches):
        send, keep, *rest = run_encoder(
            core_arg, tokens, batch, enc_consts, cotangent if batch == 0 else None
        )
        if batch == 0:
            *rest, half = rest
            cot_recv = lax.ppermute(half, axes, to_previous)
        handed.append((keep, lax.ppermute(send, axes, to_previous)))
        saved.append(rest)
    dec_sums = None
    returned, ys = [], []
    to_decoder = [(t, blocks + t) for t in range(blocks)]
    to_encoder = [(blocks + t, t) for t in range(blocks)]
    to_after = [(blocks + t, blocks + (t + 1) % blocks) for t in range(blocks)]
    for batch in range(batches):
        out_all, out_tail, own, halo, dec_sums = run_decoder(
            core_arg, *handed[batch], cotangent, cot_recv, batch, dec_sums, dec_consts
        )
        returned.append((own, lax.ppermute(halo, axes, to_next)))
        y_halo = lax.ppermute(out_tail, axes, to_after)
        ys.append((out_all, y_halo, lax.ppermute(out_all, axes, to_decoder)))
    old = None
    backs = []
    for batch in range(batches):
        arrived = backs[:1] if batch == batches - 1 else []
        ends, back, enc_sums = run_encoder_back(
            core_arg, batch, *returned[batch], ys[batch], arrived, saved[batch], old,
            enc_back_consts, tokens,
        )
        old = (ends, enc_sums)
        backs.append(lax.ppermute(back, axes, to_encoder))

    layout = Layout(channels, up_weight.shape[2], blocks)
    total, sib_kv = run_sum(enc_sums, dec_sums, layout, blocks)
    (
        ends, g_ln1_gain, g_ln1_bias, g_q_weight, g_q_bias, g_kv_weight, g_v_bias, g_out_weight,
        g_out_bias, g_table, g_ln2_gain, g_ln2_bias, g_up_weight, g_up_bias, g_down_weight, g_down_bias,
    ) = run_finish(core_arg, total, sib_kv, backs[1:], ends, layout)
    return (
        ends[None],
        g_ln1_gain,
        g_ln1_bias,
        g_q_weight[None],
        g_q_bias,
        g_kv_weight[None],
        g_v_bias,
        g_out_weight[None],
        g_out_bias,
        g_table.transpose(1, 0, 2),
        g_ln2_gain,
        g_ln2_bias,
        g_up_weight[None],
        g_up_bias,
        g_down_weight.T[None],
        g_down_bias,
    )


def solution(mesh):
    in_specs = (
        P(None, "tok", None, None, None),
        P(None, "tok", None, None, None),
        P("section", None),
        P("section", None),
        P("section", None, None),
        P("section", None),
        P(),
        P(),
        P("section", None, None),
        P("section", None),
        P("section", None, None),
        P("section", None),
        P("section", None),
        P("section", None, None),
        P("section", None),
        P("section", None, None),
        P("section", None),
    )
    out_specs = (
        P("section", None, "tok", None, None, None),
        P("section", None),
        P("section", None),
        P("section", None, None),
        P("section", None),
        P("section", None, None),
        P("section", None),
        P("section", None, None),
        P("section", None),
        P("section", None, None),
        P("section", None),
        P("section", None),
        P("section", None, None),
        P("section", None),
        P("section", None, None),
        P("section", None),
    )
    return jax.shard_map(body, mesh=mesh, in_specs=in_specs, out_specs=out_specs, check_vma=False)
```

```python
import functools

import jax
import jax.numpy as jnp
import numpy as np
from jax import lax
from jax.experimental import pallas as pl
from jax.experimental.pallas import tpu as pltpu
from jax.sharding import PartitionSpec as P

HEADS = 6
HD = 32
WIN = 4
SHIFT = 2
CELLS = WIN**3
SPAN = 2 * WIN - 1
HEADS_A = 4
LANES_A = HEADS_A * HD
COLS_A = HEADS_A * CELLS

eps_norm = 1e-05
mask_fill = -100.0
log2_e = 1.4426950408889634
root_half = 0.7071067811865476
inv_root_two_pi = 0.3989422804014327
scale = HD ** (-0.5)
VMEM_BYTES = 63 * 1024 * 1024

F32 = jnp.float32
BF16 = jnp.bfloat16


def nn(left, right):
    return lax.dot_general(left, right, (((1,), (0,)), ((), ())), preferred_element_type=F32)


def nt(left, right):
    return lax.dot_general(left, right, (((1,), (1,)), ((), ())), preferred_element_type=F32)


def tn(left, right):
    return lax.dot_general(left, right, (((0,), (0,)), ((), ())), preferred_element_type=F32)


def order_matrix(rows_z, rolled):
    count = 4 * rows_z
    matrix = np.zeros((count, count), np.float32)
    units = rows_z // 2
    for unit in range(units):
        for dx in range(2):
            for dy in range(2):
                for dz in range(2):
                    z = (2 * (unit + rolled) + dz) % rows_z
                    matrix[unit * 8 + dx * 4 + dy * 2 + dz, (dx * 2 + dy) * rows_z + z] = 1.0
    return matrix


def windows_of(pieces):
    count, rows, channels = pieces.shape
    return pieces.reshape(count, rows // 16, 16, channels).transpose(1, 0, 2, 3).reshape(-1, channels)


def pieces_of(windows):
    rows, channels = windows.shape
    return (
        windows.reshape(rows // CELLS, 4, 16, channels)
        .transpose(1, 0, 2, 3)
        .reshape(4, rows // 4, channels)
    )


def roll_rows(pieces, steps):
    return jnp.concatenate([pieces[:, steps:], pieces[:, :steps]], 1)


def pack_slab(pieces):
    half = pieces.shape[1] // 2
    rest = pieces[:, :, LANES_A:]
    return jnp.concatenate(
        [pieces[:, :, :LANES_A], jnp.concatenate([rest[:, :half], rest[:, half:]], 2)], 1
    ).astype(BF16)


def unpack_slab(block):
    size = block.shape[0] * 2 // 3
    half = LANES_A // 2
    rest = jnp.concatenate([block[size:, :half], block[size:, half:]], 0)
    return jnp.concatenate([block[:size], rest], 1)


def normalize(rows):
    mean = jnp.mean(rows, -1, keepdims=True)
    centered = rows - mean
    inv_std = lax.rsqrt(jnp.mean(centered * centered, -1, keepdims=True) + eps_norm)
    return centered * inv_std, inv_std


def norm_back(grad_rows, unit_rows, inv_std, gain):
    scaled = grad_rows * gain
    return inv_std * (
        scaled
        - jnp.mean(scaled, -1, keepdims=True)
        - unit_rows * jnp.mean(scaled * unit_rows, -1, keepdims=True)
    )


def gelu_pair(rows):
    upper = 0.5 * lax.erf(rows * root_half) + 0.5
    bell = jnp.exp2(rows * rows * (-0.5 * log2_e))
    return rows * upper, upper + rows * bell * inv_root_two_pi


def head_masks(width):
    heads = lax.broadcasted_iota(jnp.int32, (1, width), 1) // HD
    return [jnp.where(heads == h, 1.0, 0.0).astype(BF16) for h in range(width // HD)]


def expand(rows):
    masks = head_masks(rows.shape[1])
    return jnp.concatenate([rows * mask for mask in masks], 0)


def collapse(stacked):
    width = stacked.shape[1]
    lanes = lax.broadcasted_iota(jnp.int32, (CELLS, width), 1)
    total = stacked[:CELLS]
    for h in range(1, width // HD):
        total = jnp.where(lanes >= h * HD, stacked[h * CELLS : (h + 1) * CELLS], total)
    return total


def split(rows):
    return rows[:, :LANES_A], rows[:, LANES_A:]


def attend(parts, bias):
    queries, keys, values = zip(*[[split(rows) for rows in part] for part in parts])
    wide = [[expand(half) for half in q] for q in queries]
    scores = [
        jnp.concatenate([nt(k[0], q[0]), nt(k[1], q[1])], 1) for k, q in zip(keys, wide)
    ]
    scores = [s * (scale * log2_e) + b for s, b in zip(scores, bias)]
    exponents = [jnp.exp2(s - jnp.max(s, 0, keepdims=True)) for s in scores]
    probs = [e * (1.0 / jnp.sum(e, 0, keepdims=True)) for e in exponents]
    low = [p.astype(BF16) for p in probs]
    mixed = [
        (tn(p[:, :COLS_A], v[0]), tn(p[:, COLS_A:], v[1])) for p, v in zip(low, values)
    ]
    mixed = [jnp.concatenate([collapse(m[0]), collapse(m[1])], 1).astype(BF16) for m in mixed]
    return mixed, probs


def attend_back(parts):
    queries, keys, values, grads = zip(
        *[[split(rows) for rows in part[:3] + part[4:]] for part in parts]
    )
    probs = [part[3] for part in parts]
    wide_g = [[expand(half) for half in g] for g in grads]
    d_probs = [
        jnp.concatenate([nt(v[0], g[0]), nt(v[1], g[1])], 1) for v, g in zip(values, wide_g)
    ]
    low = [part[3].astype(BF16) for part in parts]
    d_values = [
        jnp.concatenate([nn(p[:, :COLS_A], g[0]), nn(p[:, COLS_A:], g[1])], 1)
        for p, g in zip(low, wide_g)
    ]
    wide_q = [[expand(half) for half in q] for q in queries]
    d_scores = [
        p * (d - jnp.sum(d * p, 0, keepdims=True)) for p, d in zip(probs, d_probs)
    ]
    low_d = [d.astype(BF16) for d in d_scores]
    d_keys = [
        jnp.concatenate([nn(d[:, :COLS_A], q[0]), nn(d[:, COLS_A:], q[1])], 1) * scale
        for d, q in zip(low_d, wide_q)
    ]
    d_queries = [
        (tn(d[:, :COLS_A], k[0]), tn(d[:, COLS_A:], k[1])) for d, k in zip(low_d, keys)
    ]
    d_queries = [
        jnp.concatenate([collapse(d[0]), collapse(d[1])], 1) * scale for d in d_queries
    ]
    table = d_scores[0]
    for d in d_scores[1:]:
        table = table + d
    return d_queries, d_keys, d_values, table


def window_groups(count):
    return [range(k, min(k + TOGETHER, count)) for k in range(0, count, TOGETHER)]


def window_rows(k):
    return slice(k * CELLS, (k + 1) * CELLS)


def with_ones(rows):
    return jnp.concatenate([rows.T, jnp.ones((16, rows.shape[0]), BF16)], 0)


def col_sum(rows):
    return jnp.sum(rows, 0, keepdims=True)


def start_sums(old, new):
    @pl.when(pl.program_id(0) == 0)
    def _():
        new[...] = jnp.zeros_like(new) if old is None else old[...]


def restore(matrix, rows):
    high = rows.astype(BF16)
    low = (rows - high.astype(F32)).astype(BF16)
    return tn(matrix, high) + tn(matrix, low)


CHUNK = 256
BLOCK = 256
TOGETHER = 8


class View:
    def __init__(self, ref, row, rows, col, cols):
        self.ref, self.row, self.col, self.shape = ref, row, col, (rows, cols)

    def place(self, key):
        key = (slice(None), slice(None)) if key is Ellipsis else key
        key = key if isinstance(key, tuple) else (key, slice(None))
        return tuple(
            slice(start + part.indices(size)[0], start + part.indices(size)[1])
            for part, start, size in zip(key, (self.row, self.col), self.shape)
        )

    def __getitem__(self, key):
        return self.ref[self.place(key)]

    def __setitem__(self, key, value):
        self.ref[self.place(key)] = value

    def first_columns(self, cols):
        return View(self.ref, self.row, self.shape[0], self.col, cols)


def layer_views(weights, vectors):
    hidden = weights.shape[1]
    channels = weights.shape[0] // 4
    q_cols = 768

    def rows(k, cols):
        return View(weights, k * channels, channels, 0, cols)

    return (
        View(vectors, 0, 8, 0, channels),
        View(vectors, 8, 1, 0, hidden),
        View(vectors, 9, 1, 0, q_cols),
        rows(0, hidden),
        rows(1, hidden),
        rows(2, q_cols),
        rows(3, channels),
    )


def sum_rows(channels, encoder):
    tall = channels + 16
    return 2 * tall + channels + (tall if encoder else 0)


def sum_views(sums, channels, encoder):
    tall = channels + 16
    base = tall + channels

    def view(row, rows, col, cols):
        return View(sums, row, rows, col, cols)

    fields = [view(base, tall, 256 * k, channels) for k in range(3 if encoder else 2)]
    last = base + (tall if encoder else 0)
    side = 256 if encoder else 512
    out = view(last, tall, 0, channels) if encoder else fields[1]
    bias = (view(last, CELLS, side, COLS_A), view(last + CELLS, CELLS, side, 2 * CELLS))
    vec = view(last + 2 * CELLS, 8, side, channels)
    return (
        view(0, tall, 0, sums.shape[1]),
        view(tall, channels, 0, sums.shape[1]),
        fields[:3] if encoder else fields[:1],
        out,
        vec,
        bias,
    )


def add_bias(views, table):
    views[0][...] += table[:, :COLS_A]
    views[1][...] += table[:, COLS_A:]


def encoder_forward(cuts, count, groups, core_ref, tok, order, weights, vectors, bias, *rest):
    vec, b_up, b_qkv, w_up, w_down, w_qkv, w_out = layer_views(weights, vectors)
    cut_in, rest = rest[:cuts], rest[cuts:]
    sends, rest = rest[:count], rest[count:]
    keep, wide_out, low_out, *cut_out, qkv = rest
    hidden_cols = w_up.shape[1]
    s_start, p_start, o_start = hidden_cols, 2 * hidden_cols, 2 * hidden_cols + HEADS * CELLS
    for source, target in zip(cut_in, cut_out):
        target[...] = source[...]
    rows_z = tok.shape[3]
    size = 4 * rows_z
    pieces = []
    for x in range(2):
        for y in range(2):
            part = tok[0, 2 * x : 2 * x + 2, 2 * y : 2 * y + 2].reshape(size, -1)
            pieces.append(nn(order[...], part))
    entry = windows_of(jnp.stack(pieces))
    unit, inv_std = normalize(entry)
    channels = entry.shape[1]
    wide = jnp.broadcast_to(inv_std, (entry.shape[0], 256 - channels))
    wide_out[0, :, :channels] = unit
    wide_out[0, :, channels:256] = wide
    left = (unit * vec[0:1] + vec[1:2]).astype(BF16)
    triple = nn(left, w_qkv[...]) + b_qkv[...]
    qkv[...] = triple.astype(BF16)
    for together in window_groups(entry.shape[0] // CELLS):
        parts = [
            [qkv[window_rows(k), 256 * f : 256 * f + 192] for f in range(3)] for k in together
        ]
        mixed, probs = attend(parts, [bias[...]] * len(parts))
        for k, o, p in zip(together, mixed, probs):
            low_out[0, window_rows(k), p_start:o_start] = p.astype(BF16)
            low_out[0, window_rows(k), o_start : o_start + channels] = o
    mixed = low_out[0, :, o_start : o_start + channels]
    middle = entry + nn(mixed, w_out[...]) + vec[4:5]
    unit, inv_std = normalize(middle)
    wide = jnp.broadcast_to(inv_std, (entry.shape[0], 256 - channels))
    wide_out[0, :, 256 : 256 + channels] = unit
    wide_out[0, :, 256 + channels :] = wide
    left = (unit * vec[2:3] + vec[3:4]).astype(BF16)
    results = []
    for k in range(entry.shape[0] // CHUNK):
        rows = slice(k * CHUNK, (k + 1) * CHUNK)
        hidden, slope = gelu_pair(nn(left[rows], w_up[...]) + b_up[...])
        hidden = hidden.astype(BF16)
        low_out[0, rows, :s_start] = hidden
        low_out[0, rows, s_start:p_start] = slope.astype(BF16)
        results.append(nt(hidden, w_down[...]))
    result = middle + jnp.concatenate(results, 0) + vec[5:6]
    send_rows = []
    for field, rows in enumerate((result, triple[:, 256:448], triple[:, 512:704])):
        rolled = pack_slab(roll_rows(pieces_of(rows), 8))
        keep[0, :, field] = rolled[2:]
        send_rows.append(rolled[:2])
    for k, send in enumerate(sends):

        @pl.when(pl.program_id(0) // groups == k)
        def _(send=send):
            for field, rows in enumerate(send_rows):
                send[0, :, field] = rows


def run_together(*works):
    works = list(works)
    while works:
        for work in list(works):
            try:
                next(work)
            except StopIteration:
                works.remove(work)


def row_blocks(count, size):
    return [slice(k, k + size) for k in range(0, count, size)]


def norm_back_steps(rows_grad, base, unit, inv_std, gain, g_vec, row, results):
    sums = [None, None]
    for rows in row_blocks(base.shape[0], BLOCK):
        grad = rows_grad(rows)
        found = (col_sum(grad * unit[rows]), col_sum(grad))
        sums = [f if total is None else total + f for f, total in zip(found, sums)]
        results.append(base[rows] + norm_back(grad, unit[rows], inv_std[rows], gain))
        yield
    g_vec[row : row + 1] += sums[0]
    g_vec[row + 1 : row + 2] += sums[1]


def product_steps(products):
    for target, cols, left, right in products:
        target[:, cols] += nn(left, right)
        yield


def mlp_back(grad, grad_low, hidden, slope, left_two, unit, inv_std, w_up, w_down, vec, sums):
    g_up, g_down, g_vec = sums
    backs, pres = [], []
    for rows in row_blocks(grad.shape[0], CHUNK):
        d_pre = (nn(grad_low[rows], w_down[...]) * slope(rows)).astype(BF16)
        pres.append(d_pre)
        backs.append(nt(d_pre, w_up[...]))
    d_pre = jnp.concatenate(pres, 0)
    d_normed = jnp.concatenate(backs, 0)
    ones, turned = with_ones(left_two), grad_low.T
    tiles = row_blocks(w_up.shape[1], 256)
    products = [(g_up, cols, ones, d_pre[:, cols]) for cols in tiles]
    products += [(g_down, cols, turned, hidden[:, cols]) for cols in tiles]
    results = []
    run_together(
        norm_back_steps(
            lambda rows: d_normed[rows], grad, unit, inv_std, vec[2:3], g_vec, 2, results
        ),
        product_steps(products),
    )
    g_vec[4:5] += col_sum(grad)
    return jnp.concatenate(results, 0)


def start_all(copies):
    for copy in copies:
        copy.start()


def wait_all(copies):
    for copy in copies:
        copy.wait()


def place_outputs(refs, ends, batch, step, semaphores):
    copies = []
    if refs:
        y_own, y_halo, y_sib = refs
        rows_y = ends.shape[2]
        for start, planes, ref in ((0, 2, y_halo), (2, 4, y_sib), (6, 2, y_own)):
            for half in range(2):
                rows = pl.ds(lax.rem(step * WIN + SHIFT + 2 * half, rows_y), 2)
                target = ends.at[batch, pl.ds(start, planes), rows]
                copies.append((ref.at[0, :, pl.ds(2 * half, 2)], target))
    return [
        pltpu.make_async_copy(source, target, semaphores.at[k])
        for k, (source, target) in enumerate(copies)
    ]


def strips(ys, rows_z, channels):
    if ys is None:
        return [], []
    arrays, slot = ys
    specs = [
        pl.BlockSpec((1, n, WIN, rows_z, channels), lambda i, c: (slot, 0, i * c[0], 0, 0))
        for n in (2, 2, 4)
    ]
    return list(arrays), specs


def encoder_backward(
    first, batch, returns, outputs, core_ref, order, weights, vectors,
    keep_a, keep_b, recv_a, recv_b,
    wide_in, low_in, *rest,
):
    y_refs, rest = rest[:outputs], rest[outputs:]
    vec, _, b_qkv, w_up, w_down, w_qkv, w_out = layer_views(weights, vectors)
    channels, hidden_cols = w_up.shape
    s_start, p_start, o_start = hidden_cols, 2 * hidden_cols, 2 * hidden_cols + HEADS * CELLS
    returned, rest = rest[:returns], rest[returns:]
    old, rest = (None, rest) if first else (rest[0], rest[2:])
    ends, back, sums, qkv, dqkv, buffer, out_sem, copy_sem = rest
    g_up, g_down, g_fields, g_out, g_vec, g_bias = sum_views(sums, channels, True)
    step, steps = pl.program_id(0), pl.num_programs(0)
    is_encoder = core_ref[0] == 0
    slot = lax.rem(step, 2)

    def output_copies():
        return place_outputs(y_refs, ends, batch - 1, step, copy_sem)

    def gradient_copies():
        return [
            pltpu.make_async_copy(
                ref, ends.at[k, pl.ds(WIN, WIN), pl.ds(step * WIN, WIN)], copy_sem.at[8 + k]
            )
            for k, ref in enumerate(returned)
        ]

    def result_copy(index, to_ends):
        target = (
            ends.at[batch, pl.ds(0, WIN), pl.ds(index * WIN, WIN)]
            if to_ends
            else back.at[:, pl.ds(index * WIN, WIN)]
        )
        at = lax.rem(index, 2)
        return pltpu.make_async_copy(buffer.at[at], target, out_sem.at[at])

    def for_core(encoder_work, decoder_work):
        pl.when(is_encoder)(encoder_work)
        pl.when(jnp.logical_not(is_encoder))(decoder_work)

    for_core(lambda: start_all(gradient_copies()), lambda: start_all(output_copies()))

    @pl.when(step >= 2)
    def _():
        for_core(
            lambda: result_copy(step - 2, True).wait(), lambda: result_copy(step - 2, False).wait()
        )

    start_sums(old, sums)
    fields = []
    for field in range(3):
        pieces = jnp.stack(
            [unpack_slab(ref[0, 0, field]) for ref in (recv_b, recv_a, keep_b, keep_a)]
        )
        fields.append(windows_of(pieces))
    grad_low, d_key_1, d_value_1 = fields
    grad = grad_low.astype(F32)
    unit_1, unit_2 = wide_in[0, :, :channels], wide_in[0, :, 256 : 256 + channels]
    wide_1, wide_2 = [wide_in[0, :, k + channels : k + channels + 1] for k in (0, 256)]
    left_1 = (unit_1 * vec[0:1] + vec[1:2]).astype(BF16)
    left_2 = (unit_2 * vec[2:3] + vec[3:4]).astype(BF16)
    qkv[...] = (nn(left_1, w_qkv[...]) + b_qkv[...]).astype(BF16)
    d_middle = mlp_back(
        grad, grad_low, low_in[0, :, :s_start], lambda rows: low_in[0, rows, s_start:p_start].astype(F32),
        left_2, unit_2, wide_2, w_up, w_down, vec,
        (g_up, g_down, g_vec),
    )
    branch = d_middle.astype(BF16)
    d_mixed = nt(branch, w_out[...]).astype(BF16)
    d_table = None
    for together in window_groups(grad.shape[0] // CELLS):
        parts = [
            [qkv[window_rows(k), 256 * f : 256 * f + 192] for f in range(3)]
            + [low_in[0, window_rows(k), p_start:o_start].astype(F32), d_mixed[window_rows(k)]]
            for k in together
        ]
        *d_qkv, d_s = attend_back(parts)
        for k, d_q, d_k, d_v in zip(together, *d_qkv):
            rows = window_rows(k)
            dqkv[0, rows] = d_q.astype(BF16)
            dqkv[1, rows] = (d_k + d_key_1[rows].astype(F32)).astype(BF16)
            dqkv[2, rows] = (d_v + d_value_1[rows].astype(F32)).astype(BF16)
        d_table = d_s if d_table is None else d_table + d_s
    add_bias(g_bias, d_table)
    ones = with_ones(left_1)
    every = slice(None)
    mixed = with_ones(low_in[0, :, o_start : o_start + channels])
    products = [(g_field, every, ones, dqkv[k]) for k, g_field in enumerate(g_fields)]
    products.append((g_out, every, mixed, branch))

    def rows_grad(rows):
        parts = [
            nt(dqkv[k, rows], w_qkv[:, 256 * k : 256 * k + channels]) for k in range(3)
        ]
        return parts[0] + parts[1] + parts[2]

    results = []
    run_together(
        norm_back_steps(rows_grad, d_middle, unit_1, wide_1, vec[0:1], g_vec, 0, results),
        product_steps(products),
    )
    result = pieces_of(jnp.concatenate(results, 0))
    rows_z = ends.shape[3]
    for x in range(2):
        for y in range(2):
            part = restore(order[...], result[2 * x + y])
            buffer[slot, 2 * x : 2 * x + 2, 2 * y : 2 * y + 2] = part.reshape(2, 2, rows_z, -1)
    for_core(lambda: result_copy(step, True).start(), lambda: result_copy(step, False).start())

    @pl.when(step == steps - 1)
    def _():
        def finish(to_ends):
            result_copy(step - 1, to_ends).wait()
            result_copy(step, to_ends).wait()

        for_core(lambda: finish(True), lambda: finish(False))

    for_core(lambda: wait_all(gradient_copies()), lambda: wait_all(output_copies()))


def decoder(
    first, kept, core_ref, order, weights, vectors, bias,
    keep_1, keep_0, recv_1, recv_0, cot_1, cot_0, cot_r1, cot_r0, *rest,
):
    vec, b_up, b_qkv, w_up, w_down, w_qkv, w_out = layer_views(weights, vectors)
    channels = w_up.shape[0]
    w_q, b_q = w_qkv.first_columns(channels), b_qkv.first_columns(channels)
    old, new = (None, rest) if first else (rest[0], rest[1:])
    new = new[kept:]
    out_all, out_tail, own, halo, sums, p_scr, o_scr, a_scr, s_scr, dqkv = new
    g_up, g_down, (g_q,), g_out, g_vec, g_bias = sum_views(sums, channels, False)
    start_sums(old, sums)
    fields = []
    for field in range(3):
        pieces = jnp.stack([unpack_slab(ref[0, 0, field]) for ref in (keep_1, keep_0, recv_1, recv_0)])
        fields.append(windows_of(pieces))
    entry_low, keys, values = fields
    entry = entry_low.astype(F32)
    unit_1, inv_1 = normalize(entry)
    left_1 = (unit_1 * vec[0:1] + vec[1:2]).astype(BF16)
    queries = (nn(left_1, w_q[...]) + b_q[...]).astype(BF16)
    windows = entry.shape[0] // CELLS
    for together in window_groups(windows):
        parts = [[rows[window_rows(k)] for rows in (queries, keys, values)] for k in together]
        mixed, probs = attend(parts, [bias[0, 1 if k == windows - 1 else 0] for k in together])
        for k, o, p in zip(together, mixed, probs):
            p_scr[k] = p
            o_scr[window_rows(k)] = o
    middle = entry + nn(o_scr[...], w_out[...]) + vec[4:5]
    unit_2, inv_2 = normalize(middle)
    left_2 = (unit_2 * vec[2:3] + vec[3:4]).astype(BF16)
    results = []
    for k in range(entry.shape[0] // CHUNK):
        rows = slice(k * CHUNK, (k + 1) * CHUNK)
        hidden, slope = gelu_pair(nn(left_2[rows], w_up[...]) + b_up[...])
        hidden = hidden.astype(BF16)
        a_scr[rows] = hidden
        s_scr[rows] = slope
        results.append(nt(hidden, w_down[...]))
    result = pieces_of(middle + jnp.concatenate(results, 0) + vec[5:6])
    rows_z = out_all.shape[3]
    size = 4 * rows_z
    for x in range(2):
        for y in range(2):
            part = restore(order[...], result[2 * x + y]).reshape(2, 2, rows_z, -1)
            out_all[0, 2 * x : 2 * x + 2, 2 * y : 2 * y + 2] = part
            if x == 1:
                out_tail[0, :, 2 * y : 2 * y + 2] = part

    cots = [
        nn(order[...], ref[0].reshape(size, -1)).astype(BF16) for ref in (cot_1, cot_0, cot_r1, cot_r0)
    ]
    grad_low = windows_of(jnp.stack(cots))
    grad = grad_low.astype(F32)
    d_middle = mlp_back(
        grad, grad_low, a_scr[...], lambda rows: s_scr[rows], left_2, unit_2, inv_2, w_up, w_down, vec,
        (g_up, g_down, g_vec),
    )
    branch = d_middle.astype(BF16)
    d_mixed = nt(branch, w_out[...]).astype(BF16)
    d_table = None
    for together in window_groups(windows):
        parts = [
            [rows[window_rows(k)] for rows in (queries, keys, values)]
            + [p_scr[k], d_mixed[window_rows(k)]]
            for k in together
        ]
        *d_qkv, d_s = attend_back(parts)
        for k, *grads in zip(together, *d_qkv):
            for f in range(3):
                dqkv[f, window_rows(k)] = grads[f]
        d_table = d_s if d_table is None else d_table + d_s
    add_bias(g_bias, d_table)
    d_queries = dqkv[0].astype(BF16)
    every = slice(None)
    products = [
        (g_q, every, with_ones(left_1), d_queries),
        (g_out, every, with_ones(o_scr[...]), branch),
    ]
    results = []
    run_together(
        norm_back_steps(
            lambda rows: nt(d_queries[rows], w_q[...]), d_middle, unit_1, inv_1, vec[0:1], g_vec, 0,
            results,
        ),
        product_steps(products),
    )
    d_entry = jnp.concatenate(results, 0)
    for field, rows in enumerate((d_entry, dqkv[1], dqkv[2])):
        turned = pack_slab(roll_rows(pieces_of(rows), size - 8))
        own[0, :, field] = turned[:2]
        halo[0, :, field] = turned[2:]


def whole(array):
    zeros = (0,) * array.ndim
    return pl.BlockSpec(array.shape, lambda *_: zeros)


def cost(cells, per_cell, hbm):
    return pl.CostEstimate(
        flops=2 * cells * per_cell, bytes_accessed=hbm, transcendentals=cells * 1536
    )


params = pltpu.CompilerParams(
    dimension_semantics=("arbitrary",), vmem_limit_bytes=VMEM_BYTES
)


class Layout:
    def __init__(self, channels, hidden, blocks):
        tall = channels + 16
        self.tall, self.channels = tall, channels
        self.tiles = hidden // LANES_A
        self.up = 0
        self.down = self.tiles * tall
        self.q = self.down + self.tiles * channels
        self.out = self.q + tall
        self.rest = self.out + tall
        self.kv = self.rest + tall
        self.bias = self.kv + 2 * tall
        self.vec = self.bias + HEADS * CELLS // LANES_A * CELLS
        self.end = self.vec + 16
        units = -(-self.end // (16 * blocks))
        self.chunks = (units // 2 * 16, (units - units // 2) * 16)
        self.starts = (0, self.chunks[0] * blocks)
        self.rows = units * 16 * blocks


def fill(buffer, layout, up, down, q, out, kv, bias, vec):
    kind, half = buffer.dtype, LANES_A // 2
    tall, channels = layout.tall, layout.channels
    for k in range(layout.tiles):
        cols = slice(k * LANES_A, (k + 1) * LANES_A)
        buffer[layout.up + k * tall : layout.up + (k + 1) * tall] = up[:, cols].astype(kind)
        buffer[layout.down + k * channels : layout.down + (k + 1) * channels] = down[
            :, cols
        ].astype(kind)
    buffer[layout.q : layout.q + tall] = q[:, :LANES_A].astype(kind)
    buffer[layout.out : layout.out + tall] = out[:, :LANES_A].astype(kind)
    rests = jnp.concatenate([q[:, LANES_A:], out[:, LANES_A:]], 1)
    buffer[layout.rest : layout.rest + tall] = rests.astype(kind)
    buffer[layout.kv : layout.kv + tall] = kv[:, :LANES_A].astype(kind)
    rests = jnp.concatenate([kv[:, LANES_A:], jnp.zeros((tall, half), F32)], 1)
    buffer[layout.kv + tall : layout.kv + 2 * tall] = rests.astype(kind)
    tiles = [bias[0][:, :LANES_A], bias[0][:, LANES_A:], bias[1][...]]
    for k, tile in enumerate(tiles):
        start = layout.bias + k * CELLS
        buffer[start : start + CELLS] = tile.astype(kind)
    rests = jnp.concatenate([vec[:, LANES_A:], jnp.zeros((8, half), F32)], 1)
    both = jnp.concatenate([vec[:, :LANES_A], rests], 0)
    buffer[layout.vec : layout.vec + 16] = both.astype(kind)
    if layout.rows > layout.end:
        buffer[layout.end :] = jnp.zeros((layout.rows - layout.end, LANES_A), kind)


MESH = pl.DeviceIdType.MESH


def groups_of(blocks):
    near = 4 if blocks % 4 == 0 else blocks
    return near, blocks // near


def sum_gradients(layout, blocks, *refs):
    (
        enc_in, dec_in, total_out, kv_out,
        enc, dec, own, theirs, from_sib, low, total, sib_kv, landed_0, landed_1, near_low_0, near_low_1,
        far_landed_0, far_landed_1, load_sem, sib_send, sib_recv, send_sem, recv_sem,
    ) = refs
    landed, near_low = (landed_0, landed_1), (near_low_0, near_low_1)
    far_landed = (far_landed_0, far_landed_1)
    core, me = lax.axis_index("section"), lax.axis_index("tok")
    sibling = {"section": 1 - core}
    near, far = groups_of(blocks)
    inner, outer = lax.rem(me, near), lax.div(me, near)

    def near_peer(offset):
        return lax.rem(inner + offset, near)

    def far_peer(offset):
        return lax.rem(outer + offset, far)

    def near_device(offset):
        return {"tok": outer * near + near_peer(offset)}

    def far_device(offset):
        return {"tok": far_peer(offset) * near + inner}

    def each(count, work):
        def run(offset, carry):
            work(offset)
            return carry

        lax.fori_loop(1, count, run, 0)

    enc_load = pltpu.make_async_copy(enc_in, enc, load_sem.at[0])
    dec_load = pltpu.make_async_copy(dec_in, dec, load_sem.at[1])
    enc_load.start()
    dec_load.start()
    barrier = pltpu.get_barrier_semaphore()
    pl.semaphore_signal(barrier, inc=1, device_id=sibling, device_id_type=MESH)
    for count, device in ((near, near_device), (far, far_device)):
        each(
            count,
            lambda offset, device=device: pl.semaphore_signal(
                barrier, inc=1, device_id=device(offset), device_id_type=MESH
            ),
        )
    enc_load.wait()
    dec_load.wait()
    channels = layout.channels
    e_up, e_down, (e_q, e_k, e_v), e_out, e_vec, e_bias = sum_views(enc, channels, True)
    d_up, d_down, (d_q,), d_out, d_vec, d_bias = sum_views(dec, channels, False)

    def fill_enc(buffer, kv):
        fill(buffer, layout, e_up, e_down, e_q, e_out, kv, e_bias, e_vec)

    def fill_dec(buffer, kv):
        fill(buffer, layout, d_up, d_down, d_q, d_out, kv, d_bias, d_vec)

    pl.when(core == 0)(lambda: fill_dec(theirs, e_v))
    pl.when(core == 1)(lambda: fill_enc(theirs, e_k))
    pl.semaphore_wait(barrier, near + far - 1)

    def to_sibling(source, target, k):
        return pltpu.make_async_remote_copy(
            src_ref=source, dst_ref=target, send_sem=sib_send.at[k], recv_sem=sib_recv.at[k],
            device_id=sibling, device_id_type=MESH,
        )

    def piece_rows(p):
        return slice(layout.starts[p], layout.starts[p] + layout.chunks[p] * blocks)

    swaps = [to_sibling(theirs.at[piece_rows(p)], from_sib.at[piece_rows(p)], p) for p in range(2)]
    start_all(swaps)
    pl.when(core == 0)(lambda: fill_enc(own, e_k))
    pl.when(core == 1)(lambda: fill_dec(own, e_v))

    def quarter_of(p, position):
        size = far * layout.chunks[p]
        return pl.ds(pl.multiple_of(layout.starts[p] + position * size, 16), size)

    def chunk_of(p, position):
        return pl.ds(pl.multiple_of(position * layout.chunks[p], 16), layout.chunks[p])

    def rows_of(p, position):
        start = layout.starts[p] + (inner * far + position) * layout.chunks[p]
        return pl.ds(pl.multiple_of(start, 16), layout.chunks[p])

    def exchange(p, stage, offset, source, target, device):
        return pltpu.make_async_remote_copy(
            src_ref=source, dst_ref=target,
            send_sem=send_sem.at[p, stage, offset], recv_sem=recv_sem.at[p, stage, offset],
            device_id=device(offset), device_id_type=MESH,
        )

    def near_scatter(p, offset):
        source = low.at[quarter_of(p, near_peer(offset))]
        return exchange(p, 0, offset, source, landed[p].at[offset], near_device)

    def far_scatter(p, offset):
        source = near_low[p].at[chunk_of(p, far_peer(offset))]
        return exchange(p, 1, offset, source, far_landed[p].at[offset], far_device)

    def far_gather(p, offset, owner):
        rows = rows_of(p, owner)
        return exchange(p, 2, offset, total.at[rows], total.at[rows], far_device)

    def near_gather(p, offset, owner):
        rows = quarter_of(p, owner)
        return exchange(p, 3, offset, total.at[rows], total.at[rows], near_device)

    def reduced(count, copy, landing, start):
        def add(offset, carry):
            copy(offset).wait_recv()
            return carry + landing[offset].astype(F32)

        return lax.fori_loop(1, count, add, start)

    def send_near(p):
        swaps[p].wait()
        rows = piece_rows(p)
        own[rows] += from_sib[rows].astype(F32)
        low[rows] = own[rows].astype(BF16)
        each(near, lambda offset: near_scatter(p, offset).start())

    def send_far(p):
        rows = quarter_of(p, inner)
        near_sum = reduced(near, lambda o: near_scatter(p, o), landed[p], own[rows])
        own[rows] = near_sum
        near_low[p][...] = near_sum.astype(BF16)
        each(far, lambda offset: far_scatter(p, offset).start())

    def return_far(p):
        rows = rows_of(p, outer)
        far_sum = reduced(far, lambda o: far_scatter(p, o), far_landed[p], own[rows])
        total[rows] = far_sum.astype(BF16)
        each(far, lambda offset: far_gather(p, offset, outer).start())

    def return_near(p):
        each(far, lambda o: far_gather(p, o, lax.rem(outer + far - o, far)).wait_recv())
        each(near, lambda offset: near_gather(p, offset, inner).start())

    def arrive(p):
        each(near, lambda o: near_gather(p, o, lax.rem(inner + near - o, near)).wait_recv())

    send_near(0)
    send_near(1)
    send_far(0)
    return_far(0)
    send_far(1)
    return_near(0)
    return_far(1)
    return_near(1)
    arrive(0)
    arrive(1)
    third = to_sibling(total.at[layout.kv : layout.kv + 2 * layout.tall], sib_kv, 2)
    third.start()
    total_out[...] = total[...]
    for p in range(2):
        each(near, lambda offset, p=p: near_scatter(p, offset).wait_send())
        each(far, lambda offset, p=p: far_scatter(p, offset).wait_send())
        each(far, lambda offset, p=p: far_gather(p, offset, outer).wait_send())
        each(near, lambda offset, p=p: near_gather(p, offset, inner).wait_send())
    third.wait()
    kv_out[...] = sib_kv[...]


def run_sum(enc_sums, dec_sums, layout, blocks):
    rows, tall = layout.rows, layout.tall
    near, far = groups_of(blocks)
    dma = pltpu.SemaphoreType.DMA
    vmem = pl.BlockSpec(memory_space=pltpu.VMEM)
    args = [enc_sums, dec_sums]

    def buffers(*shape):
        return [pltpu.VMEM((*shape, far * c, LANES_A), BF16) for c in layout.chunks]

    return pl.pallas_call(
        functools.partial(sum_gradients, layout, blocks),
        in_specs=[pl.BlockSpec(memory_space=pl.ANY)] * len(args),
        out_specs=[vmem] * 2,
        out_shape=[
            jax.ShapeDtypeStruct((rows, LANES_A), BF16),
            jax.ShapeDtypeStruct((2 * tall, LANES_A), BF16),
        ],
        scratch_shapes=[
            *[pltpu.VMEM(a.shape, F32) for a in args],
            pltpu.VMEM((rows, LANES_A), F32),
            *[pltpu.VMEM((rows, LANES_A), BF16)] * 4,
            pltpu.VMEM((2 * tall, LANES_A), BF16),
            *buffers(near),
            *buffers(),
            *[pltpu.VMEM((far, c, LANES_A), BF16) for c in layout.chunks],
            dma((2,)),
            dma((3,)),
            dma((3,)),
            *[dma((2, 4, max(near, far)))] * 2,
        ],
        compiler_params=pltpu.CompilerParams(
            collective_id=0, has_side_effects=True, vmem_limit_bytes=VMEM_BYTES
        ),
        name="sum_gradients",
    )(*args)


def finish(layout, batches, returns, core_ref, total, sib_kv, *refs):
    returned, y_refs, refs = refs[:returns], refs[returns : returns + 3], refs[returns + 4 :]
    (
        ends, ln1_gain, ln1_bias, q_weight, q_bias, kv_weight, v_bias, out_weight, out_bias, table,
        ln2_gain, ln2_bias, up_weight, up_bias, down_weight, down_bias, placed, copy_sem,
    ) = refs
    is_encoder = core_ref[0] == 0
    step = pl.program_id(0)

    def copies():
        return [
            pltpu.make_async_copy(
                ref,
                ends.at[batches - returns + k, pl.ds(WIN, WIN), pl.ds(step * WIN, WIN)],
                copy_sem.at[6 + k],
            )
            for k, ref in enumerate(returned)
        ]

    def output_copies():
        return place_outputs(y_refs, ends, batches - 1, step, copy_sem)

    pl.when(is_encoder)(lambda: start_all(copies()))
    pl.when(jnp.logical_not(is_encoder))(lambda: start_all(output_copies()))

    @pl.when(step == 0)
    def _():
        unpack(
            layout, is_encoder, total, sib_kv, ln1_gain, ln1_bias, q_weight, q_bias, kv_weight,
            v_bias, out_weight, out_bias, table, ln2_gain, ln2_bias, up_weight, up_bias, down_weight,
            down_bias, placed,
        )

    pl.when(is_encoder)(lambda: wait_all(copies()))
    pl.when(jnp.logical_not(is_encoder))(lambda: wait_all(output_copies()))


def unpack(
    layout, is_encoder, total, sib_kv, ln1_gain, ln1_bias, q_weight, q_bias, kv_weight,
    v_bias, out_weight, out_bias, table, ln2_gain, ln2_bias, up_weight, up_bias, down_weight, down_bias,
    placed,
):
    channels, tall, half = layout.channels, layout.tall, LANES_A // 2

    def at(start, rows):
        return total[start : start + rows].astype(F32)

    vec = at(layout.vec, 16)
    vec = jnp.concatenate([vec[:8], vec[8:, :half]], 1)
    for row, ref in enumerate((ln1_gain, ln1_bias, ln2_gain, ln2_bias, down_bias)):
        ref[...] = vec[row : row + 1]

    for k in range(layout.tiles):
        cols = slice(k * LANES_A, (k + 1) * LANES_A)
        tile = at(layout.up + k * tall, tall)
        up_weight[:, cols] = tile[:channels]
        up_bias[:, cols] = tile[channels : channels + 1]
        down_weight[:, cols] = at(layout.down + k * channels, channels)
    rest = at(layout.rest, tall)
    q = jnp.concatenate([at(layout.q, tall), rest[:, :half]], 1)
    out = jnp.concatenate([at(layout.out, tall), rest[:, half:]], 1)
    q_weight[...] = q[:channels]
    q_bias[...] = q[channels : channels + 1]
    out_weight[...] = out[:channels]
    out_bias[...] = out[channels : channels + 1]
    mine = at(layout.kv, 2 * tall)
    other = sib_kv[...].astype(F32)
    for start, side in ((0, jnp.where(is_encoder, mine, other)), (channels, jnp.where(is_encoder, other, mine))):
        side = jnp.concatenate([side[:tall], side[tall:, :half]], 1)
        kv_weight[:, start : start + channels] = side[:channels]
    v_bias[...] = side[channels : channels + 1]
    placed[...] = jnp.zeros_like(placed)
    positions = [position_matrix(False), position_matrix(True)]
    for h in range(HEADS):
        start = layout.bias + h // 2 * CELLS
        placed[h, :, :256] = nt(total[start : start + CELLS], positions[h % 2])
    entries = jnp.zeros((8, 384), F32)
    for j in range(CELLS):
        entries += pltpu.roll(placed[:, j, :], CENTRE - cell_position(j), 1)
    table[...] = entries[:HEADS, : SPAN**3][:, None]


def run_finish(core, total, sib_kv, returned, ys, ends, layout):
    arrays, specs = strips(ys, *ends.shape[3:])
    channels = layout.channels
    hidden = layout.tiles * LANES_A
    _, _, rows_y, rows_z, _ = ends.shape
    any_spec = pl.BlockSpec(memory_space=pl.ANY)
    shapes = [
        (1, channels), (1, channels), (channels, channels), (1, channels), (channels, 2 * channels),
        (1, channels), (channels, channels), (1, channels), (HEADS, 1, SPAN**3),
        (1, channels), (1, channels), (channels, hidden), (1, hidden), (channels, hidden), (1, channels),
    ]
    shapes = [jax.ShapeDtypeStruct(shape, F32) for shape in shapes]
    return pl.pallas_call(
        functools.partial(finish, layout, ends.shape[0], len(returned)),
        grid_spec=pltpu.PrefetchScalarGridSpec(
            num_scalar_prefetch=1,
            grid=(rows_y // WIN,),
            in_specs=[
                *[whole(a) for a in (total, sib_kv)],
                *[
                    pl.BlockSpec(
                        (WIN, WIN, rows_z, channels), lambda i, c: (0, i * (1 - c[0]), 0, 0)
                    )
                ]
                * len(returned),
                *specs,
                any_spec,
            ],
            out_specs=[any_spec, *[whole(a) for a in shapes]],
            scratch_shapes=[
                pltpu.VMEM((8, CELLS, 384), F32),
                pltpu.SemaphoreType.DMA((6 + len(returned),)),
            ],
        ),
        out_shape=[jax.ShapeDtypeStruct(ends.shape, F32), *shapes],
        input_output_aliases={3 + len(returned) + len(arrays): 0},
        compiler_params=params,
        name="finish",
    )(core, total, sib_kv, *returned, *arrays, ends)


def cell_position(ids):
    x = 2 * (ids // 32) + ids // 4 % 2
    y = 2 * (ids // 16 % 2) + ids // 2 % 2
    z = 2 * (ids // 8 % 2) + ids % 2
    return (x * SPAN + y) * SPAN + z


CENTRE = (WIN - 1) * (SPAN * SPAN + SPAN + 1)
TABLE_ROW = 8


def position_matrix(odd):
    rows = lax.broadcasted_iota(jnp.int32, (256, 2 * CELLS), 0)
    ids = lax.broadcasted_iota(jnp.int32, (256, 2 * CELLS), 1) - (CELLS if odd else 0)
    hit = (ids >= 0) & (ids < CELLS) & (rows == cell_position(ids))
    return jnp.where(hit, 1.0, 0.0).astype(BF16)


def spread_bias(table, shifted):
    for j in range(CELLS):
        turned = pltpu.roll(table, (384 - CENTRE + cell_position(j)) % 384, 1)
        for h in range(HEADS):
            shifted[h, j : j + 1] = turned[h : h + 1, :256]
    even, odd = position_matrix(False), position_matrix(True)
    pairs = [
        nn(shifted[2 * p].astype(BF16), even) + nn(shifted[2 * p + 1].astype(BF16), odd)
        for p in range(HEADS // 2)
    ]
    return jnp.concatenate(pairs, 1) * log2_e


def prepare(
    blocks, q_w, out_w, up_w, down_w, kv_w, v_b, ln1_g, ln1_b, ln2_g, ln2_b, out_b, down_b, q_b, up_b, table,
    weights_e, vectors_e, bias_e, weights_d, vectors_d, bias_d,
    small, small_sib, q_sib, out_sib, up_sib, down_sib, shifted, send_sem, recv_sem,
):
    core, block = lax.axis_index("section"), lax.axis_index("tok")
    channels, hidden = up_w.shape
    sibling = {"section": 1 - core}
    barrier = pltpu.get_barrier_semaphore()
    pl.semaphore_signal(barrier, inc=1, device_id=sibling, device_id_type=MESH)
    small[...] = jnp.zeros_like(small)
    for row, ref in enumerate((ln1_g, ln1_b, ln2_g, ln2_b, out_b, down_b, q_b)):
        small[row : row + 1, :channels] = ref[...].astype(F32)
    small[7:8, :hidden] = up_b[...].astype(F32)
    small[TABLE_ROW : TABLE_ROW + HEADS, : SPAN**3] = table[...].astype(F32)
    pl.semaphore_wait(barrier, 1)
    pairs = ((small, small_sib), (q_w, q_sib), (out_w, out_sib), (up_w, up_sib), (down_w, down_sib))
    copies = [
        pltpu.make_async_remote_copy(
            src_ref=source, dst_ref=target, send_sem=send_sem.at[k], recv_sem=recv_sem.at[k],
            device_id=sibling, device_id_type=MESH,
        )
        for k, (source, target) in enumerate(pairs)
    ]
    for copy in copies:
        copy.start()
    for copy in copies:
        copy.wait()

    def place(enc, dec):
        e_small, d_small = enc[0], dec[0]
        for weights, vectors, (source, q, out, up, down) in (
            (weights_e, vectors_e, enc), (weights_d, vectors_d, dec),
        ):
            weights[2 * channels :] = jnp.zeros((2 * channels, hidden), BF16)
            weights[:channels] = up[...]
            weights[channels : 2 * channels] = down[...]
            weights[2 * channels : 3 * channels, :channels] = q[...]
            weights[3 * channels :, :channels] = out[...]
            vectors[...] = jnp.zeros_like(vectors)
            vectors[:8, :channels] = source[:8, :channels]
            vectors[8:9, :hidden] = source[7:8, :hidden]
            vectors[9:10, :channels] = source[6:7, :channels]
        weights_e[2 * channels : 3 * channels, 256 : 256 + channels] = kv_w[:, :channels]
        weights_e[2 * channels : 3 * channels, 512 : 512 + channels] = kv_w[:, channels:]
        vectors_e[9:10, 512 : 512 + channels] = v_b[...].astype(F32)
        rows = slice(TABLE_ROW, TABLE_ROW + 8)
        bias_e[...] = spread_bias(e_small[rows, :384], shifted)
        return spread_bias(d_small[rows, :384], shifted)

    own = (small, q_w, out_w, up_w, down_w)
    sib = (small_sib, q_sib, out_sib, up_sib, down_sib)

    def masked(base):
        shape = (CELLS, HEADS * CELLS)
        keys = lax.broadcasted_iota(jnp.int32, shape, 0)
        queries = lax.broadcasted_iota(jnp.int32, shape, 1) % CELLS

        def differ(unit):
            return jnp.where(keys // unit % 2 != queries // unit % 2, 1.0, 0.0)

        last = jnp.where((core == 1) & (block == blocks - 1), 1.0, 0.0)
        for y in range(2):
            for z in range(2):
                apart = jnp.maximum(last * differ(32), jnp.maximum(y * differ(16), z * differ(8)))
                bias_d[y, z] = base + apart * (mask_fill * log2_e)

    @pl.when(core == 0)
    def _():
        masked(place(own, sib))

    @pl.when(core == 1)
    def _():
        masked(place(sib, own))


def run_prepare(blocks, weights, smalls, table, kv_weight, v_bias):
    q_w, out_w, up_w, down_w = weights
    channels, hidden = up_w.shape
    vmem = pl.BlockSpec(memory_space=pltpu.VMEM)
    args = [*weights, kv_weight, v_bias, *smalls, table]
    bias = (CELLS, HEADS * CELLS)
    square = (channels, channels)
    layer = [
        jax.ShapeDtypeStruct((4 * channels, hidden), BF16),
        jax.ShapeDtypeStruct((16, hidden), F32),
    ]
    shapes = [
        *layer,
        jax.ShapeDtypeStruct(bias, F32),
        *layer,
        jax.ShapeDtypeStruct((2, 2, *bias), F32),
    ]
    return pl.pallas_call(
        functools.partial(prepare, blocks),
        in_specs=[vmem] * len(args),
        out_specs=[vmem] * len(shapes),
        out_shape=shapes,
        scratch_shapes=[
            pltpu.VMEM((TABLE_ROW + 8, hidden), F32),
            pltpu.VMEM((TABLE_ROW + 8, hidden), F32),
            pltpu.VMEM(square, BF16),
            pltpu.VMEM(square, BF16),
            pltpu.VMEM((channels, hidden), BF16),
            pltpu.VMEM((channels, hidden), BF16),
            pltpu.VMEM((HEADS, CELLS, 256), F32),
            pltpu.SemaphoreType.DMA((5,)),
            pltpu.SemaphoreType.DMA((5,)),
        ],
        compiler_params=pltpu.CompilerParams(
            collective_id=1, has_side_effects=True, vmem_limit_bytes=VMEM_BYTES
        ),
        name="prepare",
    )(*args)


def run_encoder(core, tokens, first, count, consts, cotangent):
    _, _, rows_y, rows_z, channels = tokens.shape
    groups, size = rows_y // WIN, 4 * rows_z
    cells = 4 * size
    hidden = consts[1].shape[1]
    slab = (2, 3, size * 3 // 2, LANES_A)
    steps = count * groups
    sends = [jax.ShapeDtypeStruct((groups, *slab), BF16)] * count
    outs = [
        jax.ShapeDtypeStruct((steps, *slab), BF16),
        jax.ShapeDtypeStruct((steps, cells, 512), F32),
        jax.ShapeDtypeStruct((steps, cells, 2 * hidden + HEADS * CELLS + 256), BF16),
    ]

    def send_spec(k):
        def place(i, c):
            return (jnp.clip(i - k * groups, 0, groups - 1), 0, 0, 0, 0)

        return pl.BlockSpec((1, *slab), place)

    def row(array):
        zeros = (0,) * (array.ndim - 1)
        return pl.BlockSpec((1, *array.shape[1:]), lambda i, c: (i, *zeros))

    batches = tokens.shape[0]
    cut = [] if cotangent is None else [cotangent]
    cut_block = (batches, SHIFT, WIN, rows_z, channels)
    cut_outs = [
        jax.ShapeDtypeStruct((batches, SHIFT, rows_y, rows_z, channels), a.dtype) for a in cut
    ]
    return pl.pallas_call(
        functools.partial(encoder_forward, len(cut), count, groups),
        grid_spec=pltpu.PrefetchScalarGridSpec(
            num_scalar_prefetch=1,
            grid=(steps,),
            in_specs=[
                pl.BlockSpec(
                    (1, WIN, WIN, rows_z, channels),
                    lambda i, c: (first + i // groups, c[0], i % groups, 0, 0),
                ),
                *[whole(a) for a in consts],
                *[pl.BlockSpec(cut_block, lambda i, c: (0, 2 * c[0], i, 0, 0)) for _ in cut],
            ],
            out_specs=[
                *[send_spec(k) for k in range(count)],
                *[row(a) for a in outs],
                *[pl.BlockSpec(cut_block, lambda i, c: (0, 0, i, 0, 0)) for _ in cut],
            ],
            scratch_shapes=[pltpu.VMEM((cells, 768), BF16)],
        ),
        out_shape=[*sends, *outs, *cut_outs],
        compiler_params=params,
        cost_estimate=cost(steps * cells, 466944, steps * cells * 7500),
        name="encoder_forward",
    )(core, tokens, *consts, *cut)


def run_encoder_back(core, batch, own, halo, ys, returned, kept, old, consts, tokens):
    saved, at = kept
    groups, _, _, packed, _ = own.shape
    batches, planes, rows_y, rows_z, channels = tokens.shape
    size = 4 * rows_z
    hidden = consts[1].shape[1]
    first = old is None
    sums = jax.ShapeDtypeStruct((sum_rows(channels, True), hidden), F32)
    outs = [
        jax.ShapeDtypeStruct(tokens.shape, F32),
        jax.ShapeDtypeStruct((WIN, rows_y, rows_z, channels), F32),
        sums,
    ]

    def slab(unit):
        def place(i, c):
            return ((i if unit == 0 else (i + groups - 1) % groups), unit, 0, 0, 0)

        return pl.BlockSpec((1, 1, 3, packed, LANES_A), place)

    def row(array):
        zeros = (0,) * (array.ndim - 1)
        return pl.BlockSpec((1, *array.shape[1:]), lambda i, c: (at * groups + i, *zeros))

    arrays, specs = strips(ys, rows_z, channels)
    back_spec = pl.BlockSpec((WIN, WIN, rows_z, channels), lambda i, c: (0, i * (1 - c[0]), 0, 0))
    any_spec = pl.BlockSpec(memory_space=pl.ANY)
    olds = [] if first else [old[1], old[0]]
    args = [core, *consts, own, own, halo, halo, *saved, *arrays, *returned, *olds]
    return pl.pallas_call(
        functools.partial(encoder_backward, first, batch, len(returned), len(arrays)),
        grid_spec=pltpu.PrefetchScalarGridSpec(
            num_scalar_prefetch=1,
            grid=(groups,),
            in_specs=[
                *[whole(a) for a in consts],
                slab(0),
                slab(1),
                slab(0),
                slab(1),
                *[row(a) for a in saved],
                *specs,
                *[back_spec] * len(returned),
                *[whole(a) for a in olds[:-1]],
                *[any_spec] * (0 if first else 1),
            ],
            out_specs=[any_spec, any_spec, whole(sums)],
            scratch_shapes=[
                pltpu.VMEM((4 * size, 768), BF16),
                pltpu.VMEM((3, 4 * size, channels), BF16),
                pltpu.VMEM((2, WIN, WIN, rows_z, channels), F32),
                pltpu.SemaphoreType.DMA((2,)),
                pltpu.SemaphoreType.DMA((8 + batches,)),
            ],
        ),
        out_shape=outs,
        input_output_aliases={} if first else {len(args) - 1: 0},
        compiler_params=params,
        cost_estimate=cost(groups * 4 * size, 933888, groups * 4 * size * 9000),
        name="encoder_backward",
    )(*args)


def run_decoder(core, keep, at, recv, cotangent, cot_recv, batch, old, outputs, slot, consts):
    groups, _, _, packed, _ = recv.shape
    rows_z, channels = cotangent.shape[3:]
    size = 4 * rows_z
    hidden = consts[1].shape[1]
    windows = rows_z // WIN
    first = old is None
    sums = jax.ShapeDtypeStruct((sum_rows(channels, False), hidden), F32)
    slab_shape = jax.ShapeDtypeStruct((groups, 2, 3, packed, LANES_A), BF16)
    outs = [
        *[jax.ShapeDtypeStruct(shape, F32) for shape in outputs[0]],
        slab_shape,
        slab_shape,
        sums,
    ]

    def slab(unit, start):
        def place(i, c):
            return (start + (i if unit == 1 else (i + 1) % groups), unit, 0, 0, 0)

        return pl.BlockSpec((1, 1, 3, packed, LANES_A), place)

    def cot(unit, own):
        def place(i, c):
            y = 2 * i + 1 if unit == 1 else (2 * i + 2) % (2 * groups)
            return (batch, 2 * c[0] + 1 if own else 0, y, 0, 0)

        return pl.BlockSpec((1, 2, 2, rows_z, channels), place)

    def bias_place(i, c):
        return (i // (groups - 1), 0, 0, 0)

    specs = [whole(a) for a in consts]
    specs[3] = pl.BlockSpec((1, *consts[3].shape[1:]), bias_place)
    olds = [] if first else [old]
    out_slab = pl.BlockSpec((1, 2, 3, packed, LANES_A), lambda i, c: (i, 0, 0, 0, 0))
    args = [
        core, *consts, keep, keep, recv, recv, cotangent, cotangent, cot_recv, cot_recv, *olds, *outputs[1],
    ]
    return pl.pallas_call(
        functools.partial(decoder, first, len(outputs[1])),
        grid_spec=pltpu.PrefetchScalarGridSpec(
            num_scalar_prefetch=1,
            grid=(groups,),
            in_specs=[
                *specs,
                slab(1, at * groups),
                slab(0, at * groups),
                slab(1, 0),
                slab(0, 0),
                cot(1, True),
                cot(0, True),
                cot(1, False),
                cot(0, False),
                *[whole(a) for a in olds],
                *[pl.BlockSpec(memory_space=pl.ANY)] * len(outputs[1]),
            ],
            out_specs=[
                *[
                    pl.BlockSpec((1, n, WIN, rows_z, channels), lambda i, c: (slot, 0, i, 0, 0))
                    for n in (4, 2)
                ],
                out_slab,
                out_slab,
                whole(sums),
            ],
            scratch_shapes=[
                pltpu.VMEM((windows, CELLS, HEADS * CELLS), F32),
                pltpu.VMEM((4 * size, channels), BF16),
                pltpu.VMEM((4 * size, hidden), BF16),
                pltpu.VMEM((4 * size, hidden), F32),
                pltpu.VMEM((3, 4 * size, channels), F32),
            ],
        ),
        out_shape=outs,
        input_output_aliases={
            len(args) - len(outputs[1]) + k: k for k in range(len(outputs[1]))
        },
        compiler_params=params,
        cost_estimate=cost(groups * 4 * size, 1253376, groups * 4 * size * 4000),
        name="decoder",
    )(*args)


def body(
    tokens,
    cotangent,
    ln1_gain,
    ln1_bias,
    q_weight,
    q_bias,
    kv_weight,
    v_bias,
    out_weight,
    out_bias,
    rel_table,
    ln2_gain,
    ln2_bias,
    up_weight,
    up_bias,
    down_weight,
    down_bias,
):
    batches, planes, rows_y, rows_z, channels = tokens.shape
    axes = ("section", "tok")
    core = lax.axis_index("section")
    block = lax.axis_index("tok")
    blocks = lax.axis_size("tok")
    is_encoder = core == 0
    core_arg = core.astype(jnp.int32).reshape(1)

    def device(position):
        position = position % (2 * blocks)
        return (position % 2) * blocks + position // 2

    to_previous = [(device(r), device(r - 1)) for r in range(2 * blocks)]
    to_next = [(device(r), device(r + 1)) for r in range(2 * blocks)]

    weights_e, vectors_e, bias_e, weights_d, vectors_d, bias_d = run_prepare(
        blocks,
        (q_weight[0], out_weight[0], up_weight[0], down_weight[0].T),
        (ln1_gain, ln1_bias, ln2_gain, ln2_bias, out_bias, down_bias, q_bias, up_bias),
        rel_table[0],
        kv_weight,
        v_bias[None],
    )
    order = jnp.asarray(order_matrix(rows_z, 0), BF16)
    order_rolled = jnp.asarray(order_matrix(rows_z, 1), BF16)

    enc_consts = (order, weights_e, vectors_e, bias_e)
    enc_back_consts = (order, weights_e, vectors_e)
    dec_consts = (order_rolled, weights_d, vectors_d, bias_d)

    handed, saved = [], []
    for first, count in ((0, 1), (1, batches - 1)):
        results = run_encoder(
            core_arg, tokens, first, count, enc_consts, cotangent if first == 0 else None
        )
        sends, (keep, *rest) = results[:count], results[count:]
        if first == 0:
            *rest, half = rest
            cot_recv = lax.ppermute(half, axes, to_previous)
        for k in range(count):
            handed.append((keep, k, lax.ppermute(sends[k], axes, to_previous)))
            saved.append((rest, k))
    dec_sums = None
    returned, ys = [], []
    to_decoder = [(t, blocks + t) for t in range(blocks)]
    to_encoder = [(blocks + t, t) for t in range(blocks)]
    to_after = [(blocks + t, blocks + (t + 1) % blocks) for t in range(blocks)]
    for batch in range(batches):
        last = batch == batches - 1
        share = 1 if last else batches - 1
        if batch == 0 or last:
            kept = []
        shapes = [(share, n, rows_y, rows_z, channels) for n in (4, 2)]
        slot = 0 if last else batch
        *kept, own, halo, dec_sums = run_decoder(
            core_arg, *handed[batch], cotangent, cot_recv, batch, dec_sums, (shapes, kept), slot, dec_consts
        )
        returned.append((own, lax.ppermute(halo, axes, to_next)))
        if batch >= batches - 2:
            out_all, out_tail = kept
            arrays = (
                out_all, lax.ppermute(out_tail, axes, to_after), lax.ppermute(out_all, axes, to_decoder),
            )
            ys += [(arrays, k) for k in range(share)]
    old = None
    backs = []
    for batch in range(batches):
        arrived = backs[:1] if batch == batches - 1 else []
        ends, back, enc_sums = run_encoder_back(
            core_arg, batch, *returned[batch], ys[batch - 1] if batch else None, arrived, saved[batch], old,
            enc_back_consts, tokens,
        )
        old = (ends, enc_sums)
        backs.append(lax.ppermute(back, axes, to_encoder))

    layout = Layout(channels, up_weight.shape[2], blocks)
    total, sib_kv = run_sum(enc_sums, dec_sums, layout, blocks)
    (
        ends, g_ln1_gain, g_ln1_bias, g_q_weight, g_q_bias, g_kv_weight, g_v_bias, g_out_weight,
        g_out_bias, g_table, g_ln2_gain, g_ln2_bias, g_up_weight, g_up_bias, g_down_weight, g_down_bias,
    ) = run_finish(core_arg, total, sib_kv, backs[1:], ys[-1], ends, layout)
    return (
        ends[None],
        g_ln1_gain,
        g_ln1_bias,
        g_q_weight[None],
        g_q_bias,
        g_kv_weight[None],
        g_v_bias,
        g_out_weight[None],
        g_out_bias,
        g_table.transpose(1, 0, 2),
        g_ln2_gain,
        g_ln2_bias,
        g_up_weight[None],
        g_up_bias,
        g_down_weight.T[None],
        g_down_bias,
    )


def solution(mesh):
    in_specs = (
        P(None, "tok", None, None, None),
        P(None, "tok", None, None, None),
        P("section", None),
        P("section", None),
        P("section", None, None),
        P("section", None),
        P(),
        P(),
        P("section", None, None),
        P("section", None),
        P("section", None, None),
        P("section", None),
        P("section", None),
        P("section", None, None),
        P("section", None),
        P("section", None, None),
        P("section", None),
    )
    out_specs = (
        P("section", None, "tok", None, None, None),
        P("section", None),
        P("section", None),
        P("section", None, None),
        P("section", None),
        P("section", None, None),
        P("section", None),
        P("section", None, None),
        P("section", None),
        P("section", None, None),
        P("section", None),
        P("section", None),
        P("section", None, None),
        P("section", None),
        P("section", None, None),
        P("section", None),
    )
    return jax.shard_map(body, mesh=mesh, in_specs=in_specs, out_specs=out_specs, check_vma=False)
```

```python
import functools

import jax
import jax.numpy as jnp
import numpy as np
from jax import lax
from jax.experimental import pallas as pl
from jax.experimental.pallas import tpu as pltpu
from jax.sharding import PartitionSpec as P

HEADS = 6
HD = 32
WIN = 4
SHIFT = 2
CELLS = WIN**3
SPAN = 2 * WIN - 1
HEADS_A = 4
LANES_A = HEADS_A * HD
COLS_A = HEADS_A * CELLS

eps_norm = 1e-05
mask_fill = -100.0
log2_e = 1.4426950408889634
root_half = 0.7071067811865476
inv_root_two_pi = 0.3989422804014327
scale = HD ** (-0.5)
VMEM_BYTES = 63 * 1024 * 1024

F32 = jnp.float32
BF16 = jnp.bfloat16


def nn(left, right):
    return lax.dot_general(left, right, (((1,), (0,)), ((), ())), preferred_element_type=F32)


def nt(left, right):
    return lax.dot_general(left, right, (((1,), (1,)), ((), ())), preferred_element_type=F32)


def tn(left, right):
    return lax.dot_general(left, right, (((0,), (0,)), ((), ())), preferred_element_type=F32)


def order_matrix(rows_z, rolled):
    count = 4 * rows_z
    matrix = np.zeros((count, count), np.float32)
    units = rows_z // 2
    for unit in range(units):
        for dx in range(2):
            for dy in range(2):
                for dz in range(2):
                    z = (2 * (unit + rolled) + dz) % rows_z
                    matrix[unit * 8 + dx * 4 + dy * 2 + dz, (dx * 2 + dy) * rows_z + z] = 1.0
    return np.concatenate([matrix, matrix.T, matrix.T], 1)


def windows_of(pieces):
    count, rows, channels = pieces.shape
    return pieces.reshape(count, rows // 16, 16, channels).transpose(1, 0, 2, 3).reshape(-1, channels)


def pieces_of(windows):
    rows, channels = windows.shape
    return (
        windows.reshape(rows // CELLS, 4, 16, channels)
        .transpose(1, 0, 2, 3)
        .reshape(4, rows // 4, channels)
    )


def roll_rows(pieces, steps):
    return jnp.concatenate([pieces[:, steps:], pieces[:, :steps]], 1)


def pack_slab(pieces):
    half = pieces.shape[1] // 2
    rest = pieces[:, :, LANES_A:]
    return jnp.concatenate(
        [pieces[:, :, :LANES_A], jnp.concatenate([rest[:, :half], rest[:, half:]], 2)], 1
    ).astype(BF16)


def unpack_slab(block):
    size = block.shape[0] * 2 // 3
    half = LANES_A // 2
    rest = jnp.concatenate([block[size:, :half], block[size:, half:]], 0)
    return jnp.concatenate([block[:size], rest], 1)


def normalize(rows):
    mean = jnp.mean(rows, -1, keepdims=True)
    centered = rows - mean
    inv_std = lax.rsqrt(jnp.mean(centered * centered, -1, keepdims=True) + eps_norm)
    return centered * inv_std, inv_std


def norm_back(grad_rows, unit_rows, inv_std, gain):
    scaled = grad_rows * gain
    return inv_std * (
        scaled
        - jnp.mean(scaled, -1, keepdims=True)
        - unit_rows * jnp.mean(scaled * unit_rows, -1, keepdims=True)
    )


def gelu_pair(rows):
    upper = 0.5 * lax.erf(rows * root_half) + 0.5
    bell = jnp.exp2(rows * rows * (-0.5 * log2_e))
    return rows * upper, upper + rows * bell * inv_root_two_pi


def head_masks(width):
    heads = lax.broadcasted_iota(jnp.int32, (1, width), 1) // HD
    return [jnp.where(heads == h, 1.0, 0.0).astype(BF16) for h in range(width // HD)]


def expand(rows):
    masks = head_masks(rows.shape[1])
    return jnp.concatenate([rows * mask for mask in masks], 0)


def collapse(stacked):
    width = stacked.shape[1]
    lanes = lax.broadcasted_iota(jnp.int32, (CELLS, width), 1)
    total = stacked[:CELLS]
    for h in range(1, width // HD):
        total = jnp.where(lanes >= h * HD, stacked[h * CELLS : (h + 1) * CELLS], total)
    return total


def split(rows):
    return rows[:, :LANES_A], rows[:, LANES_A:]


def attend(parts, bias):
    queries, keys, values = zip(*[[split(rows) for rows in part] for part in parts])
    wide = [[expand(half) for half in q] for q in queries]
    scores = [
        jnp.concatenate([nt(k[0], q[0]), nt(k[1], q[1])], 1) for k, q in zip(keys, wide)
    ]
    scores = [s * (scale * log2_e) + b for s, b in zip(scores, bias)]
    exponents = [jnp.exp2(s - jnp.max(s, 0, keepdims=True)) for s in scores]
    probs = [e * (1.0 / jnp.sum(e, 0, keepdims=True)) for e in exponents]
    low = [p.astype(BF16) for p in probs]
    mixed = [
        (tn(p[:, :COLS_A], v[0]), tn(p[:, COLS_A:], v[1])) for p, v in zip(low, values)
    ]
    mixed = [jnp.concatenate([collapse(m[0]), collapse(m[1])], 1).astype(BF16) for m in mixed]
    return mixed, probs


def attend_back(parts):
    queries, keys, values, grads = zip(
        *[[split(rows) for rows in part[:3] + part[4:]] for part in parts]
    )
    probs = [part[3] for part in parts]
    wide_g = [[expand(half) for half in g] for g in grads]
    d_probs = [
        jnp.concatenate([nt(v[0], g[0]), nt(v[1], g[1])], 1) for v, g in zip(values, wide_g)
    ]
    low = [part[3].astype(BF16) for part in parts]
    d_values = [
        jnp.concatenate([nn(p[:, :COLS_A], g[0]), nn(p[:, COLS_A:], g[1])], 1)
        for p, g in zip(low, wide_g)
    ]
    wide_q = [[expand(half) for half in q] for q in queries]
    d_scores = [
        p * (d - jnp.sum(d * p, 0, keepdims=True)) for p, d in zip(probs, d_probs)
    ]
    low_d = [d.astype(BF16) for d in d_scores]
    d_keys = [
        jnp.concatenate([nn(d[:, :COLS_A], q[0]), nn(d[:, COLS_A:], q[1])], 1) * scale
        for d, q in zip(low_d, wide_q)
    ]
    d_queries = [
        (tn(d[:, :COLS_A], k[0]), tn(d[:, COLS_A:], k[1])) for d, k in zip(low_d, keys)
    ]
    d_queries = [
        jnp.concatenate([collapse(d[0]), collapse(d[1])], 1) * scale for d in d_queries
    ]
    table = d_scores[0]
    for d in d_scores[1:]:
        table = table + d
    return d_queries, d_keys, d_values, table


def window_groups(count):
    return [range(k, min(k + TOGETHER, count)) for k in range(0, count, TOGETHER)]


def window_rows(k):
    return slice(k * CELLS, (k + 1) * CELLS)


def with_ones(rows):
    return jnp.concatenate([rows.T, jnp.ones((16, rows.shape[0]), BF16)], 0)


def col_sum(rows):
    return jnp.sum(rows, 0, keepdims=True)


def start_sums(old, new):
    @pl.when(pl.program_id(0) == 0)
    def _():
        new[...] = jnp.zeros_like(new) if old is None else old[...]


def arrange(order, rows):
    return nn(order[:, : order.shape[0]], rows)


def restore(order, rows):
    high = rows.astype(BF16)
    low = (rows - high.astype(F32)).astype(BF16)
    return nn(order[:, order.shape[0] :], jnp.concatenate([high, low], 0))


CHUNK = 256
BLOCK = 256
TOGETHER = 8


class View:
    def __init__(self, ref, row, rows, col, cols):
        self.ref, self.row, self.col, self.shape = ref, row, col, (rows, cols)

    def place(self, key):
        key = (slice(None), slice(None)) if key is Ellipsis else key
        key = key if isinstance(key, tuple) else (key, slice(None))
        return tuple(
            slice(start + part.indices(size)[0], start + part.indices(size)[1])
            for part, start, size in zip(key, (self.row, self.col), self.shape)
        )

    def __getitem__(self, key):
        return self.ref[self.place(key)]

    def __setitem__(self, key, value):
        self.ref[self.place(key)] = value

    def first_columns(self, cols):
        return View(self.ref, self.row, self.shape[0], self.col, cols)


def layer_views(weights, vectors):
    hidden = weights.shape[1]
    channels = weights.shape[0] // 4
    q_cols = 768

    def rows(k, cols):
        return View(weights, k * channels, channels, 0, cols)

    return (
        View(vectors, 0, 8, 0, channels),
        View(vectors, 8, 1, 0, hidden),
        View(vectors, 9, 1, 0, q_cols),
        rows(0, hidden),
        rows(1, hidden),
        rows(2, q_cols),
        rows(3, channels),
    )


def sum_rows(channels, encoder):
    tall = channels + 16
    return 2 * tall + channels + (tall if encoder else 0)


def sum_views(sums, channels, encoder):
    tall = channels + 16
    base = tall + channels

    def view(row, rows, col, cols):
        return View(sums, row, rows, col, cols)

    fields = [view(base, tall, 256 * k, channels) for k in range(3 if encoder else 2)]
    last = base + (tall if encoder else 0)
    side = 256 if encoder else 512
    out = view(last, tall, 0, channels) if encoder else fields[1]
    bias = (view(last, CELLS, side, COLS_A), view(last + CELLS, CELLS, side, 2 * CELLS))
    vec = view(last + 2 * CELLS, 8, side, channels)
    return (
        view(0, tall, 0, sums.shape[1]),
        view(tall, channels, 0, sums.shape[1]),
        fields[:3] if encoder else fields[:1],
        out,
        vec,
        bias,
    )


def add_bias(views, table):
    views[0][...] += table[:, :COLS_A]
    views[1][...] += table[:, COLS_A:]


def encoder_forward(cuts, core_ref, tok, order, weights, vectors, bias, *rest):
    vec, b_up, b_qkv, w_up, w_down, w_qkv, w_out = layer_views(weights, vectors)
    cut_in, rest = rest[:cuts], rest[cuts:]
    send, keep, wide_out, low_out, *cut_out, qkv = rest
    hidden_cols = w_up.shape[1]
    s_start, p_start, o_start = hidden_cols, 2 * hidden_cols, 2 * hidden_cols + HEADS * CELLS
    for source, target in zip(cut_in, cut_out):
        target[...] = source[...]
    rows_z = tok.shape[3]
    size = 4 * rows_z
    pieces = []
    for x in range(2):
        for y in range(2):
            part = tok[0, 2 * x : 2 * x + 2, 2 * y : 2 * y + 2].reshape(size, -1)
            pieces.append(arrange(order, part))
    entry = windows_of(jnp.stack(pieces))
    unit, inv_std = normalize(entry)
    channels = entry.shape[1]
    wide = jnp.broadcast_to(inv_std, (entry.shape[0], 256 - channels))
    wide_out[0, :, :channels] = unit
    wide_out[0, :, channels:256] = wide
    left = (unit * vec[0:1] + vec[1:2]).astype(BF16)
    triple = nn(left, w_qkv[...]) + b_qkv[...]
    qkv[...] = triple.astype(BF16)
    for together in window_groups(entry.shape[0] // CELLS):
        parts = [
            [qkv[window_rows(k), 256 * f : 256 * f + 192] for f in range(3)] for k in together
        ]
        mixed, probs = attend(parts, [bias[...]] * len(parts))
        for k, o, p in zip(together, mixed, probs):
            low_out[0, window_rows(k), p_start:o_start] = p.astype(BF16)
            low_out[0, window_rows(k), o_start : o_start + channels] = o
    mixed = low_out[0, :, o_start : o_start + channels]
    middle = entry + nn(mixed, w_out[...]) + vec[4:5]
    unit, inv_std = normalize(middle)
    wide = jnp.broadcast_to(inv_std, (entry.shape[0], 256 - channels))
    wide_out[0, :, 256 : 256 + channels] = unit
    wide_out[0, :, 256 + channels :] = wide
    left = (unit * vec[2:3] + vec[3:4]).astype(BF16)
    results = []
    for k in range(entry.shape[0] // CHUNK):
        rows = slice(k * CHUNK, (k + 1) * CHUNK)
        hidden, slope = gelu_pair(nn(left[rows], w_up[...]) + b_up[...])
        hidden = hidden.astype(BF16)
        low_out[0, rows, :s_start] = hidden
        low_out[0, rows, s_start:p_start] = slope.astype(BF16)
        results.append(nt(hidden, w_down[...]))
    result = middle + jnp.concatenate(results, 0) + vec[5:6]
    for field, rows in enumerate((result, triple[:, 256:448], triple[:, 512:704])):
        rolled = pack_slab(roll_rows(pieces_of(rows), 8))
        send[0, :, field] = rolled[:2]
        keep[0, :, field] = rolled[2:]


def run_together(*works):
    works = list(works)
    while works:
        for work in list(works):
            try:
                next(work)
            except StopIteration:
                works.remove(work)


def row_blocks(count, size):
    return [slice(k, k + size) for k in range(0, count, size)]


def norm_back_steps(rows_grad, base, unit, inv_std, gain, g_vec, row, results):
    sums = [None, None]
    for rows in row_blocks(base.shape[0], BLOCK):
        grad = rows_grad(rows)
        found = (col_sum(grad * unit[rows]), col_sum(grad))
        sums = [f if total is None else total + f for f, total in zip(found, sums)]
        results.append(base[rows] + norm_back(grad, unit[rows], inv_std[rows], gain))
        yield
    g_vec[row : row + 1] += sums[0]
    g_vec[row + 1 : row + 2] += sums[1]


def product_steps(products):
    for target, cols, left, right in products:
        target[:, cols] += nn(left, right)
        yield


def mlp_back(grad, grad_low, hidden, slope, left_two, unit, inv_std, w_up, w_down, vec, sums):
    g_up, g_down, g_vec = sums
    backs, pres = [], []
    for rows in row_blocks(grad.shape[0], CHUNK):
        d_pre = (nn(grad_low[rows], w_down[...]) * slope(rows)).astype(BF16)
        pres.append(d_pre)
        backs.append(nt(d_pre, w_up[...]))
    d_pre = jnp.concatenate(pres, 0)
    d_normed = jnp.concatenate(backs, 0)
    ones, turned = with_ones(left_two), grad_low.T
    tiles = row_blocks(w_up.shape[1], 256)
    products = [(g_up, cols, ones, d_pre[:, cols]) for cols in tiles]
    products += [(g_down, cols, turned, hidden[:, cols]) for cols in tiles]
    results = []
    run_together(
        norm_back_steps(
            lambda rows: d_normed[rows], grad, unit, inv_std, vec[2:3], g_vec, 2, results
        ),
        product_steps(products),
    )
    g_vec[4:5] += col_sum(grad)
    return jnp.concatenate(results, 0)


def start_all(copies):
    for copy in copies:
        copy.start()


def wait_all(copies):
    for copy in copies:
        copy.wait()


def encoder_backward(
    first, batch, returns, core_ref, order, weights, vectors,
    y_own, y_halo, y_sib,
    keep_a, keep_b, recv_a, recv_b,
    wide_in, low_in, *rest,
):
    vec, _, b_qkv, w_up, w_down, w_qkv, w_out = layer_views(weights, vectors)
    channels, hidden_cols = w_up.shape
    s_start, p_start, o_start = hidden_cols, 2 * hidden_cols, 2 * hidden_cols + HEADS * CELLS
    returned, rest = rest[:returns], rest[returns:]
    old, rest = (None, rest) if first else (rest[0], rest[2:])
    ends, back, sums, qkv, dqkv, buffer, out_sem, copy_sem = rest
    g_up, g_down, g_fields, g_out, g_vec, g_bias = sum_views(sums, channels, True)
    step, steps = pl.program_id(0), pl.num_programs(0)
    is_encoder = core_ref[0] == 0
    rows_y = ends.shape[2]
    slot = lax.rem(step, 2)

    def output_copies():
        copies = []
        for start, planes, ref in ((0, 2, y_halo), (2, 4, y_sib), (6, 2, y_own)):
            for half in range(2):
                rows = pl.ds(lax.rem(step * WIN + SHIFT + 2 * half, rows_y), 2)
                target = ends.at[batch, pl.ds(start, planes), rows]
                copies.append((ref.at[:, pl.ds(2 * half, 2)], target))
        return [
            pltpu.make_async_copy(source, target, copy_sem.at[k])
            for k, (source, target) in enumerate(copies)
        ]

    def gradient_copies():
        return [
            pltpu.make_async_copy(
                ref, ends.at[k, pl.ds(WIN, WIN), pl.ds(step * WIN, WIN)], copy_sem.at[8 + k]
            )
            for k, ref in enumerate(returned)
        ]

    def result_copy(index, to_ends):
        target = (
            ends.at[batch, pl.ds(0, WIN), pl.ds(index * WIN, WIN)]
            if to_ends
            else back.at[:, pl.ds(index * WIN, WIN)]
        )
        at = lax.rem(index, 2)
        return pltpu.make_async_copy(buffer.at[at], target, out_sem.at[at])

    def for_core(encoder_work, decoder_work):
        pl.when(is_encoder)(encoder_work)
        pl.when(jnp.logical_not(is_encoder))(decoder_work)

    for_core(lambda: start_all(gradient_copies()), lambda: start_all(output_copies()))

    @pl.when(step >= 2)
    def _():
        for_core(
            lambda: result_copy(step - 2, True).wait(), lambda: result_copy(step - 2, False).wait()
        )

    start_sums(old, sums)
    fields = []
    for field in range(3):
        pieces = jnp.stack(
            [unpack_slab(ref[0, 0, field]) for ref in (recv_b, recv_a, keep_b, keep_a)]
        )
        fields.append(windows_of(pieces))
    grad_low, d_key_1, d_value_1 = fields
    grad = grad_low.astype(F32)
    unit_1, unit_2 = wide_in[0, :, :channels], wide_in[0, :, 256 : 256 + channels]
    wide_1, wide_2 = [wide_in[0, :, k + channels : k + channels + 1] for k in (0, 256)]
    left_1 = (unit_1 * vec[0:1] + vec[1:2]).astype(BF16)
    left_2 = (unit_2 * vec[2:3] + vec[3:4]).astype(BF16)
    qkv[...] = (nn(left_1, w_qkv[...]) + b_qkv[...]).astype(BF16)
    d_middle = mlp_back(
        grad, grad_low, low_in[0, :, :s_start], lambda rows: low_in[0, rows, s_start:p_start].astype(F32),
        left_2, unit_2, wide_2, w_up, w_down, vec,
        (g_up, g_down, g_vec),
    )
    branch = d_middle.astype(BF16)
    d_mixed = nt(branch, w_out[...]).astype(BF16)
    d_table = None
    for together in window_groups(grad.shape[0] // CELLS):
        parts = [
            [qkv[window_rows(k), 256 * f : 256 * f + 192] for f in range(3)]
            + [low_in[0, window_rows(k), p_start:o_start].astype(F32), d_mixed[window_rows(k)]]
            for k in together
        ]
        *d_qkv, d_s = attend_back(parts)
        for k, d_q, d_k, d_v in zip(together, *d_qkv):
            rows = window_rows(k)
            dqkv[0, rows] = d_q.astype(BF16)
            dqkv[1, rows] = (d_k + d_key_1[rows].astype(F32)).astype(BF16)
            dqkv[2, rows] = (d_v + d_value_1[rows].astype(F32)).astype(BF16)
        d_table = d_s if d_table is None else d_table + d_s
    add_bias(g_bias, d_table)
    ones = with_ones(left_1)
    every = slice(None)
    mixed = with_ones(low_in[0, :, o_start : o_start + channels])
    products = [(g_field, every, ones, dqkv[k]) for k, g_field in enumerate(g_fields)]
    products.append((g_out, every, mixed, branch))

    def rows_grad(rows):
        parts = [
            nt(dqkv[k, rows], w_qkv[:, 256 * k : 256 * k + channels]) for k in range(3)
        ]
        return parts[0] + parts[1] + parts[2]

    results = []
    run_together(
        norm_back_steps(rows_grad, d_middle, unit_1, wide_1, vec[0:1], g_vec, 0, results),
        product_steps(products),
    )
    result = pieces_of(jnp.concatenate(results, 0))
    rows_z = ends.shape[3]
    for x in range(2):
        for y in range(2):
            part = restore(order, result[2 * x + y])
            buffer[slot, 2 * x : 2 * x + 2, 2 * y : 2 * y + 2] = part.reshape(2, 2, rows_z, -1)
    for_core(lambda: result_copy(step, True).start(), lambda: result_copy(step, False).start())

    @pl.when(step == steps - 1)
    def _():
        def finish(to_ends):
            result_copy(step - 1, to_ends).wait()
            result_copy(step, to_ends).wait()

        for_core(lambda: finish(True), lambda: finish(False))

    for_core(lambda: wait_all(gradient_copies()), lambda: wait_all(output_copies()))


def decoder(
    first, core_ref, order, weights, vectors, bias,
    keep_1, keep_0, recv_1, recv_0, cot_1, cot_0, cot_r1, cot_r0, *rest,
):
    vec, b_up, b_qkv, w_up, w_down, w_qkv, w_out = layer_views(weights, vectors)
    channels = w_up.shape[0]
    w_q, b_q = w_qkv.first_columns(channels), b_qkv.first_columns(channels)
    old, new = (None, rest) if first else (rest[0], rest[1:])
    out_all, out_tail, own, halo, sums, a_scr, s_scr = new
    g_up, g_down, (g_q,), g_out, g_vec, g_bias = sum_views(sums, channels, False)
    start_sums(old, sums)
    fields = []
    for field in range(3):
        pieces = jnp.stack([unpack_slab(ref[0, 0, field]) for ref in (keep_1, keep_0, recv_1, recv_0)])
        fields.append(windows_of(pieces))
    entry_low, keys, values = fields
    entry = entry_low.astype(F32)
    unit_1, inv_1 = normalize(entry)
    left_1 = (unit_1 * vec[0:1] + vec[1:2]).astype(BF16)
    queries = (nn(left_1, w_q[...]) + b_q[...]).astype(BF16)
    windows = entry.shape[0] // CELLS
    all_probs, all_mixed = [], []
    for together in window_groups(windows):
        parts = [[rows[window_rows(k)] for rows in (queries, keys, values)] for k in together]
        mixed, probs = attend(parts, [bias[0, 1 if k == windows - 1 else 0] for k in together])
        all_probs += probs
        all_mixed += mixed
    mixed = jnp.concatenate(all_mixed, 0)
    middle = entry + nn(mixed, w_out[...]) + vec[4:5]
    unit_2, inv_2 = normalize(middle)
    left_2 = (unit_2 * vec[2:3] + vec[3:4]).astype(BF16)
    results = []
    for k in range(entry.shape[0] // CHUNK):
        rows = slice(k * CHUNK, (k + 1) * CHUNK)
        hidden, slope = gelu_pair(nn(left_2[rows], w_up[...]) + b_up[...])
        hidden = hidden.astype(BF16)
        a_scr[rows] = hidden
        s_scr[rows] = slope
        results.append(nt(hidden, w_down[...]))
    result = pieces_of(middle + jnp.concatenate(results, 0) + vec[5:6])
    rows_z = out_all.shape[2]
    size = 4 * rows_z
    for x in range(2):
        for y in range(2):
            part = restore(order, result[2 * x + y]).reshape(2, 2, rows_z, -1)
            out_all[2 * x : 2 * x + 2, 2 * y : 2 * y + 2] = part
            if x == 1:
                out_tail[:, 2 * y : 2 * y + 2] = part

    cots = [
        arrange(order, ref[0].reshape(size, -1)).astype(BF16) for ref in (cot_1, cot_0, cot_r1, cot_r0)
    ]
    grad_low = windows_of(jnp.stack(cots))
    grad = grad_low.astype(F32)
    d_middle = mlp_back(
        grad, grad_low, a_scr[...], lambda rows: s_scr[rows], left_2, unit_2, inv_2, w_up, w_down, vec,
        (g_up, g_down, g_vec),
    )
    branch = d_middle.astype(BF16)
    d_mixed = nt(branch, w_out[...]).astype(BF16)
    d_table = None
    found = [[], [], []]
    for together in window_groups(windows):
        parts = [
            [rows[window_rows(k)] for rows in (queries, keys, values)]
            + [all_probs[k], d_mixed[window_rows(k)]]
            for k in together
        ]
        *d_qkv, d_s = attend_back(parts)
        for f in range(3):
            found[f] += d_qkv[f]
        d_table = d_s if d_table is None else d_table + d_s
    add_bias(g_bias, d_table)
    d_queries, d_keys, d_values = [jnp.concatenate(rows, 0) for rows in found]
    d_queries = d_queries.astype(BF16)
    every = slice(None)
    products = [
        (g_q, every, with_ones(left_1), d_queries),
        (g_out, every, with_ones(mixed), branch),
    ]
    results = []
    run_together(
        norm_back_steps(
            lambda rows: nt(d_queries[rows], w_q[...]), d_middle, unit_1, inv_1, vec[0:1], g_vec, 0,
            results,
        ),
        product_steps(products),
    )
    d_entry = jnp.concatenate(results, 0)
    for field, rows in enumerate((d_entry, d_keys, d_values)):
        turned = pack_slab(roll_rows(pieces_of(rows), size - 8))
        own[0, :, field] = turned[:2]
        halo[0, :, field] = turned[2:]


def whole(array):
    zeros = (0,) * array.ndim
    return pl.BlockSpec(array.shape, lambda *_: zeros)


def cost(cells, per_cell, hbm):
    return pl.CostEstimate(
        flops=2 * cells * per_cell, bytes_accessed=hbm, transcendentals=cells * 1536
    )


params = pltpu.CompilerParams(
    dimension_semantics=("arbitrary",), vmem_limit_bytes=VMEM_BYTES
)


class Layout:
    def __init__(self, channels, hidden, blocks):
        tall = channels + 16
        self.tall, self.channels = tall, channels
        self.tiles = hidden // LANES_A
        self.up = 0
        self.down = self.tiles * tall
        self.q = self.down + self.tiles * channels
        self.out = self.q + tall
        self.rest = self.out + tall
        self.kv = self.rest + tall
        self.bias = self.kv + 2 * tall
        self.vec = self.bias + HEADS * CELLS // LANES_A * CELLS
        self.end = self.vec + 16
        units = -(-self.end // (16 * blocks))
        self.chunks = (units // 2 * 16, (units - units // 2) * 16)
        self.starts = (0, self.chunks[0] * blocks)
        self.rows = units * 16 * blocks


def fill(buffer, layout, up, down, q, out, kv, bias, vec):
    kind, half = buffer.dtype, LANES_A // 2
    tall, channels = layout.tall, layout.channels
    for k in range(layout.tiles):
        cols = slice(k * LANES_A, (k + 1) * LANES_A)
        buffer[layout.up + k * tall : layout.up + (k + 1) * tall] = up[:, cols].astype(kind)
        buffer[layout.down + k * channels : layout.down + (k + 1) * channels] = down[
            :, cols
        ].astype(kind)
    buffer[layout.q : layout.q + tall] = q[:, :LANES_A].astype(kind)
    buffer[layout.out : layout.out + tall] = out[:, :LANES_A].astype(kind)
    rests = jnp.concatenate([q[:, LANES_A:], out[:, LANES_A:]], 1)
    buffer[layout.rest : layout.rest + tall] = rests.astype(kind)
    buffer[layout.kv : layout.kv + tall] = kv[:, :LANES_A].astype(kind)
    rests = jnp.concatenate([kv[:, LANES_A:], jnp.zeros((tall, half), F32)], 1)
    buffer[layout.kv + tall : layout.kv + 2 * tall] = rests.astype(kind)
    tiles = [bias[0][:, :LANES_A], bias[0][:, LANES_A:], bias[1][...]]
    for k, tile in enumerate(tiles):
        start = layout.bias + k * CELLS
        buffer[start : start + CELLS] = tile.astype(kind)
    rests = jnp.concatenate([vec[:, LANES_A:], jnp.zeros((8, half), F32)], 1)
    both = jnp.concatenate([vec[:, :LANES_A], rests], 0)
    buffer[layout.vec : layout.vec + 16] = both.astype(kind)
    if layout.rows > layout.end:
        buffer[layout.end :] = jnp.zeros((layout.rows - layout.end, LANES_A), kind)


MESH = pl.DeviceIdType.MESH


def groups_of(blocks):
    near = 4 if blocks % 4 == 0 else blocks
    return near, blocks // near


def sum_gradients(layout, blocks, *refs):
    (
        enc_in, dec_in, total_out, kv_out,
        enc, dec, own, theirs, from_sib, low, total, sib_kv, landed_0, landed_1, near_low_0, near_low_1,
        far_landed_0, far_landed_1, load_sem, sib_send, sib_recv, send_sem, recv_sem,
    ) = refs
    landed, near_low = (landed_0, landed_1), (near_low_0, near_low_1)
    far_landed = (far_landed_0, far_landed_1)
    core, me = lax.axis_index("section"), lax.axis_index("tok")
    sibling = {"section": 1 - core}
    near, far = groups_of(blocks)
    inner, outer = lax.rem(me, near), lax.div(me, near)

    def near_peer(offset):
        return lax.rem(inner + offset, near)

    def far_peer(offset):
        return lax.rem(outer + offset, far)

    def near_device(offset):
        return {"tok": outer * near + near_peer(offset)}

    def far_device(offset):
        return {"tok": far_peer(offset) * near + inner}

    def each(count, work):
        def run(offset, carry):
            work(offset)
            return carry

        lax.fori_loop(1, count, run, 0)

    enc_load = pltpu.make_async_copy(enc_in, enc, load_sem.at[0])
    dec_load = pltpu.make_async_copy(dec_in, dec, load_sem.at[1])
    enc_load.start()
    dec_load.start()
    barrier = pltpu.get_barrier_semaphore()
    pl.semaphore_signal(barrier, inc=1, device_id=sibling, device_id_type=MESH)
    for count, device in ((near, near_device), (far, far_device)):
        each(
            count,
            lambda offset, device=device: pl.semaphore_signal(
                barrier, inc=1, device_id=device(offset), device_id_type=MESH
            ),
        )
    enc_load.wait()
    dec_load.wait()
    channels = layout.channels
    e_up, e_down, (e_q, e_k, e_v), e_out, e_vec, e_bias = sum_views(enc, channels, True)
    d_up, d_down, (d_q,), d_out, d_vec, d_bias = sum_views(dec, channels, False)

    def fill_enc(buffer, kv):
        fill(buffer, layout, e_up, e_down, e_q, e_out, kv, e_bias, e_vec)

    def fill_dec(buffer, kv):
        fill(buffer, layout, d_up, d_down, d_q, d_out, kv, d_bias, d_vec)

    pl.when(core == 0)(lambda: fill_dec(theirs, e_v))
    pl.when(core == 1)(lambda: fill_enc(theirs, e_k))
    pl.semaphore_wait(barrier, near + far - 1)

    def to_sibling(source, target, k):
        return pltpu.make_async_remote_copy(
            src_ref=source, dst_ref=target, send_sem=sib_send.at[k], recv_sem=sib_recv.at[k],
            device_id=sibling, device_id_type=MESH,
        )

    def piece_rows(p):
        return slice(layout.starts[p], layout.starts[p] + layout.chunks[p] * blocks)

    swaps = [to_sibling(theirs.at[piece_rows(p)], from_sib.at[piece_rows(p)], p) for p in range(2)]
    start_all(swaps)
    pl.when(core == 0)(lambda: fill_enc(own, e_k))
    pl.when(core == 1)(lambda: fill_dec(own, e_v))

    def quarter_of(p, position):
        size = far * layout.chunks[p]
        return pl.ds(pl.multiple_of(layout.starts[p] + position * size, 16), size)

    def chunk_of(p, position):
        return pl.ds(pl.multiple_of(position * layout.chunks[p], 16), layout.chunks[p])

    def rows_of(p, position):
        start = layout.starts[p] + (inner * far + position) * layout.chunks[p]
        return pl.ds(pl.multiple_of(start, 16), layout.chunks[p])

    def exchange(p, stage, offset, source, target, device):
        return pltpu.make_async_remote_copy(
            src_ref=source, dst_ref=target,
            send_sem=send_sem.at[p, stage, offset], recv_sem=recv_sem.at[p, stage, offset],
            device_id=device(offset), device_id_type=MESH,
        )

    def near_scatter(p, offset):
        source = low.at[quarter_of(p, near_peer(offset))]
        return exchange(p, 0, offset, source, landed[p].at[offset], near_device)

    def far_scatter(p, offset):
        source = near_low[p].at[chunk_of(p, far_peer(offset))]
        return exchange(p, 1, offset, source, far_landed[p].at[offset], far_device)

    def far_gather(p, offset, owner):
        rows = rows_of(p, owner)
        return exchange(p, 2, offset, total.at[rows], total.at[rows], far_device)

    def near_gather(p, offset, owner):
        rows = quarter_of(p, owner)
        return exchange(p, 3, offset, total.at[rows], total.at[rows], near_device)

    def reduced(count, copy, landing, start):
        def add(offset, carry):
            copy(offset).wait_recv()
            return carry + landing[offset].astype(F32)

        return lax.fori_loop(1, count, add, start)

    def send_near(p):
        swaps[p].wait()
        rows = piece_rows(p)
        own[rows] += from_sib[rows].astype(F32)
        low[rows] = own[rows].astype(BF16)
        each(near, lambda offset: near_scatter(p, offset).start())

    def send_far(p):
        rows = quarter_of(p, inner)
        near_sum = reduced(near, lambda o: near_scatter(p, o), landed[p], own[rows])
        own[rows] = near_sum
        near_low[p][...] = near_sum.astype(BF16)
        each(far, lambda offset: far_scatter(p, offset).start())

    def return_far(p):
        rows = rows_of(p, outer)
        far_sum = reduced(far, lambda o: far_scatter(p, o), far_landed[p], own[rows])
        total[rows] = far_sum.astype(BF16)
        each(far, lambda offset: far_gather(p, offset, outer).start())

    def return_near(p):
        each(far, lambda o: far_gather(p, o, lax.rem(outer + far - o, far)).wait_recv())
        each(near, lambda offset: near_gather(p, offset, inner).start())

    def arrive(p):
        each(near, lambda o: near_gather(p, o, lax.rem(inner + near - o, near)).wait_recv())

    send_near(0)
    send_near(1)
    send_far(0)
    return_far(0)
    send_far(1)
    return_near(0)
    return_far(1)
    return_near(1)
    arrive(0)
    arrive(1)
    third = to_sibling(total.at[layout.kv : layout.kv + 2 * layout.tall], sib_kv, 2)
    third.start()
    total_out[...] = total[...]
    for p in range(2):
        each(near, lambda offset, p=p: near_scatter(p, offset).wait_send())
        each(far, lambda offset, p=p: far_scatter(p, offset).wait_send())
        each(far, lambda offset, p=p: far_gather(p, offset, outer).wait_send())
        each(near, lambda offset, p=p: near_gather(p, offset, inner).wait_send())
    third.wait()
    kv_out[...] = sib_kv[...]


def run_sum(enc_sums, dec_sums, layout, blocks):
    rows, tall = layout.rows, layout.tall
    near, far = groups_of(blocks)
    dma = pltpu.SemaphoreType.DMA
    vmem = pl.BlockSpec(memory_space=pltpu.VMEM)
    args = [enc_sums, dec_sums]

    def buffers(*shape):
        return [pltpu.VMEM((*shape, far * c, LANES_A), BF16) for c in layout.chunks]

    return pl.pallas_call(
        functools.partial(sum_gradients, layout, blocks),
        in_specs=[pl.BlockSpec(memory_space=pl.ANY)] * len(args),
        out_specs=[vmem] * 2,
        out_shape=[
            jax.ShapeDtypeStruct((rows, LANES_A), BF16),
            jax.ShapeDtypeStruct((2 * tall, LANES_A), BF16),
        ],
        scratch_shapes=[
            *[pltpu.VMEM(a.shape, F32) for a in args],
            pltpu.VMEM((rows, LANES_A), F32),
            *[pltpu.VMEM((rows, LANES_A), BF16)] * 4,
            pltpu.VMEM((2 * tall, LANES_A), BF16),
            *buffers(near),
            *buffers(),
            *[pltpu.VMEM((far, c, LANES_A), BF16) for c in layout.chunks],
            dma((2,)),
            dma((3,)),
            dma((3,)),
            *[dma((2, 4, max(near, far)))] * 2,
        ],
        compiler_params=pltpu.CompilerParams(
            collective_id=0, has_side_effects=True, vmem_limit_bytes=VMEM_BYTES
        ),
        name="sum_gradients",
    )(*args)


def finish(layout, batches, returns, core_ref, total, sib_kv, *refs):
    returned, refs = refs[:returns], refs[returns + 1 :]
    (
        ends, ln1_gain, ln1_bias, q_weight, q_bias, kv_weight, v_bias, out_weight, out_bias, table,
        ln2_gain, ln2_bias, up_weight, up_bias, down_weight, down_bias, placed, copy_sem,
    ) = refs
    is_encoder = core_ref[0] == 0
    step = pl.program_id(0)

    def copies():
        return [
            pltpu.make_async_copy(
                ref,
                ends.at[batches - returns + k, pl.ds(WIN, WIN), pl.ds(step * WIN, WIN)],
                copy_sem.at[k],
            )
            for k, ref in enumerate(returned)
        ]

    pl.when(is_encoder)(lambda: start_all(copies()))

    @pl.when(step == 0)
    def _():
        unpack(
            layout, is_encoder, total, sib_kv, ln1_gain, ln1_bias, q_weight, q_bias, kv_weight,
            v_bias, out_weight, out_bias, table, ln2_gain, ln2_bias, up_weight, up_bias, down_weight,
            down_bias, placed,
        )

    pl.when(is_encoder)(lambda: wait_all(copies()))


def unpack(
    layout, is_encoder, total, sib_kv, ln1_gain, ln1_bias, q_weight, q_bias, kv_weight,
    v_bias, out_weight, out_bias, table, ln2_gain, ln2_bias, up_weight, up_bias, down_weight, down_bias,
    placed,
):
    channels, tall, half = layout.channels, layout.tall, LANES_A // 2

    def at(start, rows):
        return total[start : start + rows].astype(F32)

    vec = at(layout.vec, 16)
    vec = jnp.concatenate([vec[:8], vec[8:, :half]], 1)
    for row, ref in enumerate((ln1_gain, ln1_bias, ln2_gain, ln2_bias, down_bias)):
        ref[...] = vec[row : row + 1]

    for k in range(layout.tiles):
        cols = slice(k * LANES_A, (k + 1) * LANES_A)
        tile = at(layout.up + k * tall, tall)
        up_weight[:, cols] = tile[:channels]
        up_bias[:, cols] = tile[channels : channels + 1]
        down_weight[:, cols] = at(layout.down + k * channels, channels)
    rest = at(layout.rest, tall)
    q = jnp.concatenate([at(layout.q, tall), rest[:, :half]], 1)
    out = jnp.concatenate([at(layout.out, tall), rest[:, half:]], 1)
    q_weight[...] = q[:channels]
    q_bias[...] = q[channels : channels + 1]
    out_weight[...] = out[:channels]
    out_bias[...] = out[channels : channels + 1]
    mine = at(layout.kv, 2 * tall)
    other = sib_kv[...].astype(F32)
    for start, side in ((0, jnp.where(is_encoder, mine, other)), (channels, jnp.where(is_encoder, other, mine))):
        side = jnp.concatenate([side[:tall], side[tall:, :half]], 1)
        kv_weight[:, start : start + channels] = side[:channels]
    v_bias[...] = side[channels : channels + 1]
    placed[...] = jnp.zeros_like(placed)
    positions = [position_matrix(False), position_matrix(True)]
    for h in range(HEADS):
        start = layout.bias + h // 2 * CELLS
        placed[h, :, :256] = nt(total[start : start + CELLS], positions[h % 2])
    entries = jnp.zeros((8, 384), F32)
    for j in range(CELLS):
        entries += pltpu.roll(placed[:, j, :], CENTRE - cell_position(j), 1)
    table[...] = entries[:HEADS, : SPAN**3][:, None]


def run_finish(core, total, sib_kv, returned, ends, layout):
    channels = layout.channels
    hidden = layout.tiles * LANES_A
    _, _, rows_y, rows_z, _ = ends.shape
    any_spec = pl.BlockSpec(memory_space=pl.ANY)
    shapes = [
        (1, channels), (1, channels), (channels, channels), (1, channels), (channels, 2 * channels),
        (1, channels), (channels, channels), (1, channels), (HEADS, 1, SPAN**3),
        (1, channels), (1, channels), (channels, hidden), (1, hidden), (channels, hidden), (1, channels),
    ]
    shapes = [jax.ShapeDtypeStruct(shape, F32) for shape in shapes]
    return pl.pallas_call(
        functools.partial(finish, layout, ends.shape[0], len(returned)),
        grid_spec=pltpu.PrefetchScalarGridSpec(
            num_scalar_prefetch=1,
            grid=(rows_y // WIN,),
            in_specs=[
                *[whole(a) for a in (total, sib_kv)],
                *[
                    pl.BlockSpec(
                        (WIN, WIN, rows_z, channels), lambda i, c: (0, i * (1 - c[0]), 0, 0)
                    )
                ]
                * len(returned),
                any_spec,
            ],
            out_specs=[any_spec, *[whole(a) for a in shapes]],
            scratch_shapes=[
                pltpu.VMEM((8, CELLS, 384), F32),
                pltpu.SemaphoreType.DMA((len(returned),)),
            ],
        ),
        out_shape=[jax.ShapeDtypeStruct(ends.shape, F32), *shapes],
        input_output_aliases={3 + len(returned): 0},
        compiler_params=params,
        name="finish",
    )(core, total, sib_kv, *returned, ends)


def cell_position(ids):
    x = 2 * (ids // 32) + ids // 4 % 2
    y = 2 * (ids // 16 % 2) + ids // 2 % 2
    z = 2 * (ids // 8 % 2) + ids % 2
    return (x * SPAN + y) * SPAN + z


CENTRE = (WIN - 1) * (SPAN * SPAN + SPAN + 1)
TABLE_ROW = 8


def position_matrix(odd):
    rows = lax.broadcasted_iota(jnp.int32, (256, 2 * CELLS), 0)
    ids = lax.broadcasted_iota(jnp.int32, (256, 2 * CELLS), 1) - (CELLS if odd else 0)
    hit = (ids >= 0) & (ids < CELLS) & (rows == cell_position(ids))
    return jnp.where(hit, 1.0, 0.0).astype(BF16)


def spread_bias(table, shifted):
    for j in range(CELLS):
        turned = pltpu.roll(table, (384 - CENTRE + cell_position(j)) % 384, 1)
        for h in range(HEADS):
            shifted[h, j : j + 1] = turned[h : h + 1, :256]
    even, odd = position_matrix(False), position_matrix(True)
    pairs = [
        nn(shifted[2 * p].astype(BF16), even) + nn(shifted[2 * p + 1].astype(BF16), odd)
        for p in range(HEADS // 2)
    ]
    return jnp.concatenate(pairs, 1) * log2_e


def prepare(
    blocks, q_w, out_w, up_w, down_w, kv_w, v_b, ln1_g, ln1_b, ln2_g, ln2_b, out_b, down_b, q_b, up_b, table,
    weights_e, vectors_e, bias_e, weights_d, vectors_d, bias_d,
    small, small_sib, q_sib, out_sib, up_sib, down_sib, shifted, send_sem, recv_sem,
):
    core, block = lax.axis_index("section"), lax.axis_index("tok")
    channels, hidden = up_w.shape
    sibling = {"section": 1 - core}
    barrier = pltpu.get_barrier_semaphore()
    pl.semaphore_signal(barrier, inc=1, device_id=sibling, device_id_type=MESH)
    small[...] = jnp.zeros_like(small)
    for row, ref in enumerate((ln1_g, ln1_b, ln2_g, ln2_b, out_b, down_b, q_b)):
        small[row : row + 1, :channels] = ref[...].astype(F32)
    small[7:8, :hidden] = up_b[...].astype(F32)
    small[TABLE_ROW : TABLE_ROW + HEADS, : SPAN**3] = table[...].astype(F32)
    pl.semaphore_wait(barrier, 1)
    pairs = ((small, small_sib), (q_w, q_sib), (out_w, out_sib), (up_w, up_sib), (down_w, down_sib))
    copies = [
        pltpu.make_async_remote_copy(
            src_ref=source, dst_ref=target, send_sem=send_sem.at[k], recv_sem=recv_sem.at[k],
            device_id=sibling, device_id_type=MESH,
        )
        for k, (source, target) in enumerate(pairs)
    ]
    for copy in copies:
        copy.start()
    for copy in copies:
        copy.wait()

    def place(enc, dec):
        e_small, d_small = enc[0], dec[0]
        for weights, vectors, (source, q, out, up, down) in (
            (weights_e, vectors_e, enc), (weights_d, vectors_d, dec),
        ):
            weights[2 * channels :] = jnp.zeros((2 * channels, hidden), BF16)
            weights[:channels] = up[...]
            weights[channels : 2 * channels] = down[...]
            weights[2 * channels : 3 * channels, :channels] = q[...]
            weights[3 * channels :, :channels] = out[...]
            vectors[...] = jnp.zeros_like(vectors)
            vectors[:8, :channels] = source[:8, :channels]
            vectors[8:9, :hidden] = source[7:8, :hidden]
            vectors[9:10, :channels] = source[6:7, :channels]
        weights_e[2 * channels : 3 * channels, 256 : 256 + channels] = kv_w[:, :channels]
        weights_e[2 * channels : 3 * channels, 512 : 512 + channels] = kv_w[:, channels:]
        vectors_e[9:10, 512 : 512 + channels] = v_b[...].astype(F32)[None]
        rows = slice(TABLE_ROW, TABLE_ROW + 8)
        bias_e[...] = spread_bias(e_small[rows, :384], shifted)
        return spread_bias(d_small[rows, :384], shifted)

    own = (small, q_w, out_w, up_w, down_w)
    sib = (small_sib, q_sib, out_sib, up_sib, down_sib)

    def masked(base):
        shape = (CELLS, HEADS * CELLS)
        keys = lax.broadcasted_iota(jnp.int32, shape, 0)
        queries = lax.broadcasted_iota(jnp.int32, shape, 1) % CELLS

        def differ(unit):
            return jnp.where(keys // unit % 2 != queries // unit % 2, 1.0, 0.0)

        last = jnp.where((core == 1) & (block == blocks - 1), 1.0, 0.0)
        for y in range(2):
            for z in range(2):
                apart = jnp.maximum(last * differ(32), jnp.maximum(y * differ(16), z * differ(8)))
                bias_d[y, z] = base + apart * (mask_fill * log2_e)

    @pl.when(core == 0)
    def _():
        masked(place(own, sib))

    @pl.when(core == 1)
    def _():
        masked(place(sib, own))


def run_prepare(blocks, weights, smalls, table, kv_weight, v_bias):
    q_w, out_w, up_w, down_w = weights
    channels, hidden = up_w.shape
    vmem = pl.BlockSpec(memory_space=pltpu.VMEM)
    args = [*weights, kv_weight, v_bias, *smalls, table]
    bias = (CELLS, HEADS * CELLS)
    square = (channels, channels)
    layer = [
        jax.ShapeDtypeStruct((4 * channels, hidden), BF16),
        jax.ShapeDtypeStruct((16, hidden), F32),
    ]
    shapes = [
        *layer,
        jax.ShapeDtypeStruct(bias, F32),
        *layer,
        jax.ShapeDtypeStruct((2, 2, *bias), F32),
    ]
    return pl.pallas_call(
        functools.partial(prepare, blocks),
        in_specs=[vmem] * len(args),
        out_specs=[vmem] * len(shapes),
        out_shape=shapes,
        scratch_shapes=[
            pltpu.VMEM((TABLE_ROW + 8, hidden), F32),
            pltpu.VMEM((TABLE_ROW + 8, hidden), F32),
            pltpu.VMEM(square, BF16),
            pltpu.VMEM(square, BF16),
            pltpu.VMEM((channels, hidden), BF16),
            pltpu.VMEM((channels, hidden), BF16),
            pltpu.VMEM((HEADS, CELLS, 256), F32),
            pltpu.SemaphoreType.DMA((5,)),
            pltpu.SemaphoreType.DMA((5,)),
        ],
        compiler_params=pltpu.CompilerParams(
            collective_id=1, has_side_effects=True, vmem_limit_bytes=VMEM_BYTES
        ),
        name="prepare",
    )(*args)


def run_encoder(core, tokens, batch, consts, cotangent):
    _, _, rows_y, rows_z, channels = tokens.shape
    groups, size = rows_y // WIN, 4 * rows_z
    cells = 4 * size
    hidden = consts[1].shape[1]
    slab = jax.ShapeDtypeStruct((groups, 2, 3, size * 3 // 2, LANES_A), BF16)
    outs = [
        slab,
        slab,
        jax.ShapeDtypeStruct((groups, cells, 512), F32),
        jax.ShapeDtypeStruct((groups, cells, 2 * hidden + HEADS * CELLS + 256), BF16),
    ]

    def row(array):
        zeros = (0,) * (array.ndim - 1)
        return pl.BlockSpec((1, *array.shape[1:]), lambda i, c: (i, *zeros))

    batches = tokens.shape[0]
    cut = [] if cotangent is None else [cotangent]
    cut_block = (batches, SHIFT, WIN, rows_z, channels)
    cut_outs = [
        jax.ShapeDtypeStruct((batches, SHIFT, rows_y, rows_z, channels), a.dtype) for a in cut
    ]
    return pl.pallas_call(
        functools.partial(encoder_forward, len(cut)),
        grid_spec=pltpu.PrefetchScalarGridSpec(
            num_scalar_prefetch=1,
            grid=(groups,),
            in_specs=[
                pl.BlockSpec(
                    (1, WIN, WIN, rows_z, channels), lambda i, c: (batch, c[0], i, 0, 0)
                ),
                *[whole(a) for a in consts],
                *[pl.BlockSpec(cut_block, lambda i, c: (0, 2 * c[0], i, 0, 0)) for _ in cut],
            ],
            out_specs=[
                *[row(a) for a in outs],
                *[pl.BlockSpec(cut_block, lambda i, c: (0, 0, i, 0, 0)) for _ in cut],
            ],
            scratch_shapes=[pltpu.VMEM((cells, 768), BF16)],
        ),
        out_shape=[*outs, *cut_outs],
        compiler_params=params,
        cost_estimate=cost(groups * cells, 466944, groups * cells * 7500),
        name="encoder_forward",
    )(core, tokens, *consts, *cut)


def run_encoder_back(core, batch, own, halo, ys, returned, saved, old, consts, tokens):
    groups, _, _, packed, _ = own.shape
    batches, planes, rows_y, rows_z, channels = tokens.shape
    size = 4 * rows_z
    hidden = consts[1].shape[1]
    first = old is None
    sums = jax.ShapeDtypeStruct((sum_rows(channels, True), hidden), F32)
    outs = [
        jax.ShapeDtypeStruct(tokens.shape, F32),
        jax.ShapeDtypeStruct((WIN, rows_y, rows_z, channels), F32),
        sums,
    ]

    def slab(unit):
        def place(i, c):
            return ((i if unit == 0 else (i + groups - 1) % groups), unit, 0, 0, 0)

        return pl.BlockSpec((1, 1, 3, packed, LANES_A), place)

    def row(array):
        zeros = (0,) * (array.ndim - 1)
        return pl.BlockSpec((1, *array.shape[1:]), lambda i, c: (i, *zeros))

    def for_core(core, planes_here):
        def place(i, c):
            return (0, i * (c[0] if core == 1 else 1 - c[0]), 0, 0)

        return pl.BlockSpec((planes_here, WIN, rows_z, channels), place)

    any_spec = pl.BlockSpec(memory_space=pl.ANY)
    olds = [] if first else [old[1], old[0]]
    args = [core, *consts, *ys, own, own, halo, halo, *saved, *returned, *olds]
    return pl.pallas_call(
        functools.partial(encoder_backward, first, batch, len(returned)),
        grid_spec=pltpu.PrefetchScalarGridSpec(
            num_scalar_prefetch=1,
            grid=(groups,),
            in_specs=[
                *[whole(a) for a in consts],
                *[for_core(1, n) for n in (2, 2, 4)],
                slab(0),
                slab(1),
                slab(0),
                slab(1),
                *[row(a) for a in saved],
                *[for_core(0, WIN)] * len(returned),
                *[whole(a) for a in olds[:-1]],
                *[any_spec] * (0 if first else 1),
            ],
            out_specs=[any_spec, any_spec, whole(sums)],
            scratch_shapes=[
                pltpu.VMEM((4 * size, 768), BF16),
                pltpu.VMEM((3, 4 * size, channels), BF16),
                pltpu.VMEM((2, WIN, WIN, rows_z, channels), F32),
                pltpu.SemaphoreType.DMA((2,)),
                pltpu.SemaphoreType.DMA((8 + batches,)),
            ],
        ),
        out_shape=outs,
        input_output_aliases={} if first else {len(args) - 1: 0},
        compiler_params=params,
        cost_estimate=cost(groups * 4 * size, 933888, groups * 4 * size * 9000),
        name="encoder_backward",
    )(*args)


def run_decoder(core, keep, recv, cotangent, cot_recv, batch, old, consts):
    groups, _, _, packed, _ = keep.shape
    rows_z, channels = cotangent.shape[3:]
    size = 4 * rows_z
    hidden = consts[1].shape[1]
    first = old is None
    sums = jax.ShapeDtypeStruct((sum_rows(channels, False), hidden), F32)
    slab_shape = jax.ShapeDtypeStruct((groups, 2, 3, packed, LANES_A), BF16)
    outs = [
        *[jax.ShapeDtypeStruct((n, groups * WIN, rows_z, channels), F32) for n in (4, 2)],
        slab_shape,
        slab_shape,
        sums,
    ]

    def slab(unit):
        def place(i, c):
            return ((i if unit == 1 else (i + 1) % groups), unit, 0, 0, 0)

        return pl.BlockSpec((1, 1, 3, packed, LANES_A), place)

    def cot(unit, own):
        def place(i, c):
            y = 2 * i + 1 if unit == 1 else (2 * i + 2) % (2 * groups)
            return (batch, 2 * c[0] + 1 if own else 0, y, 0, 0)

        return pl.BlockSpec((1, 2, 2, rows_z, channels), place)

    def bias_place(i, c):
        return (i // (groups - 1), 0, 0, 0)

    specs = [whole(a) for a in consts]
    specs[3] = pl.BlockSpec((1, *consts[3].shape[1:]), bias_place)
    olds = [] if first else [old]
    out_slab = pl.BlockSpec((1, 2, 3, packed, LANES_A), lambda i, c: (i, 0, 0, 0, 0))
    return pl.pallas_call(
        functools.partial(decoder, first),
        grid_spec=pltpu.PrefetchScalarGridSpec(
            num_scalar_prefetch=1,
            grid=(groups,),
            in_specs=[
                *specs,
                slab(1),
                slab(0),
                slab(1),
                slab(0),
                cot(1, True),
                cot(0, True),
                cot(1, False),
                cot(0, False),
                *[whole(a) for a in olds],
            ],
            out_specs=[
                *[pl.BlockSpec((n, WIN, rows_z, channels), lambda i, c: (0, i, 0, 0)) for n in (4, 2)],
                out_slab,
                out_slab,
                whole(sums),
            ],
            scratch_shapes=[
                pltpu.VMEM((4 * size, hidden), BF16),
                pltpu.VMEM((4 * size, hidden), F32),
            ],
        ),
        out_shape=outs,
        compiler_params=params,
        cost_estimate=cost(groups * 4 * size, 1253376, groups * 4 * size * 4000),
        name="decoder",
    )(core, *consts, keep, keep, recv, recv, cotangent, cotangent, cot_recv, cot_recv, *olds)


def body(
    tokens,
    cotangent,
    ln1_gain,
    ln1_bias,
    q_weight,
    q_bias,
    kv_weight,
    v_bias,
    out_weight,
    out_bias,
    rel_table,
    ln2_gain,
    ln2_bias,
    up_weight,
    up_bias,
    down_weight,
    down_bias,
):
    batches, planes, rows_y, rows_z, channels = tokens.shape
    axes = ("section", "tok")
    core = lax.axis_index("section")
    block = lax.axis_index("tok")
    blocks = lax.axis_size("tok")
    is_encoder = core == 0
    core_arg = core.astype(jnp.int32).reshape(1)

    def device(position):
        position = position % (2 * blocks)
        return (position % 2) * blocks + position // 2

    to_previous = [(device(r), device(r - 1)) for r in range(2 * blocks)]
    to_next = [(device(r), device(r + 1)) for r in range(2 * blocks)]

    weights_e, vectors_e, bias_e, weights_d, vectors_d, bias_d = run_prepare(
        blocks,
        (q_weight[0], out_weight[0], up_weight[0], down_weight[0].T),
        (ln1_gain, ln1_bias, ln2_gain, ln2_bias, out_bias, down_bias, q_bias, up_bias),
        rel_table[0],
        kv_weight,
        v_bias,
    )
    order = jnp.asarray(order_matrix(rows_z, 0), BF16)
    order_rolled = jnp.asarray(order_matrix(rows_z, 1), BF16)

    enc_consts = (order, weights_e, vectors_e, bias_e)
    enc_back_consts = (order, weights_e, vectors_e)
    dec_consts = (order_rolled, weights_d, vectors_d, bias_d)

    handed, saved = [], []
    for batch in range(batches):
        send, keep, *rest = run_encoder(
            core_arg, tokens, batch, enc_consts, cotangent if batch == 0 else None
        )
        if batch == 0:
            *rest, half = rest
            cot_recv = lax.ppermute(half, axes, to_previous)
        handed.append((keep, lax.ppermute(send, axes, to_previous)))
        saved.append(rest)
    dec_sums = None
    returned, ys = [], []
    to_decoder = [(t, blocks + t) for t in range(blocks)]
    to_encoder = [(blocks + t, t) for t in range(blocks)]
    to_after = [(blocks + t, blocks + (t + 1) % blocks) for t in range(blocks)]
    for batch in range(batches):
        out_all, out_tail, own, halo, dec_sums = run_decoder(
            core_arg, *handed[batch], cotangent, cot_recv, batch, dec_sums, dec_consts
        )
        returned.append((own, lax.ppermute(halo, axes, to_next)))
        y_halo = lax.ppermute(out_tail, axes, to_after)
        ys.append((out_all, y_halo, lax.ppermute(out_all, axes, to_decoder)))
    old = None
    backs = []
    for batch in range(batches):
        arrived = backs[:1] if batch == batches - 1 else []
        ends, back, enc_sums = run_encoder_back(
            core_arg, batch, *returned[batch], ys[batch], arrived, saved[batch], old,
            enc_back_consts, tokens,
        )
        old = (ends, enc_sums)
        backs.append(lax.ppermute(back, axes, to_encoder))

    layout = Layout(channels, up_weight.shape[2], blocks)
    total, sib_kv = run_sum(enc_sums, dec_sums, layout, blocks)
    (
        ends, g_ln1_gain, g_ln1_bias, g_q_weight, g_q_bias, g_kv_weight, g_v_bias, g_out_weight,
        g_out_bias, g_table, g_ln2_gain, g_ln2_bias, g_up_weight, g_up_bias, g_down_weight, g_down_bias,
    ) = run_finish(core_arg, total, sib_kv, backs[1:], ends, layout)
    return (
        ends[None],
        g_ln1_gain,
        g_ln1_bias,
        g_q_weight[None],
        g_q_bias,
        g_kv_weight[None],
        g_v_bias,
        g_out_weight[None],
        g_out_bias,
        g_table.transpose(1, 0, 2),
        g_ln2_gain,
        g_ln2_bias,
        g_up_weight[None],
        g_up_bias,
        g_down_weight.T[None],
        g_down_bias,
    )


def solution(mesh):
    in_specs = (
        P(None, "tok", None, None, None),
        P(None, "tok", None, None, None),
        P("section", None),
        P("section", None),
        P("section", None, None),
        P("section", None),
        P(),
        P(),
        P("section", None, None),
        P("section", None),
        P("section", None, None),
        P("section", None),
        P("section", None),
        P("section", None, None),
        P("section", None),
        P("section", None, None),
        P("section", None),
    )
    out_specs = (
        P("section", None, "tok", None, None, None),
        P("section", None),
        P("section", None),
        P("section", None, None),
        P("section", None),
        P("section", None, None),
        P("section", None),
        P("section", None, None),
        P("section", None),
        P("section", None, None),
        P("section", None),
        P("section", None),
        P("section", None, None),
        P("section", None),
        P("section", None, None),
        P("section", None),
    )
    return jax.shard_map(body, mesh=mesh, in_specs=in_specs, out_specs=out_specs, check_vma=False)
```

```python
import functools

import jax
import jax.numpy as jnp
import numpy as np
from jax import lax
from jax.experimental import pallas as pl
from jax.experimental.pallas import tpu as pltpu
from jax.sharding import PartitionSpec as P

HEADS = 6
HD = 32
WIN = 4
SHIFT = 2
CELLS = WIN**3
SPAN = 2 * WIN - 1
HEADS_A = 4
LANES_A = HEADS_A * HD
COLS_A = HEADS_A * CELLS

eps_norm = 1e-05
mask_fill = -100.0
log2_e = 1.4426950408889634
root_half = 0.7071067811865476
inv_root_two_pi = 0.3989422804014327
scale = HD ** (-0.5)
VMEM_BYTES = 63 * 1024 * 1024

F32 = jnp.float32
BF16 = jnp.bfloat16


def nn(left, right):
    return lax.dot_general(left, right, (((1,), (0,)), ((), ())), preferred_element_type=F32)


def nt(left, right):
    return lax.dot_general(left, right, (((1,), (1,)), ((), ())), preferred_element_type=F32)


def tn(left, right):
    return lax.dot_general(left, right, (((0,), (0,)), ((), ())), preferred_element_type=F32)


def order_matrix(rows_z, rolled):
    count = 4 * rows_z
    matrix = np.zeros((count, count), np.float32)
    units = rows_z // 2
    for unit in range(units):
        for dx in range(2):
            for dy in range(2):
                for dz in range(2):
                    z = (2 * (unit + rolled) + dz) % rows_z
                    matrix[unit * 8 + dx * 4 + dy * 2 + dz, (dx * 2 + dy) * rows_z + z] = 1.0
    return np.concatenate([matrix, matrix.T, matrix.T], 1)


def windows_of(pieces):
    count, rows, channels = pieces.shape
    return pieces.reshape(count, rows // 16, 16, channels).transpose(1, 0, 2, 3).reshape(-1, channels)


def pieces_of(windows):
    rows, channels = windows.shape
    return (
        windows.reshape(rows // CELLS, 4, 16, channels)
        .transpose(1, 0, 2, 3)
        .reshape(4, rows // 4, channels)
    )


def roll_rows(pieces, steps):
    return jnp.concatenate([pieces[:, steps:], pieces[:, :steps]], 1)


def pack_slab(pieces):
    half = pieces.shape[1] // 2
    rest = pieces[:, :, LANES_A:]
    return jnp.concatenate(
        [pieces[:, :, :LANES_A], jnp.concatenate([rest[:, :half], rest[:, half:]], 2)], 1
    ).astype(BF16)


def unpack_slab(block):
    size = block.shape[0] * 2 // 3
    half = LANES_A // 2
    rest = jnp.concatenate([block[size:, :half], block[size:, half:]], 0)
    return jnp.concatenate([block[:size], rest], 1)


def normalize(rows):
    mean = jnp.mean(rows, -1, keepdims=True)
    centered = rows - mean
    inv_std = lax.rsqrt(jnp.mean(centered * centered, -1, keepdims=True) + eps_norm)
    return centered * inv_std, inv_std


def norm_back(grad_rows, unit_rows, inv_std, gain):
    scaled = grad_rows * gain
    return inv_std * (
        scaled
        - jnp.mean(scaled, -1, keepdims=True)
        - unit_rows * jnp.mean(scaled * unit_rows, -1, keepdims=True)
    )


def gelu_pair(rows):
    upper = 0.5 * lax.erf(rows * root_half) + 0.5
    bell = jnp.exp2(rows * rows * (-0.5 * log2_e))
    return rows * upper, upper + rows * bell * inv_root_two_pi


def head_masks(width):
    heads = lax.broadcasted_iota(jnp.int32, (1, width), 1) // HD
    return [jnp.where(heads == h, 1.0, 0.0).astype(BF16) for h in range(width // HD)]


def expand(rows):
    masks = head_masks(rows.shape[1])
    return jnp.concatenate([rows * mask for mask in masks], 0)


def collapse(stacked):
    width = stacked.shape[1]
    lanes = lax.broadcasted_iota(jnp.int32, (CELLS, width), 1)
    total = stacked[:CELLS]
    for h in range(1, width // HD):
        total = jnp.where(lanes >= h * HD, stacked[h * CELLS : (h + 1) * CELLS], total)
    return total


def split(rows):
    return rows[:, :LANES_A], rows[:, LANES_A:]


def attend(parts, bias):
    queries, keys, values = zip(*[[split(rows) for rows in part] for part in parts])
    wide = [[expand(half) for half in q] for q in queries]
    scores = [
        jnp.concatenate([nt(k[0], q[0]), nt(k[1], q[1])], 1) for k, q in zip(keys, wide)
    ]
    scores = [s * (scale * log2_e) + b for s, b in zip(scores, bias)]
    exponents = [jnp.exp2(s - jnp.max(s, 0, keepdims=True)) for s in scores]
    probs = [e * (1.0 / jnp.sum(e, 0, keepdims=True)) for e in exponents]
    low = [p.astype(BF16) for p in probs]
    mixed = [
        (tn(p[:, :COLS_A], v[0]), tn(p[:, COLS_A:], v[1])) for p, v in zip(low, values)
    ]
    mixed = [jnp.concatenate([collapse(m[0]), collapse(m[1])], 1).astype(BF16) for m in mixed]
    return mixed, probs


def attend_back(parts):
    queries, keys, values, grads = zip(
        *[[split(rows) for rows in part[:3] + part[4:]] for part in parts]
    )
    probs = [part[3] for part in parts]
    wide_g = [[expand(half) for half in g] for g in grads]
    d_probs = [
        jnp.concatenate([nt(v[0], g[0]), nt(v[1], g[1])], 1) for v, g in zip(values, wide_g)
    ]
    low = [part[3].astype(BF16) for part in parts]
    d_values = [
        jnp.concatenate([nn(p[:, :COLS_A], g[0]), nn(p[:, COLS_A:], g[1])], 1)
        for p, g in zip(low, wide_g)
    ]
    wide_q = [[expand(half) for half in q] for q in queries]
    d_scores = [
        p * (d - jnp.sum(d * p, 0, keepdims=True)) for p, d in zip(probs, d_probs)
    ]
    low_d = [d.astype(BF16) for d in d_scores]
    d_keys = [
        jnp.concatenate([nn(d[:, :COLS_A], q[0]), nn(d[:, COLS_A:], q[1])], 1) * scale
        for d, q in zip(low_d, wide_q)
    ]
    d_queries = [
        (tn(d[:, :COLS_A], k[0]), tn(d[:, COLS_A:], k[1])) for d, k in zip(low_d, keys)
    ]
    d_queries = [
        jnp.concatenate([collapse(d[0]), collapse(d[1])], 1) * scale for d in d_queries
    ]
    table = d_scores[0]
    for d in d_scores[1:]:
        table = table + d
    return d_queries, d_keys, d_values, table


def window_groups(count):
    return [range(k, min(k + TOGETHER, count)) for k in range(0, count, TOGETHER)]


def window_rows(k):
    return slice(k * CELLS, (k + 1) * CELLS)


def with_ones(rows):
    return jnp.concatenate([rows.T, jnp.ones((16, rows.shape[0]), BF16)], 0)


def col_sum(rows):
    return jnp.sum(rows, 0, keepdims=True)


def start_sums(old, new):
    @pl.when(pl.program_id(0) == 0)
    def _():
        new[...] = jnp.zeros_like(new) if old is None else old[...]


def arrange(order, rows):
    return nn(order[:, : order.shape[0]], rows)


def restore(order, rows):
    high = rows.astype(BF16)
    low = (rows - high.astype(F32)).astype(BF16)
    return nn(order[:, order.shape[0] :], jnp.concatenate([high, low], 0))


CHUNK = 256
BLOCK = 256
TOGETHER = 8


class View:
    def __init__(self, ref, row, rows, col, cols):
        self.ref, self.row, self.col, self.shape = ref, row, col, (rows, cols)

    def place(self, key):
        key = (slice(None), slice(None)) if key is Ellipsis else key
        key = key if isinstance(key, tuple) else (key, slice(None))
        return tuple(
            slice(start + part.indices(size)[0], start + part.indices(size)[1])
            for part, start, size in zip(key, (self.row, self.col), self.shape)
        )

    def __getitem__(self, key):
        return self.ref[self.place(key)]

    def __setitem__(self, key, value):
        self.ref[self.place(key)] = value

    def first_columns(self, cols):
        return View(self.ref, self.row, self.shape[0], self.col, cols)


def layer_views(weights, vectors):
    hidden = weights.shape[1]
    channels = weights.shape[0] // 4
    q_cols = 768

    def rows(k, cols):
        return View(weights, k * channels, channels, 0, cols)

    return (
        View(vectors, 0, 8, 0, channels),
        View(vectors, 8, 1, 0, hidden),
        View(vectors, 9, 1, 0, q_cols),
        rows(0, hidden),
        rows(1, hidden),
        rows(2, q_cols),
        rows(3, channels),
    )


def sum_rows(channels, encoder):
    tall = channels + 16
    return 2 * tall + channels + (tall if encoder else 0)


def sum_views(sums, channels, encoder):
    tall = channels + 16
    base = tall + channels

    def view(row, rows, col, cols):
        return View(sums, row, rows, col, cols)

    fields = [view(base, tall, 256 * k, channels) for k in range(3 if encoder else 2)]
    last = base + (tall if encoder else 0)
    side = 256 if encoder else 512
    out = view(last, tall, 0, channels) if encoder else fields[1]
    bias = (view(last, CELLS, side, COLS_A), view(last + CELLS, CELLS, side, 2 * CELLS))
    vec = view(last + 2 * CELLS, 8, side, channels)
    return (
        view(0, tall, 0, sums.shape[1]),
        view(tall, channels, 0, sums.shape[1]),
        fields[:3] if encoder else fields[:1],
        out,
        vec,
        bias,
    )


def add_bias(views, table):
    views[0][...] += table[:, :COLS_A]
    views[1][...] += table[:, COLS_A:]


def encoder_forward(cuts, core_ref, tok, order, weights, vectors, bias, *rest):
    vec, b_up, b_qkv, w_up, w_down, w_qkv, w_out = layer_views(weights, vectors)
    cut_in, rest = rest[:cuts], rest[cuts:]
    send, keep, wide_out, low_out, *cut_out, qkv = rest
    hidden_cols = w_up.shape[1]
    s_start, p_start, o_start = hidden_cols, 2 * hidden_cols, 2 * hidden_cols + HEADS * CELLS
    for source, target in zip(cut_in, cut_out):
        target[...] = source[...]
    rows_z = tok.shape[3]
    size = 4 * rows_z
    pieces = []
    for x in range(2):
        for y in range(2):
            part = tok[0, 2 * x : 2 * x + 2, 2 * y : 2 * y + 2].reshape(size, -1)
            pieces.append(arrange(order, part))
    entry = windows_of(jnp.stack(pieces))
    unit, inv_std = normalize(entry)
    channels = entry.shape[1]
    wide = jnp.broadcast_to(inv_std, (entry.shape[0], 256 - channels))
    wide_out[0, :, :channels] = unit
    wide_out[0, :, channels:256] = wide
    left = (unit * vec[0:1] + vec[1:2]).astype(BF16)
    triple = nn(left, w_qkv[...]) + b_qkv[...]
    qkv[...] = triple.astype(BF16)
    for together in window_groups(entry.shape[0] // CELLS):
        parts = [
            [qkv[window_rows(k), 256 * f : 256 * f + 192] for f in range(3)] for k in together
        ]
        mixed, probs = attend(parts, [bias[...]] * len(parts))
        for k, o, p in zip(together, mixed, probs):
            low_out[0, window_rows(k), p_start:o_start] = p.astype(BF16)
            low_out[0, window_rows(k), o_start : o_start + channels] = o
    mixed = low_out[0, :, o_start : o_start + channels]
    middle = entry + nn(mixed, w_out[...]) + vec[4:5]
    unit, inv_std = normalize(middle)
    wide = jnp.broadcast_to(inv_std, (entry.shape[0], 256 - channels))
    wide_out[0, :, 256 : 256 + channels] = unit
    wide_out[0, :, 256 + channels :] = wide
    left = (unit * vec[2:3] + vec[3:4]).astype(BF16)
    results = []
    for k in range(entry.shape[0] // CHUNK):
        rows = slice(k * CHUNK, (k + 1) * CHUNK)
        hidden, slope = gelu_pair(nn(left[rows], w_up[...]) + b_up[...])
        hidden = hidden.astype(BF16)
        low_out[0, rows, :s_start] = hidden
        low_out[0, rows, s_start:p_start] = slope.astype(BF16)
        results.append(nt(hidden, w_down[...]))
    result = middle + jnp.concatenate(results, 0) + vec[5:6]
    for field, rows in enumerate((result, triple[:, 256:448], triple[:, 512:704])):
        rolled = pack_slab(roll_rows(pieces_of(rows), 8))
        send[0, :, field] = rolled[:2]
        keep[0, :, field] = rolled[2:]


def run_together(*works):
    works = list(works)
    while works:
        for work in list(works):
            try:
                next(work)
            except StopIteration:
                works.remove(work)


def row_blocks(count, size):
    return [slice(k, k + size) for k in range(0, count, size)]


def norm_back_steps(rows_grad, base, unit, inv_std, gain, g_vec, row, results):
    sums = [None, None]
    for rows in row_blocks(base.shape[0], BLOCK):
        grad = rows_grad(rows)
        found = (col_sum(grad * unit[rows]), col_sum(grad))
        sums = [f if total is None else total + f for f, total in zip(found, sums)]
        results.append(base[rows] + norm_back(grad, unit[rows], inv_std[rows], gain))
        yield
    g_vec[row : row + 1] += sums[0]
    g_vec[row + 1 : row + 2] += sums[1]


def product_steps(products):
    for target, cols, left, right in products:
        target[:, cols] += nn(left, right)
        yield


def mlp_back(grad, grad_low, hidden, slope, left_two, unit, inv_std, w_up, w_down, vec, sums):
    g_up, g_down, g_vec = sums
    backs, pres = [], []
    for rows in row_blocks(grad.shape[0], CHUNK):
        d_pre = (nn(grad_low[rows], w_down[...]) * slope(rows)).astype(BF16)
        pres.append(d_pre)
        backs.append(nt(d_pre, w_up[...]))
    d_pre = jnp.concatenate(pres, 0)
    d_normed = jnp.concatenate(backs, 0)
    ones, turned = with_ones(left_two), grad_low.T
    tiles = row_blocks(w_up.shape[1], 256)
    products = [(g_up, cols, ones, d_pre[:, cols]) for cols in tiles]
    products += [(g_down, cols, turned, hidden[:, cols]) for cols in tiles]
    results = []
    run_together(
        norm_back_steps(
            lambda rows: d_normed[rows], grad, unit, inv_std, vec[2:3], g_vec, 2, results
        ),
        product_steps(products),
    )
    g_vec[4:5] += col_sum(grad)
    return jnp.concatenate(results, 0)


def start_all(copies):
    for copy in copies:
        copy.start()


def wait_all(copies):
    for copy in copies:
        copy.wait()


def encoder_backward(
    first, batch, returns, core_ref, order, weights, vectors,
    y_own, y_halo, y_sib,
    keep_a, keep_b, recv_a, recv_b,
    wide_in, low_in, *rest,
):
    vec, _, b_qkv, w_up, w_down, w_qkv, w_out = layer_views(weights, vectors)
    channels, hidden_cols = w_up.shape
    s_start, p_start, o_start = hidden_cols, 2 * hidden_cols, 2 * hidden_cols + HEADS * CELLS
    returned, rest = rest[:returns], rest[returns:]
    old, rest = (None, rest) if first else (rest[0], rest[2:])
    ends, back, sums, qkv, dqkv, buffer, out_sem, copy_sem = rest
    g_up, g_down, g_fields, g_out, g_vec, g_bias = sum_views(sums, channels, True)
    step, steps = pl.program_id(0), pl.num_programs(0)
    is_encoder = core_ref[0] == 0
    rows_y = ends.shape[2]
    slot = lax.rem(step, 2)

    def output_copies():
        copies = []
        for start, planes, ref in ((0, 2, y_halo), (2, 4, y_sib), (6, 2, y_own)):
            for half in range(2):
                rows = pl.ds(lax.rem(step * WIN + SHIFT + 2 * half, rows_y), 2)
                target = ends.at[batch, pl.ds(start, planes), rows]
                copies.append((ref.at[:, pl.ds(2 * half, 2)], target))
        return [
            pltpu.make_async_copy(source, target, copy_sem.at[k])
            for k, (source, target) in enumerate(copies)
        ]

    def gradient_copies():
        return [
            pltpu.make_async_copy(
                ref, ends.at[k, pl.ds(WIN, WIN), pl.ds(step * WIN, WIN)], copy_sem.at[8 + k]
            )
            for k, ref in enumerate(returned)
        ]

    def result_copy(index, to_ends):
        target = (
            ends.at[batch, pl.ds(0, WIN), pl.ds(index * WIN, WIN)]
            if to_ends
            else back.at[:, pl.ds(index * WIN, WIN)]
        )
        at = lax.rem(index, 2)
        return pltpu.make_async_copy(buffer.at[at], target, out_sem.at[at])

    def for_core(encoder_work, decoder_work):
        pl.when(is_encoder)(encoder_work)
        pl.when(jnp.logical_not(is_encoder))(decoder_work)

    for_core(lambda: start_all(gradient_copies()), lambda: start_all(output_copies()))

    @pl.when(step >= 2)
    def _():
        for_core(
            lambda: result_copy(step - 2, True).wait(), lambda: result_copy(step - 2, False).wait()
        )

    start_sums(old, sums)
    fields = []
    for field in range(3):
        pieces = jnp.stack(
            [unpack_slab(ref[0, 0, field]) for ref in (recv_b, recv_a, keep_b, keep_a)]
        )
        fields.append(windows_of(pieces))
    grad_low, d_key_1, d_value_1 = fields
    grad = grad_low.astype(F32)
    unit_1, unit_2 = wide_in[0, :, :channels], wide_in[0, :, 256 : 256 + channels]
    wide_1, wide_2 = [wide_in[0, :, k + channels : k + channels + 1] for k in (0, 256)]
    left_1 = (unit_1 * vec[0:1] + vec[1:2]).astype(BF16)
    left_2 = (unit_2 * vec[2:3] + vec[3:4]).astype(BF16)
    qkv[...] = (nn(left_1, w_qkv[...]) + b_qkv[...]).astype(BF16)
    d_middle = mlp_back(
        grad, grad_low, low_in[0, :, :s_start], lambda rows: low_in[0, rows, s_start:p_start].astype(F32),
        left_2, unit_2, wide_2, w_up, w_down, vec,
        (g_up, g_down, g_vec),
    )
    branch = d_middle.astype(BF16)
    d_mixed = nt(branch, w_out[...]).astype(BF16)
    d_table = None
    for together in window_groups(grad.shape[0] // CELLS):
        parts = [
            [qkv[window_rows(k), 256 * f : 256 * f + 192] for f in range(3)]
            + [low_in[0, window_rows(k), p_start:o_start].astype(F32), d_mixed[window_rows(k)]]
            for k in together
        ]
        *d_qkv, d_s = attend_back(parts)
        for k, d_q, d_k, d_v in zip(together, *d_qkv):
            rows = window_rows(k)
            dqkv[0, rows] = d_q.astype(BF16)
            dqkv[1, rows] = (d_k + d_key_1[rows].astype(F32)).astype(BF16)
            dqkv[2, rows] = (d_v + d_value_1[rows].astype(F32)).astype(BF16)
        d_table = d_s if d_table is None else d_table + d_s
    add_bias(g_bias, d_table)
    ones = with_ones(left_1)
    every = slice(None)
    mixed = with_ones(low_in[0, :, o_start : o_start + channels])
    products = [(g_field, every, ones, dqkv[k]) for k, g_field in enumerate(g_fields)]
    products.append((g_out, every, mixed, branch))

    def rows_grad(rows):
        parts = [
            nt(dqkv[k, rows], w_qkv[:, 256 * k : 256 * k + channels]) for k in range(3)
        ]
        return parts[0] + parts[1] + parts[2]

    results = []
    run_together(
        norm_back_steps(rows_grad, d_middle, unit_1, wide_1, vec[0:1], g_vec, 0, results),
        product_steps(products),
    )
    result = pieces_of(jnp.concatenate(results, 0))
    rows_z = ends.shape[3]
    for x in range(2):
        for y in range(2):
            part = restore(order, result[2 * x + y])
            buffer[slot, 2 * x : 2 * x + 2, 2 * y : 2 * y + 2] = part.reshape(2, 2, rows_z, -1)
    for_core(lambda: result_copy(step, True).start(), lambda: result_copy(step, False).start())

    @pl.when(step == steps - 1)
    def _():
        def finish(to_ends):
            result_copy(step - 1, to_ends).wait()
            result_copy(step, to_ends).wait()

        for_core(lambda: finish(True), lambda: finish(False))

    for_core(lambda: wait_all(gradient_copies()), lambda: wait_all(output_copies()))


def decoder(
    first, core_ref, order, weights, vectors, bias,
    keep_1, keep_0, recv_1, recv_0, cot_1, cot_0, cot_r1, cot_r0, *rest,
):
    vec, b_up, b_qkv, w_up, w_down, w_qkv, w_out = layer_views(weights, vectors)
    channels = w_up.shape[0]
    w_q, b_q = w_qkv.first_columns(channels), b_qkv.first_columns(channels)
    old, new = (None, rest) if first else (rest[0], rest[1:])
    out_all, out_tail, own, halo, sums, a_scr, s_scr = new
    g_up, g_down, (g_q,), g_out, g_vec, g_bias = sum_views(sums, channels, False)
    start_sums(old, sums)
    fields = []
    for field in range(3):
        pieces = jnp.stack([unpack_slab(ref[0, 0, field]) for ref in (keep_1, keep_0, recv_1, recv_0)])
        fields.append(windows_of(pieces))
    entry_low, keys, values = fields
    entry = entry_low.astype(F32)
    unit_1, inv_1 = normalize(entry)
    left_1 = (unit_1 * vec[0:1] + vec[1:2]).astype(BF16)
    queries = (nn(left_1, w_q[...]) + b_q[...]).astype(BF16)
    windows = entry.shape[0] // CELLS
    all_probs, all_mixed = [], []
    for together in window_groups(windows):
        parts = [[rows[window_rows(k)] for rows in (queries, keys, values)] for k in together]
        mixed, probs = attend(parts, [bias[0, 1 if k == windows - 1 else 0] for k in together])
        all_probs += probs
        all_mixed += mixed
    mixed = jnp.concatenate(all_mixed, 0)
    middle = entry + nn(mixed, w_out[...]) + vec[4:5]
    unit_2, inv_2 = normalize(middle)
    left_2 = (unit_2 * vec[2:3] + vec[3:4]).astype(BF16)
    results = []
    for k in range(entry.shape[0] // CHUNK):
        rows = slice(k * CHUNK, (k + 1) * CHUNK)
        hidden, slope = gelu_pair(nn(left_2[rows], w_up[...]) + b_up[...])
        hidden = hidden.astype(BF16)
        a_scr[rows] = hidden
        s_scr[rows] = slope
        results.append(nt(hidden, w_down[...]))
    result = pieces_of(middle + jnp.concatenate(results, 0) + vec[5:6])
    rows_z = out_all.shape[2]
    size = 4 * rows_z
    for x in range(2):
        for y in range(2):
            part = restore(order, result[2 * x + y]).reshape(2, 2, rows_z, -1)
            out_all[2 * x : 2 * x + 2, 2 * y : 2 * y + 2] = part
            if x == 1:
                out_tail[:, 2 * y : 2 * y + 2] = part

    cots = [
        arrange(order, ref[0].reshape(size, -1)).astype(BF16) for ref in (cot_1, cot_0, cot_r1, cot_r0)
    ]
    grad_low = windows_of(jnp.stack(cots))
    grad = grad_low.astype(F32)
    d_middle = mlp_back(
        grad, grad_low, a_scr[...], lambda rows: s_scr[rows], left_2, unit_2, inv_2, w_up, w_down, vec,
        (g_up, g_down, g_vec),
    )
    branch = d_middle.astype(BF16)
    d_mixed = nt(branch, w_out[...]).astype(BF16)
    d_table = None
    found = [[], [], []]
    for together in window_groups(windows):
        parts = [
            [rows[window_rows(k)] for rows in (queries, keys, values)]
            + [all_probs[k], d_mixed[window_rows(k)]]
            for k in together
        ]
        *d_qkv, d_s = attend_back(parts)
        for f in range(3):
            found[f] += d_qkv[f]
        d_table = d_s if d_table is None else d_table + d_s
    add_bias(g_bias, d_table)
    d_queries, d_keys, d_values = [jnp.concatenate(rows, 0) for rows in found]
    d_queries = d_queries.astype(BF16)
    every = slice(None)
    products = [
        (g_q, every, with_ones(left_1), d_queries),
        (g_out, every, with_ones(mixed), branch),
    ]
    results = []
    run_together(
        norm_back_steps(
            lambda rows: nt(d_queries[rows], w_q[...]), d_middle, unit_1, inv_1, vec[0:1], g_vec, 0,
            results,
        ),
        product_steps(products),
    )
    d_entry = jnp.concatenate(results, 0)
    for field, rows in enumerate((d_entry, d_keys, d_values)):
        turned = pack_slab(roll_rows(pieces_of(rows), size - 8))
        own[0, :, field] = turned[:2]
        halo[0, :, field] = turned[2:]


def whole(array):
    zeros = (0,) * array.ndim
    return pl.BlockSpec(array.shape, lambda *_: zeros)


def cost(cells, per_cell, hbm):
    return pl.CostEstimate(
        flops=10 * cells * per_cell, bytes_accessed=5 * hbm, transcendentals=0
    )


params = pltpu.CompilerParams(
    dimension_semantics=("arbitrary",), vmem_limit_bytes=VMEM_BYTES
)


class Layout:
    def __init__(self, channels, hidden, blocks):
        tall = channels + 16
        self.tall, self.channels = tall, channels
        self.tiles = hidden // LANES_A
        self.up = 0
        self.down = self.tiles * tall
        self.q = self.down + self.tiles * channels
        self.out = self.q + tall
        self.rest = self.out + tall
        self.kv = self.rest + tall
        self.bias = self.kv + 2 * tall
        self.vec = self.bias + HEADS * CELLS // LANES_A * CELLS
        self.end = self.vec + 16
        units = -(-self.end // (16 * blocks))
        self.chunks = (units // 2 * 16, (units - units // 2) * 16)
        self.starts = (0, self.chunks[0] * blocks)
        self.rows = units * 16 * blocks


def fill(buffer, layout, up, down, q, out, kv, bias, vec):
    kind, half = buffer.dtype, LANES_A // 2
    tall, channels = layout.tall, layout.channels
    for k in range(layout.tiles):
        cols = slice(k * LANES_A, (k + 1) * LANES_A)
        buffer[layout.up + k * tall : layout.up + (k + 1) * tall] = up[:, cols].astype(kind)
        buffer[layout.down + k * channels : layout.down + (k + 1) * channels] = down[
            :, cols
        ].astype(kind)
    buffer[layout.q : layout.q + tall] = q[:, :LANES_A].astype(kind)
    buffer[layout.out : layout.out + tall] = out[:, :LANES_A].astype(kind)
    rests = jnp.concatenate([q[:, LANES_A:], out[:, LANES_A:]], 1)
    buffer[layout.rest : layout.rest + tall] = rests.astype(kind)
    buffer[layout.kv : layout.kv + tall] = kv[:, :LANES_A].astype(kind)
    rests = jnp.concatenate([kv[:, LANES_A:], jnp.zeros((tall, half), F32)], 1)
    buffer[layout.kv + tall : layout.kv + 2 * tall] = rests.astype(kind)
    tiles = [bias[0][:, :LANES_A], bias[0][:, LANES_A:], bias[1][...]]
    for k, tile in enumerate(tiles):
        start = layout.bias + k * CELLS
        buffer[start : start + CELLS] = tile.astype(kind)
    rests = jnp.concatenate([vec[:, LANES_A:], jnp.zeros((8, half), F32)], 1)
    both = jnp.concatenate([vec[:, :LANES_A], rests], 0)
    buffer[layout.vec : layout.vec + 16] = both.astype(kind)
    if layout.rows > layout.end:
        buffer[layout.end :] = jnp.zeros((layout.rows - layout.end, LANES_A), kind)


MESH = pl.DeviceIdType.MESH


def groups_of(blocks):
    near = 4 if blocks % 4 == 0 else blocks
    return near, blocks // near


def sum_gradients(layout, blocks, *refs):
    (
        enc_in, dec_in, total_out, kv_out,
        enc, dec, own, theirs, from_sib, low, total, sib_kv, landed_0, landed_1, near_low_0, near_low_1,
        far_landed_0, far_landed_1, load_sem, sib_send, sib_recv, send_sem, recv_sem,
    ) = refs
    landed, near_low = (landed_0, landed_1), (near_low_0, near_low_1)
    far_landed = (far_landed_0, far_landed_1)
    core, me = lax.axis_index("section"), lax.axis_index("tok")
    sibling = {"section": 1 - core}
    near, far = groups_of(blocks)
    inner, outer = lax.rem(me, near), lax.div(me, near)

    def near_peer(offset):
        return lax.rem(inner + offset, near)

    def far_peer(offset):
        return lax.rem(outer + offset, far)

    def near_device(offset):
        return {"tok": outer * near + near_peer(offset)}

    def far_device(offset):
        return {"tok": far_peer(offset) * near + inner}

    def each(count, work):
        def run(offset, carry):
            work(offset)
            return carry

        lax.fori_loop(1, count, run, 0)

    enc_load = pltpu.make_async_copy(enc_in, enc, load_sem.at[0])
    dec_load = pltpu.make_async_copy(dec_in, dec, load_sem.at[1])
    enc_load.start()
    dec_load.start()
    barrier = pltpu.get_barrier_semaphore()
    pl.semaphore_signal(barrier, inc=1, device_id=sibling, device_id_type=MESH)
    for count, device in ((near, near_device), (far, far_device)):
        each(
            count,
            lambda offset, device=device: pl.semaphore_signal(
                barrier, inc=1, device_id=device(offset), device_id_type=MESH
            ),
        )
    enc_load.wait()
    dec_load.wait()
    channels = layout.channels
    e_up, e_down, (e_q, e_k, e_v), e_out, e_vec, e_bias = sum_views(enc, channels, True)
    d_up, d_down, (d_q,), d_out, d_vec, d_bias = sum_views(dec, channels, False)

    def fill_enc(buffer, kv):
        fill(buffer, layout, e_up, e_down, e_q, e_out, kv, e_bias, e_vec)

    def fill_dec(buffer, kv):
        fill(buffer, layout, d_up, d_down, d_q, d_out, kv, d_bias, d_vec)

    pl.when(core == 0)(lambda: fill_dec(theirs, e_v))
    pl.when(core == 1)(lambda: fill_enc(theirs, e_k))
    pl.semaphore_wait(barrier, near + far - 1)

    def to_sibling(source, target, k):
        return pltpu.make_async_remote_copy(
            src_ref=source, dst_ref=target, send_sem=sib_send.at[k], recv_sem=sib_recv.at[k],
            device_id=sibling, device_id_type=MESH,
        )

    def piece_rows(p):
        return slice(layout.starts[p], layout.starts[p] + layout.chunks[p] * blocks)

    swaps = [to_sibling(theirs.at[piece_rows(p)], from_sib.at[piece_rows(p)], p) for p in range(2)]
    start_all(swaps)
    pl.when(core == 0)(lambda: fill_enc(own, e_k))
    pl.when(core == 1)(lambda: fill_dec(own, e_v))

    def quarter_of(p, position):
        size = far * layout.chunks[p]
        return pl.ds(pl.multiple_of(layout.starts[p] + position * size, 16), size)

    def chunk_of(p, position):
        return pl.ds(pl.multiple_of(position * layout.chunks[p], 16), layout.chunks[p])

    def rows_of(p, position):
        start = layout.starts[p] + (inner * far + position) * layout.chunks[p]
        return pl.ds(pl.multiple_of(start, 16), layout.chunks[p])

    def exchange(p, stage, offset, source, target, device):
        return pltpu.make_async_remote_copy(
            src_ref=source, dst_ref=target,
            send_sem=send_sem.at[p, stage, offset], recv_sem=recv_sem.at[p, stage, offset],
            device_id=device(offset), device_id_type=MESH,
        )

    def near_scatter(p, offset):
        source = low.at[quarter_of(p, near_peer(offset))]
        return exchange(p, 0, offset, source, landed[p].at[offset], near_device)

    def far_scatter(p, offset):
        source = near_low[p].at[chunk_of(p, far_peer(offset))]
        return exchange(p, 1, offset, source, far_landed[p].at[offset], far_device)

    def far_gather(p, offset, owner):
        rows = rows_of(p, owner)
        return exchange(p, 2, offset, total.at[rows], total.at[rows], far_device)

    def near_gather(p, offset, owner):
        rows = quarter_of(p, owner)
        return exchange(p, 3, offset, total.at[rows], total.at[rows], near_device)

    def reduced(count, copy, landing, start):
        def add(offset, carry):
            copy(offset).wait_recv()
            return carry + landing[offset].astype(F32)

        return lax.fori_loop(1, count, add, start)

    def send_near(p):
        swaps[p].wait()
        rows = piece_rows(p)
        own[rows] += from_sib[rows].astype(F32)
        low[rows] = own[rows].astype(BF16)
        each(near, lambda offset: near_scatter(p, offset).start())

    def send_far(p):
        rows = quarter_of(p, inner)
        near_sum = reduced(near, lambda o: near_scatter(p, o), landed[p], own[rows])
        own[rows] = near_sum
        near_low[p][...] = near_sum.astype(BF16)
        each(far, lambda offset: far_scatter(p, offset).start())

    def return_far(p):
        rows = rows_of(p, outer)
        far_sum = reduced(far, lambda o: far_scatter(p, o), far_landed[p], own[rows])
        total[rows] = far_sum.astype(BF16)
        each(far, lambda offset: far_gather(p, offset, outer).start())

    def return_near(p):
        each(far, lambda o: far_gather(p, o, lax.rem(outer + far - o, far)).wait_recv())
        each(near, lambda offset: near_gather(p, offset, inner).start())

    def arrive(p):
        each(near, lambda o: near_gather(p, o, lax.rem(inner + near - o, near)).wait_recv())

    send_near(0)
    send_near(1)
    send_far(0)
    return_far(0)
    send_far(1)
    return_near(0)
    return_far(1)
    return_near(1)
    arrive(0)
    arrive(1)
    third = to_sibling(total.at[layout.kv : layout.kv + 2 * layout.tall], sib_kv, 2)
    third.start()
    total_out[...] = total[...]
    for p in range(2):
        each(near, lambda offset, p=p: near_scatter(p, offset).wait_send())
        each(far, lambda offset, p=p: far_scatter(p, offset).wait_send())
        each(far, lambda offset, p=p: far_gather(p, offset, outer).wait_send())
        each(near, lambda offset, p=p: near_gather(p, offset, inner).wait_send())
    third.wait()
    kv_out[...] = sib_kv[...]


def run_sum(enc_sums, dec_sums, layout, blocks):
    rows, tall = layout.rows, layout.tall
    near, far = groups_of(blocks)
    dma = pltpu.SemaphoreType.DMA
    vmem = pl.BlockSpec(memory_space=pltpu.VMEM)
    args = [enc_sums, dec_sums]

    def buffers(*shape):
        return [pltpu.VMEM((*shape, far * c, LANES_A), BF16) for c in layout.chunks]

    return pl.pallas_call(
        functools.partial(sum_gradients, layout, blocks),
        in_specs=[pl.BlockSpec(memory_space=pl.ANY)] * len(args),
        out_specs=[vmem] * 2,
        out_shape=[
            jax.ShapeDtypeStruct((rows, LANES_A), BF16),
            jax.ShapeDtypeStruct((2 * tall, LANES_A), BF16),
        ],
        scratch_shapes=[
            *[pltpu.VMEM(a.shape, F32) for a in args],
            pltpu.VMEM((rows, LANES_A), F32),
            *[pltpu.VMEM((rows, LANES_A), BF16)] * 4,
            pltpu.VMEM((2 * tall, LANES_A), BF16),
            *buffers(near),
            *buffers(),
            *[pltpu.VMEM((far, c, LANES_A), BF16) for c in layout.chunks],
            dma((2,)),
            dma((3,)),
            dma((3,)),
            *[dma((2, 4, max(near, far)))] * 2,
        ],
        compiler_params=pltpu.CompilerParams(
            collective_id=0, has_side_effects=True, vmem_limit_bytes=VMEM_BYTES
        ),
        name="sum_gradients",
    )(*args)


def finish(layout, batches, returns, core_ref, total, sib_kv, *refs):
    returned, refs = refs[:returns], refs[returns + 1 :]
    (
        ends, ln1_gain, ln1_bias, q_weight, q_bias, kv_weight, v_bias, out_weight, out_bias, table,
        ln2_gain, ln2_bias, up_weight, up_bias, down_weight, down_bias, placed, copy_sem,
    ) = refs
    is_encoder = core_ref[0] == 0
    step = pl.program_id(0)

    def copies():
        return [
            pltpu.make_async_copy(
                ref,
                ends.at[batches - returns + k, pl.ds(WIN, WIN), pl.ds(step * WIN, WIN)],
                copy_sem.at[k],
            )
            for k, ref in enumerate(returned)
        ]

    pl.when(is_encoder)(lambda: start_all(copies()))

    @pl.when(step == 0)
    def _():
        unpack(
            layout, is_encoder, total, sib_kv, ln1_gain, ln1_bias, q_weight, q_bias, kv_weight,
            v_bias, out_weight, out_bias, table, ln2_gain, ln2_bias, up_weight, up_bias, down_weight,
            down_bias, placed,
        )

    pl.when(is_encoder)(lambda: wait_all(copies()))


def unpack(
    layout, is_encoder, total, sib_kv, ln1_gain, ln1_bias, q_weight, q_bias, kv_weight,
    v_bias, out_weight, out_bias, table, ln2_gain, ln2_bias, up_weight, up_bias, down_weight, down_bias,
    placed,
):
    channels, tall, half = layout.channels, layout.tall, LANES_A // 2

    def at(start, rows):
        return total[start : start + rows].astype(F32)

    vec = at(layout.vec, 16)
    vec = jnp.concatenate([vec[:8], vec[8:, :half]], 1)
    for row, ref in enumerate((ln1_gain, ln1_bias, ln2_gain, ln2_bias, down_bias)):
        ref[...] = vec[row : row + 1]

    for k in range(layout.tiles):
        cols = slice(k * LANES_A, (k + 1) * LANES_A)
        tile = at(layout.up + k * tall, tall)
        up_weight[:, cols] = tile[:channels]
        up_bias[:, cols] = tile[channels : channels + 1]
        down_weight[:, cols] = at(layout.down + k * channels, channels)
    rest = at(layout.rest, tall)
    q = jnp.concatenate([at(layout.q, tall), rest[:, :half]], 1)
    out = jnp.concatenate([at(layout.out, tall), rest[:, half:]], 1)
    q_weight[...] = q[:channels]
    q_bias[...] = q[channels : channels + 1]
    out_weight[...] = out[:channels]
    out_bias[...] = out[channels : channels + 1]
    mine = at(layout.kv, 2 * tall)
    other = sib_kv[...].astype(F32)
    for start, side in ((0, jnp.where(is_encoder, mine, other)), (channels, jnp.where(is_encoder, other, mine))):
        side = jnp.concatenate([side[:tall], side[tall:, :half]], 1)
        kv_weight[:, start : start + channels] = side[:channels]
    v_bias[...] = side[channels : channels + 1]
    placed[...] = jnp.zeros_like(placed)
    positions = [position_matrix(False), position_matrix(True)]
    for h in range(HEADS):
        start = layout.bias + h // 2 * CELLS
        placed[h, :, :256] = nt(total[start : start + CELLS], positions[h % 2])
    entries = jnp.zeros((8, 384), F32)
    for j in range(CELLS):
        entries += pltpu.roll(placed[:, j, :], CENTRE - cell_position(j), 1)
    table[...] = entries[:HEADS, : SPAN**3][:, None]


def run_finish(core, total, sib_kv, returned, ends, layout):
    channels = layout.channels
    hidden = layout.tiles * LANES_A
    _, _, rows_y, rows_z, _ = ends.shape
    any_spec = pl.BlockSpec(memory_space=pl.ANY)
    shapes = [
        (1, channels), (1, channels), (channels, channels), (1, channels), (channels, 2 * channels),
        (1, channels), (channels, channels), (1, channels), (HEADS, 1, SPAN**3),
        (1, channels), (1, channels), (channels, hidden), (1, hidden), (channels, hidden), (1, channels),
    ]
    shapes = [jax.ShapeDtypeStruct(shape, F32) for shape in shapes]
    return pl.pallas_call(
        functools.partial(finish, layout, ends.shape[0], len(returned)),
        grid_spec=pltpu.PrefetchScalarGridSpec(
            num_scalar_prefetch=1,
            grid=(rows_y // WIN,),
            in_specs=[
                *[whole(a) for a in (total, sib_kv)],
                *[
                    pl.BlockSpec(
                        (WIN, WIN, rows_z, channels), lambda i, c: (0, i * (1 - c[0]), 0, 0)
                    )
                ]
                * len(returned),
                any_spec,
            ],
            out_specs=[any_spec, *[whole(a) for a in shapes]],
            scratch_shapes=[
                pltpu.VMEM((8, CELLS, 384), F32),
                pltpu.SemaphoreType.DMA((len(returned),)),
            ],
        ),
        out_shape=[jax.ShapeDtypeStruct(ends.shape, F32), *shapes],
        input_output_aliases={3 + len(returned): 0},
        compiler_params=params,
        name="finish",
    )(core, total, sib_kv, *returned, ends)


def cell_position(ids):
    x = 2 * (ids // 32) + ids // 4 % 2
    y = 2 * (ids // 16 % 2) + ids // 2 % 2
    z = 2 * (ids // 8 % 2) + ids % 2
    return (x * SPAN + y) * SPAN + z


CENTRE = (WIN - 1) * (SPAN * SPAN + SPAN + 1)
TABLE_ROW = 8


def position_matrix(odd):
    rows = lax.broadcasted_iota(jnp.int32, (256, 2 * CELLS), 0)
    ids = lax.broadcasted_iota(jnp.int32, (256, 2 * CELLS), 1) - (CELLS if odd else 0)
    hit = (ids >= 0) & (ids < CELLS) & (rows == cell_position(ids))
    return jnp.where(hit, 1.0, 0.0).astype(BF16)


def spread_bias(table, shifted):
    for j in range(CELLS):
        turned = pltpu.roll(table, (384 - CENTRE + cell_position(j)) % 384, 1)
        for h in range(HEADS):
            shifted[h, j : j + 1] = turned[h : h + 1, :256]
    even, odd = position_matrix(False), position_matrix(True)
    pairs = [
        nn(shifted[2 * p].astype(BF16), even) + nn(shifted[2 * p + 1].astype(BF16), odd)
        for p in range(HEADS // 2)
    ]
    return jnp.concatenate(pairs, 1) * log2_e


def prepare(
    blocks, q_w, out_w, up_w, down_w, kv_w, v_b, ln1_g, ln1_b, ln2_g, ln2_b, out_b, down_b, q_b, up_b, table,
    weights_e, vectors_e, bias_e, weights_d, vectors_d, bias_d,
    small, small_sib, q_sib, out_sib, up_sib, down_sib, shifted, send_sem, recv_sem,
):
    core, block = lax.axis_index("section"), lax.axis_index("tok")
    channels, hidden = up_w.shape
    sibling = {"section": 1 - core}
    barrier = pltpu.get_barrier_semaphore()
    pl.semaphore_signal(barrier, inc=1, device_id=sibling, device_id_type=MESH)
    small[...] = jnp.zeros_like(small)
    for row, ref in enumerate((ln1_g, ln1_b, ln2_g, ln2_b, out_b, down_b, q_b)):
        small[row : row + 1, :channels] = ref[...].astype(F32)
    small[7:8, :hidden] = up_b[...].astype(F32)
    small[TABLE_ROW : TABLE_ROW + HEADS, : SPAN**3] = table[...].astype(F32)
    pl.semaphore_wait(barrier, 1)
    pairs = ((small, small_sib), (q_w, q_sib), (out_w, out_sib), (up_w, up_sib), (down_w, down_sib))
    copies = [
        pltpu.make_async_remote_copy(
            src_ref=source, dst_ref=target, send_sem=send_sem.at[k], recv_sem=recv_sem.at[k],
            device_id=sibling, device_id_type=MESH,
        )
        for k, (source, target) in enumerate(pairs)
    ]
    for copy in copies:
        copy.start()
    for copy in copies:
        copy.wait()

    def place(enc, dec):
        e_small, d_small = enc[0], dec[0]
        for weights, vectors, (source, q, out, up, down) in (
            (weights_e, vectors_e, enc), (weights_d, vectors_d, dec),
        ):
            weights[2 * channels :] = jnp.zeros((2 * channels, hidden), BF16)
            weights[:channels] = up[...]
            weights[channels : 2 * channels] = down[...]
            weights[2 * channels : 3 * channels, :channels] = q[...]
            weights[3 * channels :, :channels] = out[...]
            vectors[...] = jnp.zeros_like(vectors)
            vectors[:8, :channels] = source[:8, :channels]
            vectors[8:9, :hidden] = source[7:8, :hidden]
            vectors[9:10, :channels] = source[6:7, :channels]
        weights_e[2 * channels : 3 * channels, 256 : 256 + channels] = kv_w[:, :channels]
        weights_e[2 * channels : 3 * channels, 512 : 512 + channels] = kv_w[:, channels:]
        vectors_e[9:10, 512 : 512 + channels] = v_b[...].astype(F32)[None]
        rows = slice(TABLE_ROW, TABLE_ROW + 8)
        bias_e[...] = spread_bias(e_small[rows, :384], shifted)
        return spread_bias(d_small[rows, :384], shifted)

    own = (small, q_w, out_w, up_w, down_w)
    sib = (small_sib, q_sib, out_sib, up_sib, down_sib)

    def masked(base):
        shape = (CELLS, HEADS * CELLS)
        keys = lax.broadcasted_iota(jnp.int32, shape, 0)
        queries = lax.broadcasted_iota(jnp.int32, shape, 1) % CELLS

        def differ(unit):
            return jnp.where(keys // unit % 2 != queries // unit % 2, 1.0, 0.0)

        last = jnp.where((core == 1) & (block == blocks - 1), 1.0, 0.0)
        for y in range(2):
            for z in range(2):
                apart = jnp.maximum(last * differ(32), jnp.maximum(y * differ(16), z * differ(8)))
                bias_d[y, z] = base + apart * (mask_fill * log2_e)

    @pl.when(core == 0)
    def _():
        masked(place(own, sib))

    @pl.when(core == 1)
    def _():
        masked(place(sib, own))


def run_prepare(blocks, weights, smalls, table, kv_weight, v_bias):
    q_w, out_w, up_w, down_w = weights
    channels, hidden = up_w.shape
    vmem = pl.BlockSpec(memory_space=pltpu.VMEM)
    args = [*weights, kv_weight, v_bias, *smalls, table]
    bias = (CELLS, HEADS * CELLS)
    square = (channels, channels)
    layer = [
        jax.ShapeDtypeStruct((4 * channels, hidden), BF16),
        jax.ShapeDtypeStruct((16, hidden), F32),
    ]
    shapes = [
        *layer,
        jax.ShapeDtypeStruct(bias, F32),
        *layer,
        jax.ShapeDtypeStruct((2, 2, *bias), F32),
    ]
    return pl.pallas_call(
        functools.partial(prepare, blocks),
        in_specs=[vmem] * len(args),
        out_specs=[vmem] * len(shapes),
        out_shape=shapes,
        scratch_shapes=[
            pltpu.VMEM((TABLE_ROW + 8, hidden), F32),
            pltpu.VMEM((TABLE_ROW + 8, hidden), F32),
            pltpu.VMEM(square, BF16),
            pltpu.VMEM(square, BF16),
            pltpu.VMEM((channels, hidden), BF16),
            pltpu.VMEM((channels, hidden), BF16),
            pltpu.VMEM((HEADS, CELLS, 256), F32),
            pltpu.SemaphoreType.DMA((5,)),
            pltpu.SemaphoreType.DMA((5,)),
        ],
        compiler_params=pltpu.CompilerParams(
            collective_id=1, has_side_effects=True, vmem_limit_bytes=VMEM_BYTES
        ),
        name="prepare",
    )(*args)


def run_encoder(core, tokens, batch, consts, cotangent):
    _, _, rows_y, rows_z, channels = tokens.shape
    groups, size = rows_y // WIN, 4 * rows_z
    cells = 4 * size
    hidden = consts[1].shape[1]
    slab = jax.ShapeDtypeStruct((groups, 2, 3, size * 3 // 2, LANES_A), BF16)
    outs = [
        slab,
        slab,
        jax.ShapeDtypeStruct((groups, cells, 512), F32),
        jax.ShapeDtypeStruct((groups, cells, 2 * hidden + HEADS * CELLS + 256), BF16),
    ]

    def row(array):
        zeros = (0,) * (array.ndim - 1)
        return pl.BlockSpec((1, *array.shape[1:]), lambda i, c: (i, *zeros))

    batches = tokens.shape[0]
    cut = [] if cotangent is None else [cotangent]
    cut_block = (batches, SHIFT, WIN, rows_z, channels)
    cut_outs = [
        jax.ShapeDtypeStruct((batches, SHIFT, rows_y, rows_z, channels), a.dtype) for a in cut
    ]
    return pl.pallas_call(
        functools.partial(encoder_forward, len(cut)),
        grid_spec=pltpu.PrefetchScalarGridSpec(
            num_scalar_prefetch=1,
            grid=(groups,),
            in_specs=[
                pl.BlockSpec(
                    (1, WIN, WIN, rows_z, channels), lambda i, c: (batch, c[0], i, 0, 0)
                ),
                *[whole(a) for a in consts],
                *[pl.BlockSpec(cut_block, lambda i, c: (0, 2 * c[0], i, 0, 0)) for _ in cut],
            ],
            out_specs=[
                *[row(a) for a in outs],
                *[pl.BlockSpec(cut_block, lambda i, c: (0, 0, i, 0, 0)) for _ in cut],
            ],
            scratch_shapes=[pltpu.VMEM((cells, 768), BF16)],
        ),
        out_shape=[*outs, *cut_outs],
        compiler_params=params,
        cost_estimate=cost(groups * cells, 466944, groups * cells * 7500),
        name="encoder_forward",
    )(core, tokens, *consts, *cut)


def run_encoder_back(core, batch, own, halo, ys, returned, saved, old, consts, tokens):
    groups, _, _, packed, _ = own.shape
    batches, planes, rows_y, rows_z, channels = tokens.shape
    size = 4 * rows_z
    hidden = consts[1].shape[1]
    first = old is None
    sums = jax.ShapeDtypeStruct((sum_rows(channels, True), hidden), F32)
    outs = [
        jax.ShapeDtypeStruct(tokens.shape, F32),
        jax.ShapeDtypeStruct((WIN, rows_y, rows_z, channels), F32),
        sums,
    ]

    def slab(unit):
        def place(i, c):
            return ((i if unit == 0 else (i + groups - 1) % groups), unit, 0, 0, 0)

        return pl.BlockSpec((1, 1, 3, packed, LANES_A), place)

    def row(array):
        zeros = (0,) * (array.ndim - 1)
        return pl.BlockSpec((1, *array.shape[1:]), lambda i, c: (i, *zeros))

    def for_core(core, planes_here):
        def place(i, c):
            return (0, i * (c[0] if core == 1 else 1 - c[0]), 0, 0)

        return pl.BlockSpec((planes_here, WIN, rows_z, channels), place)

    any_spec = pl.BlockSpec(memory_space=pl.ANY)
    olds = [] if first else [old[1], old[0]]
    args = [core, *consts, *ys, own, own, halo, halo, *saved, *returned, *olds]
    return pl.pallas_call(
        functools.partial(encoder_backward, first, batch, len(returned)),
        grid_spec=pltpu.PrefetchScalarGridSpec(
            num_scalar_prefetch=1,
            grid=(groups,),
            in_specs=[
                *[whole(a) for a in consts],
                *[for_core(1, n) for n in (2, 2, 4)],
                slab(0),
                slab(1),
                slab(0),
                slab(1),
                *[row(a) for a in saved],
                *[for_core(0, WIN)] * len(returned),
                *[whole(a) for a in olds[:-1]],
                *[any_spec] * (0 if first else 1),
            ],
            out_specs=[any_spec, any_spec, whole(sums)],
            scratch_shapes=[
                pltpu.VMEM((4 * size, 768), BF16),
                pltpu.VMEM((3, 4 * size, channels), BF16),
                pltpu.VMEM((2, WIN, WIN, rows_z, channels), F32),
                pltpu.SemaphoreType.DMA((2,)),
                pltpu.SemaphoreType.DMA((8 + batches,)),
            ],
        ),
        out_shape=outs,
        input_output_aliases={} if first else {len(args) - 1: 0},
        compiler_params=params,
        cost_estimate=cost(groups * 4 * size, 933888, groups * 4 * size * 9000),
        name="encoder_backward",
    )(*args)


def run_decoder(core, keep, recv, cotangent, cot_recv, batch, old, consts):
    groups, _, _, packed, _ = keep.shape
    rows_z, channels = cotangent.shape[3:]
    size = 4 * rows_z
    hidden = consts[1].shape[1]
    first = old is None
    sums = jax.ShapeDtypeStruct((sum_rows(channels, False), hidden), F32)
    slab_shape = jax.ShapeDtypeStruct((groups, 2, 3, packed, LANES_A), BF16)
    outs = [
        *[jax.ShapeDtypeStruct((n, groups * WIN, rows_z, channels), F32) for n in (4, 2)],
        slab_shape,
        slab_shape,
        sums,
    ]

    def slab(unit):
        def place(i, c):
            return ((i if unit == 1 else (i + 1) % groups), unit, 0, 0, 0)

        return pl.BlockSpec((1, 1, 3, packed, LANES_A), place)

    def cot(unit, own):
        def place(i, c):
            y = 2 * i + 1 if unit == 1 else (2 * i + 2) % (2 * groups)
            return (batch, 2 * c[0] + 1 if own else 0, y, 0, 0)

        return pl.BlockSpec((1, 2, 2, rows_z, channels), place)

    def bias_place(i, c):
        return (i // (groups - 1), 0, 0, 0)

    specs = [whole(a) for a in consts]
    specs[3] = pl.BlockSpec((1, *consts[3].shape[1:]), bias_place)
    olds = [] if first else [old]
    out_slab = pl.BlockSpec((1, 2, 3, packed, LANES_A), lambda i, c: (i, 0, 0, 0, 0))
    return pl.pallas_call(
        functools.partial(decoder, first),
        grid_spec=pltpu.PrefetchScalarGridSpec(
            num_scalar_prefetch=1,
            grid=(groups,),
            in_specs=[
                *specs,
                slab(1),
                slab(0),
                slab(1),
                slab(0),
                cot(1, True),
                cot(0, True),
                cot(1, False),
                cot(0, False),
                *[whole(a) for a in olds],
            ],
            out_specs=[
                *[pl.BlockSpec((n, WIN, rows_z, channels), lambda i, c: (0, i, 0, 0)) for n in (4, 2)],
                out_slab,
                out_slab,
                whole(sums),
            ],
            scratch_shapes=[
                pltpu.VMEM((4 * size, hidden), BF16),
                pltpu.VMEM((4 * size, hidden), F32),
            ],
        ),
        out_shape=outs,
        compiler_params=params,
        cost_estimate=cost(groups * 4 * size, 1253376, groups * 4 * size * 4000),
        name="decoder",
    )(core, *consts, keep, keep, recv, recv, cotangent, cotangent, cot_recv, cot_recv, *olds)


def body(
    tokens,
    cotangent,
    ln1_gain,
    ln1_bias,
    q_weight,
    q_bias,
    kv_weight,
    v_bias,
    out_weight,
    out_bias,
    rel_table,
    ln2_gain,
    ln2_bias,
    up_weight,
    up_bias,
    down_weight,
    down_bias,
):
    batches, planes, rows_y, rows_z, channels = tokens.shape
    axes = ("section", "tok")
    core = lax.axis_index("section")
    block = lax.axis_index("tok")
    blocks = lax.axis_size("tok")
    is_encoder = core == 0
    core_arg = core.astype(jnp.int32).reshape(1)

    def device(position):
        position = position % (2 * blocks)
        return (position % 2) * blocks + position // 2

    to_previous = [(device(r), device(r - 1)) for r in range(2 * blocks)]
    to_next = [(device(r), device(r + 1)) for r in range(2 * blocks)]

    weights_e, vectors_e, bias_e, weights_d, vectors_d, bias_d = run_prepare(
        blocks,
        (q_weight[0], out_weight[0], up_weight[0], down_weight[0].T),
        (ln1_gain, ln1_bias, ln2_gain, ln2_bias, out_bias, down_bias, q_bias, up_bias),
        rel_table[0],
        kv_weight,
        v_bias,
    )
    order = jnp.asarray(order_matrix(rows_z, 0), BF16)
    order_rolled = jnp.asarray(order_matrix(rows_z, 1), BF16)

    enc_consts = (order, weights_e, vectors_e, bias_e)
    enc_back_consts = (order, weights_e, vectors_e)
    dec_consts = (order_rolled, weights_d, vectors_d, bias_d)

    handed, saved = [], []
    for batch in range(batches):
        send, keep, *rest = run_encoder(
            core_arg, tokens, batch, enc_consts, cotangent if batch == 0 else None
        )
        if batch == 0:
            *rest, half = rest
            cot_recv = lax.ppermute(half, axes, to_previous)
        handed.append((keep, lax.ppermute(send, axes, to_previous)))
        saved.append(rest)
    dec_sums = None
    returned, ys = [], []
    to_decoder = [(t, blocks + t) for t in range(blocks)]
    to_encoder = [(blocks + t, t) for t in range(blocks)]
    to_after = [(blocks + t, blocks + (t + 1) % blocks) for t in range(blocks)]
    for batch in range(batches):
        out_all, out_tail, own, halo, dec_sums = run_decoder(
            core_arg, *handed[batch], cotangent, cot_recv, batch, dec_sums, dec_consts
        )
        returned.append((own, lax.ppermute(halo, axes, to_next)))
        y_halo = lax.ppermute(out_tail, axes, to_after)
        ys.append((out_all, y_halo, lax.ppermute(out_all, axes, to_decoder)))
    old = None
    backs = []
    for batch in range(batches):
        arrived = backs[:1] if batch == batches - 1 else []
        ends, back, enc_sums = run_encoder_back(
            core_arg, batch, *returned[batch], ys[batch], arrived, saved[batch], old,
            enc_back_consts, tokens,
        )
        old = (ends, enc_sums)
        backs.append(lax.ppermute(back, axes, to_encoder))

    layout = Layout(channels, up_weight.shape[2], blocks)
    total, sib_kv = run_sum(enc_sums, dec_sums, layout, blocks)
    (
        ends, g_ln1_gain, g_ln1_bias, g_q_weight, g_q_bias, g_kv_weight, g_v_bias, g_out_weight,
        g_out_bias, g_table, g_ln2_gain, g_ln2_bias, g_up_weight, g_up_bias, g_down_weight, g_down_bias,
    ) = run_finish(core_arg, total, sib_kv, backs[1:], ends, layout)
    return (
        ends[None],
        g_ln1_gain,
        g_ln1_bias,
        g_q_weight[None],
        g_q_bias,
        g_kv_weight[None],
        g_v_bias,
        g_out_weight[None],
        g_out_bias,
        g_table.transpose(1, 0, 2),
        g_ln2_gain,
        g_ln2_bias,
        g_up_weight[None],
        g_up_bias,
        g_down_weight.T[None],
        g_down_bias,
    )


def solution(mesh):
    in_specs = (
        P(None, "tok", None, None, None),
        P(None, "tok", None, None, None),
        P("section", None),
        P("section", None),
        P("section", None, None),
        P("section", None),
        P(),
        P(),
        P("section", None, None),
        P("section", None),
        P("section", None, None),
        P("section", None),
        P("section", None),
        P("section", None, None),
        P("section", None),
        P("section", None, None),
        P("section", None),
    )
    out_specs = (
        P("section", None, "tok", None, None, None),
        P("section", None),
        P("section", None),
        P("section", None, None),
        P("section", None),
        P("section", None, None),
        P("section", None),
        P("section", None, None),
        P("section", None),
        P("section", None, None),
        P("section", None),
        P("section", None),
        P("section", None, None),
        P("section", None),
        P("section", None, None),
        P("section", None),
    )
    return jax.shard_map(body, mesh=mesh, in_specs=in_specs, out_specs=out_specs, check_vma=False)
```
